256 devices in a mesh: gx: 32 (over z_hi, x, core), gy: 8 (over z_lo, y).
Axes of the slice: x: 4, y: 4, z: 8 (z_hi: 4, z_lo: 2; z = z_hi * 2 + z_lo), core: 2. Of those that a mesh axis runs over, the one named last changes fastest.
Arguments:
- displacement: float32 [3, 128, 256, 128], P(None, 'gx', 'gy'), may hold values from -4 to 4
- rhs: float32 [3, 128, 256, 128], P(None, 'gx', 'gy'), may hold values from -6 to 6
- labels: int32 [128, 256, 128], P('gx', 'gy'), may hold values from 0 to 7
- stiffness: float32 [8, 6], replicated, may hold values from -6 to 20, as said below
- rows: int32 [32, 8, 1024], P('gx', 'gy'), may hold values from 0 to 16383, as said below
- counts: int32 [32, 8], P('gx', 'gy'), may hold values from 128 to 1024, as said below
- multipliers: float32 [3, 32, 8, 1024], P(None, 'gx', 'gy'), may hold values from -6 to 6
Outputs:
- smoothed: float32 [3, 128, 256, 128], P(None, 'gx', 'gy')
- coarse: float32 [3, 64, 128, 64], P(None, 'gx')
- updated: float32 [3, 32, 8, 1024], P(None, 'gx', 'gy')
The draws below stay inside these ranges and needn't reach their ends.
Inputs may be any that keep to these rules, and one draw needn't show every extreme that they name: `rows`: each block's 1024 entries are distinct cell numbers (x * 32 + y) * 128 + z of that block. `counts`: some block has all 1024 slots live in every draw. `stiffness`: diagonal entries are positive; each off-diagonal entry is at most 0.3 times the geometric mean of its two diagonal entries.
All inputs are finite; a program needn't handle non-finite values.
Results may differ from the reference program's by a relative error of at most 0.00002.
Values sent between devices are 32-bit elements; how exact they have to be, the bound alone decides.
No kernel may reach another device: no remote copies, remote signals or barrier semaphores. Data moves between devices by JAX's collectives and lax.ppermute only.
A program may use at most 192 MiB of HBM per device.

```python
import math
import jax
import jax.numpy as jnp

CX = 4
CY = 32
NZ = 128
IB = 1024
LABELS = 8
NX = 128
NY = 256
N_GX = 32
N_GY = 8


def draw_stiffness(key, part):
    key = jax.random.fold_in(key, 13)
    first_key, second_key = jax.random.split(key)
    diagonal = jnp.exp(jax.random.uniform(first_key, (LABELS, 3), jnp.float32, 0.0, math.log(10.0)))
    coupling = jax.random.uniform(second_key, (LABELS, 3), jnp.float32, -0.3, 0.3)
    means = jnp.stack([jnp.sqrt(diagonal[:, 0] * diagonal[:, 1]), jnp.sqrt(diagonal[:, 0] * diagonal[:, 2]), jnp.sqrt(diagonal[:, 1] * diagonal[:, 2])], axis=1)
    return jnp.concatenate([diagonal, coupling * means], axis=1).astype(jnp.float32)


def draw_rows(key, part):
    key = jax.random.fold_in(key, 11)
    volume = CX * CY * NZ
    blocks = N_GX * N_GY
    scores = jax.random.randint(key, (blocks, volume), 0, max(2 ** 30 // volume, 1))
    ranking = jnp.argsort(scores * volume + jnp.arange(volume, dtype=jnp.int32)[None, :], axis=1)
    return ranking[:, :IB].reshape(N_GX, N_GY, IB).astype(jnp.int32)


def draw_counts(key, part):
    key = jax.random.fold_in(key, 12)
    first_key, second_key = jax.random.split(key)
    blocks = N_GX * N_GY
    halving = jax.random.randint(first_key, (blocks,), 0, 4)
    values = jnp.right_shift(jnp.full((blocks,), IB, jnp.int32), halving)
    chosen = jax.random.randint(second_key, (), 0, blocks)
    values = jnp.where(jnp.arange(blocks, dtype=jnp.int32) == chosen, IB, values)
    return values.reshape(N_GX, N_GY).astype(jnp.int32)


def plant(array, stream_key, least, high):
    spot = [jax.random.randint(jax.random.fold_in(stream_key, axis), (), 0, length) for axis, length in enumerate(array.shape)]
    longest = array.shape.index(max(array.shape))
    next_to = spot[:longest] + [(spot[longest] + 1) % array.shape[longest]] + spot[longest + 1:]
    return array.at[tuple(spot)].set(least).at[tuple(next_to)].set(high)


def steps_of(stream_key, extent, cuts, low, top_value):
    def one(axis_at, blocks):
        steps = jax.random.uniform(jax.random.fold_in(jax.random.fold_in(stream_key, 6), axis_at), (blocks,), jnp.float32, low / len(cuts), top_value / len(cuts))
        return jnp.repeat(jnp.exp(steps), extent[axis_at] // blocks).reshape((-1,) + (1,) * (len(extent) - axis_at - 1))

    gain = one(*cuts[0])
    for cut in cuts[1:]:
        gain = gain * one(*cut)
    return gain


def centred(key, dims, spread, most, pieces=(), kind=jnp.bfloat16):
    values = spread * jax.random.normal(key, dims, jnp.float32)
    if pieces:
        values = values * steps_of(key, dims, pieces, -0.22, 0.18)
    return jnp.clip(values, -most, most).astype(kind)


def setup_inputs(seed: int = 0) -> dict:
    streams_of = jax.random.split(jax.random.key(seed), 8)
    displacement = centred(streams_of[0], (3, NX, NY, NZ), 0.5, 4.0, ((1, 32), (2, 8)), jnp.float32)
    rhs = centred(streams_of[1], (3, NX, NY, NZ), 1.0, 6.0, ((1, 32), (2, 8)), jnp.float32)
    labels = plant(jax.random.randint(streams_of[2], (NX, NY, NZ), 0, LABELS), jax.random.fold_in(streams_of[2], 1), 0, LABELS - 1).astype(jnp.int32)
    stiffness = draw_stiffness(jax.random.fold_in(streams_of[7], 71), 0)
    rows = draw_rows(jax.random.fold_in(streams_of[7], 71), 0)
    counts = draw_counts(jax.random.fold_in(streams_of[7], 71), 0)
    multipliers = centred(streams_of[6], (3, N_GX, N_GY, IB), 1.0, 6.0, ((1, 32), (2, 8)), jnp.float32)
    return {"displacement": displacement, "rhs": rhs, "labels": labels, "stiffness": stiffness, "rows": rows, "counts": counts, "multipliers": multipliers}


SYMMETRIC_INDEX = ((0, 3, 4), (3, 1, 5), (4, 5, 2))
OFFSET_WEIGHTS = (0.0, 1.0, 0.5, 0.25)
DAMPING = 0.6
MASS_SHIFT = 1.0
PENALTY = 1.0


def coefficient_field(padded_labels, stiffness):
    summed = jnp.zeros((6,) + padded_labels.shape, jnp.float32)
    for material in range(stiffness.shape[0]):
        indicator = jnp.where(padded_labels == material, 1.0, 0.0).astype(jnp.float32)
        summed = summed + indicator[None] * stiffness[material][:, None, None, None]
    return summed


def stencil(field_pad, coeff_pad):
    size_x = field_pad.shape[1] - 2
    size_y = field_pad.shape[2] - 2
    size_z = field_pad.shape[3] - 2
    centre = field_pad[:, 1:size_x + 1, 1:size_y + 1, 1:size_z + 1]
    coeff_centre = coeff_pad[:, 1:size_x + 1, 1:size_y + 1, 1:size_z + 1]
    totals = [jnp.zeros(centre.shape[1:], jnp.float32) for channel in range(3)]
    diagonal = jnp.zeros(centre.shape, jnp.float32)
    for step_x in (-1, 0, 1):
        for step_y in (-1, 0, 1):
            for step_z in (-1, 0, 1):
                reach = abs(step_x) + abs(step_y) + abs(step_z)
                if reach == 0:
                    continue
                weight = OFFSET_WEIGHTS[reach]
                neighbour = field_pad[:, 1 + step_x:1 + step_x + size_x, 1 + step_y:1 + step_y + size_y, 1 + step_z:1 + step_z + size_z]
                coeff_side = coeff_pad[:, 1 + step_x:1 + step_x + size_x, 1 + step_y:1 + step_y + size_y, 1 + step_z:1 + step_z + size_z]
                coupling = (0.5 * weight) * (coeff_centre + coeff_side)
                difference = centre - neighbour
                for channel in range(3):
                    entries = SYMMETRIC_INDEX[channel]
                    totals[channel] = totals[channel] + coupling[entries[0]] * difference[0] + coupling[entries[1]] * difference[1] + coupling[entries[2]] * difference[2]
                diagonal = diagonal + coupling[0:3]
    image = MASS_SHIFT * centre + jnp.stack(totals)
    return image, MASS_SHIFT + diagonal


def reference(displacement, rhs, labels, stiffness, rows, counts, multipliers):
    padding = ((0, 0), (1, 1), (1, 1), (1, 1))
    coeff_pad = coefficient_field(jnp.pad(labels, 1), stiffness)
    current = displacement
    for sweep_index in range(2):
        image, diagonal = stencil(jnp.pad(current, padding), coeff_pad)
        current = current + DAMPING * (rhs - image) / diagonal
    smoothed = current
    padded = jnp.pad(smoothed, padding)
    image, diagonal = stencil(padded, coeff_pad)
    block_x = jnp.arange(N_GX, dtype=jnp.int32)[:, None, None]
    block_y = jnp.arange(N_GY, dtype=jnp.int32)[None, :, None]
    plane_x = (rows // (CY * NZ) + block_x * CX).astype(jnp.int32)
    plane_y = ((rows // NZ) % CY + block_y * CY).astype(jnp.int32)
    plane_z = (rows % NZ).astype(jnp.int32)
    live = jnp.arange(IB, dtype=jnp.int32)[None, None, :] < counts[:, :, None]
    own = padded[:, plane_x + 1, plane_y + 1, plane_z + 1]
    partner = padded[:, plane_x + 2, plane_y + 1, plane_z + 1]
    updated = jnp.where(live[None], multipliers + PENALTY * (own - partner), multipliers)
    force = jnp.where(live[None], updated, jnp.float32(0.0))
    forces = jnp.zeros((3, NX + 1, NY, NZ), jnp.float32)
    forces = forces.at[:, plane_x, plane_y, plane_z].add(force)
    forces = forces.at[:, plane_x + 1, plane_y, plane_z].add(-force)
    residual = (rhs - image) - forces[:, :NX]
    coarse = residual.reshape(3, NX // 2, 2, NY // 2, 2, NZ // 2, 2).sum(axis=(2, 4, 6))
    return smoothed, coarse, updated
```

```python
import jax
import jax.numpy as jnp
from jax import lax
from jax.experimental import pallas as pl
from jax.experimental.pallas import tpu as pltpu
from jax.sharding import PartitionSpec as P

SYMMETRIC_INDEX = ((0, 3, 4), (3, 1, 5), (4, 5, 2))
DAMPING = 0.6
MASS_SHIFT = 1.0
PENALTY = 1.0

CX, CY, NZ, SLOTS = 4, 32, 128, 1024
N_GX, N_GY = 32, 8
NX, NY = CX * N_GX, CY * N_GY
LABELS = 8
HALO = 3
PX = CX + 2 * HALO
PR = PX - 2
ROWS = 40
LAB0 = 3 * PX
RHS0 = LAB0 + PX
FIELDS = RHS0 + 3 * PR
SIDE = (3 * HALO + HALO + 3 * (HALO - 1)) * CY
IFACE = SIDE
SLOT_ROWS = SLOTS // 128
UP_ROWS = SIDE + 5 * SLOT_ROWS
VMEM = pl.BlockSpec(memory_space=pltpu.VMEM)
SMEM = pl.BlockSpec(memory_space=pltpu.SMEM)
F32 = jnp.float32
BF16 = jnp.bfloat16
PARAMS = pltpu.CompilerParams(vmem_limit_bytes=48 * 1024 * 1024)


def f32(*shape):
    return jax.ShapeDtypeStruct(shape, F32)


def pieces_of(value):
    high = value.astype(BF16)
    rest = value - high.astype(F32)
    middle = rest.astype(BF16)
    low = (rest - middle.astype(F32)).astype(BF16)
    return (high, middle, low)


def pack_x(disp, rhs, labels, cells, counts, mult, up, down):
    for c in range(3):
        for k in range(HALO):
            up[pl.ds((c * HALO + k) * CY, CY), :] = disp[c, CX - HALO + k]
            down[pl.ds((c * HALO + k) * CY, CY), :] = disp[c, k]
        for k in range(HALO - 1):
            row = (4 * HALO + c * (HALO - 1) + k) * CY
            up[pl.ds(row, CY), :] = rhs[c, CX - HALO + 1 + k]
            down[pl.ds(row, CY), :] = rhs[c, k]
    for k in range(HALO):
        row = (3 * HALO + k) * CY
        up[pl.ds(row, CY), :] = labels[CX - HALO + k].astype(F32)
        down[pl.ds(row, CY), :] = labels[k].astype(F32)
    up[pl.ds(IFACE, SLOT_ROWS), :] = cells[...].astype(F32)
    for c in range(3):
        up[pl.ds(IFACE + (1 + c) * SLOT_ROWS, SLOT_ROWS), :] = mult[c]
    up[pl.ds(IFACE + 4 * SLOT_ROWS, SLOT_ROWS), :] = jnp.full(
        (SLOT_ROWS, 128), counts[0, 0].astype(F32), F32
    )


def spread(cells, live, mult, first, columns):
    column = cells // NZ - first
    depth = jnp.where(live, cells % NZ, -1)
    total = jnp.zeros((columns, 10 * NZ), F32)
    parts = [pieces_of(mult[c]) for c in range(3)]
    for j in range(SLOT_ROWS // 2):
        def pair(array):
            return jnp.concatenate([array[2 * j : 2 * j + 1], array[2 * j + 1 : 2 * j + 2]], axis=1)

        at_column = lax.broadcasted_iota(jnp.int32, (columns, 256), 0) == pair(column)
        at_depth = lax.broadcasted_iota(jnp.int32, (NZ, 256), 0) == pair(depth)
        left = jnp.where(at_column, 1.0, 0.0).astype(BF16)
        right = []
        for c in range(3):
            for piece in parts[c]:
                right.append(jnp.where(at_depth, pair(piece.astype(F32)), 0.0).astype(BF16))
        right.append(jnp.where(at_depth, 1.0, 0.0).astype(BF16))
        total = total + lax.dot_general(
            left, jnp.concatenate(right, axis=0), (((1,), (1,)), ((), ())), preferred_element_type=F32
        )
    out = []
    for c in range(3):
        at = 3 * c * NZ
        out.append(total[:, at : at + NZ] + total[:, at + NZ : at + 2 * NZ] + total[:, at + 2 * NZ : at + 3 * NZ])
    return out, total[:, 9 * NZ :]


def slot_number():
    return lax.broadcasted_iota(jnp.int32, (SLOT_ROWS, 128), 0) * 128 + lax.broadcasted_iota(
        jnp.int32, (SLOT_ROWS, 128), 1
    )


def spread_own(cells, counts, mult, dense):
    live = slot_number() < counts[0, 0]
    values, flags = spread(cells[...], live, mult, 0, CX * CY)
    for c in range(3):
        dense[c] = values[c]
    dense[3] = flags


def spread_before(received, dense):
    cells = received[pl.ds(IFACE, SLOT_ROWS), :].astype(jnp.int32)
    live = slot_number() < received[pl.ds(IFACE + 4 * SLOT_ROWS, SLOT_ROWS), :].astype(jnp.int32)
    mult = [received[pl.ds(IFACE + (1 + c) * SLOT_ROWS, SLOT_ROWS), :] for c in range(3)]
    values, flags = spread(cells, live, mult, (CX - 1) * CY, CY)
    present = jnp.where(lax.axis_index("gx") > 0, 1.0, 0.0).astype(F32)
    for c in range(3):
        dense[c] = values[c]
    dense[3] = flags * present


def inside_x():
    here = lax.axis_index("gx")
    return (
        jnp.where(here > 0, 1.0, 0.0).astype(F32),
        jnp.where(here < N_GX - 1, 1.0, 0.0).astype(F32),
    )


def pack_y(disp, rhs, labels, before, after, up, down):
    near, far = inside_x()
    for out, start in ((up, CY - HALO), (down, 0)):
        for k in range(HALO):
            y = start + k
            for c in range(3):
                at = c * PX
                out[k, pl.ds(at, HALO), :] = near * before[pl.ds(c * HALO * CY + y, HALO, stride=CY), :]
                out[k, pl.ds(at + HALO, CX), :] = disp[pl.ds(c * CX * CY + y, CX, stride=CY), :]
                out[k, pl.ds(at + HALO + CX, HALO), :] = far * after[pl.ds(c * HALO * CY + y, HALO, stride=CY), :]
                at = RHS0 + c * PR
                row = (4 * HALO + c * (HALO - 1)) * CY + y
                out[k, pl.ds(at, HALO - 1), :] = before[pl.ds(row, HALO - 1, stride=CY), :]
                out[k, pl.ds(at + HALO - 1, CX), :] = rhs[pl.ds(c * CX * CY + y, CX, stride=CY), :]
                out[k, pl.ds(at + HALO - 1 + CX, HALO - 1), :] = after[pl.ds(row, HALO - 1, stride=CY), :]
            row = 3 * HALO * CY + y
            out[k, pl.ds(LAB0, HALO), :] = near * before[pl.ds(row, HALO, stride=CY), :]
            out[k, pl.ds(LAB0 + HALO, CX), :] = labels[pl.ds(y, CX, stride=CY), :].astype(F32)
            out[k, pl.ds(LAB0 + HALO + CX, HALO), :] = far * after[pl.ds(row, HALO, stride=CY), :]


def plane(ref, j, rows=ROWS):
    return ref[pl.ds(pl.multiple_of(j * ROWS, 8), rows), :]


def put(ref, j, value):
    ref[pl.ds(pl.multiple_of(j * ROWS, 8), value.shape[0]), :] = value


def times(k, v):
    return [
        k[SYMMETRIC_INDEX[c][0]] * v[0] + k[SYMMETRIC_INDEX[c][1]] * v[1] + k[SYMMETRIC_INDEX[c][2]] * v[2]
        for c in range(3)
    ]


def smooth_and_restrict(
    stiffness, disp, rhs, labels, before, after, y_before, y_after, dense, dense_before,
    smoothed, jumps, message,
    fields, coeff, total_coeff, scale, flux, first, flux_first, second, flux_second, coarse,
):
    near, far = inside_x()
    here_x, here_y = lax.axis_index("gx"), lax.axis_index("gy")
    for c in range(3):
        for k in range(HALO):
            row = (c * HALO + k) * CY
            put(fields, c * PX + k, near * before[pl.ds(row, CY), :])
            put(fields, c * PX + HALO + CX + k, far * after[pl.ds(row, CY), :])
        for k in range(CX):
            put(fields, c * PX + HALO + k, disp[c, k])
            put(fields, RHS0 + c * PR + HALO - 1 + k, rhs[c, k])
        for k in range(HALO - 1):
            row = (4 * HALO + c * (HALO - 1) + k) * CY
            put(fields, RHS0 + c * PR + k, before[pl.ds(row, CY), :])
            put(fields, RHS0 + c * PR + HALO - 1 + CX + k, after[pl.ds(row, CY), :])
    for k in range(HALO):
        row = (3 * HALO + k) * CY
        put(fields, LAB0 + k, near * before[pl.ds(row, CY), :])
        put(fields, LAB0 + HALO + CX + k, far * after[pl.ds(row, CY), :])
    for k in range(CX):
        put(fields, LAB0 + HALO + k, labels[k].astype(F32))
    low = jnp.where(here_y > 0, 1.0, 0.0).astype(F32)
    high = jnp.where(here_y < N_GY - 1, 1.0, 0.0).astype(F32)
    for k in range(HALO):
        fields[pl.ds(CY + k, FIELDS, stride=ROWS), :] = high * y_after[k]
        fields[pl.ds(ROWS - HALO + k, FIELDS, stride=ROWS), :] = low * y_before[k]
    for k in range(CY + HALO, ROWS - HALO):
        fields[pl.ds(k, FIELDS, stride=ROWS), :] = jnp.zeros((FIELDS, NZ), F32)

    row_at = lax.broadcasted_iota(jnp.int32, (ROWS, NZ), 0)
    lane_at = lax.broadcasted_iota(jnp.int32, (ROWS, NZ), 1)
    row_y = here_y * CY + jnp.where(row_at < CY + HALO, row_at, row_at - ROWS)
    row_inside = (row_y >= 0) & (row_y < NY) & ((row_at < CY + HALO) | (row_at >= ROWS - HALO))
    first_lane, last_lane = lane_at == 0, lane_at == NZ - 1

    def inside(p):
        x = here_x * CX + p - HALO
        return row_inside & ((x >= 0) & (x < NX))

    def summed(ref, j, edge=0.0):
        centre = plane(ref, j) + 0.5 * (plane(ref, j - 1) + plane(ref, j + 1))
        centre = centre + 0.5 * (pltpu.roll(centre, 1, 0) + pltpu.roll(centre, ROWS - 1, 0))
        left = jnp.where(first_lane, edge, pltpu.roll(centre, 1, 1))
        right = jnp.where(last_lane, edge, pltpu.roll(centre, NZ - 1, 1))
        return centre + 0.5 * (left + right)

    def coefficients(p, carry):
        label = plane(fields, LAB0 + p)
        k = [jnp.full((ROWS, NZ), stiffness[0, e], F32) for e in range(6)]
        for m in range(1, LABELS):
            at = label == float(m)
            k = [jnp.where(at, stiffness[m, e], k[e]) for e in range(6)]
        for e in range(6):
            put(coeff, e * PX + p, k[e])
        pushed = times(k, [plane(fields, c * PX + p) for c in range(3)])
        for c in range(3):
            put(flux, c * PX + p, pushed[c])
        return carry

    lax.fori_loop(0, PX, coefficients, 0)

    def weights(p, carry):
        for e in range(6):
            k = plane(coeff, e * PX + p)
            around = summed(coeff, e * PX + p, 4.0 * stiffness[0, e])
            put(total_coeff, e * PX + p, 8.0 * k + around)
            if e < 3:
                put(scale, e * PX + p, DAMPING / (MASS_SHIFT + 6.0 * k + around))
        return carry

    lax.fori_loop(1, PX - 1, weights, 0)

    def image(p, v_ref, flux_ref):
        v = [plane(v_ref, c * PX + p) for c in range(3)]
        k = [plane(coeff, e * PX + p) for e in range(6)]
        m = [plane(total_coeff, e * PX + p) for e in range(6)]
        around = [summed(v_ref, c * PX + p) for c in range(3)]
        pushed = [summed(flux_ref, c * PX + p) for c in range(3)]
        mine, theirs = times(m, v), times(k, around)
        return v, k, [MASS_SHIFT * v[c] + (mine[c] - theirs[c] - pushed[c]) for c in range(3)]

    def sweep(v_ref, flux_ref, to_ref, to_flux):
        def step(p, carry):
            v, k, a = image(p, v_ref, flux_ref)
            keep = inside(p)
            new = []
            for c in range(3):
                right_side = plane(fields, RHS0 + c * PR + p - 1)
                value = v[c] + (right_side - a[c]) * plane(scale, c * PX + p)
                value = jnp.where(keep, value, 0.0)
                put(to_ref, c * PX + p, value)
                new.append(value)
            pushed = times(k, new)
            for c in range(3):
                put(to_flux, c * PX + p, pushed[c])
            return carry

        return step

    lax.fori_loop(1, PX - 1, sweep(fields, flux, first, flux_first), 0)
    lax.fori_loop(2, PX - 2, sweep(first, flux_first, second, flux_second), 0)

    def jump_at(c, p):
        return plane(second, c * PX + p, CY) - plane(second, c * PX + p + 1, CY)

    for c in range(3):
        forced = jnp.where(dense_before[3] > 0.5, dense_before[c] + PENALTY * jump_at(c, HALO - 1), 0.0)
        coarse[pl.ds((6 + c) * CY, CY), :] = forced

    def restrict(q, carry):
        half = q % 2
        v, k, a = image(q + HALO, second, flux_second)
        at = pl.ds(pl.multiple_of(q * CY, CY), CY)
        live = dense[3, at, :] > 0.5
        for c in range(3):
            own = v[c][:CY]
            smoothed[c, q] = own
            jump = jump_at(c, q + HALO)
            jumps[c, at, :] = jump
            forced = jnp.where(live, dense[c, at, :] + PENALTY * jump, 0.0)
            pulled = coarse[pl.ds((6 + c) * CY, CY), :]
            residual = plane(fields, RHS0 + c * PR + q + HALO - 1, CY) - a[c][:CY] - (forced - pulled)
            coarse[pl.ds((6 + c) * CY, CY), :] = forced
            spot = pl.ds(pl.multiple_of((c * 2 + q // 2) * CY, CY), CY)

            @pl.when(half == 0)
            def _():
                coarse[spot, :] = residual

            @pl.when(half == 1)
            def _():
                coarse[spot, :] = coarse[spot, :] + residual

        return carry

    lax.fori_loop(0, CX, restrict, 0)

    total = jnp.zeros((3 * CY // 2, NZ), F32)
    for x in range(2):
        rows = []
        for c in range(3):
            base = (c * 2 + x) * CY
            rows.append(
                coarse[pl.ds(base, CY // 2, stride=2), :] + coarse[pl.ds(base + 1, CY // 2, stride=2), :]
            )
        lane_in = lax.broadcasted_iota(jnp.int32, (NZ, NZ), 0)
        lane_out = lax.broadcasted_iota(jnp.int32, (NZ, NZ), 1)
        pick = jnp.where(lane_in // 2 + x * (NZ // 2) == lane_out, 1.0, 0.0).astype(BF16)
        for piece in pieces_of(jnp.concatenate(rows, axis=0)):
            total = total + jnp.dot(piece, pick, preferred_element_type=F32)
    for s in range(N_GY):
        message[s] = total


def finish(cells, counts, mult, jumps, gathered, updated, out):
    for s in range(N_GY):
        for c in range(3):
            rows = gathered[s, pl.ds(c * CY // 2, CY // 2), :]
            at = pl.ds(s * (CY // 2), CY // 2)
            out[c, 0, at, :] = rows[:, : NZ // 2]
            out[c, 1, at, :] = rows[:, NZ // 2 :]
    column, depth = cells[...] // NZ, cells[...] % NZ
    left = jnp.concatenate(
        [jnp.concatenate(pieces_of(jumps[c]), axis=1) for c in range(3)], axis=0
    )
    live = slot_number() < counts[0, 0]
    for j in range(SLOT_ROWS):
        at_depth = lax.broadcasted_iota(jnp.int32, (NZ, 128), 0) == depth[j : j + 1]
        right = jnp.where(at_depth, 1.0, 0.0).astype(BF16)
        picked = jnp.dot(left, jnp.concatenate([right] * 3, axis=0), preferred_element_type=F32)
        at_column = lax.broadcasted_iota(jnp.int32, (CX * CY, 128), 0) == column[j : j + 1]
        for c in range(3):
            jump = jnp.sum(
                jnp.where(at_column, picked[c * CX * CY : (c + 1) * CX * CY], 0.0), axis=0, keepdims=True
            )
            old = mult[c, j : j + 1, :]
            updated[c, j : j + 1, :] = jnp.where(live[j : j + 1], old + PENALTY * jump, old)


def cost(flops, nbytes):
    return pl.CostEstimate(flops=flops, bytes_accessed=nbytes, transcendentals=0)


def body(displacement, rhs, labels, stiffness, rows, counts, multipliers):
    cells = rows.reshape(SLOT_ROWS, 128)
    mult = multipliers.reshape(3, SLOT_ROWS, 128)
    up, down = pl.pallas_call(
        pack_x,
        out_shape=(f32(UP_ROWS, NZ), f32(SIDE, NZ)),
        in_specs=[VMEM, VMEM, VMEM, VMEM, SMEM, VMEM],
        out_specs=(VMEM, VMEM),
        compiler_params=PARAMS,
    )(displacement, rhs, labels, cells, counts, mult)
    ring = [(i, (i + 1) % N_GX) for i in range(N_GX)]
    before = lax.ppermute(up, "gx", ring)
    after = lax.ppermute(down, "gx", [(j, i) for i, j in ring])
    dense = pl.pallas_call(
        spread_own,
        out_shape=f32(4, CX * CY, NZ),
        in_specs=[VMEM, SMEM, VMEM],
        out_specs=VMEM,
        compiler_params=PARAMS,
        cost_estimate=cost(300_000_000, 400_000),
    )(cells, counts, mult)
    y_up, y_down = pl.pallas_call(
        pack_y,
        out_shape=(f32(HALO, FIELDS, NZ), f32(HALO, FIELDS, NZ)),
        in_specs=[VMEM] * 5,
        out_specs=(VMEM, VMEM),
        compiler_params=PARAMS,
    )(
        displacement.reshape(3 * CX * CY, NZ),
        rhs.reshape(3 * CX * CY, NZ),
        labels.reshape(CX * CY, NZ),
        before,
        after,
    )
    ring = [(i, (i + 1) % N_GY) for i in range(N_GY)]
    y_before = lax.ppermute(y_up, "gy", ring)
    y_after = lax.ppermute(y_down, "gy", [(j, i) for i, j in ring])
    dense_before = pl.pallas_call(
        spread_before,
        out_shape=f32(4, CY, NZ),
        in_specs=[VMEM],
        out_specs=VMEM,
        compiler_params=PARAMS,
        cost_estimate=cost(100_000_000, 400_000),
    )(before)
    wide = pltpu.VMEM((3 * PX * ROWS, NZ), F32)
    smoothed, jumps, message = pl.pallas_call(
        smooth_and_restrict,
        out_shape=(f32(3, CX, CY, NZ), f32(3, CX * CY, NZ), f32(N_GY, 3 * CY // 2, NZ)),
        in_specs=[SMEM] + [VMEM] * 9,
        out_specs=(VMEM, VMEM, VMEM),
        scratch_shapes=[
            pltpu.VMEM((FIELDS * ROWS, NZ), F32),
            pltpu.VMEM((6 * PX * ROWS, NZ), F32),
            pltpu.VMEM((6 * PX * ROWS, NZ), F32),
            wide,
            wide,
            wide,
            wide,
            wide,
            wide,
            pltpu.VMEM((9 * CY, NZ), F32),
        ],
        compiler_params=PARAMS,
    )(stiffness, displacement, rhs, labels, before, after, y_before, y_after, dense, dense_before)
    gathered = lax.all_to_all(message, "gy", 0, 0)
    updated, coarse = pl.pallas_call(
        finish,
        out_shape=(f32(3, SLOT_ROWS, 128), f32(3, CX // 2, NY // 2, NZ // 2)),
        in_specs=[VMEM, SMEM, VMEM, VMEM, VMEM],
        out_specs=(VMEM, VMEM),
        compiler_params=PARAMS,
    )(cells, counts, mult, jumps, gathered)
    return (smoothed, coarse, updated.reshape(3, 1, 1, SLOTS))


def solution(mesh):
    return jax.shard_map(
        body,
        mesh=mesh,
        in_specs=(
            P(None, "gx", "gy", None),
            P(None, "gx", "gy", None),
            P("gx", "gy", None),
            P(),
            P("gx", "gy", None),
            P("gx", "gy"),
            P(None, "gx", "gy", None),
        ),
        out_specs=(P(None, "gx", "gy", None), P(None, "gx", None, None), P(None, "gx", "gy", None)),
        check_vma=False,
    )
```

```python
import jax
import jax.numpy as jnp
from jax import lax
from jax.experimental import pallas as pl
from jax.experimental.pallas import tpu as pltpu
from jax.sharding import PartitionSpec as P

SYMMETRIC_INDEX = ((0, 3, 4), (3, 1, 5), (4, 5, 2))
DAMPING = 0.6
MASS_SHIFT = 1.0
PENALTY = 1.0

CX, CY, NZ, SLOTS = 4, 32, 128, 1024
N_GX, N_GY = 32, 8
NX, NY = CX * N_GX, CY * N_GY
LABELS = 8
HALO = 3
PX = CX + 2 * HALO
PR = PX - 2
EDGE = 16
LAB0 = 3 * PX
RHS0 = LAB0 + PX
FIELDS = RHS0 + 3 * PR
SIDE = (3 * HALO + HALO + 3 * (HALO - 1)) * CY
IFACE = SIDE
SLOT_ROWS = SLOTS // 128
UP_ROWS = SIDE + 4 * SLOT_ROWS
VMEM = pl.BlockSpec(memory_space=pltpu.VMEM)
SMEM = pl.BlockSpec(memory_space=pltpu.SMEM)
HBM = pl.BlockSpec(memory_space=pltpu.HBM)
F32 = jnp.float32
BF16 = jnp.bfloat16
PARAMS = pltpu.CompilerParams(vmem_limit_bytes=48 * 1024 * 1024)


def f32(*shape):
    return jax.ShapeDtypeStruct(shape, F32)


def pieces_of(value):
    high = value.astype(BF16)
    rest = value - high.astype(F32)
    middle = rest.astype(BF16)
    low = (rest - middle.astype(F32)).astype(BF16)
    return (high, middle, low)


def slot_number():
    return lax.broadcasted_iota(jnp.int32, (SLOT_ROWS, 128), 0) * 128 + lax.broadcasted_iota(
        jnp.int32, (SLOT_ROWS, 128), 1
    )


def pack_x(
    count, disp_in, rhs_in, labels_in, cells_in, mult_in,
    up, down, disp, rhs, labels, cells, mult,
    raw_labels, raw_cells, arrived,
):
    pairs = (
        (cells_in, raw_cells), (labels_in, raw_labels), (disp_in, disp), (rhs_in, rhs), (mult_in, mult)
    )
    copies = [pltpu.make_async_copy(a, b, arrived.at[i]) for i, (a, b) in enumerate(pairs)]
    for copy in copies:
        copy.start()
    for copy in copies[:2]:
        copy.wait()
    live = slot_number() < count[0, 0]
    live_cells = jnp.where(live, raw_cells[...], -1)
    cells[...] = live_cells
    up[pl.ds(IFACE, SLOT_ROWS), :] = live_cells.astype(F32)
    labels[...] = raw_labels[...].astype(F32)
    for k in range(HALO):
        row = (3 * HALO + k) * CY
        up[pl.ds(row, CY), :] = raw_labels[pl.ds((CX - HALO + k) * CY, CY), :].astype(F32)
        down[pl.ds(row, CY), :] = raw_labels[pl.ds(k * CY, CY), :].astype(F32)
    for copy in copies[2:]:
        copy.wait()
    for c in range(3):
        for k in range(HALO):
            row = (c * HALO + k) * CY
            up[pl.ds(row, CY), :] = disp[pl.ds((c * CX + CX - HALO + k) * CY, CY), :]
            down[pl.ds(row, CY), :] = disp[pl.ds((c * CX + k) * CY, CY), :]
        for k in range(HALO - 1):
            row = (4 * HALO + c * (HALO - 1) + k) * CY
            up[pl.ds(row, CY), :] = rhs[pl.ds((c * CX + CX - HALO + 1 + k) * CY, CY), :]
            down[pl.ds(row, CY), :] = rhs[pl.ds((c * CX + k) * CY, CY), :]
        up[pl.ds(IFACE + (1 + c) * SLOT_ROWS, SLOT_ROWS), :] = mult[c]


def paired(array, j):
    return jnp.concatenate([array[2 * j : 2 * j + 1], array[2 * j + 1 : 2 * j + 2]], axis=1)


def spread(cells, mult, first, columns):
    column = jnp.where(cells < 0, -1, cells // NZ - first)
    depth = cells % NZ
    total = jnp.zeros((10 * columns, NZ), F32)
    parts = [piece for c in range(3) for piece in pieces_of(mult[c])]
    for j in range(SLOT_ROWS // 2):
        at_column = lax.broadcasted_iota(jnp.int32, (columns, 256), 0) == paired(column, j)
        at_depth = lax.broadcasted_iota(jnp.int32, (NZ, 256), 0) == paired(depth, j)
        left = [jnp.where(at_column, paired(piece.astype(F32), j), 0.0).astype(BF16) for piece in parts]
        left.append(jnp.where(at_column, 1.0, 0.0).astype(BF16))
        total = total + lax.dot_general(
            jnp.concatenate(left, axis=0),
            jnp.where(at_depth, 1.0, 0.0).astype(BF16),
            (((1,), (1,)), ((), ())),
            preferred_element_type=F32,
        )
    part = [total[i * columns : (i + 1) * columns] for i in range(10)]
    return [part[3 * c] + part[3 * c + 1] + part[3 * c + 2] for c in range(3)] + [part[9]]


def spread_own(cells, mult, dense):
    values = spread(cells[...], [mult[c] for c in range(3)], 0, CX * CY)
    for i in range(4):
        dense[i] = values[i]


def inside_x():
    here = lax.axis_index("gx")
    return (
        jnp.where(here > 0, 1.0, 0.0).astype(F32),
        jnp.where(here < N_GX - 1, 1.0, 0.0).astype(F32),
    )


def pack_y(disp, rhs, labels, before, after, dense, up, down):
    near, far = inside_x()
    for out, start in ((up, CY - HALO), (down, 0)):
        for k in range(HALO):
            y = start + k
            for c in range(3):
                at = c * PX
                out[k, pl.ds(at, HALO), :] = near * before[pl.ds(c * HALO * CY + y, HALO, stride=CY), :]
                out[k, pl.ds(at + HALO, CX), :] = disp[pl.ds(c * CX * CY + y, CX, stride=CY), :]
                out[k, pl.ds(at + HALO + CX, HALO), :] = far * after[pl.ds(c * HALO * CY + y, HALO, stride=CY), :]
                at = RHS0 + c * PR
                row = (4 * HALO + c * (HALO - 1)) * CY + y
                out[k, pl.ds(at, HALO - 1), :] = before[pl.ds(row, HALO - 1, stride=CY), :]
                out[k, pl.ds(at + HALO - 1, CX), :] = rhs[pl.ds(c * CX * CY + y, CX, stride=CY), :]
                out[k, pl.ds(at + HALO - 1 + CX, HALO - 1), :] = after[pl.ds(row, HALO - 1, stride=CY), :]
            row = 3 * HALO * CY + y
            out[k, pl.ds(LAB0, HALO), :] = near * before[pl.ds(row, HALO, stride=CY), :]
            out[k, pl.ds(LAB0 + HALO, CX), :] = labels[pl.ds(y, CX, stride=CY), :]
            out[k, pl.ds(LAB0 + HALO + CX, HALO), :] = far * after[pl.ds(row, HALO, stride=CY), :]


def times(k, v):
    return [
        k[SYMMETRIC_INDEX[c][0]] * v[0] + k[SYMMETRIC_INDEX[c][1]] * v[1] + k[SYMMETRIC_INDEX[c][2]] * v[2]
        for c in range(3)
    ]


class Stencil:
    def __init__(self, rows, entry, fields, row_inside, scratch):
        self.rows, self.entry, self.fields, self.row_inside = rows, entry, fields, row_inside
        self.coeff, self.total, self.scale, self.flux = scratch
        lane = lax.broadcasted_iota(jnp.int32, (1, NZ), 1)
        self.not_first = jnp.where(lane == 0, 0.0, 0.5)
        self.not_last = jnp.where(lane == NZ - 1, 0.0, 0.5)
        self.ends = jnp.where((lane == 0) | (lane == NZ - 1), 16.0, 0.0)

    def get(self, ref, j):
        return ref[pl.ds(j * self.rows, self.rows), :]

    def put(self, ref, j, value):
        ref[pl.ds(j * self.rows, self.rows), :] = value

    def inside(self, p, value):
        x = lax.axis_index("gx") * CX + p - HALO
        if HALO <= p < HALO + CX:
            keep = self.row_inside
        else:
            keep = (x >= 0) & (x < NX)
            if self.row_inside is not None:
                keep = self.row_inside & keep
        return value if keep is None else jnp.where(keep, value, 0.0)

    def summed(self, ref, j, edge=None):
        f = self.get(ref, j)
        f = (f + f) + (self.get(ref, j - 1) + self.get(ref, j + 1))
        f = (f + f) + (pltpu.roll(f, 1, 0) + pltpu.roll(f, self.rows - 1, 0))
        f = f + (pltpu.roll(f, 1, 1) * self.not_first + pltpu.roll(f, NZ - 1, 1) * self.not_last)
        if edge is not None:
            f = f + self.ends * (0.5 * edge)
        return f + f

    def coefficients(self):
        for p in range(PX):
            label = self.get(self.fields, LAB0 + p)
            k = [jnp.broadcast_to(self.entry(0, e), label.shape) for e in range(6)]
            for m in range(1, LABELS):
                at = label == float(m)
                k = [jnp.where(at, self.entry(m, e), k[e]) for e in range(6)]
            for e in range(6):
                self.put(self.coeff, e * PX + p, k[e])
            self.push(self.flux, p, [self.get(self.fields, c * PX + p) for c in range(3)])
        for p in range(1, PX - 1):
            for e in range(6):
                k = self.get(self.coeff, e * PX + p)
                around = self.summed(self.coeff, e * PX + p, self.entry(0, e))
                self.put(self.total, e * PX + p, 64.0 * k + around)
                if e < 3:
                    self.put(self.scale, e * PX + p, DAMPING / (MASS_SHIFT + 6.0 * k + 0.125 * around))

    def push(self, flux, p, v):
        pushed = times([self.get(self.coeff, e * PX + p) for e in range(6)], v)
        for c in range(3):
            self.put(flux, c * PX + p, pushed[c])

    def image(self, p, v_ref, flux):
        v = [self.get(v_ref, c * PX + p) for c in range(3)]
        k = [self.get(self.coeff, e * PX + p) for e in range(6)]
        m = [self.get(self.total, e * PX + p) for e in range(6)]
        around = [self.summed(v_ref, c * PX + p) for c in range(3)]
        pushed = [self.summed(flux, c * PX + p) for c in range(3)]
        mine, theirs = times(m, v), times(k, around)
        return v, [MASS_SHIFT * v[c] + 0.125 * (mine[c] - theirs[c] - pushed[c]) for c in range(3)]

    def right_side(self, c, p):
        return self.get(self.fields, RHS0 + c * PR + p - 1)

    def sweep(self, first, v_ref, flux, to_ref, to_flux, settle):
        for p in range(first, PX - first):
            v, a = self.image(p, v_ref, flux)
            new = []
            for c in range(3):
                value = v[c] + (self.right_side(c, p) - a[c]) * self.get(self.scale, c * PX + p)
                value = settle(c, p, self.inside(p, value))
                self.put(to_ref, c * PX + p, value)
                new.append(value)
            self.push(to_flux, p, new)

    def restrict(self, v_ref, flux, dense, settled):
        def forced(c, x):
            jump = self.get(v_ref, c * PX + x + HALO) - self.get(v_ref, c * PX + x + HALO + 1)
            value, live = dense(c, x), dense(3, x)
            return jump, jnp.where(live > 0.5, value + PENALTY * jump, 0.0)

        pulled = [forced(c, -1)[1] for c in range(3)]
        sums = []
        for x in range(CX):
            v, a = self.image(x + HALO, v_ref, flux)
            for c in range(3):
                jump, pushed = forced(c, x)
                settled(c, x, v[c], jump)
                part = self.right_side(c, x + HALO) - a[c] - (pushed - pulled[c])
                pulled[c] = pushed
                if x % 2 == 0:
                    sums.append(part)
                else:
                    sums[x // 2 * 3 + c] = sums[x // 2 * 3 + c] + part
        return sums


def to_edge(value, ref, j):
    ref[pl.ds(j * EDGE + HALO, 5), :] = value[:5]
    ref[pl.ds(j * EDGE + 8, 4), :] = value[CY - 4 :]


def inner_part(
    stiffness, disp, rhs, labels, before, after, dense,
    smoothed, jumps, residual, edge_fields, edge_first, edge_second, edge_dense, table,
    fields, coeff, total, scale, flux, first, flux_first, second, flux_second,
):
    near, far = inside_x()
    zero = jnp.zeros((EDGE, NZ), F32)

    def place(j, value):
        fields[pl.ds(j * CY, CY), :] = value
        edge_fields[pl.ds(j * EDGE, EDGE), :] = zero
        to_edge(value, edge_fields, j)

    def part(ref, k):
        return ref[pl.ds(k * CY, CY), :]

    for c in range(3):
        for k in range(HALO):
            place(c * PX + k, near * part(before, c * HALO + k))
            place(c * PX + HALO + CX + k, far * part(after, c * HALO + k))
        for k in range(CX):
            place(c * PX + HALO + k, part(disp, c * CX + k))
            place(RHS0 + c * PR + HALO - 1 + k, part(rhs, c * CX + k))
        for k in range(HALO - 1):
            row = 4 * HALO + c * (HALO - 1) + k
            place(RHS0 + c * PR + k, part(before, row))
            place(RHS0 + c * PR + HALO - 1 + CX + k, part(after, row))
    for k in range(HALO):
        place(LAB0 + k, near * part(before, 3 * HALO + k))
        place(LAB0 + HALO + CX + k, far * part(after, 3 * HALO + k))
    for k in range(CX):
        place(LAB0 + HALO + k, part(labels, k))
    for m in range(LABELS):
        for e in range(6):
            table[pl.ds(m * 6 + e, 1), :] = jnp.full((1, NZ), stiffness[m, e], F32)

    cells = before[pl.ds(IFACE, SLOT_ROWS), :].astype(jnp.int32)
    mult = [before[pl.ds(IFACE + (1 + c) * SLOT_ROWS, SLOT_ROWS), :] for c in range(3)]
    dense_before = spread(cells, mult, (CX - 1) * CY, CY)
    dense_before[3] = dense_before[3] * near
    for i in range(4):
        to_edge(dense_before[i], edge_dense, i * (CX + 1))
        for x in range(CX):
            to_edge(dense[i, pl.ds(x * CY, CY), :], edge_dense, i * (CX + 1) + 1 + x)

    grid = Stencil(CY, lambda m, e: stiffness[m, e], fields, None, (coeff, total, scale, flux))
    grid.coefficients()

    def keep(ref, count):
        def settle(c, p, value):
            to_edge(value, ref, c * count + p - (PX - count) // 2)
            return value

        return settle

    grid.sweep(1, fields, flux, first, flux_first, keep(edge_first, PX - 2))
    grid.sweep(2, first, flux_first, second, flux_second, keep(edge_second, PX - 4))

    def settled(c, x, v, jump):
        smoothed[pl.ds((c * CX + x) * CY, CY), :] = v
        jumps[pl.ds((c * CX + x) * CY, CY), :] = jump

    def cell_values(i, x):
        return dense_before[i] if x < 0 else dense[i, pl.ds(x * CY, CY), :]

    sums = grid.restrict(second, flux_second, cell_values, settled)
    for i in range(6):
        residual[pl.ds(i * CY, CY), :] = sums[i]


def edge_part(
    y_before, y_after, inner_smoothed, inner_jumps, inner_residual,
    edge_fields, edge_first, edge_second, edge_dense, table,
    smoothed, jumps, message,
    fields, coeff, total, scale, flux, first, flux_first, second, flux_second, coarse,
):
    here_y = lax.axis_index("gy")
    low = jnp.where(here_y > 0, 1.0, 0.0).astype(F32)
    high = jnp.where(here_y < N_GY - 1, 1.0, 0.0).astype(F32)
    fields[...] = edge_fields[...]
    for k in range(HALO):
        fields[pl.ds(k, FIELDS, stride=EDGE), :] = low * y_before[k]
        fields[pl.ds(8 + 4 + k, FIELDS, stride=EDGE), :] = high * y_after[k]
    smoothed[...] = inner_smoothed[...]
    jumps[...] = inner_jumps[...]
    coarse[...] = inner_residual[...]

    row = lax.broadcasted_iota(jnp.int32, (EDGE, NZ), 0)
    y = here_y * CY + jnp.where(row < 8, row - HALO, row + CY - 12)
    row_inside = (y >= 0) & (y < NY)

    grid = Stencil(
        EDGE, lambda m, e: table[pl.ds(m * 6 + e, 1), :], fields, row_inside, (coeff, total, scale, flux)
    )
    grid.coefficients()

    def join(ref, count, depth):
        outer = (row < HALO + depth) | (row >= 12 - depth)

        def settle(c, p, value):
            return jnp.where(outer, value, grid.get(ref, c * count + p - (PX - count) // 2))

        return settle

    grid.sweep(1, fields, flux, first, flux_first, join(edge_first, PX - 2, 1))
    grid.sweep(2, first, flux_first, second, flux_second, join(edge_second, PX - 4, 2))

    def settled(c, x, v, jump):
        at = (c * CX + x) * CY
        for ref, value in ((smoothed, v), (jumps, jump)):
            ref[pl.ds(at, 2), :] = value[HALO : HALO + 2]
            ref[pl.ds(at + CY - 2, 2), :] = value[10:12]

    sums = grid.restrict(
        second, flux_second, lambda i, x: grid.get(edge_dense, i * (CX + 1) + 1 + x), settled
    )
    for i in range(6):
        coarse[pl.ds(i * CY, 3), :] = sums[i][HALO : HALO + 3]
        coarse[pl.ds(i * CY + CY - 3, 3), :] = sums[i][9:12]

    out = jnp.zeros((3 * CY // 2, NZ), F32)
    lane_in = lax.broadcasted_iota(jnp.int32, (NZ, NZ), 0)
    lane_out = lax.broadcasted_iota(jnp.int32, (NZ, NZ), 1)
    for x in range(2):
        at = 3 * x * CY
        rows = coarse[pl.ds(at, 3 * CY // 2, stride=2), :] + coarse[pl.ds(at + 1, 3 * CY // 2, stride=2), :]
        pick = jnp.where(lane_in // 2 + x * (NZ // 2) == lane_out, 1.0, 0.0).astype(BF16)
        for piece in pieces_of(rows):
            out = out + jnp.dot(piece, pick, preferred_element_type=F32)
    for s in range(N_GY):
        message[s] = out


def finish(
    cells, mult, jumps, smoothed, gathered,
    smoothed_out, updated_out, coarse_out,
    updated, coarse, done,
):
    copies = [
        pltpu.make_async_copy(smoothed, smoothed_out, done.at[0]),
        pltpu.make_async_copy(coarse, coarse_out, done.at[1]),
        pltpu.make_async_copy(updated, updated_out, done.at[2]),
    ]
    copies[0].start()
    for c in range(3):
        parts = [gathered[s, pl.ds(c * CY // 2, CY // 2), :] for s in range(N_GY)]
        coarse[c] = jnp.transpose(jnp.concatenate(parts, axis=0))
    copies[1].start()
    live = cells[...] >= 0
    column, depth = cells[...] // NZ, cells[...] % NZ
    block = CX * CY
    left = jnp.concatenate(
        [jnp.concatenate(pieces_of(jumps[pl.ds(c * block, block), :]), axis=1) for c in range(3)], axis=0
    )
    for j in range(SLOT_ROWS):
        at_depth = lax.broadcasted_iota(jnp.int32, (NZ, 128), 0) == depth[j : j + 1]
        right = jnp.where(at_depth, 1.0, 0.0).astype(BF16)
        picked = jnp.dot(left, jnp.concatenate([right] * 3, axis=0), preferred_element_type=F32)
        at_column = lax.broadcasted_iota(jnp.int32, (block, 128), 0) == column[j : j + 1]
        for c in range(3):
            jump = jnp.sum(
                jnp.where(at_column, picked[c * block : (c + 1) * block], 0.0), axis=0, keepdims=True
            )
            old = mult[c, j : j + 1, :]
            updated[c, j : j + 1, :] = jnp.where(live[j : j + 1], old + PENALTY * jump, old)
    copies[2].start()
    for copy in copies:
        copy.wait()


def cost(flops, nbytes):
    return pl.CostEstimate(flops=flops, bytes_accessed=nbytes, transcendentals=0)


def in_hbm(array):
    return pltpu.with_memory_space_constraint(array, pltpu.HBM)


def scratch_of(rows):
    wide = pltpu.VMEM((3 * PX * rows, NZ), F32)
    six = pltpu.VMEM((6 * PX * rows, NZ), F32)
    return [pltpu.VMEM((FIELDS * rows, NZ), F32), six, six] + [wide] * 6


def call(kernel, outs, ins, out_specs=None, scratch=(), flops=1_000_000):
    return pl.pallas_call(
        kernel,
        out_shape=outs,
        in_specs=ins,
        out_specs=out_specs or [VMEM] * len(outs),
        scratch_shapes=list(scratch),
        compiler_params=PARAMS,
        cost_estimate=cost(flops, 1_000_000),
    )


def body(displacement, rhs, labels, stiffness, rows, counts, multipliers):
    block = CX * CY
    up, down, disp, rhs, labels, cells, mult = call(
        pack_x,
        [
            f32(UP_ROWS, NZ), f32(SIDE, NZ), f32(3 * block, NZ), f32(3 * block, NZ), f32(block, NZ),
            jax.ShapeDtypeStruct((SLOT_ROWS, 128), jnp.int32), f32(3, SLOT_ROWS, 128),
        ],
        [SMEM] + [HBM] * 5,
        scratch=[
            pltpu.VMEM((block, NZ), jnp.int32),
            pltpu.VMEM((SLOT_ROWS, 128), jnp.int32),
            pltpu.SemaphoreType.DMA((5,)),
        ],
    )(
        counts,
        in_hbm(displacement.reshape(3 * block, NZ)),
        in_hbm(rhs.reshape(3 * block, NZ)),
        in_hbm(labels.reshape(block, NZ)),
        in_hbm(rows.reshape(SLOT_ROWS, 128)),
        in_hbm(multipliers.reshape(3, SLOT_ROWS, 128)),
    )
    ring = [(i, (i + 1) % N_GX) for i in range(N_GX)]
    before = lax.ppermute(up, "gx", ring)
    after = lax.ppermute(down, "gx", [(j, i) for i, j in ring])
    (dense,) = call(spread_own, [f32(4, block, NZ)], [VMEM] * 2, flops=300_000_000)(cells, mult)
    y_up, y_down = call(pack_y, [f32(HALO, FIELDS, NZ)] * 2, [VMEM] * 6)(disp, rhs, labels, before, after, dense)
    ring = [(i, (i + 1) % N_GY) for i in range(N_GY)]
    y_before = lax.ppermute(y_up, "gy", ring)
    y_after = lax.ppermute(y_down, "gy", [(j, i) for i, j in ring])
    inner = call(
        inner_part,
        [
            f32(3 * block, NZ), f32(3 * block, NZ), f32(6 * CY, NZ), f32(FIELDS * EDGE, NZ),
            f32(3 * PR * EDGE, NZ), f32(3 * (PR - 2) * EDGE, NZ), f32(4 * (CX + 1) * EDGE, NZ), f32(LABELS * 6, NZ),
        ],
        [SMEM] + [VMEM] * 6,
        scratch=scratch_of(CY),
        flops=1_000_000_000,
    )(stiffness, disp, rhs, labels, before, after, dense)
    smoothed, jumps, message = call(
        edge_part,
        [f32(3 * block, NZ), f32(3 * block, NZ), f32(N_GY, 3 * CY // 2, NZ)],
        [VMEM] * 10,
        scratch=scratch_of(EDGE) + [pltpu.VMEM((6 * CY, NZ), F32)],
    )(y_before, y_after, *inner)
    gathered = lax.all_to_all(message, "gy", 0, 0)
    smoothed, updated, coarse = call(
        finish,
        [pltpu.HBM(s, F32) for s in ((3 * block, NZ), (3, SLOT_ROWS, 128), (3, CX // 2 * NZ // 2, NY // 2))],
        [VMEM] * 5,
        out_specs=[HBM] * 3,
        scratch=[
            pltpu.VMEM((3, SLOT_ROWS, 128), F32),
            pltpu.VMEM((3, CX // 2 * NZ // 2, NY // 2), F32),
            pltpu.SemaphoreType.DMA((3,)),
        ],
    )(cells, mult, jumps, smoothed, gathered)
    coarse = jnp.swapaxes(coarse.reshape(3, CX // 2, NZ // 2, NY // 2), 2, 3)
    return (smoothed.reshape(3, CX, CY, NZ), coarse, updated.reshape(3, 1, 1, SLOTS))


def solution(mesh):
    return jax.shard_map(
        body,
        mesh=mesh,
        in_specs=(
            P(None, "gx", "gy", None),
            P(None, "gx", "gy", None),
            P("gx", "gy", None),
            P(),
            P("gx", "gy", None),
            P("gx", "gy"),
            P(None, "gx", "gy", None),
        ),
        out_specs=(P(None, "gx", "gy", None), P(None, "gx", None, None), P(None, "gx", "gy", None)),
        check_vma=False,
    )
```

```python
import jax
import jax.numpy as jnp
from jax import lax
from jax.experimental import pallas as pl
from jax.experimental.pallas import tpu as pltpu
from jax.sharding import PartitionSpec as P

SYMMETRIC_INDEX = ((0, 3, 4), (3, 1, 5), (4, 5, 2))
DAMPING = 0.6
MASS_SHIFT = 1.0
PENALTY = 1.0

CX, CY, NZ, SLOTS = 4, 32, 128, 1024
N_GX, N_GY = 32, 8
NX, NY = CX * N_GX, CY * N_GY
LABELS = 8
HALO = 3
PX = CX + 2 * HALO
PR = PX - 2
ROWS = 40
TILE = ROWS - CY
LAB0 = 3 * PX
RHS0 = LAB0 + PX
FIELDS = RHS0 + 3 * PR
OWN_LAB0 = 3 * CX
OWN_RHS0 = OWN_LAB0 + CX
OWN = OWN_RHS0 + 3 * CX
SIDE = 3 * HALO + HALO + 3 * (HALO - 1)
SLOT_ROWS = SLOTS // 128
IFACE = 4 * SLOT_ROWS
VMEM = pl.BlockSpec(memory_space=pltpu.VMEM)
SMEM = pl.BlockSpec(memory_space=pltpu.SMEM)
HBM = pl.BlockSpec(memory_space=pltpu.HBM)
F32 = jnp.float32
BF16 = jnp.bfloat16
PARAMS = pltpu.CompilerParams(vmem_limit_bytes=32 * 1024 * 1024)


def f32(*shape):
    return jax.ShapeDtypeStruct(shape, F32)


def pieces_of(value):
    high = value.astype(BF16)
    rest = value - high.astype(F32)
    middle = rest.astype(BF16)
    low = (rest - middle.astype(F32)).astype(BF16)
    return (high, middle, low)


def odd(axis):
    return lax.rem(lax.axis_index(axis), 2)


def rows_of(j, height):
    return pl.ds(j * height if isinstance(j, int) else pl.multiple_of(j * height, height), height)


def sent_planes():
    place = 0
    for first, depth in [(c * CX, HALO) for c in range(3)] + [(OWN_LAB0, HALO)] + [
        (OWN_RHS0 + c * CX, HALO - 1) for c in range(3)
    ]:
        for k in range(depth):
            yield place, first, k
            place += 1


def halo_planes():
    place = 0
    for first, depth in [(c * PX, HALO) for c in range(3)] + [(LAB0, HALO)] + [
        (RHS0 + c * PR - 1, HALO - 1) for c in range(3)
    ]:
        for k in range(depth):
            yield place, first, k
            place += 1


def slot_number():
    return lax.broadcasted_iota(jnp.int32, (SLOT_ROWS, 128), 0) * 128 + lax.broadcasted_iota(
        jnp.int32, (SLOT_ROWS, 128), 1
    )


def pack_first(
    count, disp, rhs, labels, cells_in, mult_in,
    far, y_pair, y_other, own, cells, mult,
    raw_labels, raw_cells, arrived,
):
    flip = odd("gx")
    pairs = [(cells_in, raw_cells), (mult_in, mult)]
    for g in range(CX):
        x = g + flip * (CX - 1 - 2 * g)
        pairs.append((labels.at[rows_of(x, CY)], raw_labels.at[rows_of(g, CY)]))
        for c in range(3):
            pairs.append((disp.at[rows_of(c * CX + x, CY)], own.at[rows_of(c * CX + g, CY)]))
            pairs.append((rhs.at[rows_of(c * CX + x, CY)], own.at[rows_of(OWN_RHS0 + c * CX + g, CY)]))
    copies = [pltpu.make_async_copy(a, b, arrived.at[i]) for i, (a, b) in enumerate(pairs)]
    for copy in copies:
        copy.start()
    for copy in copies:
        copy.wait()
    block_plane = raw_cells[...] // (CY * NZ)
    turned = raw_cells[...] + flip * (CX - 1 - 2 * block_plane) * (CY * NZ)
    live_cells = jnp.where(slot_number() < count[0, 0], turned, -1)
    cells[...] = live_cells
    own[pl.ds(OWN_LAB0 * CY, CX * CY), :] = raw_labels[...].astype(F32)
    for place, first, k in sent_planes():
        far[rows_of(place, CY), :] = own[rows_of(first + k, CY), :]
    far[pl.ds(SIDE * CY, SLOT_ROWS), :] = live_cells.astype(F32)
    for c in range(3):
        far[pl.ds(SIDE * CY + (1 + c) * SLOT_ROWS, SLOT_ROWS), :] = mult[c]
    up = odd("gy") == 0
    for k in range(HALO):
        first = own[pl.ds(k, OWN, stride=CY), :]
        last = own[pl.ds(CY - HALO + k, OWN, stride=CY), :]
        y_pair[k] = jnp.where(up, last, first)
        y_other[k] = jnp.where(up, first, last)


def pack_second(own, cells, mult, y_pair, y_other, dense, near, corner, wide):
    here = lax.axis_index("gy")
    to = 1 - odd("gx")
    up = odd("gy") == 0
    low = jnp.where(here > 0, 1.0, 0.0).astype(F32)
    high = jnp.where(here < N_GY - 1, 1.0, 0.0).astype(F32)
    for j in range(OWN):
        wide[pl.ds(j * ROWS, CY), :] = own[rows_of(j, CY), :]
    for k in range(HALO):
        after = jnp.where(up, y_pair[k], y_other[k])
        before = jnp.where(up, y_other[k], y_pair[k])
        wide[pl.ds(CY + k, OWN, stride=ROWS), :] = high * after
        wide[pl.ds(ROWS - HALO + k, OWN, stride=ROWS), :] = low * before
    for k in range(CY + HALO, ROWS - HALO):
        wide[pl.ds(k, OWN, stride=ROWS), :] = jnp.zeros((OWN, NZ), F32)
    for place, first, k in sent_planes():
        corner[rows_of(place, TILE), :] = wide[pl.ds((first + k) * ROWS + CY, TILE), :]
        near[to, rows_of(place, ROWS), :] = wide[rows_of(first + CX - 1 - k, ROWS), :]
    near[to, pl.ds(SIDE * ROWS, SLOT_ROWS), :] = cells[...].astype(F32)
    for c in range(3):
        near[to, pl.ds(SIDE * ROWS + (1 + c) * SLOT_ROWS, SLOT_ROWS), :] = mult[c]


def paired(array, j):
    return jnp.concatenate([array[2 * j : 2 * j + 1], array[2 * j + 1 : 2 * j + 2]], axis=1)


def spread(cells, mult, first, columns):
    column = jnp.where(cells < 0, -1, cells // NZ - first)
    depth = cells % NZ
    total = jnp.zeros((10 * columns, NZ), F32)
    parts = [piece for c in range(3) for piece in pieces_of(mult[c])]
    for j in range(SLOT_ROWS // 2):
        at_column = lax.broadcasted_iota(jnp.int32, (columns, 256), 0) == paired(column, j)
        at_depth = lax.broadcasted_iota(jnp.int32, (NZ, 256), 0) == paired(depth, j)
        left = [jnp.where(at_column, paired(piece.astype(F32), j), 0.0).astype(BF16) for piece in parts]
        left.append(jnp.where(at_column, 1.0, 0.0).astype(BF16))
        total = total + lax.dot_general(
            jnp.concatenate(left, axis=0),
            jnp.where(at_depth, 1.0, 0.0).astype(BF16),
            (((1,), (1,)), ((), ())),
            preferred_element_type=F32,
        )
    part = [total[i * columns : (i + 1) * columns] for i in range(10)]
    return [part[3 * c] + part[3 * c + 1] + part[3 * c + 2] for c in range(3)] + [part[9]]


def spread_own(cells, mult, dense):
    values = spread(cells[...], [mult[c] for c in range(3)], 0, CX * CY)
    for i in range(4):
        dense[i] = values[i]


def is_inside():
    here = lax.axis_index("gx")
    return jnp.where((here > 0) & (here < N_GX - 1), 1.0, 0.0).astype(F32)


def spread_before(far, near, dense, last, ribbon):
    flip = odd("gx")

    def at(i):
        a = far[pl.ds(SIDE * CY + i * SLOT_ROWS, SLOT_ROWS), :]
        b = near[0, pl.ds(SIDE * ROWS + i * SLOT_ROWS, SLOT_ROWS), :]
        return jnp.where(flip == 1, b, a)

    values = spread(at(0).astype(jnp.int32), [at(1 + c) for c in range(3)], flip * (CX - 1) * CY, CY)
    values[3] = values[3] * jnp.where(flip == 1, 1.0, is_inside())
    for i in range(4):
        ribbon[i, pl.ds(0, CY), :] = values[i]
        ribbon[i, pl.ds(CY, CX * CY), :] = dense[i]
        ribbon[i, pl.ds((CX + 1) * CY, CY), :] = values[i]


def times(k, v):
    return [
        k[SYMMETRIC_INDEX[c][0]] * v[0] + k[SYMMETRIC_INDEX[c][1]] * v[1] + k[SYMMETRIC_INDEX[c][2]] * v[2]
        for c in range(3)
    ]


class Split:
    def __init__(self, at, low, high):
        self.at, self.low, self.high = at, low, high

    def of(self, c, p, count=PX, base=0):
        ref = self.low if p < self.at else self.high
        return ref, rows_of(base + c * count + p, ROWS)


class Stencil:
    def __init__(self, entry, fields, coeff, total, scale, flux):
        self.entry, self.fields, self.coeff, self.total, self.scale, self.flux = (
            entry, fields, coeff, total, scale, flux
        )
        lane = lax.broadcasted_iota(jnp.int32, (1, NZ), 1)
        self.not_first = jnp.where(lane == 0, 0.0, 0.5)
        self.not_last = jnp.where(lane == NZ - 1, 0.0, 0.5)
        self.ends = jnp.where((lane == 0) | (lane == NZ - 1), 16.0, 0.0)
        row = lax.broadcasted_iota(jnp.int32, (ROWS, NZ), 0)
        y = lax.axis_index("gy") * CY + jnp.where(row < CY + HALO, row, row - ROWS)
        self.row_inside = (y >= 0) & (y < NY) & ((row < CY + HALO) | (row >= ROWS - HALO))

    def get(self, split, c, p):
        ref, at = split.of(c, p)
        return ref[at, :]

    def put(self, split, c, p, value):
        ref, at = split.of(c, p)
        ref[at, :] = value

    def label(self, p):
        ref, at = self.fields.of(0, p, base=LAB0)
        return ref[at, :]

    def right_side(self, c, p):
        ref, at = self.fields.of(c, p, count=PR, base=RHS0 - 1)
        return ref[at, :]

    def summed(self, split, c, p, edge=None):
        f = self.get(split, c, p)
        f = (f + f) + (self.get(split, c, p - 1) + self.get(split, c, p + 1))
        f = (f + f) + (pltpu.roll(f, 1, 0) + pltpu.roll(f, ROWS - 1, 0))
        f = f + (pltpu.roll(f, 1, 1) * self.not_first + pltpu.roll(f, NZ - 1, 1) * self.not_last)
        if edge is not None:
            f = f + self.ends * (0.5 * edge)
        return f + f

    def coefficients(self, planes):
        for p in planes:
            label = self.label(p)
            k = [jnp.broadcast_to(self.entry(0, e), label.shape) for e in range(6)]
            for m in range(1, LABELS):
                at = label == float(m)
                k = [jnp.where(at, self.entry(m, e), k[e]) for e in range(6)]
            for e in range(6):
                self.put(self.coeff, e, p, k[e])
            self.push(self.flux, p, [self.get(self.fields, c, p) for c in range(3)])

    def weights(self, planes):
        for p in planes:
            for e in range(6):
                k = self.get(self.coeff, e, p)
                around = self.summed(self.coeff, e, p, self.entry(0, e))
                self.put(self.total, e, p, 64.0 * k + around)
                if e < 3:
                    self.put(self.scale, e, p, DAMPING / (MASS_SHIFT + 6.0 * k + 0.125 * around))

    def push(self, flux, p, v):
        pushed = times([self.get(self.coeff, e, p) for e in range(6)], v)
        for c in range(3):
            self.put(flux, c, p, pushed[c])

    def image(self, p, v_split, flux):
        v = [self.get(v_split, c, p) for c in range(3)]
        k = [self.get(self.coeff, e, p) for e in range(6)]
        m = [self.get(self.total, e, p) for e in range(6)]
        around = [self.summed(v_split, c, p) for c in range(3)]
        pushed = [self.summed(flux, c, p) for c in range(3)]
        mine, theirs = times(m, v), times(k, around)
        return v, [MASS_SHIFT * v[c] + 0.125 * (mine[c] - theirs[c] - pushed[c]) for c in range(3)]

    def sweep(self, planes, v_split, flux, to, to_flux, inside=None):
        for p in planes:
            keep = self.row_inside if p >= HALO else self.row_inside & (inside > 0.5)
            v, a = self.image(p, v_split, flux)
            new = []
            for c in range(3):
                value = v[c] + (self.right_side(c, p) - a[c]) * self.get(self.scale, c, p)
                value = jnp.where(keep, value, 0.0)
                self.put(to, c, p, value)
                new.append(value)
            self.push(to_flux, p, new)

    def remainder(self, p, v_split, flux):
        a = self.image(p, v_split, flux)[1]
        return [(self.right_side(c, p) - a[c])[:CY] for c in range(3)]


def near_part(
    stiffness, own, near,
    fields, coeff, total, scale, flux, first, flux_first, second, flux_second, table, last,
):
    sent = 1 - odd("gx")
    for c in range(3):
        for g in range(CX):
            fields[rows_of(c * PX + HALO + g, ROWS), :] = own[rows_of(c * CX + g, ROWS), :]
            fields[rows_of(RHS0 - 1 + c * PR + HALO + g, ROWS), :] = own[rows_of(OWN_RHS0 + c * CX + g, ROWS), :]
    for g in range(CX):
        fields[rows_of(LAB0 + HALO + g, ROWS), :] = own[rows_of(OWN_LAB0 + g, ROWS), :]
    for place, at, k in halo_planes():
        fields[rows_of(at + HALO + CX + k, ROWS), :] = near[sent, rows_of(place, ROWS), :]
    for m in range(LABELS):
        for e in range(6):
            table[pl.ds(m * 6 + e, 1), :] = jnp.full((1, NZ), stiffness[m, e], F32)

    def whole(ref):
        return Split(0, None, ref)

    grid = Stencil(
        lambda m, e: stiffness[m, e], whole(fields), whole(coeff), whole(total), whole(scale), whole(flux)
    )
    grid.coefficients(range(HALO, PX))
    grid.weights(range(HALO + 1, PX - 1))
    grid.sweep(range(HALO + 1, PX - 1), whole(fields), whole(flux), whole(first), whole(flux_first))
    grid.sweep(range(HALO + 2, PX - 2), whole(first), whole(flux_first), whole(second), whole(flux_second))
    remainder = grid.remainder(HALO + 3, whole(second), whole(flux_second))
    for c in range(3):
        last[rows_of(c, CY), :] = remainder[c]


def far_part(
    far, corner, ribbon,
    near_fields, near_coeff, near_total, near_scale, near_flux,
    near_first, near_flux_first, near_second, near_flux_second, table, last,
    smoothed, jumps, message,
    fields, coeff, total, scale, flux, first, flux_first, second, flux_second, coarse,
):
    inside = is_inside()
    flip = odd("gx")
    sign = jnp.where(flip == 1, -1.0, 1.0).astype(F32)
    for place, at, k in halo_planes():
        plane = (at + HALO - 1 - k) * ROWS
        fields[pl.ds(plane, CY), :] = inside * far[rows_of(place, CY), :]
        fields[pl.ds(plane + CY, TILE), :] = inside * corner[rows_of(place, TILE), :]
    v0, flux0 = Split(HALO, fields, near_fields), Split(HALO, flux, near_flux)
    v1, flux1 = Split(HALO + 1, first, near_first), Split(HALO + 1, flux_first, near_flux_first)
    v2, flux2 = Split(HALO + 2, second, near_second), Split(HALO + 2, flux_second, near_flux_second)
    grid = Stencil(
        lambda m, e: table[pl.ds(m * 6 + e, 1), :],
        v0,
        Split(HALO, coeff, near_coeff),
        Split(HALO + 1, total, near_total),
        Split(HALO + 1, scale, near_scale),
        flux0,
    )
    grid.coefficients(range(HALO))
    grid.weights(range(1, HALO + 1))
    grid.sweep(range(1, HALO + 1), v0, flux0, v1, flux1, inside)
    grid.sweep(range(2, HALO + 2), v1, flux1, v2, flux2, inside)
    remainders = [grid.remainder(HALO + g, v2, flux2) for g in range(CX - 1)]
    remainders.append([last[rows_of(c, CY), :] for c in range(3)])

    for c in range(3):
        planes = [grid.get(v2, c, HALO - 1 + i)[:CY] for i in range(CX + 2)]
        for g in range(CX):
            x = g + flip * (CX - 1 - 2 * g)
            smoothed[rows_of(c * CX + x, CY), :] = planes[1 + g]
        pushed = []
        for i in range(CX + 1):
            jump = sign * (planes[i] - planes[i + 1])
            jumps[c, rows_of(i, CY), :] = jump
            at = rows_of(i + flip, CY)
            pushed.append(jnp.where(ribbon[3, at, :] > 0.5, ribbon[c, at, :] + PENALTY * jump, 0.0))
        parts = [remainders[g][c] - sign * (pushed[g + 1] - pushed[g]) for g in range(CX)]
        for half in range(2):
            coarse[rows_of(half * 3 + c, CY), :] = parts[2 * half] + parts[2 * half + 1]

    out = jnp.zeros((3 * CY // 2, NZ), F32)
    lane_in = lax.broadcasted_iota(jnp.int32, (NZ, NZ), 0)
    lane_out = lax.broadcasted_iota(jnp.int32, (NZ, NZ), 1)
    for half in range(2):
        at = 3 * half * CY
        rows = coarse[pl.ds(at, 3 * CY // 2, stride=2), :] + coarse[pl.ds(at + 1, 3 * CY // 2, stride=2), :]
        x = half + flip * (1 - 2 * half)
        pick = jnp.where(lane_in // 2 + x * (NZ // 2) == lane_out, 1.0, 0.0).astype(BF16)
        for piece in pieces_of(rows):
            out = out + jnp.dot(piece, pick, preferred_element_type=F32)
    for s in range(N_GY):
        message[s] = out


def finish(
    cells, mult, jumps, smoothed, gathered,
    smoothed_out, updated_out, coarse_out,
    updated, coarse, done,
):
    copies = [
        pltpu.make_async_copy(smoothed, smoothed_out, done.at[0]),
        pltpu.make_async_copy(coarse, coarse_out, done.at[1]),
        pltpu.make_async_copy(updated, updated_out, done.at[2]),
    ]
    copies[0].start()
    for c in range(3):
        parts = [gathered[s, pl.ds(c * CY // 2, CY // 2), :] for s in range(N_GY)]
        coarse[c] = jnp.transpose(jnp.concatenate(parts, axis=0))
    copies[1].start()
    live = cells[...] >= 0
    column, depth = cells[...] // NZ, cells[...] % NZ
    block = CX * CY
    start = pl.multiple_of((1 - odd("gx")) * CY, CY)
    left = jnp.concatenate(
        [jnp.concatenate(pieces_of(jumps[c, pl.ds(start, block), :]), axis=1) for c in range(3)], axis=0
    )
    for j in range(SLOT_ROWS):
        at_depth = lax.broadcasted_iota(jnp.int32, (NZ, 128), 0) == depth[j : j + 1]
        right = jnp.where(at_depth, 1.0, 0.0).astype(BF16)
        picked = jnp.dot(left, jnp.concatenate([right] * 3, axis=0), preferred_element_type=F32)
        at_column = lax.broadcasted_iota(jnp.int32, (block, 128), 0) == column[j : j + 1]
        for c in range(3):
            jump = jnp.sum(
                jnp.where(at_column, picked[c * block : (c + 1) * block], 0.0), axis=0, keepdims=True
            )
            old = mult[c, j : j + 1, :]
            updated[c, j : j + 1, :] = jnp.where(live[j : j + 1], old + PENALTY * jump, old)
    copies[2].start()
    for copy in copies:
        copy.wait()


def in_hbm(array):
    return pltpu.with_memory_space_constraint(array, pltpu.HBM)


def call(kernel, outs, ins, out_specs=None, scratch=()):
    return pl.pallas_call(
        kernel,
        out_shape=outs,
        in_specs=ins,
        out_specs=out_specs or [VMEM] * len(outs),
        scratch_shapes=list(scratch),
        compiler_params=PARAMS,
        cost_estimate=pl.CostEstimate(flops=1000, bytes_accessed=1000, transcendentals=0),
    )


def pair(n):
    return [(i, i ^ 1) for i in range(n)]


def other(n):
    return [(i, (((i + 1) % n ^ 1) - 1) % n) for i in range(n)]


def body(displacement, rhs, labels, stiffness, rows, counts, multipliers):
    block = CX * CY
    copies = 2 + 7 * CX
    far, y_pair, y_other, own, cells, mult = call(
        pack_first,
        [
            f32(SIDE * CY + IFACE, NZ), f32(HALO, OWN, NZ), f32(HALO, OWN, NZ), f32(OWN * CY, NZ),
            jax.ShapeDtypeStruct((SLOT_ROWS, 128), jnp.int32), f32(3, SLOT_ROWS, 128),
        ],
        [SMEM] + [HBM] * 5,
        scratch=[
            pltpu.VMEM((block, NZ), jnp.int32),
            pltpu.VMEM((SLOT_ROWS, 128), jnp.int32),
            pltpu.SemaphoreType.DMA((copies,)),
        ],
    )(
        counts,
        in_hbm(displacement.reshape(3 * block, NZ)),
        in_hbm(rhs.reshape(3 * block, NZ)),
        in_hbm(labels.reshape(block, NZ)),
        in_hbm(rows.reshape(SLOT_ROWS, 128)),
        in_hbm(multipliers.reshape(3, SLOT_ROWS, 128)),
    )
    far = lax.ppermute(far, "gx", other(N_GX))
    y_other = lax.ppermute(y_other, "gy", other(N_GY))
    y_pair = lax.ppermute(y_pair, "gy", pair(N_GY))
    (dense,) = call(spread_own, [f32(4, block, NZ)], [VMEM] * 2)(cells, mult)
    near, corner, own = call(
        pack_second, [f32(2, SIDE * ROWS + IFACE, NZ), f32(SIDE * TILE, NZ), f32(OWN * ROWS, NZ)], [VMEM] * 6
    )(own, cells, mult, y_pair, y_other, dense)
    corner = lax.ppermute(corner, "gx", other(N_GX))
    near = lax.all_to_all(near, "gx", 0, 0, axis_index_groups=[[i, i + 1] for i in range(0, N_GX, 2)])
    three, six = f32(3 * PX * ROWS, NZ), f32(6 * PX * ROWS, NZ)
    arrays = [f32(FIELDS * ROWS, NZ), six, six] + [three] * 6
    half = call(
        near_part, arrays + [f32(LABELS * 6, NZ), f32(3 * CY, NZ)], [SMEM, VMEM, VMEM]
    )(stiffness, own, near)
    (ribbon,) = call(spread_before, [f32(4, (CX + 2) * CY, NZ)], [VMEM] * 4)(far, near, dense, half[-1])
    smoothed, jumps, message = call(
        far_part,
        [f32(3 * block, NZ), f32(3, (CX + 1) * CY, NZ), f32(N_GY, 3 * CY // 2, NZ)],
        [VMEM] * (3 + len(half)),
        scratch=[pltpu.VMEM(a.shape, F32) for a in arrays] + [pltpu.VMEM((6 * CY, NZ), F32)],
    )(far, corner, ribbon, *half)
    gathered = lax.all_to_all(message, "gy", 0, 0)
    smoothed, updated, coarse = call(
        finish,
        [pltpu.HBM(s, F32) for s in ((3 * block, NZ), (3, SLOT_ROWS, 128), (3, CX // 2 * NZ // 2, NY // 2))],
        [VMEM] * 5,
        out_specs=[HBM] * 3,
        scratch=[
            pltpu.VMEM((3, SLOT_ROWS, 128), F32),
            pltpu.VMEM((3, CX // 2 * NZ // 2, NY // 2), F32),
            pltpu.SemaphoreType.DMA((3,)),
        ],
    )(cells, mult, jumps, smoothed, gathered)
    coarse = jnp.swapaxes(coarse.reshape(3, CX // 2, NZ // 2, NY // 2), 2, 3)
    return (smoothed.reshape(3, CX, CY, NZ), coarse, updated.reshape(3, 1, 1, SLOTS))


def solution(mesh):
    return jax.shard_map(
        body,
        mesh=mesh,
        in_specs=(
            P(None, "gx", "gy", None),
            P(None, "gx", "gy", None),
            P("gx", "gy", None),
            P(),
            P("gx", "gy", None),
            P("gx", "gy"),
            P(None, "gx", "gy", None),
        ),
        out_specs=(P(None, "gx", "gy", None), P(None, "gx", None, None), P(None, "gx", "gy", None)),
        check_vma=False,
    )
```

```python
import jax
import jax.numpy as jnp
from jax import lax
from jax.experimental import pallas as pl
from jax.experimental.pallas import tpu as pltpu
from jax.sharding import PartitionSpec as P

SYMMETRIC_INDEX = ((0, 3, 4), (3, 1, 5), (4, 5, 2))
DAMPING = 0.6
MASS_SHIFT = 1.0
PENALTY = 1.0

CX, CY, NZ, SLOTS = 4, 32, 128, 1024
N_GX, N_GY = 32, 8
NX, NY = CX * N_GX, CY * N_GY
LABELS = 8
HALO = 3
PX = CX + 2 * HALO
PR = PX - 2
ROWS = 40
TILE = ROWS - CY
LAB0 = 3 * PX
RHS0 = LAB0 + PX
FIELDS = RHS0 + 3 * PR
OWN_LAB0 = 3 * CX
OWN_RHS0 = OWN_LAB0 + CX
OWN = OWN_RHS0 + 3 * CX
SIDE = 3 * HALO + HALO + 3 * (HALO - 1)
SLOT_ROWS = SLOTS // 128
IFACE = 4 * SLOT_ROWS
VMEM = pl.BlockSpec(memory_space=pltpu.VMEM)
SMEM = pl.BlockSpec(memory_space=pltpu.SMEM)
HBM = pl.BlockSpec(memory_space=pltpu.HBM)
F32 = jnp.float32
BF16 = jnp.bfloat16
PARAMS = pltpu.CompilerParams(vmem_limit_bytes=32 * 1024 * 1024)


def f32(*shape):
    return jax.ShapeDtypeStruct(shape, F32)


def pieces_of(value):
    high = value.astype(BF16)
    rest = value - high.astype(F32)
    middle = rest.astype(BF16)
    low = (rest - middle.astype(F32)).astype(BF16)
    return (high, middle, low)


def odd(axis):
    return lax.rem(lax.axis_index(axis), 2)


def rows_of(j, height):
    return pl.ds(j * height if isinstance(j, int) else pl.multiple_of(j * height, height), height)


def sent_planes():
    place = 0
    for first, depth in [(c * CX, HALO) for c in range(3)] + [(OWN_LAB0, HALO)] + [
        (OWN_RHS0 + c * CX, HALO - 1) for c in range(3)
    ]:
        for k in range(depth):
            yield place, first, k
            place += 1


def halo_planes():
    place = 0
    for first, depth in [(c * PX, HALO) for c in range(3)] + [(LAB0, HALO)] + [
        (RHS0 + c * PR - 1, HALO - 1) for c in range(3)
    ]:
        for k in range(depth):
            yield place, first, k
            place += 1


def slot_number():
    return lax.broadcasted_iota(jnp.int32, (SLOT_ROWS, 128), 0) * 128 + lax.broadcasted_iota(
        jnp.int32, (SLOT_ROWS, 128), 1
    )


def pack_first(
    count, disp, rhs, labels, cells_in, mult_in,
    far, y_pair, y_other, own, cells, mult,
    raw_labels, raw_cells, arrived,
):
    flip = odd("gx")
    pairs = [(cells_in, raw_cells), (mult_in, mult)]
    for g in range(CX):
        x = g + flip * (CX - 1 - 2 * g)
        pairs.append((labels.at[rows_of(x, CY)], raw_labels.at[rows_of(g, CY)]))
        for c in range(3):
            pairs.append((disp.at[rows_of(c * CX + x, CY)], own.at[rows_of(c * CX + g, CY)]))
            pairs.append((rhs.at[rows_of(c * CX + x, CY)], own.at[rows_of(OWN_RHS0 + c * CX + g, CY)]))
    copies = [pltpu.make_async_copy(a, b, arrived.at[i]) for i, (a, b) in enumerate(pairs)]
    for copy in copies:
        copy.start()
    for copy in copies:
        copy.wait()
    block_plane = raw_cells[...] // (CY * NZ)
    turned = raw_cells[...] + flip * (CX - 1 - 2 * block_plane) * (CY * NZ)
    live_cells = jnp.where(slot_number() < count[0, 0], turned, -1)
    cells[...] = live_cells
    own[pl.ds(OWN_LAB0 * CY, CX * CY), :] = raw_labels[...].astype(F32)
    for place, first, k in sent_planes():
        far[rows_of(place, CY), :] = own[rows_of(first + k, CY), :]
    far[pl.ds(SIDE * CY, SLOT_ROWS), :] = live_cells.astype(F32)
    for c in range(3):
        far[pl.ds(SIDE * CY + (1 + c) * SLOT_ROWS, SLOT_ROWS), :] = mult[c]
    up = odd("gy") == 0
    for k in range(HALO):
        first = own[pl.ds(k, OWN, stride=CY), :]
        last = own[pl.ds(CY - HALO + k, OWN, stride=CY), :]
        y_pair[k] = jnp.where(up, last, first)
        y_other[k] = jnp.where(up, first, last)


def pack_second(own, cells, mult, y_pair, y_other, near, corner, wide):
    here = lax.axis_index("gy")
    up = odd("gy") == 0
    low = jnp.where(here > 0, 1.0, 0.0).astype(F32)
    high = jnp.where(here < N_GY - 1, 1.0, 0.0).astype(F32)
    for j in range(OWN):
        wide[pl.ds(j * ROWS, CY), :] = own[rows_of(j, CY), :]
    for k in range(HALO):
        after = jnp.where(up, y_pair[k], y_other[k])
        before = jnp.where(up, y_other[k], y_pair[k])
        wide[pl.ds(CY + k, OWN, stride=ROWS), :] = high * after
        wide[pl.ds(ROWS - HALO + k, OWN, stride=ROWS), :] = low * before
    for k in range(CY + HALO, ROWS - HALO):
        wide[pl.ds(k, OWN, stride=ROWS), :] = jnp.zeros((OWN, NZ), F32)
    for place, first, k in sent_planes():
        corner[rows_of(place, TILE), :] = wide[pl.ds((first + k) * ROWS + CY, TILE), :]
        near[rows_of(place, ROWS), :] = wide[rows_of(first + CX - 1 - k, ROWS), :]
    near[pl.ds(SIDE * ROWS, SLOT_ROWS), :] = cells[...].astype(F32)
    for c in range(3):
        near[pl.ds(SIDE * ROWS + (1 + c) * SLOT_ROWS, SLOT_ROWS), :] = mult[c]


def paired(array, j):
    return jnp.concatenate([array[2 * j : 2 * j + 1], array[2 * j + 1 : 2 * j + 2]], axis=1)


def spread(cells, mult, first, columns):
    column = jnp.where(cells < 0, -1, cells // NZ - first)
    depth = cells % NZ
    total = jnp.zeros((10 * columns, NZ), F32)
    parts = [piece for c in range(3) for piece in pieces_of(mult[c])]
    for j in range(SLOT_ROWS // 2):
        at_column = lax.broadcasted_iota(jnp.int32, (columns, 256), 0) == paired(column, j)
        at_depth = lax.broadcasted_iota(jnp.int32, (NZ, 256), 0) == paired(depth, j)
        left = [jnp.where(at_column, paired(piece.astype(F32), j), 0.0).astype(BF16) for piece in parts]
        left.append(jnp.where(at_column, 1.0, 0.0).astype(BF16))
        total = total + lax.dot_general(
            jnp.concatenate(left, axis=0),
            jnp.where(at_depth, 1.0, 0.0).astype(BF16),
            (((1,), (1,)), ((), ())),
            preferred_element_type=F32,
        )
    part = [total[i * columns : (i + 1) * columns] for i in range(10)]
    return [part[3 * c] + part[3 * c + 1] + part[3 * c + 2] for c in range(3)] + [part[9]]


def spread_own(cells, mult, dense):
    values = spread(cells[...], [mult[c] for c in range(3)], 0, CX * CY)
    for i in range(4):
        dense[i] = values[i]


def is_inside():
    here = lax.axis_index("gx")
    return jnp.where((here > 0) & (here < N_GX - 1), 1.0, 0.0).astype(F32)


def spread_before(far, near, dense, last, ribbon):
    flip = odd("gx")

    def at(i):
        a = far[pl.ds(SIDE * CY + i * SLOT_ROWS, SLOT_ROWS), :]
        b = near[pl.ds(SIDE * ROWS + i * SLOT_ROWS, SLOT_ROWS), :]
        return jnp.where(flip == 1, b, a)

    values = spread(at(0).astype(jnp.int32), [at(1 + c) for c in range(3)], flip * (CX - 1) * CY, CY)
    values[3] = values[3] * jnp.where(flip == 1, 1.0, is_inside())
    for i in range(4):
        ribbon[i, pl.ds(0, CY), :] = values[i]
        ribbon[i, pl.ds(CY, CX * CY), :] = dense[i]
        ribbon[i, pl.ds((CX + 1) * CY, CY), :] = values[i]


def times(k, v):
    return [
        k[SYMMETRIC_INDEX[c][0]] * v[0] + k[SYMMETRIC_INDEX[c][1]] * v[1] + k[SYMMETRIC_INDEX[c][2]] * v[2]
        for c in range(3)
    ]


class Split:
    def __init__(self, at, low, high):
        self.at, self.low, self.high = at, low, high

    def of(self, c, p, count=PX, base=0):
        ref = self.low if p < self.at else self.high
        return ref, rows_of(base + c * count + p, ROWS)


class Stencil:
    def __init__(self, entry, fields, coeff, total, scale, flux):
        self.entry, self.fields, self.coeff, self.total, self.scale, self.flux = (
            entry, fields, coeff, total, scale, flux
        )
        lane = lax.broadcasted_iota(jnp.int32, (1, NZ), 1)
        self.not_first = jnp.where(lane == 0, 0.0, 0.5)
        self.not_last = jnp.where(lane == NZ - 1, 0.0, 0.5)
        self.ends = jnp.where((lane == 0) | (lane == NZ - 1), 16.0, 0.0)
        row = lax.broadcasted_iota(jnp.int32, (ROWS, NZ), 0)
        y = lax.axis_index("gy") * CY + jnp.where(row < CY + HALO, row, row - ROWS)
        self.row_inside = (y >= 0) & (y < NY) & ((row < CY + HALO) | (row >= ROWS - HALO))

    def get(self, split, c, p):
        ref, at = split.of(c, p)
        return ref[at, :]

    def put(self, split, c, p, value):
        ref, at = split.of(c, p)
        ref[at, :] = value

    def label(self, p):
        ref, at = self.fields.of(0, p, base=LAB0)
        return ref[at, :]

    def right_side(self, c, p):
        ref, at = self.fields.of(c, p, count=PR, base=RHS0 - 1)
        return ref[at, :]

    def summed(self, split, c, p, edge=None):
        f = self.get(split, c, p)
        f = (f + f) + (self.get(split, c, p - 1) + self.get(split, c, p + 1))
        f = (f + f) + (pltpu.roll(f, 1, 0) + pltpu.roll(f, ROWS - 1, 0))
        f = f + (pltpu.roll(f, 1, 1) * self.not_first + pltpu.roll(f, NZ - 1, 1) * self.not_last)
        if edge is not None:
            f = f + self.ends * (0.5 * edge)
        return f + f

    def coefficients(self, planes):
        for p in planes:
            label = self.label(p)
            k = [jnp.broadcast_to(self.entry(0, e), label.shape) for e in range(6)]
            for m in range(1, LABELS):
                at = label == float(m)
                k = [jnp.where(at, self.entry(m, e), k[e]) for e in range(6)]
            for e in range(6):
                self.put(self.coeff, e, p, k[e])
            self.push(self.flux, p, [self.get(self.fields, c, p) for c in range(3)])

    def weights(self, planes):
        for p in planes:
            for e in range(6):
                k = self.get(self.coeff, e, p)
                around = self.summed(self.coeff, e, p, self.entry(0, e))
                self.put(self.total, e, p, 64.0 * k + around)
                if e < 3:
                    self.put(self.scale, e, p, DAMPING / (MASS_SHIFT + 6.0 * k + 0.125 * around))

    def push(self, flux, p, v):
        pushed = times([self.get(self.coeff, e, p) for e in range(6)], v)
        for c in range(3):
            self.put(flux, c, p, pushed[c])

    def image(self, p, v_split, flux):
        v = [self.get(v_split, c, p) for c in range(3)]
        k = [self.get(self.coeff, e, p) for e in range(6)]
        m = [self.get(self.total, e, p) for e in range(6)]
        around = [self.summed(v_split, c, p) for c in range(3)]
        pushed = [self.summed(flux, c, p) for c in range(3)]
        mine, theirs = times(m, v), times(k, around)
        return v, [MASS_SHIFT * v[c] + 0.125 * (mine[c] - theirs[c] - pushed[c]) for c in range(3)]

    def sweep(self, planes, v_split, flux, to, to_flux, inside=None):
        for p in planes:
            keep = self.row_inside if p >= HALO else self.row_inside & (inside > 0.5)
            v, a = self.image(p, v_split, flux)
            new = []
            for c in range(3):
                value = v[c] + (self.right_side(c, p) - a[c]) * self.get(self.scale, c, p)
                value = jnp.where(keep, value, 0.0)
                self.put(to, c, p, value)
                new.append(value)
            self.push(to_flux, p, new)

    def remainder(self, p, v_split, flux):
        a = self.image(p, v_split, flux)[1]
        return [(self.right_side(c, p) - a[c])[:CY] for c in range(3)]


def near_part(
    stiffness, own, near,
    fields, coeff, total, scale, flux, first, flux_first, second, flux_second, table, last,
):
    for c in range(3):
        for g in range(CX):
            fields[rows_of(c * PX + HALO + g, ROWS), :] = own[rows_of(c * CX + g, ROWS), :]
            fields[rows_of(RHS0 - 1 + c * PR + HALO + g, ROWS), :] = own[rows_of(OWN_RHS0 + c * CX + g, ROWS), :]
    for g in range(CX):
        fields[rows_of(LAB0 + HALO + g, ROWS), :] = own[rows_of(OWN_LAB0 + g, ROWS), :]
    for place, at, k in halo_planes():
        fields[rows_of(at + HALO + CX + k, ROWS), :] = near[rows_of(place, ROWS), :]
    for m in range(LABELS):
        for e in range(6):
            table[pl.ds(m * 6 + e, 1), :] = jnp.full((1, NZ), stiffness[m, e], F32)

    def whole(ref):
        return Split(0, None, ref)

    grid = Stencil(
        lambda m, e: stiffness[m, e], whole(fields), whole(coeff), whole(total), whole(scale), whole(flux)
    )
    grid.coefficients(range(HALO, PX))
    grid.weights(range(HALO + 1, PX - 1))
    grid.sweep(range(HALO + 1, PX - 1), whole(fields), whole(flux), whole(first), whole(flux_first))
    grid.sweep(range(HALO + 2, PX - 2), whole(first), whole(flux_first), whole(second), whole(flux_second))
    remainder = grid.remainder(HALO + 3, whole(second), whole(flux_second))
    for c in range(3):
        last[rows_of(c, CY), :] = remainder[c]


def far_part(
    far, corner, ribbon,
    near_fields, near_coeff, near_total, near_scale, near_flux,
    near_first, near_flux_first, near_second, near_flux_second, table, last,
    smoothed, jumps, message,
    fields, coeff, total, scale, flux, first, flux_first, second, flux_second, coarse,
):
    inside = is_inside()
    flip = odd("gx")
    sign = jnp.where(flip == 1, -1.0, 1.0).astype(F32)
    for place, at, k in halo_planes():
        plane = (at + HALO - 1 - k) * ROWS
        fields[pl.ds(plane, CY), :] = inside * far[rows_of(place, CY), :]
        fields[pl.ds(plane + CY, TILE), :] = inside * corner[rows_of(place, TILE), :]
    v0, flux0 = Split(HALO, fields, near_fields), Split(HALO, flux, near_flux)
    v1, flux1 = Split(HALO + 1, first, near_first), Split(HALO + 1, flux_first, near_flux_first)
    v2, flux2 = Split(HALO + 2, second, near_second), Split(HALO + 2, flux_second, near_flux_second)
    grid = Stencil(
        lambda m, e: table[pl.ds(m * 6 + e, 1), :],
        v0,
        Split(HALO, coeff, near_coeff),
        Split(HALO + 1, total, near_total),
        Split(HALO + 1, scale, near_scale),
        flux0,
    )
    grid.coefficients(range(HALO))
    grid.weights(range(1, HALO + 1))
    grid.sweep(range(1, HALO + 1), v0, flux0, v1, flux1, inside)
    grid.sweep(range(2, HALO + 2), v1, flux1, v2, flux2, inside)
    remainders = [grid.remainder(HALO + g, v2, flux2) for g in range(CX - 1)]
    remainders.append([last[rows_of(c, CY), :] for c in range(3)])

    for c in range(3):
        planes = [grid.get(v2, c, HALO - 1 + i)[:CY] for i in range(CX + 2)]
        for g in range(CX):
            x = g + flip * (CX - 1 - 2 * g)
            smoothed[rows_of(c * CX + x, CY), :] = planes[1 + g]
        pushed = []
        for i in range(CX + 1):
            jump = sign * (planes[i] - planes[i + 1])
            jumps[c, rows_of(i, CY), :] = jump
            at = rows_of(i + flip, CY)
            pushed.append(jnp.where(ribbon[3, at, :] > 0.5, ribbon[c, at, :] + PENALTY * jump, 0.0))
        parts = [remainders[g][c] - sign * (pushed[g + 1] - pushed[g]) for g in range(CX)]
        for half in range(2):
            coarse[rows_of(half * 3 + c, CY), :] = parts[2 * half] + parts[2 * half + 1]

    out = jnp.zeros((3 * CY // 2, NZ), F32)
    lane_in = lax.broadcasted_iota(jnp.int32, (NZ, NZ), 0)
    lane_out = lax.broadcasted_iota(jnp.int32, (NZ, NZ), 1)
    for half in range(2):
        at = 3 * half * CY
        rows = coarse[pl.ds(at, 3 * CY // 2, stride=2), :] + coarse[pl.ds(at + 1, 3 * CY // 2, stride=2), :]
        x = half + flip * (1 - 2 * half)
        pick = jnp.where(lane_in // 2 + x * (NZ // 2) == lane_out, 1.0, 0.0).astype(BF16)
        for piece in pieces_of(rows):
            out = out + jnp.dot(piece, pick, preferred_element_type=F32)
    for s in range(N_GY):
        message[s] = out


def finish(
    cells, mult, jumps, smoothed, gathered,
    smoothed_out, updated_out, coarse_out,
    updated, coarse, done,
):
    copies = [
        pltpu.make_async_copy(smoothed, smoothed_out, done.at[0]),
        pltpu.make_async_copy(coarse, coarse_out, done.at[1]),
        pltpu.make_async_copy(updated, updated_out, done.at[2]),
    ]
    copies[0].start()
    for c in range(3):
        parts = [gathered[s, pl.ds(c * CY // 2, CY // 2), :] for s in range(N_GY)]
        coarse[c] = jnp.transpose(jnp.concatenate(parts, axis=0))
    copies[1].start()
    live = cells[...] >= 0
    column, depth = cells[...] // NZ, cells[...] % NZ
    block = CX * CY
    start = pl.multiple_of((1 - odd("gx")) * CY, CY)
    left = jnp.concatenate(
        [jnp.concatenate(pieces_of(jumps[c, pl.ds(start, block), :]), axis=1) for c in range(3)], axis=0
    )
    for j in range(SLOT_ROWS):
        at_depth = lax.broadcasted_iota(jnp.int32, (NZ, 128), 0) == depth[j : j + 1]
        right = jnp.where(at_depth, 1.0, 0.0).astype(BF16)
        picked = jnp.dot(left, jnp.concatenate([right] * 3, axis=0), preferred_element_type=F32)
        at_column = lax.broadcasted_iota(jnp.int32, (block, 128), 0) == column[j : j + 1]
        for c in range(3):
            jump = jnp.sum(
                jnp.where(at_column, picked[c * block : (c + 1) * block], 0.0), axis=0, keepdims=True
            )
            old = mult[c, j : j + 1, :]
            updated[c, j : j + 1, :] = jnp.where(live[j : j + 1], old + PENALTY * jump, old)
    copies[2].start()
    for copy in copies:
        copy.wait()


def in_hbm(array):
    return pltpu.with_memory_space_constraint(array, pltpu.HBM)


def call(kernel, outs, ins, out_specs=None, scratch=(), flops=1000):
    return pl.pallas_call(
        kernel,
        out_shape=outs,
        in_specs=ins,
        out_specs=out_specs or [VMEM] * len(outs),
        scratch_shapes=list(scratch),
        compiler_params=PARAMS,
        cost_estimate=pl.CostEstimate(flops=flops, bytes_accessed=1000, transcendentals=0),
    )


def pair(n):
    return [(i, i ^ 1) for i in range(n)]


def other(n):
    return [(i, (((i + 1) % n ^ 1) - 1) % n) for i in range(n)]


def body(displacement, rhs, labels, stiffness, rows, counts, multipliers):
    block = CX * CY
    copies = 2 + 7 * CX
    far, y_pair, y_other, own, cells, mult = call(
        pack_first,
        [
            f32(SIDE * CY + IFACE, NZ), f32(HALO, OWN, NZ), f32(HALO, OWN, NZ), f32(OWN * CY, NZ),
            jax.ShapeDtypeStruct((SLOT_ROWS, 128), jnp.int32), f32(3, SLOT_ROWS, 128),
        ],
        [SMEM] + [HBM] * 5,
        scratch=[
            pltpu.VMEM((block, NZ), jnp.int32),
            pltpu.VMEM((SLOT_ROWS, 128), jnp.int32),
            pltpu.SemaphoreType.DMA((copies,)),
        ],
    )(
        counts,
        in_hbm(displacement.reshape(3 * block, NZ)),
        in_hbm(rhs.reshape(3 * block, NZ)),
        in_hbm(labels.reshape(block, NZ)),
        in_hbm(rows.reshape(SLOT_ROWS, 128)),
        in_hbm(multipliers.reshape(3, SLOT_ROWS, 128)),
    )
    far = lax.ppermute(far, "gx", other(N_GX))
    y_other = lax.ppermute(y_other, "gy", other(N_GY))
    y_pair = lax.ppermute(y_pair, "gy", pair(N_GY))
    (dense,) = call(spread_own, [f32(4, block, NZ)], [VMEM] * 2, flops=100000000000)(cells, mult)
    near, corner, own = call(
        pack_second, [f32(SIDE * ROWS + IFACE, NZ), f32(SIDE * TILE, NZ), f32(OWN * ROWS, NZ)], [VMEM] * 5
    )(own, cells, mult, y_pair, y_other)
    corner = lax.ppermute(corner, "gx", other(N_GX))
    near = lax.ppermute(near, "gx", pair(N_GX))
    three, six = f32(3 * PX * ROWS, NZ), f32(6 * PX * ROWS, NZ)
    arrays = [f32(FIELDS * ROWS, NZ), six, six] + [three] * 6
    half = call(
        near_part, arrays + [f32(LABELS * 6, NZ), f32(3 * CY, NZ)], [SMEM, VMEM, VMEM]
    )(stiffness, own, near)
    (ribbon,) = call(spread_before, [f32(4, (CX + 2) * CY, NZ)], [VMEM] * 4)(far, near, dense, half[-1])
    smoothed, jumps, message = call(
        far_part,
        [f32(3 * block, NZ), f32(3, (CX + 1) * CY, NZ), f32(N_GY, 3 * CY // 2, NZ)],
        [VMEM] * (3 + len(half)),
        scratch=[pltpu.VMEM(a.shape, F32) for a in arrays] + [pltpu.VMEM((6 * CY, NZ), F32)],
    )(far, corner, ribbon, *half)
    gathered = lax.all_to_all(message, "gy", 0, 0)
    smoothed, updated, coarse = call(
        finish,
        [pltpu.HBM(s, F32) for s in ((3 * block, NZ), (3, SLOT_ROWS, 128), (3, CX // 2 * NZ // 2, NY // 2))],
        [VMEM] * 5,
        out_specs=[HBM] * 3,
        scratch=[
            pltpu.VMEM((3, SLOT_ROWS, 128), F32),
            pltpu.VMEM((3, CX // 2 * NZ // 2, NY // 2), F32),
            pltpu.SemaphoreType.DMA((3,)),
        ],
    )(cells, mult, jumps, smoothed, gathered)
    coarse = jnp.swapaxes(coarse.reshape(3, CX // 2, NZ // 2, NY // 2), 2, 3)
    return (smoothed.reshape(3, CX, CY, NZ), coarse, updated.reshape(3, 1, 1, SLOTS))


def solution(mesh):
    return jax.shard_map(
        body,
        mesh=mesh,
        in_specs=(
            P(None, "gx", "gy", None),
            P(None, "gx", "gy", None),
            P("gx", "gy", None),
            P(),
            P("gx", "gy", None),
            P("gx", "gy"),
            P(None, "gx", "gy", None),
        ),
        out_specs=(P(None, "gx", "gy", None), P(None, "gx", None, None), P(None, "gx", "gy", None)),
        check_vma=False,
    )
```

```python
import jax
import jax.numpy as jnp
from jax import lax
from jax.experimental import pallas as pl
from jax.experimental.pallas import tpu as pltpu
from jax.sharding import PartitionSpec as P

SYMMETRIC_INDEX = ((0, 3, 4), (3, 1, 5), (4, 5, 2))
DAMPING = 0.6
MASS_SHIFT = 1.0
PENALTY = 1.0

CX, CY, NZ, SLOTS = 4, 32, 128, 1024
N_GX, N_GY = 32, 8
NX, NY = CX * N_GX, CY * N_GY
LABELS = 8
HALO = 3
PX = CX + 2 * HALO
PR = PX - 2
ROWS = 40
LAB0 = 3 * PX
RHS0 = LAB0 + PX
FIELDS = RHS0 + 3 * PR
OWN_LAB0 = 3 * CX
OWN_RHS0 = OWN_LAB0 + CX
OWN = OWN_RHS0 + 3 * CX
SIDE = 3 * HALO + HALO + 3 * (HALO - 1)
SLOT_ROWS = SLOTS // 128
IFACE = 4 * SLOT_ROWS
VMEM = pl.BlockSpec(memory_space=pltpu.VMEM)
SMEM = pl.BlockSpec(memory_space=pltpu.SMEM)
HBM = pl.BlockSpec(memory_space=pltpu.HBM)
F32 = jnp.float32
BF16 = jnp.bfloat16
PARAMS = pltpu.CompilerParams(vmem_limit_bytes=32 * 1024 * 1024)


def f32(*shape):
    return jax.ShapeDtypeStruct(shape, F32)


def pieces_of(value):
    high = value.astype(BF16)
    rest = value - high.astype(F32)
    middle = rest.astype(BF16)
    low = (rest - middle.astype(F32)).astype(BF16)
    return (high, middle, low)


def odd(axis):
    return lax.rem(lax.axis_index(axis), 2)


def rows_of(j, height):
    return pl.ds(j * height if isinstance(j, int) else pl.multiple_of(j * height, height), height)


def sent_planes():
    place = 0
    for first, depth in [(c * CX, HALO) for c in range(3)] + [(OWN_LAB0, HALO)] + [
        (OWN_RHS0 + c * CX, HALO - 1) for c in range(3)
    ]:
        for k in range(depth):
            yield place, first, k
            place += 1


def halo_planes():
    place = 0
    for first, depth in [(c * PX, HALO) for c in range(3)] + [(LAB0, HALO)] + [
        (RHS0 + c * PR - 1, HALO - 1) for c in range(3)
    ]:
        for k in range(depth):
            yield place, first, k
            place += 1


def slot_number():
    return lax.broadcasted_iota(jnp.int32, (SLOT_ROWS, 128), 0) * 128 + lax.broadcasted_iota(
        jnp.int32, (SLOT_ROWS, 128), 1
    )


def pack_first(
    count, disp, rhs, labels, cells_in, mult_in,
    far, y_pair, y_other, own, cells, mult,
    raw_labels, raw_cells, arrived,
):
    flip = odd("gx")
    pairs = [(cells_in, raw_cells), (mult_in, mult)]
    for g in range(CX):
        x = g + flip * (CX - 1 - 2 * g)
        pairs.append((labels.at[rows_of(x, CY)], raw_labels.at[rows_of(g, CY)]))
        for c in range(3):
            pairs.append((disp.at[rows_of(c * CX + x, CY)], own.at[rows_of(c * CX + g, CY)]))
            pairs.append((rhs.at[rows_of(c * CX + x, CY)], own.at[rows_of(OWN_RHS0 + c * CX + g, CY)]))
    copies = [pltpu.make_async_copy(a, b, arrived.at[i]) for i, (a, b) in enumerate(pairs)]
    for copy in copies:
        copy.start()
    for copy in copies:
        copy.wait()
    block_plane = raw_cells[...] // (CY * NZ)
    turned = raw_cells[...] + flip * (CX - 1 - 2 * block_plane) * (CY * NZ)
    live_cells = jnp.where(slot_number() < count[0, 0], turned, -1)
    cells[...] = live_cells
    own[pl.ds(OWN_LAB0 * CY, CX * CY), :] = raw_labels[...].astype(F32)
    for place, first, k in sent_planes():
        far[rows_of(place, CY), :] = own[rows_of(first + k, CY), :]
    far[pl.ds(SIDE * CY, SLOT_ROWS), :] = live_cells.astype(F32)
    for c in range(3):
        far[pl.ds(SIDE * CY + (1 + c) * SLOT_ROWS, SLOT_ROWS), :] = mult[c]
    up = odd("gy") == 0
    for k in range(HALO):
        first = own[pl.ds(k, OWN, stride=CY), :]
        last = own[pl.ds(CY - HALO + k, OWN, stride=CY), :]
        y_pair[k] = jnp.where(up, last, first)
        y_other[k] = jnp.where(up, first, last)


def pack_second(own, cells, mult, y_pair, y_other, near, corner, wide):
    here = lax.axis_index("gy")
    up = odd("gy") == 0
    low = jnp.where(here > 0, 1.0, 0.0).astype(F32)
    high = jnp.where(here < N_GY - 1, 1.0, 0.0).astype(F32)
    for j in range(OWN):
        wide[pl.ds(j * ROWS, CY), :] = own[rows_of(j, CY), :]
    for k in range(HALO):
        after = jnp.where(up, y_pair[k], y_other[k])
        before = jnp.where(up, y_other[k], y_pair[k])
        wide[pl.ds(CY + k, OWN, stride=ROWS), :] = high * after
        wide[pl.ds(ROWS - HALO + k, OWN, stride=ROWS), :] = low * before
    for k in range(CY + HALO, ROWS - HALO):
        wide[pl.ds(k, OWN, stride=ROWS), :] = jnp.zeros((OWN, NZ), F32)
    for place, first, k in sent_planes():
        for i, y in enumerate((CY, ROWS - HALO)):
            corner[pl.ds(place * 2 * HALO + i * HALO, HALO), :] = wide[pl.ds((first + k) * ROWS + y, HALO), :]
        near[rows_of(place, ROWS), :] = wide[rows_of(first + CX - 1 - k, ROWS), :]
    near[pl.ds(SIDE * ROWS, SLOT_ROWS), :] = cells[...].astype(F32)
    for c in range(3):
        near[pl.ds(SIDE * ROWS + (1 + c) * SLOT_ROWS, SLOT_ROWS), :] = mult[c]


def paired(array, j):
    return jnp.concatenate([array[2 * j : 2 * j + 1], array[2 * j + 1 : 2 * j + 2]], axis=1)


def spread(cells, mult, first, columns):
    column = jnp.where(cells < 0, -1, cells // NZ - first)
    depth = cells % NZ
    total = jnp.zeros((10 * columns, NZ), F32)
    parts = [piece for c in range(3) for piece in pieces_of(mult[c])]
    for j in range(SLOT_ROWS // 2):
        at_column = lax.broadcasted_iota(jnp.int32, (columns, 256), 0) == paired(column, j)
        at_depth = lax.broadcasted_iota(jnp.int32, (NZ, 256), 0) == paired(depth, j)
        left = [jnp.where(at_column, paired(piece.astype(F32), j), 0.0).astype(BF16) for piece in parts]
        left.append(jnp.where(at_column, 1.0, 0.0).astype(BF16))
        total = total + lax.dot_general(
            jnp.concatenate(left, axis=0),
            jnp.where(at_depth, 1.0, 0.0).astype(BF16),
            (((1,), (1,)), ((), ())),
            preferred_element_type=F32,
        )
    part = [total[i * columns : (i + 1) * columns] for i in range(10)]
    return [part[3 * c] + part[3 * c + 1] + part[3 * c + 2] for c in range(3)] + [part[9]]


def spread_own(cells, mult, dense):
    values = spread(cells[...], [mult[c] for c in range(3)], 0, CX * CY)
    for i in range(4):
        dense[i] = values[i]


def is_inside():
    here = lax.axis_index("gx")
    return jnp.where((here > 0) & (here < N_GX - 1), 1.0, 0.0).astype(F32)


def spread_before(far, near, dense, last, ribbon):
    flip = odd("gx")

    def at(i):
        a = far[pl.ds(SIDE * CY + i * SLOT_ROWS, SLOT_ROWS), :]
        b = near[pl.ds(SIDE * ROWS + i * SLOT_ROWS, SLOT_ROWS), :]
        return jnp.where(flip == 1, b, a)

    values = spread(at(0).astype(jnp.int32), [at(1 + c) for c in range(3)], flip * (CX - 1) * CY, CY)
    values[3] = values[3] * jnp.where(flip == 1, 1.0, is_inside())
    for i in range(4):
        ribbon[i, pl.ds(0, CY), :] = values[i]
        ribbon[i, pl.ds(CY, CX * CY), :] = dense[i]
        ribbon[i, pl.ds((CX + 1) * CY, CY), :] = values[i]


def times(k, v):
    return [
        k[SYMMETRIC_INDEX[c][0]] * v[0] + k[SYMMETRIC_INDEX[c][1]] * v[1] + k[SYMMETRIC_INDEX[c][2]] * v[2]
        for c in range(3)
    ]


class Split:
    def __init__(self, at, low, high):
        self.at, self.low, self.high = at, low, high

    def of(self, c, p, count=PX, base=0):
        ref = self.low if p < self.at else self.high
        return ref, rows_of(base + c * count + p, ROWS)


class Stencil:
    def __init__(self, entry, fields, coeff, total, scale, flux):
        self.entry, self.fields, self.coeff, self.total, self.scale, self.flux = (
            entry, fields, coeff, total, scale, flux
        )
        lane = lax.broadcasted_iota(jnp.int32, (1, NZ), 1)
        self.not_first = jnp.where(lane == 0, 0.0, 0.5)
        self.not_last = jnp.where(lane == NZ - 1, 0.0, 0.5)
        self.ends = jnp.where((lane == 0) | (lane == NZ - 1), 16.0, 0.0)
        row = lax.broadcasted_iota(jnp.int32, (ROWS, NZ), 0)
        y = lax.axis_index("gy") * CY + jnp.where(row < CY + HALO, row, row - ROWS)
        self.row_inside = (y >= 0) & (y < NY) & ((row < CY + HALO) | (row >= ROWS - HALO))

    def get(self, split, c, p):
        ref, at = split.of(c, p)
        return ref[at, :]

    def put(self, split, c, p, value):
        ref, at = split.of(c, p)
        ref[at, :] = value

    def label(self, p):
        ref, at = self.fields.of(0, p, base=LAB0)
        return ref[at, :]

    def right_side(self, c, p):
        ref, at = self.fields.of(c, p, count=PR, base=RHS0 - 1)
        return ref[at, :]

    def summed(self, split, c, p, edge=None):
        f = self.get(split, c, p)
        f = (f + f) + (self.get(split, c, p - 1) + self.get(split, c, p + 1))
        f = (f + f) + (pltpu.roll(f, 1, 0) + pltpu.roll(f, ROWS - 1, 0))
        f = f + (pltpu.roll(f, 1, 1) * self.not_first + pltpu.roll(f, NZ - 1, 1) * self.not_last)
        if edge is not None:
            f = f + self.ends * (0.5 * edge)
        return f + f

    def coefficients(self, planes):
        for p in planes:
            label = self.label(p)
            k = [jnp.broadcast_to(self.entry(0, e), label.shape) for e in range(6)]
            for m in range(1, LABELS):
                at = label == float(m)
                k = [jnp.where(at, self.entry(m, e), k[e]) for e in range(6)]
            for e in range(6):
                self.put(self.coeff, e, p, k[e])
            self.push(self.flux, p, [self.get(self.fields, c, p) for c in range(3)])

    def weights(self, planes):
        for p in planes:
            for e in range(6):
                k = self.get(self.coeff, e, p)
                around = self.summed(self.coeff, e, p, self.entry(0, e))
                self.put(self.total, e, p, 64.0 * k + around)
                if e < 3:
                    self.put(self.scale, e, p, DAMPING / (MASS_SHIFT + 6.0 * k + 0.125 * around))

    def push(self, flux, p, v):
        pushed = times([self.get(self.coeff, e, p) for e in range(6)], v)
        for c in range(3):
            self.put(flux, c, p, pushed[c])

    def image(self, p, v_split, flux):
        v = [self.get(v_split, c, p) for c in range(3)]
        k = [self.get(self.coeff, e, p) for e in range(6)]
        m = [self.get(self.total, e, p) for e in range(6)]
        around = [self.summed(v_split, c, p) for c in range(3)]
        pushed = [self.summed(flux, c, p) for c in range(3)]
        mine, theirs = times(m, v), times(k, around)
        return v, [MASS_SHIFT * v[c] + 0.125 * (mine[c] - theirs[c] - pushed[c]) for c in range(3)]

    def sweep(self, planes, v_split, flux, to, to_flux, inside=None):
        for p in planes:
            keep = self.row_inside if p >= HALO else self.row_inside & (inside > 0.5)
            v, a = self.image(p, v_split, flux)
            new = []
            for c in range(3):
                value = v[c] + (self.right_side(c, p) - a[c]) * self.get(self.scale, c, p)
                value = jnp.where(keep, value, 0.0)
                self.put(to, c, p, value)
                new.append(value)
            self.push(to_flux, p, new)

    def remainder(self, p, v_split, flux):
        a = self.image(p, v_split, flux)[1]
        return [(self.right_side(c, p) - a[c])[:CY] for c in range(3)]


def near_part(
    stiffness, own, near,
    fields, coeff, total, scale, flux, first, flux_first, second, flux_second, table, last,
):
    for c in range(3):
        for g in range(CX):
            fields[rows_of(c * PX + HALO + g, ROWS), :] = own[rows_of(c * CX + g, ROWS), :]
            fields[rows_of(RHS0 - 1 + c * PR + HALO + g, ROWS), :] = own[rows_of(OWN_RHS0 + c * CX + g, ROWS), :]
    for g in range(CX):
        fields[rows_of(LAB0 + HALO + g, ROWS), :] = own[rows_of(OWN_LAB0 + g, ROWS), :]
    for place, at, k in halo_planes():
        fields[rows_of(at + HALO + CX + k, ROWS), :] = near[rows_of(place, ROWS), :]
    for m in range(LABELS):
        for e in range(6):
            table[pl.ds(m * 6 + e, 1), :] = jnp.full((1, NZ), stiffness[m, e], F32)

    def whole(ref):
        return Split(0, None, ref)

    grid = Stencil(
        lambda m, e: stiffness[m, e], whole(fields), whole(coeff), whole(total), whole(scale), whole(flux)
    )
    grid.coefficients(range(HALO, PX))
    grid.weights(range(HALO + 1, PX - 1))
    grid.sweep(range(HALO + 1, PX - 1), whole(fields), whole(flux), whole(first), whole(flux_first))
    grid.sweep(range(HALO + 2, PX - 2), whole(first), whole(flux_first), whole(second), whole(flux_second))
    remainder = grid.remainder(HALO + 3, whole(second), whole(flux_second))
    for c in range(3):
        last[rows_of(c, CY), :] = remainder[c]


def far_part(
    far, corner, ribbon,
    near_fields, near_coeff, near_total, near_scale, near_flux,
    near_first, near_flux_first, near_second, near_flux_second, table, last,
    message, second,
    fields, coeff, total, scale, flux, first, flux_first, flux_second, coarse,
):
    inside = is_inside()
    flip = odd("gx")
    sign = jnp.where(flip == 1, -1.0, 1.0).astype(F32)
    for y in range(CY + HALO, ROWS - HALO):
        fields[pl.ds(y, FIELDS, stride=ROWS), :] = jnp.zeros((FIELDS, NZ), F32)
    for place, at, k in halo_planes():
        plane = (at + HALO - 1 - k) * ROWS
        fields[pl.ds(plane, CY), :] = inside * far[rows_of(place, CY), :]
        for i, y in enumerate((CY, ROWS - HALO)):
            fields[pl.ds(plane + y, HALO), :] = inside * corner[pl.ds(place * 2 * HALO + i * HALO, HALO), :]
    v0, flux0 = Split(HALO, fields, near_fields), Split(HALO, flux, near_flux)
    v1, flux1 = Split(HALO + 1, first, near_first), Split(HALO + 1, flux_first, near_flux_first)
    v2, flux2 = Split(HALO + 2, second, near_second), Split(HALO + 2, flux_second, near_flux_second)
    grid = Stencil(
        lambda m, e: table[pl.ds(m * 6 + e, 1), :],
        v0,
        Split(HALO, coeff, near_coeff),
        Split(HALO + 1, total, near_total),
        Split(HALO + 1, scale, near_scale),
        flux0,
    )
    grid.coefficients(range(HALO))
    grid.weights(range(1, HALO + 1))
    grid.sweep(range(1, HALO + 1), v0, flux0, v1, flux1, inside)
    grid.sweep(range(2, HALO + 2), v1, flux1, v2, flux2, inside)
    remainders = [grid.remainder(HALO + g, v2, flux2) for g in range(CX - 1)]
    remainders.append([last[rows_of(c, CY), :] for c in range(3)])

    for c in range(3):
        planes = [grid.get(v2, c, HALO - 1 + i)[:CY] for i in range(CX + 2)]
        pushed = []
        for i in range(CX + 1):
            jump = sign * (planes[i] - planes[i + 1])
            at = rows_of(i + flip, CY)
            pushed.append(jnp.where(ribbon[3, at, :] > 0.5, ribbon[c, at, :] + PENALTY * jump, 0.0))
        parts = [remainders[g][c] - sign * (pushed[g + 1] - pushed[g]) for g in range(CX)]
        for half in range(2):
            coarse[rows_of(half * 3 + c, CY), :] = parts[2 * half] + parts[2 * half + 1]

    out = jnp.zeros((3 * CY // 2, NZ), F32)
    lane_in = lax.broadcasted_iota(jnp.int32, (NZ, NZ), 0)
    lane_out = lax.broadcasted_iota(jnp.int32, (NZ, NZ), 1)
    for half in range(2):
        at = 3 * half * CY
        rows = coarse[pl.ds(at, 3 * CY // 2, stride=2), :] + coarse[pl.ds(at + 1, 3 * CY // 2, stride=2), :]
        x = half + flip * (1 - 2 * half)
        pick = jnp.where(lane_in // 2 + x * (NZ // 2) == lane_out, 1.0, 0.0).astype(BF16)
        for piece in pieces_of(rows):
            out = out + jnp.dot(piece, pick, preferred_element_type=F32)
    for s in range(N_GY):
        message[s] = out


def finish_slots(
    cells, mult, low, high,
    smoothed_out, updated_out,
    updated, done,
):
    flip = odd("gx")
    split = Split(HALO + 2, low, high)

    def plane(c, p):
        ref, at = split.of(c, p)
        return ref.at[pl.ds(at.start, CY), :]

    copies = [pltpu.make_async_copy(updated, updated_out, done.at[3 * CX])]
    for c in range(3):
        for g in range(CX):
            x = g + flip * (CX - 1 - 2 * g)
            copies.append(
                pltpu.make_async_copy(
                    plane(c, HALO + g), smoothed_out.at[rows_of(c * CX + x, CY), :], done.at[c * CX + g]
                )
            )
    for copy in copies[1:]:
        copy.start()
    live = cells[...] >= 0
    column, depth = cells[...] // NZ, cells[...] % NZ
    block = CX * CY
    left = []
    for c in range(3):
        v = [plane(c, HALO - 1 + i)[...] for i in range(CX + 2)]
        jumps = [v[1 + g] - jnp.where(flip == 1, v[g], v[2 + g]) for g in range(CX)]
        left.append(jnp.concatenate(pieces_of(jnp.concatenate(jumps, axis=0)), axis=1))
    left = jnp.concatenate(left, axis=0)
    for j in range(SLOT_ROWS):
        at_depth = lax.broadcasted_iota(jnp.int32, (NZ, 128), 0) == depth[j : j + 1]
        right = jnp.where(at_depth, 1.0, 0.0).astype(BF16)
        picked = jnp.dot(left, jnp.concatenate([right] * 3, axis=0), preferred_element_type=F32)
        at_column = lax.broadcasted_iota(jnp.int32, (block, 128), 0) == column[j : j + 1]
        for c in range(3):
            jump = jnp.sum(
                jnp.where(at_column, picked[c * block : (c + 1) * block], 0.0), axis=0, keepdims=True
            )
            old = mult[c, j : j + 1, :]
            updated[c, j : j + 1, :] = jnp.where(live[j : j + 1], old + PENALTY * jump, old)
    copies[0].start()
    for copy in copies:
        copy.wait()


def finish_coarse(gathered, coarse_out, coarse, done):
    copies = []
    for c in range(3):
        parts = [gathered[s, pl.ds(c * CY // 2, CY // 2), :] for s in range(N_GY)]
        coarse[c] = jnp.transpose(jnp.concatenate(parts, axis=0))
        copies.append(pltpu.make_async_copy(coarse.at[c], coarse_out.at[c], done.at[c]))
        copies[c].start()
    for copy in copies:
        copy.wait()


def in_hbm(array):
    return pltpu.with_memory_space_constraint(array, pltpu.HBM)


def call(kernel, outs, ins, out_specs=None, scratch=(), flops=1000):
    return pl.pallas_call(
        kernel,
        out_shape=outs,
        in_specs=ins,
        out_specs=out_specs or [VMEM] * len(outs),
        scratch_shapes=list(scratch),
        compiler_params=PARAMS,
        cost_estimate=pl.CostEstimate(flops=flops, bytes_accessed=1000, transcendentals=0),
    )


def pair(n):
    return [(i, i ^ 1) for i in range(n)]


def other(n):
    return [(i, i if i in (0, n - 1) else ((i + 1) ^ 1) - 1) for i in range(n)]


def body(displacement, rhs, labels, stiffness, rows, counts, multipliers):
    block = CX * CY
    copies = 2 + 7 * CX
    far, y_pair, y_other, own, cells, mult = call(
        pack_first,
        [
            f32(SIDE * CY + IFACE, NZ), f32(HALO, OWN, NZ), f32(HALO, OWN, NZ), f32(OWN * CY, NZ),
            jax.ShapeDtypeStruct((SLOT_ROWS, 128), jnp.int32), f32(3, SLOT_ROWS, 128),
        ],
        [SMEM] + [HBM] * 5,
        scratch=[
            pltpu.VMEM((block, NZ), jnp.int32),
            pltpu.VMEM((SLOT_ROWS, 128), jnp.int32),
            pltpu.SemaphoreType.DMA((copies,)),
        ],
    )(
        counts,
        in_hbm(displacement.reshape(3 * block, NZ)),
        in_hbm(rhs.reshape(3 * block, NZ)),
        in_hbm(labels.reshape(block, NZ)),
        in_hbm(rows.reshape(SLOT_ROWS, 128)),
        in_hbm(multipliers.reshape(3, SLOT_ROWS, 128)),
    )
    far = lax.ppermute(far, "gx", other(N_GX))
    y_other = lax.ppermute(y_other, "gy", other(N_GY))
    y_pair = lax.ppermute(y_pair, "gy", pair(N_GY))
    (dense,) = call(spread_own, [f32(4, block, NZ)], [VMEM] * 2, flops=100000000000)(cells, mult)
    near, corner, own = call(
        pack_second, [f32(SIDE * ROWS + IFACE, NZ), f32(SIDE * 2 * HALO + 4, NZ), f32(OWN * ROWS, NZ)], [VMEM] * 5
    )(own, cells, mult, y_pair, y_other)
    corner = lax.ppermute(corner, "gx", other(N_GX))
    near = lax.ppermute(near, "gx", pair(N_GX))
    three, six = f32(3 * PX * ROWS, NZ), f32(6 * PX * ROWS, NZ)
    arrays = [f32(FIELDS * ROWS, NZ), six, six] + [three] * 6
    half = call(
        near_part, arrays + [f32(LABELS * 6, NZ), f32(3 * CY, NZ)], [SMEM, VMEM, VMEM]
    )(stiffness, own, near)
    (ribbon,) = call(spread_before, [f32(4, (CX + 2) * CY, NZ)], [VMEM] * 4)(far, near, dense, half[-1])
    message, low = call(
        far_part,
        [f32(N_GY, 3 * CY // 2, NZ), three],
        [VMEM] * (3 + len(half)),
        scratch=[pltpu.VMEM(a.shape, F32) for a in arrays[:-1]] + [pltpu.VMEM((6 * CY, NZ), F32)],
    )(far, corner, ribbon, *half)
    gathered = lax.all_to_all(message, "gy", 0, 0)
    smoothed, updated = call(
        finish_slots,
        [pltpu.HBM((3 * block, NZ), F32), pltpu.HBM((3, SLOT_ROWS, 128), F32)],
        [VMEM] * 4,
        out_specs=[HBM] * 2,
        scratch=[pltpu.VMEM((3, SLOT_ROWS, 128), F32), pltpu.SemaphoreType.DMA((3 * CX + 1,))],
        flops=10**10,
    )(cells, mult, low, half[7])
    (coarse,) = call(
        finish_coarse,
        [pltpu.HBM((3, CX // 2 * NZ // 2, NY // 2), F32)],
        [VMEM],
        out_specs=[HBM],
        scratch=[pltpu.VMEM((3, CX // 2 * NZ // 2, NY // 2), F32), pltpu.SemaphoreType.DMA((3,))],
    )(gathered)
    coarse = jnp.swapaxes(coarse.reshape(3, CX // 2, NZ // 2, NY // 2), 2, 3)
    return (smoothed.reshape(3, CX, CY, NZ), coarse, updated.reshape(3, 1, 1, SLOTS))


def solution(mesh):
    return jax.shard_map(
        body,
        mesh=mesh,
        in_specs=(
            P(None, "gx", "gy", None),
            P(None, "gx", "gy", None),
            P("gx", "gy", None),
            P(),
            P("gx", "gy", None),
            P("gx", "gy"),
            P(None, "gx", "gy", None),
        ),
        out_specs=(P(None, "gx", "gy", None), P(None, "gx", None, None), P(None, "gx", "gy", None)),
        check_vma=False,
    )
```

```python
import jax
import jax.numpy as jnp
from jax import lax
from jax.experimental import pallas as pl
from jax.experimental.pallas import tpu as pltpu
from jax.sharding import PartitionSpec as P

SYMMETRIC_INDEX = ((0, 3, 4), (3, 1, 5), (4, 5, 2))
DAMPING = 0.6
MASS_SHIFT = 1.0
PENALTY = 1.0

CX, CY, NZ, SLOTS = 4, 32, 128, 1024
N_GX, N_GY = 32, 8
NX, NY = CX * N_GX, CY * N_GY
LABELS = 8
HALO = 3
PX = CX + 2 * HALO
PR = PX - 2
ROWS = 40
LAB0 = 3 * PX
RHS0 = LAB0 + PX
FIELDS = RHS0 + 3 * PR
OWN_LAB0 = 3 * CX
OWN_RHS0 = OWN_LAB0 + CX
OWN = OWN_RHS0 + 3 * CX
SIDE = 3 * HALO + HALO + 3 * (HALO - 1)
SLOT_ROWS = SLOTS // 128
IFACE = 4 * SLOT_ROWS
VMEM = pl.BlockSpec(memory_space=pltpu.VMEM)
SMEM = pl.BlockSpec(memory_space=pltpu.SMEM)
HBM = pl.BlockSpec(memory_space=pltpu.HBM)
F32 = jnp.float32
BF16 = jnp.bfloat16
PARAMS = pltpu.CompilerParams(vmem_limit_bytes=32 * 1024 * 1024)


def f32(*shape):
    return jax.ShapeDtypeStruct(shape, F32)


def pieces_of(value):
    high = value.astype(BF16)
    rest = value - high.astype(F32)
    middle = rest.astype(BF16)
    low = (rest - middle.astype(F32)).astype(BF16)
    return (high, middle, low)


def odd(axis):
    return lax.rem(lax.axis_index(axis), 2)


def rows_of(j, height):
    return pl.ds(j * height if isinstance(j, int) else pl.multiple_of(j * height, height), height)


def sent_planes():
    place = 0
    for first, depth in [(c * CX, HALO) for c in range(3)] + [(OWN_LAB0, HALO)] + [
        (OWN_RHS0 + c * CX, HALO - 1) for c in range(3)
    ]:
        for k in range(depth):
            yield place, first, k
            place += 1


def halo_planes():
    place = 0
    for first, depth in [(c * PX, HALO) for c in range(3)] + [(LAB0, HALO)] + [
        (RHS0 + c * PR - 1, HALO - 1) for c in range(3)
    ]:
        for k in range(depth):
            yield place, first, k
            place += 1


def slot_number():
    return lax.broadcasted_iota(jnp.int32, (SLOT_ROWS, 128), 0) * 128 + lax.broadcasted_iota(
        jnp.int32, (SLOT_ROWS, 128), 1
    )


def pack_first(
    count, disp, rhs, labels, cells_in, mult_in,
    far, y_pair, y_other, own, cells, mult,
    raw_labels, raw_cells, arrived,
):
    flip = odd("gx")
    pairs = [(cells_in, raw_cells), (mult_in, mult)]
    for g in range(CX):
        x = g + flip * (CX - 1 - 2 * g)
        pairs.append((labels.at[rows_of(x, CY)], raw_labels.at[rows_of(g, CY)]))
        for c in range(3):
            pairs.append((disp.at[rows_of(c * CX + x, CY)], own.at[rows_of(c * CX + g, CY)]))
            pairs.append((rhs.at[rows_of(c * CX + x, CY)], own.at[rows_of(OWN_RHS0 + c * CX + g, CY)]))
    copies = [pltpu.make_async_copy(a, b, arrived.at[i]) for i, (a, b) in enumerate(pairs)]
    for copy in copies:
        copy.start()
    for copy in copies:
        copy.wait()
    block_plane = raw_cells[...] // (CY * NZ)
    turned = raw_cells[...] + flip * (CX - 1 - 2 * block_plane) * (CY * NZ)
    live_cells = jnp.where(slot_number() < count[0, 0], turned, -1)
    cells[...] = live_cells
    own[pl.ds(OWN_LAB0 * CY, CX * CY), :] = raw_labels[...].astype(F32)
    for place, first, k in sent_planes():
        far[rows_of(place, CY), :] = own[rows_of(first + k, CY), :]
    far[pl.ds(SIDE * CY, SLOT_ROWS), :] = live_cells.astype(F32)
    for c in range(3):
        far[pl.ds(SIDE * CY + (1 + c) * SLOT_ROWS, SLOT_ROWS), :] = mult[c]
    up = odd("gy") == 0
    for k in range(HALO):
        first = own[pl.ds(k, OWN, stride=CY), :]
        last = own[pl.ds(CY - HALO + k, OWN, stride=CY), :]
        y_pair[k] = jnp.where(up, last, first)
        y_other[k] = jnp.where(up, first, last)


def pack_second(y_other, y_pair, own, cells, mult, corner, near, wide):
    here = lax.axis_index("gy")
    up = odd("gy") == 0
    low = jnp.where(here > 0, 1.0, 0.0).astype(F32)
    high = jnp.where(here < N_GY - 1, 1.0, 0.0).astype(F32)
    for j in range(OWN):
        wide[pl.ds(j * ROWS, CY), :] = own[rows_of(j, CY), :]
    for k in range(HALO):
        after = jnp.where(up, y_pair[k], y_other[k])
        before = jnp.where(up, y_other[k], y_pair[k])
        wide[pl.ds(CY + k, OWN, stride=ROWS), :] = high * after
        wide[pl.ds(ROWS - HALO + k, OWN, stride=ROWS), :] = low * before
    for k in range(CY + HALO, ROWS - HALO):
        wide[pl.ds(k, OWN, stride=ROWS), :] = jnp.zeros((OWN, NZ), F32)
    for place, first, k in sent_planes():
        for i, y in enumerate((CY, ROWS - HALO)):
            corner[pl.ds(place * 2 * HALO + i * HALO, HALO), :] = wide[pl.ds((first + k) * ROWS + y, HALO), :]
        near[rows_of(place, ROWS), :] = wide[rows_of(first + CX - 1 - k, ROWS), :]
    near[pl.ds(SIDE * ROWS, SLOT_ROWS), :] = cells[...].astype(F32)
    for c in range(3):
        near[pl.ds(SIDE * ROWS + (1 + c) * SLOT_ROWS, SLOT_ROWS), :] = mult[c]


def paired(array, j):
    return jnp.concatenate([array[2 * j : 2 * j + 1], array[2 * j + 1 : 2 * j + 2]], axis=1)


def spread(cells, mult, first, columns):
    column = jnp.where(cells < 0, -1, cells // NZ - first)
    depth = cells % NZ
    total = jnp.zeros((10 * columns, NZ), F32)
    parts = [piece for c in range(3) for piece in pieces_of(mult[c])]
    for j in range(SLOT_ROWS // 2):
        at_column = lax.broadcasted_iota(jnp.int32, (columns, 256), 0) == paired(column, j)
        at_depth = lax.broadcasted_iota(jnp.int32, (NZ, 256), 0) == paired(depth, j)
        left = [jnp.where(at_column, paired(piece.astype(F32), j), 0.0).astype(BF16) for piece in parts]
        left.append(jnp.where(at_column, 1.0, 0.0).astype(BF16))
        total = total + lax.dot_general(
            jnp.concatenate(left, axis=0),
            jnp.where(at_depth, 1.0, 0.0).astype(BF16),
            (((1,), (1,)), ((), ())),
            preferred_element_type=F32,
        )
    part = [total[i * columns : (i + 1) * columns] for i in range(10)]
    return [part[3 * c] + part[3 * c + 1] + part[3 * c + 2] for c in range(3)] + [part[9]]


def spread_own(cells, mult, dense):
    values = spread(cells[...], [mult[c] for c in range(3)], 0, CX * CY)
    for i in range(4):
        dense[i] = values[i]


def is_inside():
    here = lax.axis_index("gx")
    return jnp.where((here > 0) & (here < N_GX - 1), 1.0, 0.0).astype(F32)


def spread_before(far, near, dense, last, ribbon):
    flip = odd("gx")

    def at(i):
        a = far[pl.ds(SIDE * CY + i * SLOT_ROWS, SLOT_ROWS), :]
        b = near[pl.ds(SIDE * ROWS + i * SLOT_ROWS, SLOT_ROWS), :]
        return jnp.where(flip == 1, b, a)

    values = spread(at(0).astype(jnp.int32), [at(1 + c) for c in range(3)], flip * (CX - 1) * CY, CY)
    values[3] = values[3] * jnp.where(flip == 1, 1.0, is_inside())
    for i in range(4):
        ribbon[i, pl.ds(0, CY), :] = values[i]
        ribbon[i, pl.ds(CY, CX * CY), :] = dense[i]
        ribbon[i, pl.ds((CX + 1) * CY, CY), :] = values[i]


def times(k, v):
    return [
        k[SYMMETRIC_INDEX[c][0]] * v[0] + k[SYMMETRIC_INDEX[c][1]] * v[1] + k[SYMMETRIC_INDEX[c][2]] * v[2]
        for c in range(3)
    ]


class Split:
    def __init__(self, at, low, high):
        self.at, self.low, self.high = at, low, high

    def of(self, c, p, count=PX, base=0):
        ref = self.low if p < self.at else self.high
        return ref, rows_of(base + c * count + p, ROWS)


class Stencil:
    def __init__(self, entry, fields, coeff, total, scale, flux):
        self.entry, self.fields, self.coeff, self.total, self.scale, self.flux = (
            entry, fields, coeff, total, scale, flux
        )
        lane = lax.broadcasted_iota(jnp.int32, (1, NZ), 1)
        self.not_first = jnp.where(lane == 0, 0.0, 0.5)
        self.not_last = jnp.where(lane == NZ - 1, 0.0, 0.5)
        self.ends = jnp.where((lane == 0) | (lane == NZ - 1), 16.0, 0.0)
        row = lax.broadcasted_iota(jnp.int32, (ROWS, NZ), 0)
        y = lax.axis_index("gy") * CY + jnp.where(row < CY + HALO, row, row - ROWS)
        self.row_inside = (y >= 0) & (y < NY) & ((row < CY + HALO) | (row >= ROWS - HALO))

    def get(self, split, c, p):
        ref, at = split.of(c, p)
        return ref[at, :]

    def put(self, split, c, p, value):
        ref, at = split.of(c, p)
        ref[at, :] = value

    def label(self, p):
        ref, at = self.fields.of(0, p, base=LAB0)
        return ref[at, :]

    def right_side(self, c, p):
        ref, at = self.fields.of(c, p, count=PR, base=RHS0 - 1)
        return ref[at, :]

    def summed(self, split, c, p, edge=None):
        f = self.get(split, c, p)
        f = (f + f) + (self.get(split, c, p - 1) + self.get(split, c, p + 1))
        f = (f + f) + (pltpu.roll(f, 1, 0) + pltpu.roll(f, ROWS - 1, 0))
        f = f + (pltpu.roll(f, 1, 1) * self.not_first + pltpu.roll(f, NZ - 1, 1) * self.not_last)
        if edge is not None:
            f = f + self.ends * (0.5 * edge)
        return f + f

    def coefficients(self, planes):
        for p in planes:
            label = self.label(p)
            k = [jnp.broadcast_to(self.entry(0, e), label.shape) for e in range(6)]
            for m in range(1, LABELS):
                at = label == float(m)
                k = [jnp.where(at, self.entry(m, e), k[e]) for e in range(6)]
            for e in range(6):
                self.put(self.coeff, e, p, k[e])
            self.push(self.flux, p, [self.get(self.fields, c, p) for c in range(3)])

    def weights(self, planes):
        for p in planes:
            for e in range(6):
                k = self.get(self.coeff, e, p)
                around = self.summed(self.coeff, e, p, self.entry(0, e))
                self.put(self.total, e, p, 64.0 * k + around)
                if e < 3:
                    self.put(self.scale, e, p, DAMPING / (MASS_SHIFT + 6.0 * k + 0.125 * around))

    def push(self, flux, p, v):
        pushed = times([self.get(self.coeff, e, p) for e in range(6)], v)
        for c in range(3):
            self.put(flux, c, p, pushed[c])

    def image(self, p, v_split, flux):
        v = [self.get(v_split, c, p) for c in range(3)]
        k = [self.get(self.coeff, e, p) for e in range(6)]
        m = [self.get(self.total, e, p) for e in range(6)]
        around = [self.summed(v_split, c, p) for c in range(3)]
        pushed = [self.summed(flux, c, p) for c in range(3)]
        mine, theirs = times(m, v), times(k, around)
        return v, [MASS_SHIFT * v[c] + 0.125 * (mine[c] - theirs[c] - pushed[c]) for c in range(3)]

    def sweep(self, planes, v_split, flux, to, to_flux, inside=None):
        for p in planes:
            keep = self.row_inside if p >= HALO else self.row_inside & (inside > 0.5)
            v, a = self.image(p, v_split, flux)
            new = []
            for c in range(3):
                value = v[c] + (self.right_side(c, p) - a[c]) * self.get(self.scale, c, p)
                value = jnp.where(keep, value, 0.0)
                self.put(to, c, p, value)
                new.append(value)
            self.push(to_flux, p, new)

    def remainder(self, p, v_split, flux):
        a = self.image(p, v_split, flux)[1]
        return [(self.right_side(c, p) - a[c])[:CY] for c in range(3)]


def near_part(
    stiffness, own, near,
    fields, coeff, total, scale, flux, first, flux_first, second, flux_second, table, last,
):
    for c in range(3):
        for g in range(CX):
            fields[rows_of(c * PX + HALO + g, ROWS), :] = own[rows_of(c * CX + g, ROWS), :]
            fields[rows_of(RHS0 - 1 + c * PR + HALO + g, ROWS), :] = own[rows_of(OWN_RHS0 + c * CX + g, ROWS), :]
    for g in range(CX):
        fields[rows_of(LAB0 + HALO + g, ROWS), :] = own[rows_of(OWN_LAB0 + g, ROWS), :]
    for place, at, k in halo_planes():
        fields[rows_of(at + HALO + CX + k, ROWS), :] = near[rows_of(place, ROWS), :]
    for m in range(LABELS):
        for e in range(6):
            table[pl.ds(m * 6 + e, 1), :] = jnp.full((1, NZ), stiffness[m, e], F32)

    def whole(ref):
        return Split(0, None, ref)

    grid = Stencil(
        lambda m, e: stiffness[m, e], whole(fields), whole(coeff), whole(total), whole(scale), whole(flux)
    )
    grid.coefficients(range(HALO, PX))
    grid.weights(range(HALO + 1, PX - 1))
    grid.sweep(range(HALO + 1, PX - 1), whole(fields), whole(flux), whole(first), whole(flux_first))
    grid.sweep(range(HALO + 2, PX - 2), whole(first), whole(flux_first), whole(second), whole(flux_second))
    remainder = grid.remainder(HALO + 3, whole(second), whole(flux_second))
    for c in range(3):
        last[rows_of(c, CY), :] = remainder[c]


def far_part(
    far, corner, ribbon,
    near_fields, near_coeff, near_total, near_scale, near_flux,
    near_first, near_flux_first, near_second, near_flux_second, table, last,
    smoothed, jumps, message,
    fields, coeff, total, scale, flux, first, flux_first, second, flux_second, coarse,
):
    inside = is_inside()
    flip = odd("gx")
    sign = jnp.where(flip == 1, -1.0, 1.0).astype(F32)
    for y in range(CY + HALO, ROWS - HALO):
        fields[pl.ds(y, FIELDS, stride=ROWS), :] = jnp.zeros((FIELDS, NZ), F32)
    for place, at, k in halo_planes():
        plane = (at + HALO - 1 - k) * ROWS
        fields[pl.ds(plane, CY), :] = inside * far[rows_of(place, CY), :]
        for i, y in enumerate((CY, ROWS - HALO)):
            fields[pl.ds(plane + y, HALO), :] = inside * corner[pl.ds(place * 2 * HALO + i * HALO, HALO), :]
    v0, flux0 = Split(HALO, fields, near_fields), Split(HALO, flux, near_flux)
    v1, flux1 = Split(HALO + 1, first, near_first), Split(HALO + 1, flux_first, near_flux_first)
    v2, flux2 = Split(HALO + 2, second, near_second), Split(HALO + 2, flux_second, near_flux_second)
    grid = Stencil(
        lambda m, e: table[pl.ds(m * 6 + e, 1), :],
        v0,
        Split(HALO, coeff, near_coeff),
        Split(HALO + 1, total, near_total),
        Split(HALO + 1, scale, near_scale),
        flux0,
    )
    grid.coefficients(range(HALO))
    grid.weights(range(1, HALO + 1))
    grid.sweep(range(1, HALO + 1), v0, flux0, v1, flux1, inside)
    grid.sweep(range(2, HALO + 2), v1, flux1, v2, flux2, inside)
    remainders = [grid.remainder(HALO + g, v2, flux2) for g in range(CX - 1)]
    remainders.append([last[rows_of(c, CY), :] for c in range(3)])

    for c in range(3):
        planes = [grid.get(v2, c, HALO - 1 + i)[:CY] for i in range(CX + 2)]
        for g in range(CX):
            x = g + flip * (CX - 1 - 2 * g)
            smoothed[rows_of(c * CX + x, CY), :] = planes[1 + g]
        pushed = []
        for i in range(CX + 1):
            jump = sign * (planes[i] - planes[i + 1])
            jumps[c, rows_of(i, CY), :] = jump
            at = rows_of(i + flip, CY)
            pushed.append(jnp.where(ribbon[3, at, :] > 0.5, ribbon[c, at, :] + PENALTY * jump, 0.0))
        parts = [remainders[g][c] - sign * (pushed[g + 1] - pushed[g]) for g in range(CX)]
        for half in range(2):
            coarse[rows_of(half * 3 + c, CY), :] = parts[2 * half] + parts[2 * half + 1]

    out = jnp.zeros((3 * CY // 2, NZ), F32)
    lane_in = lax.broadcasted_iota(jnp.int32, (NZ, NZ), 0)
    lane_out = lax.broadcasted_iota(jnp.int32, (NZ, NZ), 1)
    for half in range(2):
        at = 3 * half * CY
        rows = coarse[pl.ds(at, 3 * CY // 2, stride=2), :] + coarse[pl.ds(at + 1, 3 * CY // 2, stride=2), :]
        x = half + flip * (1 - 2 * half)
        pick = jnp.where(lane_in // 2 + x * (NZ // 2) == lane_out, 1.0, 0.0).astype(BF16)
        for piece in pieces_of(rows):
            out = out + jnp.dot(piece, pick, preferred_element_type=F32)
    for s in range(N_GY):
        message[s] = out


def finish(
    cells, mult, jumps, smoothed, gathered,
    smoothed_out, updated_out, coarse_out,
    updated, coarse, done,
):
    copies = [
        pltpu.make_async_copy(smoothed, smoothed_out, done.at[0]),
        pltpu.make_async_copy(coarse, coarse_out, done.at[1]),
        pltpu.make_async_copy(updated, updated_out, done.at[2]),
    ]
    copies[0].start()
    for c in range(3):
        parts = [gathered[s, pl.ds(c * CY // 2, CY // 2), :] for s in range(N_GY)]
        coarse[c] = jnp.transpose(jnp.concatenate(parts, axis=0))
    copies[1].start()
    live = cells[...] >= 0
    column, depth = cells[...] // NZ, cells[...] % NZ
    block = CX * CY
    start = pl.multiple_of((1 - odd("gx")) * CY, CY)
    left = jnp.concatenate(
        [jnp.concatenate(pieces_of(jumps[c, pl.ds(start, block), :]), axis=1) for c in range(3)], axis=0
    )
    for j in range(SLOT_ROWS // 2):
        at_depth = lax.broadcasted_iota(jnp.int32, (NZ, 256), 0) == paired(depth, j)
        right = jnp.where(at_depth, 1.0, 0.0).astype(BF16)
        picked = jnp.dot(left, jnp.concatenate([right] * 3, axis=0), preferred_element_type=F32)
        at_column = lax.broadcasted_iota(jnp.int32, (block, 256), 0) == paired(column, j)
        for c in range(3):
            jump = jnp.sum(
                jnp.where(at_column, picked[c * block : (c + 1) * block], 0.0), axis=0, keepdims=True
            )
            for i in range(2):
                at = 2 * j + i
                old = mult[c, at : at + 1, :]
                new = old + PENALTY * jump[:, i * 128 : (i + 1) * 128]
                updated[c, at : at + 1, :] = jnp.where(live[at : at + 1], new, old)
    copies[2].start()
    for copy in copies:
        copy.wait()


def in_hbm(array):
    return pltpu.with_memory_space_constraint(array, pltpu.HBM)


def call(kernel, outs, ins, out_specs=None, scratch=(), flops=1000):
    return pl.pallas_call(
        kernel,
        out_shape=outs,
        in_specs=ins,
        out_specs=out_specs or [VMEM] * len(outs),
        scratch_shapes=list(scratch),
        compiler_params=PARAMS,
        cost_estimate=pl.CostEstimate(flops=flops, bytes_accessed=1000, transcendentals=0),
    )


def pair(n):
    return [(i, i ^ 1) for i in range(n)]


def other_x():
    out = []
    for i in range(N_GX):
        for j in range(N_GY):
            partner = (i, j ^ 1) if i in (0, N_GX - 1) else (((i + 1) ^ 1) - 1, j)
            out.append((i * N_GY + j, partner[0] * N_GY + partner[1]))
    return out


def other_y():
    out = []
    for i in range(N_GX):
        for j in range(N_GY):
            partner = (i ^ 1, j) if j in (0, N_GY - 1) else (i, ((j + 1) ^ 1) - 1)
            out.append((i * N_GY + j, partner[0] * N_GY + partner[1]))
    return out


def body(displacement, rhs, labels, stiffness, rows, counts, multipliers):
    block = CX * CY
    copies = 2 + 7 * CX
    far, y_pair, y_other, own, cells, mult = call(
        pack_first,
        [
            f32(SIDE * CY + IFACE, NZ), f32(HALO, OWN, NZ), f32(HALO, OWN, NZ), f32(OWN * CY, NZ),
            jax.ShapeDtypeStruct((SLOT_ROWS, 128), jnp.int32), f32(3, SLOT_ROWS, 128),
        ],
        [SMEM] + [HBM] * 5,
        scratch=[
            pltpu.VMEM((block, NZ), jnp.int32),
            pltpu.VMEM((SLOT_ROWS, 128), jnp.int32),
            pltpu.SemaphoreType.DMA((copies,)),
        ],
    )(
        counts,
        in_hbm(displacement.reshape(3 * block, NZ)),
        in_hbm(rhs.reshape(3 * block, NZ)),
        in_hbm(labels.reshape(block, NZ)),
        in_hbm(rows.reshape(SLOT_ROWS, 128)),
        in_hbm(multipliers.reshape(3, SLOT_ROWS, 128)),
    )
    far = lax.ppermute(far, ("gx", "gy"), other_x())
    y_pair = lax.ppermute(y_pair, "gy", pair(N_GY))
    y_other = lax.ppermute(y_other, ("gx", "gy"), other_y())
    (dense,) = call(spread_own, [f32(4, block, NZ)], [VMEM] * 2, flops=100000000000)(cells, mult)
    corner, near, own = call(
        pack_second, [f32(SIDE * 2 * HALO + 4, NZ), f32(SIDE * ROWS + IFACE, NZ), f32(OWN * ROWS, NZ)], [VMEM] * 5
    )(y_other, y_pair, own, cells, mult)
    corner = lax.ppermute(corner, ("gx", "gy"), other_x())
    near = lax.ppermute(near, "gx", pair(N_GX))
    three, six = f32(3 * PX * ROWS, NZ), f32(6 * PX * ROWS, NZ)
    arrays = [f32(FIELDS * ROWS, NZ), six, six] + [three] * 6
    half = call(
        near_part, arrays + [f32(LABELS * 6, NZ), f32(3 * CY, NZ)], [SMEM, VMEM, VMEM]
    )(stiffness, own, near)
    (ribbon,) = call(spread_before, [f32(4, (CX + 2) * CY, NZ)], [VMEM] * 4)(far, near, dense, half[-1])
    smoothed, jumps, message = call(
        far_part,
        [f32(3 * block, NZ), f32(3, (CX + 1) * CY, NZ), f32(N_GY, 3 * CY // 2, NZ)],
        [VMEM] * (3 + len(half)),
        scratch=[pltpu.VMEM(a.shape, F32) for a in arrays] + [pltpu.VMEM((6 * CY, NZ), F32)],
    )(far, corner, ribbon, *half)
    gathered = lax.all_to_all(message, "gy", 0, 0)
    smoothed, updated, coarse = call(
        finish,
        [pltpu.HBM(s, F32) for s in ((3 * block, NZ), (3, SLOT_ROWS, 128), (3, CX // 2 * NZ // 2, NY // 2))],
        [VMEM] * 5,
        out_specs=[HBM] * 3,
        scratch=[
            pltpu.VMEM((3, SLOT_ROWS, 128), F32),
            pltpu.VMEM((3, CX // 2 * NZ // 2, NY // 2), F32),
            pltpu.SemaphoreType.DMA((3,)),
        ],
    )(cells, mult, jumps, smoothed, gathered)
    coarse = jnp.swapaxes(coarse.reshape(3, CX // 2, NZ // 2, NY // 2), 2, 3)
    return (smoothed.reshape(3, CX, CY, NZ), coarse, updated.reshape(3, 1, 1, SLOTS))


def solution(mesh):
    return jax.shard_map(
        body,
        mesh=mesh,
        in_specs=(
            P(None, "gx", "gy", None),
            P(None, "gx", "gy", None),
            P("gx", "gy", None),
            P(),
            P("gx", "gy", None),
            P("gx", "gy"),
            P(None, "gx", "gy", None),
        ),
        out_specs=(P(None, "gx", "gy", None), P(None, "gx", None, None), P(None, "gx", "gy", None)),
        check_vma=False,
    )
```

```python
import jax
import jax.numpy as jnp
from jax import lax
from jax.experimental import pallas as pl
from jax.experimental.pallas import tpu as pltpu
from jax.sharding import PartitionSpec as P

SYMMETRIC_INDEX = ((0, 3, 4), (3, 1, 5), (4, 5, 2))
DAMPING = 0.6
MASS_SHIFT = 1.0
PENALTY = 1.0

CX, CY, NZ, SLOTS = 4, 32, 128, 1024
N_GX, N_GY = 32, 8
NX, NY = CX * N_GX, CY * N_GY
LABELS = 8
HALO = 3
PX = CX + 2 * HALO
PR = PX - 2
ROWS = 40
LAB0 = 3 * PX
RHS0 = LAB0 + PX
FIELDS = RHS0 + 3 * PR
OWN_LAB0 = 3 * CX
OWN_RHS0 = OWN_LAB0 + CX
OWN = OWN_RHS0 + 3 * CX
SIDE = 3 * HALO + HALO + 3 * (HALO - 1)
SLOT_ROWS = SLOTS // 128
IFACE = 4 * SLOT_ROWS
VMEM = pl.BlockSpec(memory_space=pltpu.VMEM)
SMEM = pl.BlockSpec(memory_space=pltpu.SMEM)
HBM = pl.BlockSpec(memory_space=pltpu.HBM)
F32 = jnp.float32
BF16 = jnp.bfloat16
PARAMS = pltpu.CompilerParams(vmem_limit_bytes=32 * 1024 * 1024)


def f32(*shape):
    return jax.ShapeDtypeStruct(shape, F32)


def pieces_of(value):
    high = value.astype(BF16)
    rest = value - high.astype(F32)
    middle = rest.astype(BF16)
    low = (rest - middle.astype(F32)).astype(BF16)
    return (high, middle, low)


def odd(axis):
    return lax.rem(lax.axis_index(axis), 2)


def rows_of(j, height):
    return pl.ds(j * height if isinstance(j, int) else pl.multiple_of(j * height, height), height)


def sent_planes():
    place = 0
    for first, depth in [(c * CX, HALO) for c in range(3)] + [(OWN_LAB0, HALO)] + [
        (OWN_RHS0 + c * CX, HALO - 1) for c in range(3)
    ]:
        for k in range(depth):
            yield place, first, k
            place += 1


def halo_planes():
    place = 0
    for first, depth in [(c * PX, HALO) for c in range(3)] + [(LAB0, HALO)] + [
        (RHS0 + c * PR - 1, HALO - 1) for c in range(3)
    ]:
        for k in range(depth):
            yield place, first, k
            place += 1


def slot_number():
    return lax.broadcasted_iota(jnp.int32, (SLOT_ROWS, 128), 0) * 128 + lax.broadcasted_iota(
        jnp.int32, (SLOT_ROWS, 128), 1
    )


def pack_first(
    disp, rhs, labels, cells_in, mult_in,
    y_other, y_pair, own, cells, mult,
    raw_labels, arrived,
):
    flip = odd("gx")
    pairs = []
    for g in range(CX):
        x = g + flip * (CX - 1 - 2 * g)
        pairs.append((labels.at[rows_of(x, CY)], raw_labels.at[rows_of(g, CY)]))
        for c in range(3):
            pairs.append((disp.at[rows_of(c * CX + x, CY)], own.at[rows_of(c * CX + g, CY)]))
            pairs.append((rhs.at[rows_of(c * CX + x, CY)], own.at[rows_of(OWN_RHS0 + c * CX + g, CY)]))
    pairs += [(cells_in, cells), (mult_in, mult)]
    copies = [pltpu.make_async_copy(a, b, arrived.at[i]) for i, (a, b) in enumerate(pairs)]
    for copy in copies:
        copy.start()
    for copy in copies:
        copy.wait()
    own[pl.ds(OWN_LAB0 * CY, CX * CY), :] = raw_labels[...].astype(F32)
    up = odd("gy") == 0
    for k in range(HALO):
        first = own[pl.ds(k, OWN, stride=CY), :]
        last = own[pl.ds(CY - HALO + k, OWN, stride=CY), :]
        y_pair[k] = jnp.where(up, last, first)
        y_other[k] = jnp.where(up, first, last)


def pack_far(count, own, raw_cells, mult, far, cells):
    flip = odd("gx")
    block_plane = raw_cells[...] // (CY * NZ)
    turned = raw_cells[...] + flip * (CX - 1 - 2 * block_plane) * (CY * NZ)
    live_cells = jnp.where(slot_number() < count[0, 0], turned, -1)
    cells[...] = live_cells
    for place, first, k in sent_planes():
        far[rows_of(place, CY), :] = own[rows_of(first + k, CY), :]
    far[pl.ds(SIDE * CY, SLOT_ROWS), :] = live_cells.astype(F32)
    for c in range(3):
        far[pl.ds(SIDE * CY + (1 + c) * SLOT_ROWS, SLOT_ROWS), :] = mult[c]


def pack_second(y_other, y_pair, own, cells, mult, corner, near, wide):
    here = lax.axis_index("gy")
    up = odd("gy") == 0
    low = jnp.where(here > 0, 1.0, 0.0).astype(F32)
    high = jnp.where(here < N_GY - 1, 1.0, 0.0).astype(F32)
    for j in range(OWN):
        wide[pl.ds(j * ROWS, CY), :] = own[rows_of(j, CY), :]
    for k in range(HALO):
        after = jnp.where(up, y_pair[k], y_other[k])
        before = jnp.where(up, y_other[k], y_pair[k])
        wide[pl.ds(CY + k, OWN, stride=ROWS), :] = high * after
        wide[pl.ds(ROWS - HALO + k, OWN, stride=ROWS), :] = low * before
    for k in range(CY + HALO, ROWS - HALO):
        wide[pl.ds(k, OWN, stride=ROWS), :] = jnp.zeros((OWN, NZ), F32)
    for place, first, k in sent_planes():
        for i, y in enumerate((CY, ROWS - HALO)):
            corner[pl.ds(place * 2 * HALO + i * HALO, HALO), :] = wide[pl.ds((first + k) * ROWS + y, HALO), :]
        near[rows_of(place, ROWS), :] = wide[rows_of(first + CX - 1 - k, ROWS), :]
    near[pl.ds(SIDE * ROWS, SLOT_ROWS), :] = cells[...].astype(F32)
    for c in range(3):
        near[pl.ds(SIDE * ROWS + (1 + c) * SLOT_ROWS, SLOT_ROWS), :] = mult[c]


def paired(array, j):
    return jnp.concatenate([array[2 * j : 2 * j + 1], array[2 * j + 1 : 2 * j + 2]], axis=1)


def spread(cells, mult, first, columns):
    column = jnp.where(cells < 0, -1, cells // NZ - first)
    depth = cells % NZ
    total = jnp.zeros((10 * columns, NZ), F32)
    parts = [piece for c in range(3) for piece in pieces_of(mult[c])]
    for j in range(SLOT_ROWS // 2):
        at_column = lax.broadcasted_iota(jnp.int32, (columns, 256), 0) == paired(column, j)
        at_depth = lax.broadcasted_iota(jnp.int32, (NZ, 256), 0) == paired(depth, j)
        left = [jnp.where(at_column, paired(piece.astype(F32), j), 0.0).astype(BF16) for piece in parts]
        left.append(jnp.where(at_column, 1.0, 0.0).astype(BF16))
        total = total + lax.dot_general(
            jnp.concatenate(left, axis=0),
            jnp.where(at_depth, 1.0, 0.0).astype(BF16),
            (((1,), (1,)), ((), ())),
            preferred_element_type=F32,
        )
    part = [total[i * columns : (i + 1) * columns] for i in range(10)]
    return [part[3 * c] + part[3 * c + 1] + part[3 * c + 2] for c in range(3)] + [part[9]]


def spread_own(cells, mult, dense):
    values = spread(cells[...], [mult[c] for c in range(3)], 0, CX * CY)
    for i in range(4):
        dense[i] = values[i]


def is_inside():
    here = lax.axis_index("gx")
    return jnp.where((here > 0) & (here < N_GX - 1), 1.0, 0.0).astype(F32)


def spread_before(far, near, dense, last, ribbon):
    flip = odd("gx")

    def at(i):
        a = far[pl.ds(SIDE * CY + i * SLOT_ROWS, SLOT_ROWS), :]
        b = near[pl.ds(SIDE * ROWS + i * SLOT_ROWS, SLOT_ROWS), :]
        return jnp.where(flip == 1, b, a)

    values = spread(at(0).astype(jnp.int32), [at(1 + c) for c in range(3)], flip * (CX - 1) * CY, CY)
    values[3] = values[3] * jnp.where(flip == 1, 1.0, is_inside())
    for i in range(4):
        ribbon[i, pl.ds(0, CY), :] = values[i]
        ribbon[i, pl.ds(CY, CX * CY), :] = dense[i]
        ribbon[i, pl.ds((CX + 1) * CY, CY), :] = values[i]


def times(k, v):
    return [
        k[SYMMETRIC_INDEX[c][0]] * v[0] + k[SYMMETRIC_INDEX[c][1]] * v[1] + k[SYMMETRIC_INDEX[c][2]] * v[2]
        for c in range(3)
    ]


class Split:
    def __init__(self, at, low, high):
        self.at, self.low, self.high = at, low, high

    def of(self, c, p, count=PX, base=0):
        ref = self.low if p < self.at else self.high
        return ref, rows_of(base + c * count + p, ROWS)


class Stencil:
    def __init__(self, entry, fields, coeff, total, scale, flux):
        self.entry, self.fields, self.coeff, self.total, self.scale, self.flux = (
            entry, fields, coeff, total, scale, flux
        )
        lane = lax.broadcasted_iota(jnp.int32, (1, NZ), 1)
        self.not_first = jnp.where(lane == 0, 0.0, 0.5)
        self.not_last = jnp.where(lane == NZ - 1, 0.0, 0.5)
        self.ends = jnp.where((lane == 0) | (lane == NZ - 1), 16.0, 0.0)
        row = lax.broadcasted_iota(jnp.int32, (ROWS, NZ), 0)
        y = lax.axis_index("gy") * CY + jnp.where(row < CY + HALO, row, row - ROWS)
        self.row_inside = (y >= 0) & (y < NY) & ((row < CY + HALO) | (row >= ROWS - HALO))

    def get(self, split, c, p):
        ref, at = split.of(c, p)
        return ref[at, :]

    def put(self, split, c, p, value):
        ref, at = split.of(c, p)
        ref[at, :] = value

    def label(self, p):
        ref, at = self.fields.of(0, p, base=LAB0)
        return ref[at, :]

    def right_side(self, c, p):
        ref, at = self.fields.of(c, p, count=PR, base=RHS0 - 1)
        return ref[at, :]

    def summed(self, split, c, p, edge=None):
        f = self.get(split, c, p)
        f = (f + f) + (self.get(split, c, p - 1) + self.get(split, c, p + 1))
        f = (f + f) + (pltpu.roll(f, 1, 0) + pltpu.roll(f, ROWS - 1, 0))
        f = f + (pltpu.roll(f, 1, 1) * self.not_first + pltpu.roll(f, NZ - 1, 1) * self.not_last)
        if edge is not None:
            f = f + self.ends * (0.5 * edge)
        return f + f

    def coefficients(self, planes):
        for p in planes:
            label = self.label(p)
            k = [jnp.broadcast_to(self.entry(0, e), label.shape) for e in range(6)]
            for m in range(1, LABELS):
                at = label == float(m)
                k = [jnp.where(at, self.entry(m, e), k[e]) for e in range(6)]
            for e in range(6):
                self.put(self.coeff, e, p, k[e])
            self.push(self.flux, p, [self.get(self.fields, c, p) for c in range(3)])

    def weights(self, planes):
        for p in planes:
            for e in range(6):
                k = self.get(self.coeff, e, p)
                around = self.summed(self.coeff, e, p, self.entry(0, e))
                self.put(self.total, e, p, 64.0 * k + around)
                if e < 3:
                    self.put(self.scale, e, p, DAMPING / (MASS_SHIFT + 6.0 * k + 0.125 * around))

    def push(self, flux, p, v):
        pushed = times([self.get(self.coeff, e, p) for e in range(6)], v)
        for c in range(3):
            self.put(flux, c, p, pushed[c])

    def image(self, p, v_split, flux):
        v = [self.get(v_split, c, p) for c in range(3)]
        k = [self.get(self.coeff, e, p) for e in range(6)]
        m = [self.get(self.total, e, p) for e in range(6)]
        around = [self.summed(v_split, c, p) for c in range(3)]
        pushed = [self.summed(flux, c, p) for c in range(3)]
        mine, theirs = times(m, v), times(k, around)
        return v, [MASS_SHIFT * v[c] + 0.125 * (mine[c] - theirs[c] - pushed[c]) for c in range(3)]

    def sweep(self, planes, v_split, flux, to, to_flux, inside=None):
        for p in planes:
            keep = self.row_inside if p >= HALO else self.row_inside & (inside > 0.5)
            v, a = self.image(p, v_split, flux)
            new = []
            for c in range(3):
                value = v[c] + (self.right_side(c, p) - a[c]) * self.get(self.scale, c, p)
                value = jnp.where(keep, value, 0.0)
                self.put(to, c, p, value)
                new.append(value)
            self.push(to_flux, p, new)

    def remainder(self, p, v_split, flux):
        a = self.image(p, v_split, flux)[1]
        return [(self.right_side(c, p) - a[c])[:CY] for c in range(3)]


def near_part(
    stiffness, own, near,
    fields, coeff, total, scale, flux, first, flux_first, second, flux_second, table, last,
):
    for c in range(3):
        for g in range(CX):
            fields[rows_of(c * PX + HALO + g, ROWS), :] = own[rows_of(c * CX + g, ROWS), :]
            fields[rows_of(RHS0 - 1 + c * PR + HALO + g, ROWS), :] = own[rows_of(OWN_RHS0 + c * CX + g, ROWS), :]
    for g in range(CX):
        fields[rows_of(LAB0 + HALO + g, ROWS), :] = own[rows_of(OWN_LAB0 + g, ROWS), :]
    for place, at, k in halo_planes():
        fields[rows_of(at + HALO + CX + k, ROWS), :] = near[rows_of(place, ROWS), :]
    for m in range(LABELS):
        for e in range(6):
            table[pl.ds(m * 6 + e, 1), :] = jnp.full((1, NZ), stiffness[m, e], F32)

    def whole(ref):
        return Split(0, None, ref)

    grid = Stencil(
        lambda m, e: stiffness[m, e], whole(fields), whole(coeff), whole(total), whole(scale), whole(flux)
    )
    grid.coefficients(range(HALO, PX))
    grid.weights(range(HALO + 1, PX - 1))
    grid.sweep(range(HALO + 1, PX - 1), whole(fields), whole(flux), whole(first), whole(flux_first))
    grid.sweep(range(HALO + 2, PX - 2), whole(first), whole(flux_first), whole(second), whole(flux_second))
    remainder = grid.remainder(HALO + 3, whole(second), whole(flux_second))
    for c in range(3):
        last[rows_of(c, CY), :] = remainder[c]


def far_part(
    far, corner, ribbon,
    near_fields, near_coeff, near_total, near_scale, near_flux,
    near_first, near_flux_first, near_second, near_flux_second, table, last,
    smoothed, jumps, message,
    fields, coeff, total, scale, flux, first, flux_first, second, flux_second, coarse,
):
    inside = is_inside()
    flip = odd("gx")
    sign = jnp.where(flip == 1, -1.0, 1.0).astype(F32)
    for y in range(CY + HALO, ROWS - HALO):
        fields[pl.ds(y, FIELDS, stride=ROWS), :] = jnp.zeros((FIELDS, NZ), F32)
    for place, at, k in halo_planes():
        plane = (at + HALO - 1 - k) * ROWS
        fields[pl.ds(plane, CY), :] = inside * far[rows_of(place, CY), :]
        for i, y in enumerate((CY, ROWS - HALO)):
            fields[pl.ds(plane + y, HALO), :] = inside * corner[pl.ds(place * 2 * HALO + i * HALO, HALO), :]
    v0, flux0 = Split(HALO, fields, near_fields), Split(HALO, flux, near_flux)
    v1, flux1 = Split(HALO + 1, first, near_first), Split(HALO + 1, flux_first, near_flux_first)
    v2, flux2 = Split(HALO + 2, second, near_second), Split(HALO + 2, flux_second, near_flux_second)
    grid = Stencil(
        lambda m, e: table[pl.ds(m * 6 + e, 1), :],
        v0,
        Split(HALO, coeff, near_coeff),
        Split(HALO + 1, total, near_total),
        Split(HALO + 1, scale, near_scale),
        flux0,
    )
    grid.coefficients(range(HALO))
    grid.weights(range(1, HALO + 1))
    grid.sweep(range(1, HALO + 1), v0, flux0, v1, flux1, inside)
    grid.sweep(range(2, HALO + 2), v1, flux1, v2, flux2, inside)
    remainders = [grid.remainder(HALO + g, v2, flux2) for g in range(CX - 1)]
    remainders.append([last[rows_of(c, CY), :] for c in range(3)])

    for c in range(3):
        planes = [grid.get(v2, c, HALO - 1 + i)[:CY] for i in range(CX + 2)]
        for g in range(CX):
            x = g + flip * (CX - 1 - 2 * g)
            smoothed[rows_of(c * CX + x, CY), :] = planes[1 + g]
        pushed = []
        for i in range(CX + 1):
            jump = sign * (planes[i] - planes[i + 1])
            jumps[c, rows_of(i, CY), :] = jump
            at = rows_of(i + flip, CY)
            pushed.append(jnp.where(ribbon[3, at, :] > 0.5, ribbon[c, at, :] + PENALTY * jump, 0.0))
        parts = [remainders[g][c] - sign * (pushed[g + 1] - pushed[g]) for g in range(CX)]
        for half in range(2):
            coarse[rows_of(half * 3 + c, CY), :] = parts[2 * half] + parts[2 * half + 1]

    out = jnp.zeros((3 * CY // 2, NZ), F32)
    lane_in = lax.broadcasted_iota(jnp.int32, (NZ, NZ), 0)
    lane_out = lax.broadcasted_iota(jnp.int32, (NZ, NZ), 1)
    for half in range(2):
        at = 3 * half * CY
        rows = coarse[pl.ds(at, 3 * CY // 2, stride=2), :] + coarse[pl.ds(at + 1, 3 * CY // 2, stride=2), :]
        x = half + flip * (1 - 2 * half)
        pick = jnp.where(lane_in // 2 + x * (NZ // 2) == lane_out, 1.0, 0.0).astype(BF16)
        for piece in pieces_of(rows):
            out = out + jnp.dot(piece, pick, preferred_element_type=F32)
    for s in range(N_GY):
        message[s] = out


def finish(
    cells, mult, jumps, smoothed, gathered,
    smoothed_out, updated_out, coarse_out,
    updated, coarse, done,
):
    copies = [
        pltpu.make_async_copy(smoothed, smoothed_out, done.at[0]),
        pltpu.make_async_copy(coarse, coarse_out, done.at[1]),
        pltpu.make_async_copy(updated, updated_out, done.at[2]),
    ]
    copies[0].start()
    for c in range(3):
        parts = [gathered[s, pl.ds(c * CY // 2, CY // 2), :] for s in range(N_GY)]
        coarse[c] = jnp.transpose(jnp.concatenate(parts, axis=0))
    copies[1].start()
    live = cells[...] >= 0
    column, depth = cells[...] // NZ, cells[...] % NZ
    block = CX * CY
    start = pl.multiple_of((1 - odd("gx")) * CY, CY)
    left = jnp.concatenate(
        [jnp.concatenate(pieces_of(jumps[c, pl.ds(start, block), :]), axis=1) for c in range(3)], axis=0
    )
    for j in range(SLOT_ROWS // 2):
        at_depth = lax.broadcasted_iota(jnp.int32, (NZ, 256), 0) == paired(depth, j)
        right = jnp.where(at_depth, 1.0, 0.0).astype(BF16)
        picked = jnp.dot(left, jnp.concatenate([right] * 3, axis=0), preferred_element_type=F32)
        at_column = lax.broadcasted_iota(jnp.int32, (block, 256), 0) == paired(column, j)
        for c in range(3):
            jump = jnp.sum(
                jnp.where(at_column, picked[c * block : (c + 1) * block], 0.0), axis=0, keepdims=True
            )
            for i in range(2):
                at = 2 * j + i
                old = mult[c, at : at + 1, :]
                new = old + PENALTY * jump[:, i * 128 : (i + 1) * 128]
                updated[c, at : at + 1, :] = jnp.where(live[at : at + 1], new, old)
    copies[2].start()
    for copy in copies:
        copy.wait()


def in_hbm(array):
    return pltpu.with_memory_space_constraint(array, pltpu.HBM)


def call(kernel, outs, ins, out_specs=None, scratch=(), flops=1000):
    return pl.pallas_call(
        kernel,
        out_shape=outs,
        in_specs=ins,
        out_specs=out_specs or [VMEM] * len(outs),
        scratch_shapes=list(scratch),
        compiler_params=PARAMS,
        cost_estimate=pl.CostEstimate(flops=flops, bytes_accessed=1000, transcendentals=0),
    )


def pair(n):
    return [(i, i ^ 1) for i in range(n)]


def other_x():
    out = []
    for i in range(N_GX):
        for j in range(N_GY):
            partner = (i, j ^ 1) if i in (0, N_GX - 1) else (((i + 1) ^ 1) - 1, j)
            out.append((i * N_GY + j, partner[0] * N_GY + partner[1]))
    return out


def other_y():
    out = []
    for i in range(N_GX):
        for j in range(N_GY):
            partner = (i ^ 1, j) if j in (0, N_GY - 1) else (i, ((j + 1) ^ 1) - 1)
            out.append((i * N_GY + j, partner[0] * N_GY + partner[1]))
    return out


def body(displacement, rhs, labels, stiffness, rows, counts, multipliers):
    block = CX * CY
    copies = 2 + 7 * CX
    slots = jax.ShapeDtypeStruct((SLOT_ROWS, 128), jnp.int32)
    y_other, y_pair, own, raw_cells, mult = call(
        pack_first,
        [f32(HALO, OWN, NZ), f32(HALO, OWN, NZ), f32(OWN * CY, NZ), slots, f32(3, SLOT_ROWS, 128)],
        [HBM] * 5,
        scratch=[pltpu.VMEM((block, NZ), jnp.int32), pltpu.SemaphoreType.DMA((copies,))],
    )(
        in_hbm(displacement.reshape(3 * block, NZ)),
        in_hbm(rhs.reshape(3 * block, NZ)),
        in_hbm(labels.reshape(block, NZ)),
        in_hbm(rows.reshape(SLOT_ROWS, 128)),
        in_hbm(multipliers.reshape(3, SLOT_ROWS, 128)),
    )
    far, cells = call(pack_far, [f32(SIDE * CY + IFACE, NZ), slots], [SMEM] + [VMEM] * 3)(
        counts, own, raw_cells, mult
    )
    far = lax.ppermute(far, ("gx", "gy"), other_x())
    y_pair = lax.ppermute(y_pair, "gy", pair(N_GY))
    y_other = lax.ppermute(y_other, ("gx", "gy"), other_y())
    (dense,) = call(spread_own, [f32(4, block, NZ)], [VMEM] * 2, flops=100000000000)(cells, mult)
    corner, near, own = call(
        pack_second, [f32(SIDE * 2 * HALO + 4, NZ), f32(SIDE * ROWS + IFACE, NZ), f32(OWN * ROWS, NZ)], [VMEM] * 5
    )(y_other, y_pair, own, cells, mult)
    corner = lax.ppermute(corner, ("gx", "gy"), other_x())
    near = lax.ppermute(near, "gx", pair(N_GX))
    three, six = f32(3 * PX * ROWS, NZ), f32(6 * PX * ROWS, NZ)
    arrays = [f32(FIELDS * ROWS, NZ), six, six] + [three] * 6
    half = call(
        near_part, arrays + [f32(LABELS * 6, NZ), f32(3 * CY, NZ)], [SMEM, VMEM, VMEM]
    )(stiffness, own, near)
    (ribbon,) = call(spread_before, [f32(4, (CX + 2) * CY, NZ)], [VMEM] * 4)(far, near, dense, half[-1])
    smoothed, jumps, message = call(
        far_part,
        [f32(3 * block, NZ), f32(3, (CX + 1) * CY, NZ), f32(N_GY, 3 * CY // 2, NZ)],
        [VMEM] * (3 + len(half)),
        scratch=[pltpu.VMEM(a.shape, F32) for a in arrays] + [pltpu.VMEM((6 * CY, NZ), F32)],
    )(far, corner, ribbon, *half)
    gathered = lax.all_to_all(message, "gy", 0, 0)
    smoothed, updated, coarse = call(
        finish,
        [pltpu.HBM(s, F32) for s in ((3 * block, NZ), (3, SLOT_ROWS, 128), (3, CX // 2 * NZ // 2, NY // 2))],
        [VMEM] * 5,
        out_specs=[HBM] * 3,
        scratch=[
            pltpu.VMEM((3, SLOT_ROWS, 128), F32),
            pltpu.VMEM((3, CX // 2 * NZ // 2, NY // 2), F32),
            pltpu.SemaphoreType.DMA((3,)),
        ],
    )(cells, mult, jumps, smoothed, gathered)
    coarse = jnp.swapaxes(coarse.reshape(3, CX // 2, NZ // 2, NY // 2), 2, 3)
    return (smoothed.reshape(3, CX, CY, NZ), coarse, updated.reshape(3, 1, 1, SLOTS))


def solution(mesh):
    return jax.shard_map(
        body,
        mesh=mesh,
        in_specs=(
            P(None, "gx", "gy", None),
            P(None, "gx", "gy", None),
            P("gx", "gy", None),
            P(),
            P("gx", "gy", None),
            P("gx", "gy"),
            P(None, "gx", "gy", None),
        ),
        out_specs=(P(None, "gx", "gy", None), P(None, "gx", None, None), P(None, "gx", "gy", None)),
        check_vma=False,
    )
```

```python
import jax
import jax.numpy as jnp
from jax import lax
from jax.experimental import pallas as pl
from jax.experimental.pallas import tpu as pltpu
from jax.sharding import PartitionSpec as P

SYMMETRIC_INDEX = ((0, 3, 4), (3, 1, 5), (4, 5, 2))
DAMPING = 0.6
MASS_SHIFT = 1.0
PENALTY = 1.0

CX, CY, NZ, SLOTS = 4, 32, 128, 1024
N_GX, N_GY = 32, 8
NX, NY = CX * N_GX, CY * N_GY
LABELS = 8
HALO = 3
PX = CX + 2 * HALO
PR = PX - 2
ROWS = 40
LAB0 = 3 * PX
RHS0 = LAB0 + PX
FIELDS = RHS0 + 3 * PR
OWN_LAB0 = 3 * CX
OWN_RHS0 = OWN_LAB0 + CX
OWN = OWN_RHS0 + 3 * CX
SIDE = 3 * HALO + HALO + 3 * (HALO - 1)
SLOT_ROWS = SLOTS // 128
CORNER = 112
IFACE = 4 * SLOT_ROWS
VMEM = pl.BlockSpec(memory_space=pltpu.VMEM)
SMEM = pl.BlockSpec(memory_space=pltpu.SMEM)
HBM = pl.BlockSpec(memory_space=pltpu.HBM)
F32 = jnp.float32
BF16 = jnp.bfloat16
PARAMS = pltpu.CompilerParams(vmem_limit_bytes=32 * 1024 * 1024)


def f32(*shape):
    return jax.ShapeDtypeStruct(shape, F32)


def pieces_of(value):
    high = value.astype(BF16)
    rest = value - high.astype(F32)
    middle = rest.astype(BF16)
    low = (rest - middle.astype(F32)).astype(BF16)
    return (high, middle, low)


def odd(axis):
    return lax.rem(lax.axis_index(axis), 2)


def rows_of(j, height):
    return pl.ds(j * height if isinstance(j, int) else pl.multiple_of(j * height, height), height)


def sent_planes():
    place = 0
    for first, depth in [(c * CX, HALO) for c in range(3)] + [(OWN_LAB0, HALO)] + [
        (OWN_RHS0 + c * CX, HALO - 1) for c in range(3)
    ]:
        for k in range(depth):
            yield place, first, k
            place += 1


def halo_planes():
    place = 0
    for first, depth in [(c * PX, HALO) for c in range(3)] + [(LAB0, HALO)] + [
        (RHS0 + c * PR - 1, HALO - 1) for c in range(3)
    ]:
        for k in range(depth):
            yield place, first, k
            place += 1


def slot_number():
    return lax.broadcasted_iota(jnp.int32, (SLOT_ROWS, 128), 0) * 128 + lax.broadcasted_iota(
        jnp.int32, (SLOT_ROWS, 128), 1
    )


def pack_first(
    disp, rhs, labels, cells_in, mult_in,
    y_other, y_pair, own, cells, mult,
    raw_labels, arrived,
):
    flip = odd("gx")
    pairs = []
    for g in range(CX):
        x = g + flip * (CX - 1 - 2 * g)
        pairs.append((labels.at[rows_of(x, CY)], raw_labels.at[rows_of(g, CY)]))
        for c in range(3):
            pairs.append((disp.at[rows_of(c * CX + x, CY)], own.at[rows_of(c * CX + g, CY)]))
            pairs.append((rhs.at[rows_of(c * CX + x, CY)], own.at[rows_of(OWN_RHS0 + c * CX + g, CY)]))
    pairs += [(cells_in, cells), (mult_in, mult)]
    copies = [pltpu.make_async_copy(a, b, arrived.at[i]) for i, (a, b) in enumerate(pairs)]
    for copy in copies:
        copy.start()
    for copy in copies:
        copy.wait()
    own[pl.ds(OWN_LAB0 * CY, CX * CY), :] = raw_labels[...].astype(F32)
    up = odd("gy") == 0
    for k in range(HALO):
        first = own[pl.ds(k, OWN, stride=CY), :]
        last = own[pl.ds(CY - HALO + k, OWN, stride=CY), :]
        y_pair[k] = jnp.where(up, last, first)
        y_other[k] = jnp.where(up, first, last)


def pack_far(own, raw_cells, mult, far, cells):
    flip = odd("gx")
    block_plane = raw_cells[...] // (CY * NZ)
    turned = raw_cells[...] + flip * (CX - 1 - 2 * block_plane) * (CY * NZ)
    cells[...] = turned
    for place, first, k in sent_planes():
        far[rows_of(place, CY), :] = own[rows_of(first + k, CY), :]
    far[pl.ds(SIDE * CY, SLOT_ROWS), :] = turned.astype(F32)
    for c in range(3):
        far[pl.ds(SIDE * CY + (1 + c) * SLOT_ROWS, SLOT_ROWS), :] = mult[c]


def pack_second(y_other, y_pair, count, own, cells, mult, corner, near, wide, limit):
    here = lax.axis_index("gy")
    up = odd("gy") == 0
    low = jnp.where(here > 0, 1.0, 0.0).astype(F32)
    high = jnp.where(here < N_GY - 1, 1.0, 0.0).astype(F32)
    for j in range(OWN):
        wide[pl.ds(j * ROWS, CY), :] = own[rows_of(j, CY), :]
    for k in range(HALO):
        after = jnp.where(up, y_pair[k], y_other[k])
        before = jnp.where(up, y_other[k], y_pair[k])
        wide[pl.ds(CY + k, OWN, stride=ROWS), :] = high * after
        wide[pl.ds(ROWS - HALO + k, OWN, stride=ROWS), :] = low * before
    for k in range(CY + HALO, ROWS - HALO):
        wide[pl.ds(k, OWN, stride=ROWS), :] = jnp.zeros((OWN, NZ), F32)
    for place, first, k in sent_planes():
        for i, y in enumerate((CY, ROWS - HALO)):
            corner[pl.ds(place * 2 * HALO + i * HALO, HALO), :] = wide[pl.ds((first + k) * ROWS + y, HALO), :]
        near[rows_of(place, ROWS), :] = wide[rows_of(first + CX - 1 - k, ROWS), :]
    live = jnp.full((SLOT_ROWS, 128), count[0, 0].astype(F32), F32)
    limit[...] = live
    corner[pl.ds(CORNER, SLOT_ROWS), :] = live
    near[pl.ds(SIDE * ROWS + IFACE, SLOT_ROWS), :] = live
    near[pl.ds(SIDE * ROWS, SLOT_ROWS), :] = cells[...].astype(F32)
    for c in range(3):
        near[pl.ds(SIDE * ROWS + (1 + c) * SLOT_ROWS, SLOT_ROWS), :] = mult[c]


def paired(array, j):
    return jnp.concatenate([array[2 * j : 2 * j + 1], array[2 * j + 1 : 2 * j + 2]], axis=1)


def spread(cells, mult, first, columns):
    column = cells // NZ - first
    depth = cells % NZ
    total = jnp.zeros((11 * columns, NZ), F32)
    parts = [piece for c in range(3) for piece in pieces_of(mult[c])]
    parts += pieces_of((slot_number() + 1).astype(F32))[:2]
    for j in range(SLOT_ROWS // 2):
        at_column = lax.broadcasted_iota(jnp.int32, (columns, 256), 0) == paired(column, j)
        at_depth = lax.broadcasted_iota(jnp.int32, (NZ, 256), 0) == paired(depth, j)
        left = [jnp.where(at_column, paired(piece.astype(F32), j), 0.0).astype(BF16) for piece in parts]
        total = total + lax.dot_general(
            jnp.concatenate(left, axis=0),
            jnp.where(at_depth, 1.0, 0.0).astype(BF16),
            (((1,), (1,)), ((), ())),
            preferred_element_type=F32,
        )
    part = [total[i * columns : (i + 1) * columns] for i in range(11)]
    return [part[3 * c] + part[3 * c + 1] + part[3 * c + 2] for c in range(3)] + [part[9] + part[10]]


def spread_own(cells, mult, dense):
    values = spread(cells[...], [mult[c] for c in range(3)], 0, CX * CY)
    for i in range(4):
        dense[i] = values[i]


def is_inside():
    here = lax.axis_index("gx")
    return jnp.where((here > 0) & (here < N_GX - 1), 1.0, 0.0).astype(F32)


def spread_before(far, near, dense, last, ribbon):
    flip = odd("gx")

    def at(i):
        a = far[pl.ds(SIDE * CY + i * SLOT_ROWS, SLOT_ROWS), :]
        b = near[pl.ds(SIDE * ROWS + i * SLOT_ROWS, SLOT_ROWS), :]
        return jnp.where(flip == 1, b, a)

    values = spread(at(0).astype(jnp.int32), [at(1 + c) for c in range(3)], flip * (CX - 1) * CY, CY)
    values[3] = values[3] * jnp.where(flip == 1, 1.0, is_inside())
    for i in range(4):
        ribbon[i, pl.ds(0, CY), :] = values[i]
        ribbon[i, pl.ds(CY, CX * CY), :] = dense[i]
        ribbon[i, pl.ds((CX + 1) * CY, CY), :] = values[i]


def times(k, v):
    return [
        k[SYMMETRIC_INDEX[c][0]] * v[0] + k[SYMMETRIC_INDEX[c][1]] * v[1] + k[SYMMETRIC_INDEX[c][2]] * v[2]
        for c in range(3)
    ]


class Split:
    def __init__(self, at, low, high):
        self.at, self.low, self.high = at, low, high

    def of(self, c, p, count=PX, base=0):
        ref = self.low if p < self.at else self.high
        return ref, rows_of(base + c * count + p, ROWS)


class Stencil:
    def __init__(self, entry, fields, coeff, total, scale, flux):
        self.entry, self.fields, self.coeff, self.total, self.scale, self.flux = (
            entry, fields, coeff, total, scale, flux
        )
        lane = lax.broadcasted_iota(jnp.int32, (1, NZ), 1)
        self.not_first = jnp.where(lane == 0, 0.0, 0.5)
        self.not_last = jnp.where(lane == NZ - 1, 0.0, 0.5)
        self.ends = jnp.where((lane == 0) | (lane == NZ - 1), 16.0, 0.0)
        row = lax.broadcasted_iota(jnp.int32, (ROWS, NZ), 0)
        y = lax.axis_index("gy") * CY + jnp.where(row < CY + HALO, row, row - ROWS)
        self.row_inside = (y >= 0) & (y < NY) & ((row < CY + HALO) | (row >= ROWS - HALO))

    def get(self, split, c, p):
        ref, at = split.of(c, p)
        return ref[at, :]

    def put(self, split, c, p, value):
        ref, at = split.of(c, p)
        ref[at, :] = value

    def label(self, p):
        ref, at = self.fields.of(0, p, base=LAB0)
        return ref[at, :]

    def right_side(self, c, p):
        ref, at = self.fields.of(c, p, count=PR, base=RHS0 - 1)
        return ref[at, :]

    def summed(self, split, c, p, edge=None):
        f = self.get(split, c, p)
        f = (f + f) + (self.get(split, c, p - 1) + self.get(split, c, p + 1))
        f = (f + f) + (pltpu.roll(f, 1, 0) + pltpu.roll(f, ROWS - 1, 0))
        f = f + (pltpu.roll(f, 1, 1) * self.not_first + pltpu.roll(f, NZ - 1, 1) * self.not_last)
        if edge is not None:
            f = f + self.ends * (0.5 * edge)
        return f + f

    def coefficients(self, planes):
        for p in planes:
            label = self.label(p)
            k = [jnp.broadcast_to(self.entry(0, e), label.shape) for e in range(6)]
            for m in range(1, LABELS):
                at = label == float(m)
                k = [jnp.where(at, self.entry(m, e), k[e]) for e in range(6)]
            for e in range(6):
                self.put(self.coeff, e, p, k[e])
            self.push(self.flux, p, [self.get(self.fields, c, p) for c in range(3)])

    def weights(self, planes):
        for p in planes:
            for e in range(6):
                k = self.get(self.coeff, e, p)
                around = self.summed(self.coeff, e, p, self.entry(0, e))
                self.put(self.total, e, p, 64.0 * k + around)
                if e < 3:
                    self.put(self.scale, e, p, DAMPING / (MASS_SHIFT + 6.0 * k + 0.125 * around))

    def push(self, flux, p, v):
        pushed = times([self.get(self.coeff, e, p) for e in range(6)], v)
        for c in range(3):
            self.put(flux, c, p, pushed[c])

    def image(self, p, v_split, flux):
        v = [self.get(v_split, c, p) for c in range(3)]
        k = [self.get(self.coeff, e, p) for e in range(6)]
        m = [self.get(self.total, e, p) for e in range(6)]
        around = [self.summed(v_split, c, p) for c in range(3)]
        pushed = [self.summed(flux, c, p) for c in range(3)]
        mine, theirs = times(m, v), times(k, around)
        return v, [MASS_SHIFT * v[c] + 0.125 * (mine[c] - theirs[c] - pushed[c]) for c in range(3)]

    def sweep(self, planes, v_split, flux, to, to_flux, inside=None):
        for p in planes:
            keep = self.row_inside if p >= HALO else self.row_inside & (inside > 0.5)
            v, a = self.image(p, v_split, flux)
            new = []
            for c in range(3):
                value = v[c] + (self.right_side(c, p) - a[c]) * self.get(self.scale, c, p)
                value = jnp.where(keep, value, 0.0)
                self.put(to, c, p, value)
                new.append(value)
            self.push(to_flux, p, new)

    def remainder(self, p, v_split, flux):
        a = self.image(p, v_split, flux)[1]
        return [(self.right_side(c, p) - a[c])[:CY] for c in range(3)]


def near_part(
    stiffness, own, near,
    fields, coeff, total, scale, flux, first, flux_first, second, flux_second, table, last,
):
    for c in range(3):
        for g in range(CX):
            fields[rows_of(c * PX + HALO + g, ROWS), :] = own[rows_of(c * CX + g, ROWS), :]
            fields[rows_of(RHS0 - 1 + c * PR + HALO + g, ROWS), :] = own[rows_of(OWN_RHS0 + c * CX + g, ROWS), :]
    for g in range(CX):
        fields[rows_of(LAB0 + HALO + g, ROWS), :] = own[rows_of(OWN_LAB0 + g, ROWS), :]
    for place, at, k in halo_planes():
        fields[rows_of(at + HALO + CX + k, ROWS), :] = near[rows_of(place, ROWS), :]
    for m in range(LABELS):
        for e in range(6):
            table[pl.ds(m * 6 + e, 1), :] = jnp.full((1, NZ), stiffness[m, e], F32)

    def whole(ref):
        return Split(0, None, ref)

    grid = Stencil(
        lambda m, e: stiffness[m, e], whole(fields), whole(coeff), whole(total), whole(scale), whole(flux)
    )
    grid.coefficients(range(HALO, PX))
    grid.weights(range(HALO + 1, PX - 1))
    grid.sweep(range(HALO + 1, PX - 1), whole(fields), whole(flux), whole(first), whole(flux_first))
    grid.sweep(range(HALO + 2, PX - 2), whole(first), whole(flux_first), whole(second), whole(flux_second))
    remainder = grid.remainder(HALO + 3, whole(second), whole(flux_second))
    for c in range(3):
        last[rows_of(c, CY), :] = remainder[c]


def far_part(
    far, corner, near, limit, ribbon,
    near_fields, near_coeff, near_total, near_scale, near_flux,
    near_first, near_flux_first, near_second, near_flux_second, table, last,
    smoothed, jumps, message,
    fields, coeff, total, scale, flux, first, flux_first, second, flux_second, coarse,
):
    inside = is_inside()
    flip = odd("gx")
    sign = jnp.where(flip == 1, -1.0, 1.0).astype(F32)
    for y in range(CY + HALO, ROWS - HALO):
        fields[pl.ds(y, FIELDS, stride=ROWS), :] = jnp.zeros((FIELDS, NZ), F32)
    for place, at, k in halo_planes():
        plane = (at + HALO - 1 - k) * ROWS
        fields[pl.ds(plane, CY), :] = inside * far[rows_of(place, CY), :]
        for i, y in enumerate((CY, ROWS - HALO)):
            fields[pl.ds(plane + y, HALO), :] = inside * corner[pl.ds(place * 2 * HALO + i * HALO, HALO), :]
    v0, flux0 = Split(HALO, fields, near_fields), Split(HALO, flux, near_flux)
    v1, flux1 = Split(HALO + 1, first, near_first), Split(HALO + 1, flux_first, near_flux_first)
    v2, flux2 = Split(HALO + 2, second, near_second), Split(HALO + 2, flux_second, near_flux_second)
    grid = Stencil(
        lambda m, e: table[pl.ds(m * 6 + e, 1), :],
        v0,
        Split(HALO, coeff, near_coeff),
        Split(HALO + 1, total, near_total),
        Split(HALO + 1, scale, near_scale),
        flux0,
    )
    grid.coefficients(range(HALO))
    grid.weights(range(1, HALO + 1))
    grid.sweep(range(1, HALO + 1), v0, flux0, v1, flux1, inside)
    grid.sweep(range(2, HALO + 2), v1, flux1, v2, flux2, inside)
    remainders = [grid.remainder(HALO + g, v2, flux2) for g in range(CX - 1)]
    remainders.append([last[rows_of(c, CY), :] for c in range(3)])

    mine = limit[:1]
    theirs = jnp.where(flip == 1, near[pl.ds(SIDE * ROWS + IFACE, 1), :], corner[pl.ds(CORNER, 1), :])
    live = []
    for i in range(CX + 1):
        if i == 0:
            top = jnp.where(flip == 1, mine, theirs)
        elif i == CX:
            top = jnp.where(flip == 1, theirs, mine)
        else:
            top = mine
        number = ribbon[3, rows_of(i + flip, CY), :]
        live.append((number > 0.5) & (number < top + 0.5))
    for c in range(3):
        planes = [grid.get(v2, c, HALO - 1 + i)[:CY] for i in range(CX + 2)]
        for g in range(CX):
            x = g + flip * (CX - 1 - 2 * g)
            smoothed[rows_of(c * CX + x, CY), :] = planes[1 + g]
        pushed = []
        for i in range(CX + 1):
            jump = sign * (planes[i] - planes[i + 1])
            jumps[c, rows_of(i, CY), :] = jump
            at = rows_of(i + flip, CY)
            pushed.append(jnp.where(live[i], ribbon[c, at, :] + PENALTY * jump, 0.0))
        parts = [remainders[g][c] - sign * (pushed[g + 1] - pushed[g]) for g in range(CX)]
        for half in range(2):
            coarse[rows_of(half * 3 + c, CY), :] = parts[2 * half] + parts[2 * half + 1]

    out = jnp.zeros((3 * CY // 2, NZ), F32)
    lane_in = lax.broadcasted_iota(jnp.int32, (NZ, NZ), 0)
    lane_out = lax.broadcasted_iota(jnp.int32, (NZ, NZ), 1)
    for half in range(2):
        at = 3 * half * CY
        rows = coarse[pl.ds(at, 3 * CY // 2, stride=2), :] + coarse[pl.ds(at + 1, 3 * CY // 2, stride=2), :]
        x = half + flip * (1 - 2 * half)
        pick = jnp.where(lane_in // 2 + x * (NZ // 2) == lane_out, 1.0, 0.0).astype(BF16)
        for piece in pieces_of(rows):
            out = out + jnp.dot(piece, pick, preferred_element_type=F32)
    for s in range(N_GY):
        message[s] = out


def finish(
    limit, cells, mult, jumps, smoothed, gathered,
    smoothed_out, updated_out, coarse_out,
    updated, coarse, done,
):
    copies = [
        pltpu.make_async_copy(smoothed, smoothed_out, done.at[0]),
        pltpu.make_async_copy(coarse, coarse_out, done.at[1]),
        pltpu.make_async_copy(updated, updated_out, done.at[2]),
    ]
    copies[0].start()
    for c in range(3):
        parts = [gathered[s, pl.ds(c * CY // 2, CY // 2), :] for s in range(N_GY)]
        coarse[c] = jnp.transpose(jnp.concatenate(parts, axis=0))
    copies[1].start()
    live = slot_number().astype(F32) < limit[...] - 0.5
    column, depth = cells[...] // NZ, cells[...] % NZ
    block = CX * CY
    start = pl.multiple_of((1 - odd("gx")) * CY, CY)
    left = jnp.concatenate(
        [jnp.concatenate(pieces_of(jumps[c, pl.ds(start, block), :]), axis=1) for c in range(3)], axis=0
    )
    for j in range(SLOT_ROWS // 2):
        at_depth = lax.broadcasted_iota(jnp.int32, (NZ, 256), 0) == paired(depth, j)
        right = jnp.where(at_depth, 1.0, 0.0).astype(BF16)
        picked = jnp.dot(left, jnp.concatenate([right] * 3, axis=0), preferred_element_type=F32)
        at_column = lax.broadcasted_iota(jnp.int32, (block, 256), 0) == paired(column, j)
        for c in range(3):
            jump = jnp.sum(
                jnp.where(at_column, picked[c * block : (c + 1) * block], 0.0), axis=0, keepdims=True
            )
            for i in range(2):
                at = 2 * j + i
                old = mult[c, at : at + 1, :]
                new = old + PENALTY * jump[:, i * 128 : (i + 1) * 128]
                updated[c, at : at + 1, :] = jnp.where(live[at : at + 1], new, old)
    copies[2].start()
    for copy in copies:
        copy.wait()


def in_hbm(array):
    return pltpu.with_memory_space_constraint(array, pltpu.HBM)


def call(kernel, outs, ins, out_specs=None, scratch=(), flops=1000):
    return pl.pallas_call(
        kernel,
        out_shape=outs,
        in_specs=ins,
        out_specs=out_specs or [VMEM] * len(outs),
        scratch_shapes=list(scratch),
        compiler_params=PARAMS,
        cost_estimate=pl.CostEstimate(flops=flops, bytes_accessed=1000, transcendentals=0),
    )


def pair(n):
    return [(i, i ^ 1) for i in range(n)]


def other_x():
    out = []
    for i in range(N_GX):
        for j in range(N_GY):
            partner = (i, j ^ 1) if i in (0, N_GX - 1) else (((i + 1) ^ 1) - 1, j)
            out.append((i * N_GY + j, partner[0] * N_GY + partner[1]))
    return out


def other_y():
    out = []
    for i in range(N_GX):
        for j in range(N_GY):
            partner = (i ^ 1, j) if j in (0, N_GY - 1) else (i, ((j + 1) ^ 1) - 1)
            out.append((i * N_GY + j, partner[0] * N_GY + partner[1]))
    return out


def body(displacement, rhs, labels, stiffness, rows, counts, multipliers):
    block = CX * CY
    copies = 2 + 7 * CX
    slots = jax.ShapeDtypeStruct((SLOT_ROWS, 128), jnp.int32)
    y_other, y_pair, own, raw_cells, mult = call(
        pack_first,
        [f32(HALO, OWN, NZ), f32(HALO, OWN, NZ), f32(OWN * CY, NZ), slots, f32(3, SLOT_ROWS, 128)],
        [HBM] * 5,
        scratch=[pltpu.VMEM((block, NZ), jnp.int32), pltpu.SemaphoreType.DMA((copies,))],
    )(
        in_hbm(displacement.reshape(3 * block, NZ)),
        in_hbm(rhs.reshape(3 * block, NZ)),
        in_hbm(labels.reshape(block, NZ)),
        in_hbm(rows.reshape(SLOT_ROWS, 128)),
        in_hbm(multipliers.reshape(3, SLOT_ROWS, 128)),
    )
    far, cells = call(pack_far, [f32(SIDE * CY + IFACE, NZ), slots], [VMEM] * 3)(own, raw_cells, mult)
    far = lax.ppermute(far, ("gx", "gy"), other_x())
    y_pair = lax.ppermute(y_pair, "gy", pair(N_GY))
    y_other = lax.ppermute(y_other, ("gx", "gy"), other_y())
    (dense,) = call(spread_own, [f32(4, block, NZ)], [VMEM] * 2, flops=100000000000)(cells, mult)
    corner, near, own, limit = call(
        pack_second,
        [
            f32(CORNER + SLOT_ROWS, NZ), f32(SIDE * ROWS + IFACE + SLOT_ROWS, NZ), f32(OWN * ROWS, NZ),
            f32(SLOT_ROWS, NZ),
        ],
        [VMEM, VMEM, SMEM, VMEM, VMEM, VMEM],
    )(y_other, y_pair, counts, own, cells, mult)
    corner = lax.ppermute(corner, ("gx", "gy"), other_x())
    near = lax.ppermute(near, "gx", pair(N_GX))
    three, six = f32(3 * PX * ROWS, NZ), f32(6 * PX * ROWS, NZ)
    arrays = [f32(FIELDS * ROWS, NZ), six, six] + [three] * 6
    half = call(
        near_part, arrays + [f32(LABELS * 6, NZ), f32(3 * CY, NZ)], [SMEM, VMEM, VMEM]
    )(stiffness, own, near)
    (ribbon,) = call(spread_before, [f32(4, (CX + 2) * CY, NZ)], [VMEM] * 4)(far, near, dense, half[-1])
    smoothed, jumps, message = call(
        far_part,
        [f32(3 * block, NZ), f32(3, (CX + 1) * CY, NZ), f32(N_GY, 3 * CY // 2, NZ)],
        [VMEM] * (5 + len(half)),
        scratch=[pltpu.VMEM(a.shape, F32) for a in arrays] + [pltpu.VMEM((6 * CY, NZ), F32)],
    )(far, corner, near, limit, ribbon, *half)
    gathered = lax.all_to_all(message, "gy", 0, 0)
    smoothed, updated, coarse = call(
        finish,
        [pltpu.HBM(s, F32) for s in ((3 * block, NZ), (3, SLOT_ROWS, 128), (3, CX // 2 * NZ // 2, NY // 2))],
        [VMEM] * 6,
        out_specs=[HBM] * 3,
        scratch=[
            pltpu.VMEM((3, SLOT_ROWS, 128), F32),
            pltpu.VMEM((3, CX // 2 * NZ // 2, NY // 2), F32),
            pltpu.SemaphoreType.DMA((3,)),
        ],
    )(limit, cells, mult, jumps, smoothed, gathered)
    coarse = jnp.swapaxes(coarse.reshape(3, CX // 2, NZ // 2, NY // 2), 2, 3)
    return (smoothed.reshape(3, CX, CY, NZ), coarse, updated.reshape(3, 1, 1, SLOTS))


def solution(mesh):
    return jax.shard_map(
        body,
        mesh=mesh,
        in_specs=(
            P(None, "gx", "gy", None),
            P(None, "gx", "gy", None),
            P("gx", "gy", None),
            P(),
            P("gx", "gy", None),
            P("gx", "gy"),
            P(None, "gx", "gy", None),
        ),
        out_specs=(P(None, "gx", "gy", None), P(None, "gx", None, None), P(None, "gx", "gy", None)),
        check_vma=False,
    )
```

```python
import jax
import jax.numpy as jnp
from jax import lax
from jax.experimental import pallas as pl
from jax.experimental.pallas import tpu as pltpu
from jax.sharding import PartitionSpec as P

SYMMETRIC_INDEX = ((0, 3, 4), (3, 1, 5), (4, 5, 2))
DAMPING = 0.6
MASS_SHIFT = 1.0
PENALTY = 1.0

CX, CY, NZ, SLOTS = 4, 32, 128, 1024
N_GX, N_GY = 32, 8
NX, NY = CX * N_GX, CY * N_GY
LABELS = 8
HALO = 3
PX = CX + 2 * HALO
PR = PX - 2
ROWS = 40
LAB0 = 3 * PX
RHS0 = LAB0 + PX
FIELDS = RHS0 + 3 * PR
OWN_LAB0 = 3 * CX
OWN_RHS0 = OWN_LAB0 + CX
OWN = OWN_RHS0 + 3 * CX
SIDE = 3 * HALO + HALO + 3 * (HALO - 1)
SLOT_ROWS = SLOTS // 128
CORNER = 112
IFACE = 4 * SLOT_ROWS
VMEM = pl.BlockSpec(memory_space=pltpu.VMEM)
SMEM = pl.BlockSpec(memory_space=pltpu.SMEM)
HBM = pl.BlockSpec(memory_space=pltpu.HBM)
F32 = jnp.float32
BF16 = jnp.bfloat16
PARAMS = pltpu.CompilerParams(vmem_limit_bytes=32 * 1024 * 1024)


def f32(*shape):
    return jax.ShapeDtypeStruct(shape, F32)


def pieces_of(value):
    high = value.astype(BF16)
    rest = value - high.astype(F32)
    middle = rest.astype(BF16)
    low = (rest - middle.astype(F32)).astype(BF16)
    return (high, middle, low)


def odd(axis):
    return lax.rem(lax.axis_index(axis), 2)


def rows_of(j, height):
    return pl.ds(j * height if isinstance(j, int) else pl.multiple_of(j * height, height), height)


def sent_planes():
    place = 0
    for first, depth in [(c * CX, HALO) for c in range(3)] + [(OWN_LAB0, HALO)] + [
        (OWN_RHS0 + c * CX, HALO - 1) for c in range(3)
    ]:
        for k in range(depth):
            yield place, first, k
            place += 1


def halo_planes():
    place = 0
    for first, depth in [(c * PX, HALO) for c in range(3)] + [(LAB0, HALO)] + [
        (RHS0 + c * PR - 1, HALO - 1) for c in range(3)
    ]:
        for k in range(depth):
            yield place, first, k
            place += 1


def slot_number():
    return lax.broadcasted_iota(jnp.int32, (SLOT_ROWS, 128), 0) * 128 + lax.broadcasted_iota(
        jnp.int32, (SLOT_ROWS, 128), 1
    )


def pack_first(
    disp, rhs, labels, cells_in, mult_in,
    y_other, y_pair, own, cells, mult,
    raw_labels, arrived,
):
    flip = odd("gx")
    pairs = []
    for g in range(CX):
        x = g + flip * (CX - 1 - 2 * g)
        pairs.append((labels.at[rows_of(x, CY)], raw_labels.at[rows_of(g, CY)]))
        for c in range(3):
            pairs.append((disp.at[rows_of(c * CX + x, CY)], own.at[rows_of(c * CX + g, CY)]))
            pairs.append((rhs.at[rows_of(c * CX + x, CY)], own.at[rows_of(OWN_RHS0 + c * CX + g, CY)]))
    pairs += [(cells_in, cells), (mult_in, mult)]
    copies = [pltpu.make_async_copy(a, b, arrived.at[i]) for i, (a, b) in enumerate(pairs)]
    for copy in copies:
        copy.start()
    for copy in copies:
        copy.wait()
    own[pl.ds(OWN_LAB0 * CY, CX * CY), :] = raw_labels[...].astype(F32)
    up = odd("gy") == 0
    for k in range(HALO):
        first = own[pl.ds(k, OWN, stride=CY), :]
        last = own[pl.ds(CY - HALO + k, OWN, stride=CY), :]
        y_pair[k] = jnp.where(up, last, first)
        y_other[k] = jnp.where(up, first, last)


def pack_far(own, raw_cells, mult, far, cells):
    flip = odd("gx")
    block_plane = raw_cells[...] // (CY * NZ)
    turned = raw_cells[...] + flip * (CX - 1 - 2 * block_plane) * (CY * NZ)
    cells[...] = turned
    for place, first, k in sent_planes():
        far[rows_of(place, CY), :] = own[rows_of(first + k, CY), :]
    far[pl.ds(SIDE * CY, SLOT_ROWS), :] = turned.astype(F32)
    for c in range(3):
        far[pl.ds(SIDE * CY + (1 + c) * SLOT_ROWS, SLOT_ROWS), :] = mult[c]


def pack_second(y_other, y_pair, count, own, cells, mult, corner, near, wide, limit):
    here = lax.axis_index("gy")
    up = odd("gy") == 0
    low = jnp.where(here > 0, 1.0, 0.0).astype(F32)
    high = jnp.where(here < N_GY - 1, 1.0, 0.0).astype(F32)
    for j in range(OWN):
        wide[pl.ds(j * ROWS, CY), :] = own[rows_of(j, CY), :]
    for k in range(HALO):
        after = jnp.where(up, y_pair[k], y_other[k])
        before = jnp.where(up, y_other[k], y_pair[k])
        wide[pl.ds(CY + k, OWN, stride=ROWS), :] = high * after
        wide[pl.ds(ROWS - HALO + k, OWN, stride=ROWS), :] = low * before
    for k in range(CY + HALO, ROWS - HALO):
        wide[pl.ds(k, OWN, stride=ROWS), :] = jnp.zeros((OWN, NZ), F32)
    for place, first, k in sent_planes():
        for i, y in enumerate((CY, ROWS - HALO)):
            corner[pl.ds(place * 2 * HALO + i * HALO, HALO), :] = wide[pl.ds((first + k) * ROWS + y, HALO), :]
        near[rows_of(place, ROWS), :] = wide[rows_of(first + CX - 1 - k, ROWS), :]
    live = jnp.full((SLOT_ROWS, 128), count[0, 0].astype(F32), F32)
    limit[...] = live
    corner[pl.ds(CORNER, SLOT_ROWS), :] = live
    near[pl.ds(SIDE * ROWS + IFACE, SLOT_ROWS), :] = live
    near[pl.ds(SIDE * ROWS, SLOT_ROWS), :] = cells[...].astype(F32)
    for c in range(3):
        near[pl.ds(SIDE * ROWS + (1 + c) * SLOT_ROWS, SLOT_ROWS), :] = mult[c]


def paired(array, j):
    return jnp.concatenate([array[2 * j : 2 * j + 1], array[2 * j + 1 : 2 * j + 2]], axis=1)


def spread(cells, mult, first, columns):
    column = cells // NZ - first
    depth = cells % NZ
    total = jnp.zeros((11 * columns, NZ), F32)
    parts = [piece for c in range(3) for piece in pieces_of(mult[c])]
    parts += pieces_of((slot_number() + 1).astype(F32))[:2]
    for j in range(SLOT_ROWS // 2):
        at_column = lax.broadcasted_iota(jnp.int32, (columns, 256), 0) == paired(column, j)
        at_depth = lax.broadcasted_iota(jnp.int32, (NZ, 256), 0) == paired(depth, j)
        left = [jnp.where(at_column, paired(piece.astype(F32), j), 0.0).astype(BF16) for piece in parts]
        total = total + lax.dot_general(
            jnp.concatenate(left, axis=0),
            jnp.where(at_depth, 1.0, 0.0).astype(BF16),
            (((1,), (1,)), ((), ())),
            preferred_element_type=F32,
        )
    part = [total[i * columns : (i + 1) * columns] for i in range(11)]
    return [part[3 * c] + part[3 * c + 1] + part[3 * c + 2] for c in range(3)] + [part[9] + part[10]]


def spread_own(cells, mult, dense, at_depth):
    depth = cells[...] % NZ
    for j in range(SLOT_ROWS // 2):
        hit = lax.broadcasted_iota(jnp.int32, (NZ, 256), 0) == paired(depth, j)
        at_depth[:, pl.ds(256 * j, 256)] = jnp.where(hit, 1.0, 0.0).astype(BF16)
    values = spread(cells[...], [mult[c] for c in range(3)], 0, CX * CY)
    for i in range(4):
        dense[i] = values[i]


def is_inside():
    here = lax.axis_index("gx")
    return jnp.where((here > 0) & (here < N_GX - 1), 1.0, 0.0).astype(F32)


def spread_before(far, near, dense, last, ribbon):
    flip = odd("gx")

    def at(i):
        a = far[pl.ds(SIDE * CY + i * SLOT_ROWS, SLOT_ROWS), :]
        b = near[pl.ds(SIDE * ROWS + i * SLOT_ROWS, SLOT_ROWS), :]
        return jnp.where(flip == 1, b, a)

    values = spread(at(0).astype(jnp.int32), [at(1 + c) for c in range(3)], flip * (CX - 1) * CY, CY)
    values[3] = values[3] * jnp.where(flip == 1, 1.0, is_inside())
    for i in range(4):
        ribbon[i, pl.ds(0, CY), :] = values[i]
        ribbon[i, pl.ds(CY, CX * CY), :] = dense[i]
        ribbon[i, pl.ds((CX + 1) * CY, CY), :] = values[i]


def times(k, v):
    return [
        k[SYMMETRIC_INDEX[c][0]] * v[0] + k[SYMMETRIC_INDEX[c][1]] * v[1] + k[SYMMETRIC_INDEX[c][2]] * v[2]
        for c in range(3)
    ]


class Split:
    def __init__(self, at, low, high):
        self.at, self.low, self.high = at, low, high

    def of(self, c, p, count=PX, base=0):
        ref = self.low if p < self.at else self.high
        return ref, rows_of(base + c * count + p, ROWS)


class Stencil:
    def __init__(self, entry, fields, coeff, total, scale, flux):
        self.entry, self.fields, self.coeff, self.total, self.scale, self.flux = (
            entry, fields, coeff, total, scale, flux
        )
        lane = lax.broadcasted_iota(jnp.int32, (1, NZ), 1)
        self.not_first = jnp.where(lane == 0, 0.0, 0.5)
        self.not_last = jnp.where(lane == NZ - 1, 0.0, 0.5)
        self.ends = jnp.where((lane == 0) | (lane == NZ - 1), 16.0, 0.0)
        row = lax.broadcasted_iota(jnp.int32, (ROWS, NZ), 0)
        y = lax.axis_index("gy") * CY + jnp.where(row < CY + HALO, row, row - ROWS)
        self.row_inside = (y >= 0) & (y < NY) & ((row < CY + HALO) | (row >= ROWS - HALO))

    def get(self, split, c, p):
        ref, at = split.of(c, p)
        return ref[at, :]

    def put(self, split, c, p, value):
        ref, at = split.of(c, p)
        ref[at, :] = value

    def label(self, p):
        ref, at = self.fields.of(0, p, base=LAB0)
        return ref[at, :]

    def right_side(self, c, p):
        ref, at = self.fields.of(c, p, count=PR, base=RHS0 - 1)
        return ref[at, :]

    def summed(self, split, c, p, edge=None):
        f = self.get(split, c, p)
        f = (f + f) + (self.get(split, c, p - 1) + self.get(split, c, p + 1))
        f = (f + f) + (pltpu.roll(f, 1, 0) + pltpu.roll(f, ROWS - 1, 0))
        f = f + (pltpu.roll(f, 1, 1) * self.not_first + pltpu.roll(f, NZ - 1, 1) * self.not_last)
        if edge is not None:
            f = f + self.ends * (0.5 * edge)
        return f

    def coefficients(self, planes):
        for p in planes:
            label = self.label(p)
            k = [jnp.broadcast_to(self.entry(0, e), label.shape) for e in range(6)]
            for m in range(1, LABELS):
                at = label == float(m)
                k = [jnp.where(at, self.entry(m, e), k[e]) for e in range(6)]
            for e in range(6):
                self.put(self.coeff, e, p, k[e])
            self.push(self.flux, p, [self.get(self.fields, c, p) for c in range(3)])

    def weights(self, planes):
        for p in planes:
            for e in range(6):
                k = self.get(self.coeff, e, p)
                around = self.summed(self.coeff, e, p, self.entry(0, e))
                self.put(self.total, e, p, 32.0 * k + around)
                if e < 3:
                    self.put(self.scale, e, p, DAMPING / (MASS_SHIFT + 6.0 * k + 0.25 * around))

    def push(self, flux, p, v):
        pushed = times([self.get(self.coeff, e, p) for e in range(6)], v)
        for c in range(3):
            self.put(flux, c, p, pushed[c])

    def image(self, p, v_split, flux):
        v = [self.get(v_split, c, p) for c in range(3)]
        k = [self.get(self.coeff, e, p) for e in range(6)]
        m = [self.get(self.total, e, p) for e in range(6)]
        around = [self.summed(v_split, c, p) for c in range(3)]
        pushed = [self.summed(flux, c, p) for c in range(3)]
        mine, theirs = times(m, v), times(k, around)
        return v, [MASS_SHIFT * v[c] + 0.25 * (mine[c] - theirs[c] - pushed[c]) for c in range(3)]

    def sweep(self, planes, v_split, flux, to, to_flux, inside=None):
        for p in planes:
            keep = self.row_inside if p >= HALO else self.row_inside & (inside > 0.5)
            v, a = self.image(p, v_split, flux)
            new = []
            for c in range(3):
                value = v[c] + (self.right_side(c, p) - a[c]) * self.get(self.scale, c, p)
                value = jnp.where(keep, value, 0.0)
                self.put(to, c, p, value)
                new.append(value)
            self.push(to_flux, p, new)

    def remainder(self, p, v_split, flux):
        a = self.image(p, v_split, flux)[1]
        return [(self.right_side(c, p) - a[c])[:CY] for c in range(3)]


def near_part(
    stiffness, own, near,
    fields, coeff, total, scale, flux, first, flux_first, second, flux_second, table, last,
):
    for c in range(3):
        for g in range(CX):
            fields[rows_of(c * PX + HALO + g, ROWS), :] = own[rows_of(c * CX + g, ROWS), :]
            fields[rows_of(RHS0 - 1 + c * PR + HALO + g, ROWS), :] = own[rows_of(OWN_RHS0 + c * CX + g, ROWS), :]
    for g in range(CX):
        fields[rows_of(LAB0 + HALO + g, ROWS), :] = own[rows_of(OWN_LAB0 + g, ROWS), :]
    for place, at, k in halo_planes():
        fields[rows_of(at + HALO + CX + k, ROWS), :] = near[rows_of(place, ROWS), :]
    for m in range(LABELS):
        for e in range(6):
            table[pl.ds(m * 6 + e, 1), :] = jnp.full((1, NZ), stiffness[m, e], F32)

    def whole(ref):
        return Split(0, None, ref)

    grid = Stencil(
        lambda m, e: stiffness[m, e], whole(fields), whole(coeff), whole(total), whole(scale), whole(flux)
    )
    grid.coefficients(range(HALO, PX))
    grid.weights(range(HALO + 1, PX - 1))
    grid.sweep(range(HALO + 1, PX - 1), whole(fields), whole(flux), whole(first), whole(flux_first))
    grid.sweep(range(HALO + 2, PX - 2), whole(first), whole(flux_first), whole(second), whole(flux_second))
    remainder = grid.remainder(HALO + 3, whole(second), whole(flux_second))
    for c in range(3):
        last[rows_of(c, CY), :] = remainder[c]


def far_part(
    far, corner, near, limit, ribbon, cells, mult, at_depth,
    near_fields, near_coeff, near_total, near_scale, near_flux,
    near_first, near_flux_first, near_second, near_flux_second, table, last,
    message, second, updated,
    fields, coeff, total, scale, flux, first, flux_first, flux_second, coarse,
):
    inside = is_inside()
    flip = odd("gx")
    sign = jnp.where(flip == 1, -1.0, 1.0).astype(F32)
    for y in range(CY + HALO, ROWS - HALO):
        fields[pl.ds(y, FIELDS, stride=ROWS), :] = jnp.zeros((FIELDS, NZ), F32)
    for place, at, k in halo_planes():
        plane = (at + HALO - 1 - k) * ROWS
        fields[pl.ds(plane, CY), :] = inside * far[rows_of(place, CY), :]
        for i, y in enumerate((CY, ROWS - HALO)):
            fields[pl.ds(plane + y, HALO), :] = inside * corner[pl.ds(place * 2 * HALO + i * HALO, HALO), :]
    v0, flux0 = Split(HALO, fields, near_fields), Split(HALO, flux, near_flux)
    v1, flux1 = Split(HALO + 1, first, near_first), Split(HALO + 1, flux_first, near_flux_first)
    v2, flux2 = Split(HALO + 2, second, near_second), Split(HALO + 2, flux_second, near_flux_second)
    grid = Stencil(
        lambda m, e: table[pl.ds(m * 6 + e, 1), :],
        v0,
        Split(HALO, coeff, near_coeff),
        Split(HALO + 1, total, near_total),
        Split(HALO + 1, scale, near_scale),
        flux0,
    )
    grid.coefficients(range(HALO))
    grid.weights(range(1, HALO + 1))
    grid.sweep(range(1, HALO + 1), v0, flux0, v1, flux1, inside)
    grid.sweep(range(2, HALO + 2), v1, flux1, v2, flux2, inside)
    used = slot_number().astype(F32) < limit[...] - 0.5
    column = cells[...] // NZ
    block = CX * CY
    left = []
    for c in range(3):
        v = [grid.get(v2, c, HALO - 1 + i)[:CY] for i in range(CX + 2)]
        jumps = [v[1 + g] - jnp.where(flip == 1, v[g], v[2 + g]) for g in range(CX)]
        left.append(jnp.concatenate(pieces_of(jnp.concatenate(jumps, axis=0)), axis=1))
    left = jnp.concatenate(left, axis=0)
    for j in range(SLOT_ROWS // 2):
        right = at_depth[:, pl.ds(256 * j, 256)]
        picked = jnp.dot(left, jnp.concatenate([right] * 3, axis=0), preferred_element_type=F32)
        at_column = lax.broadcasted_iota(jnp.int32, (block, 256), 0) == paired(column, j)
        for c in range(3):
            jump = jnp.sum(
                jnp.where(at_column, picked[c * block : (c + 1) * block], 0.0), axis=0, keepdims=True
            )
            for i in range(2):
                at = 2 * j + i
                old = mult[c, at : at + 1, :]
                new = old + PENALTY * jump[:, i * 128 : (i + 1) * 128]
                updated[c, at : at + 1, :] = jnp.where(used[at : at + 1], new, old)
    remainders = [grid.remainder(HALO + g, v2, flux2) for g in range(CX - 1)]
    remainders.append([last[rows_of(c, CY), :] for c in range(3)])

    mine = limit[:1]
    theirs = jnp.where(flip == 1, near[pl.ds(SIDE * ROWS + IFACE, 1), :], corner[pl.ds(CORNER, 1), :])
    live = []
    for i in range(CX + 1):
        if i == 0:
            top = jnp.where(flip == 1, mine, theirs)
        elif i == CX:
            top = jnp.where(flip == 1, theirs, mine)
        else:
            top = mine
        number = ribbon[3, rows_of(i + flip, CY), :]
        live.append((number > 0.5) & (number < top + 0.5))
    for c in range(3):
        planes = [grid.get(v2, c, HALO - 1 + i)[:CY] for i in range(CX + 2)]
        pushed = []
        for i in range(CX + 1):
            jump = sign * (planes[i] - planes[i + 1])
            at = rows_of(i + flip, CY)
            pushed.append(jnp.where(live[i], ribbon[c, at, :] + PENALTY * jump, 0.0))
        parts = [remainders[g][c] - sign * (pushed[g + 1] - pushed[g]) for g in range(CX)]
        for half in range(2):
            coarse[rows_of(half * 3 + c, CY), :] = parts[2 * half] + parts[2 * half + 1]

    pairs = []
    for half in range(2):
        at = 3 * half * CY
        rows = coarse[pl.ds(at, 3 * CY // 2, stride=2), :] + coarse[pl.ds(at + 1, 3 * CY // 2, stride=2), :]
        pairs.append(rows)
    low_x = jnp.where(flip == 1, pairs[1], pairs[0])
    high_x = jnp.where(flip == 1, pairs[0], pairs[1])
    even_lane = lax.rem(lax.broadcasted_iota(jnp.int32, (1, NZ), 1), 2) == 0
    out = jnp.where(even_lane, low_x + pltpu.roll(low_x, NZ - 1, 1), high_x + pltpu.roll(high_x, 1, 1))
    for s in range(N_GY):
        message[s] = out


def finish(
    updated, low, high, gathered,
    smoothed_out, updated_out, coarse_out,
    coarse, turned, done,
):
    flip = odd("gx")
    split = Split(HALO + 2, low, high)
    copies = [pltpu.make_async_copy(updated, updated_out, done.at[0])]
    for c in range(3):
        for g in range(CX):
            x = g + flip * (CX - 1 - 2 * g)
            ref, at = split.of(c, HALO + g)
            copies.append(
                pltpu.make_async_copy(
                    ref.at[pl.ds(at.start, CY), :], smoothed_out.at[rows_of(c * CX + x, CY), :],
                    done.at[1 + c * CX + g],
                )
            )
    for copy in copies:
        copy.start()
    for c in range(3):
        parts = [gathered[s, pl.ds(c * CY // 2, CY // 2), :] for s in range(N_GY)]
        turned[c] = jnp.transpose(jnp.concatenate(parts, axis=0))
        for x in range(CX // 2):
            coarse[c, pl.ds(x * NZ // 2, NZ // 2), :] = turned[c, pl.ds(x, NZ // 2, stride=2), :]
        copies.append(pltpu.make_async_copy(coarse.at[c], coarse_out.at[c], done.at[1 + 3 * CX + c]))
        copies[-1].start()
    for copy in copies:
        copy.wait()


def in_hbm(array):
    return pltpu.with_memory_space_constraint(array, pltpu.HBM)


def call(kernel, outs, ins, out_specs=None, scratch=(), flops=1000):
    return pl.pallas_call(
        kernel,
        out_shape=outs,
        in_specs=ins,
        out_specs=out_specs or [VMEM] * len(outs),
        scratch_shapes=list(scratch),
        compiler_params=PARAMS,
        cost_estimate=pl.CostEstimate(flops=flops, bytes_accessed=1000, transcendentals=0),
    )


def pair(n):
    return [(i, i ^ 1) for i in range(n)]


def other_x():
    out = []
    for i in range(N_GX):
        for j in range(N_GY):
            partner = (i, j ^ 1) if i in (0, N_GX - 1) else (((i + 1) ^ 1) - 1, j)
            out.append((i * N_GY + j, partner[0] * N_GY + partner[1]))
    return out


def other_y():
    out = []
    for i in range(N_GX):
        for j in range(N_GY):
            partner = (i ^ 1, j) if j in (0, N_GY - 1) else (i, ((j + 1) ^ 1) - 1)
            out.append((i * N_GY + j, partner[0] * N_GY + partner[1]))
    return out


def body(displacement, rhs, labels, stiffness, rows, counts, multipliers):
    block = CX * CY
    copies = 2 + 7 * CX
    slots = jax.ShapeDtypeStruct((SLOT_ROWS, 128), jnp.int32)
    y_other, y_pair, own, raw_cells, mult = call(
        pack_first,
        [f32(HALO, OWN, NZ), f32(HALO, OWN, NZ), f32(OWN * CY, NZ), slots, f32(3, SLOT_ROWS, 128)],
        [HBM] * 5,
        scratch=[pltpu.VMEM((block, NZ), jnp.int32), pltpu.SemaphoreType.DMA((copies,))],
    )(
        in_hbm(displacement.reshape(3 * block, NZ)),
        in_hbm(rhs.reshape(3 * block, NZ)),
        in_hbm(labels.reshape(block, NZ)),
        in_hbm(rows.reshape(SLOT_ROWS, 128)),
        in_hbm(multipliers.reshape(3, SLOT_ROWS, 128)),
    )
    far, cells = call(pack_far, [f32(SIDE * CY + IFACE, NZ), slots], [VMEM] * 3)(own, raw_cells, mult)
    far = lax.ppermute(far, ("gx", "gy"), other_x())
    y_pair = lax.ppermute(y_pair, "gy", pair(N_GY))
    y_other = lax.ppermute(y_other, ("gx", "gy"), other_y())
    dense, at_depth = call(
        spread_own, [f32(4, block, NZ), jax.ShapeDtypeStruct((NZ, 8 * 128), BF16)], [VMEM] * 2, flops=10**11
    )(cells, mult)
    corner, near, own, limit = call(
        pack_second,
        [
            f32(CORNER + SLOT_ROWS, NZ), f32(SIDE * ROWS + IFACE + SLOT_ROWS, NZ), f32(OWN * ROWS, NZ),
            f32(SLOT_ROWS, NZ),
        ],
        [VMEM, VMEM, SMEM, VMEM, VMEM, VMEM],
    )(y_other, y_pair, counts, own, cells, mult)
    corner = lax.ppermute(corner, ("gx", "gy"), other_x())
    near = lax.ppermute(near, "gx", pair(N_GX))
    three, six = f32(3 * PX * ROWS, NZ), f32(6 * PX * ROWS, NZ)
    arrays = [f32(FIELDS * ROWS, NZ), six, six] + [three] * 6
    half = call(
        near_part, arrays + [f32(LABELS * 6, NZ), f32(3 * CY, NZ)], [SMEM, VMEM, VMEM]
    )(stiffness, own, near)
    (ribbon,) = call(spread_before, [f32(4, (CX + 2) * CY, NZ)], [VMEM] * 4)(far, near, dense, half[-1])
    message, low, updated = call(
        far_part,
        [f32(N_GY, 3 * CY // 2, NZ), three, f32(3, SLOT_ROWS, 128)],
        [VMEM] * (8 + len(half)),
        scratch=[pltpu.VMEM(a.shape, F32) for a in arrays[:-1]] + [pltpu.VMEM((6 * CY, NZ), F32)],
    )(far, corner, near, limit, ribbon, cells, mult, at_depth, *half)
    gathered = lax.all_to_all(message, "gy", 0, 0)
    smoothed, updated, coarse = call(
        finish,
        [pltpu.HBM(s, F32) for s in ((3 * block, NZ), (3, SLOT_ROWS, 128), (3, CX // 2 * NZ // 2, NY // 2))],
        [VMEM] * 4,
        out_specs=[HBM] * 3,
        scratch=[
            pltpu.VMEM((3, CX // 2 * NZ // 2, NY // 2), F32),
            pltpu.VMEM((3, NZ, NY // 2), F32),
            pltpu.SemaphoreType.DMA((4 + 3 * CX,)),
        ],
    )(updated, low, half[7], gathered)
    coarse = jnp.swapaxes(coarse.reshape(3, CX // 2, NZ // 2, NY // 2), 2, 3)
    return (smoothed.reshape(3, CX, CY, NZ), coarse, updated.reshape(3, 1, 1, SLOTS))


def solution(mesh):
    return jax.shard_map(
        body,
        mesh=mesh,
        in_specs=(
            P(None, "gx", "gy", None),
            P(None, "gx", "gy", None),
            P("gx", "gy", None),
            P(),
            P("gx", "gy", None),
            P("gx", "gy"),
            P(None, "gx", "gy", None),
        ),
        out_specs=(P(None, "gx", "gy", None), P(None, "gx", None, None), P(None, "gx", "gy", None)),
        check_vma=False,
    )
```

```python
import jax
import jax.numpy as jnp
from jax import lax
from jax.experimental import pallas as pl
from jax.experimental.pallas import tpu as pltpu
from jax.sharding import PartitionSpec as P

SYMMETRIC_INDEX = ((0, 3, 4), (3, 1, 5), (4, 5, 2))
DAMPING = 0.6
MASS_SHIFT = 1.0
PENALTY = 1.0

CX, CY, NZ, SLOTS = 4, 32, 128, 1024
N_GX, N_GY = 32, 8
NX, NY = CX * N_GX, CY * N_GY
LABELS = 8
HALO = 3
PX = CX + 2 * HALO
PR = PX - 2
ROWS = 40
LAB0 = 3 * PX
RHS0 = LAB0 + PX
FIELDS = RHS0 + 3 * PR
OWN_LAB0 = 3 * CX
OWN_RHS0 = OWN_LAB0 + CX
OWN = OWN_RHS0 + 3 * CX
SIDE = 3 * HALO + HALO + 3 * (HALO - 1)
SLOT_ROWS = SLOTS // 128
IFACE = 4 * SLOT_ROWS
CORNER = 2 * (4 * HALO * HALO + 3 * (HALO - 1) ** 2)
VMEM = pl.BlockSpec(memory_space=pltpu.VMEM)
SMEM = pl.BlockSpec(memory_space=pltpu.SMEM)
HBM = pl.BlockSpec(memory_space=pltpu.HBM)
F32 = jnp.float32
BF16 = jnp.bfloat16
PARAMS = pltpu.CompilerParams(vmem_limit_bytes=32 * 1024 * 1024)


def f32(*shape):
    return jax.ShapeDtypeStruct(shape, F32)


def pieces_of(value):
    high = value.astype(BF16)
    rest = value - high.astype(F32)
    middle = rest.astype(BF16)
    low = (rest - middle.astype(F32)).astype(BF16)
    return (high, middle, low)


def odd(axis):
    return lax.rem(lax.axis_index(axis), 2)


def rows_of(j, height):
    return pl.ds(j * height if isinstance(j, int) else pl.multiple_of(j * height, height), height)


def corner_rows():
    at = 0
    for place in range(SIDE):
        depth = HALO if place < 4 * HALO else HALO - 1
        yield place, at, depth
        at += 2 * depth


def sent_planes():
    place = 0
    for first, depth in [(c * CX, HALO) for c in range(3)] + [(OWN_LAB0, HALO)] + [
        (OWN_RHS0 + c * CX, HALO - 1) for c in range(3)
    ]:
        for k in range(depth):
            yield place, first, k
            place += 1


def halo_planes():
    place = 0
    for first, depth in [(c * PX, HALO) for c in range(3)] + [(LAB0, HALO)] + [
        (RHS0 + c * PR - 1, HALO - 1) for c in range(3)
    ]:
        for k in range(depth):
            yield place, first, k
            place += 1


def slot_number():
    return lax.broadcasted_iota(jnp.int32, (SLOT_ROWS, 128), 0) * 128 + lax.broadcasted_iota(
        jnp.int32, (SLOT_ROWS, 128), 1
    )


def pack_first(
    disp, rhs, labels, cells_in, mult_in,
    y_other, own, cells, mult,
    raw_labels, arrived,
):
    flip = odd("gx")
    pairs = []
    for g in range(CX):
        x = g + flip * (CX - 1 - 2 * g)
        pairs.append((labels.at[rows_of(x, CY)], raw_labels.at[rows_of(g, CY)]))
        for c in range(3):
            pairs.append((disp.at[rows_of(c * CX + x, CY)], own.at[rows_of(c * CX + g, CY)]))
            pairs.append((rhs.at[rows_of(c * CX + x, CY)], own.at[rows_of(OWN_RHS0 + c * CX + g, CY)]))
    pairs += [(cells_in, cells), (mult_in, mult)]
    copies = [pltpu.make_async_copy(a, b, arrived.at[i]) for i, (a, b) in enumerate(pairs)]
    for copy in copies:
        copy.start()
    for copy in copies:
        copy.wait()
    own[pl.ds(OWN_LAB0 * CY, CX * CY), :] = raw_labels[...].astype(F32)
    up = odd("gy") == 0
    for k in range(HALO):
        first = own[pl.ds(k, OWN, stride=CY), :]
        last = own[pl.ds(CY - HALO + k, OWN, stride=CY), :]
        y_other[k] = jnp.where(up, first, last)


def pack_sides(own, raw_cells, mult, far, near, cells):
    flip = odd("gx")
    block_plane = raw_cells[...] // (CY * NZ)
    turned = raw_cells[...] + flip * (CX - 1 - 2 * block_plane) * (CY * NZ)
    cells[...] = turned
    for place, first, k in sent_planes():
        far[rows_of(place, CY), :] = own[rows_of(first + k, CY), :]
        near[rows_of(place, CY), :] = own[rows_of(first + CX - 1 - k, CY), :]
    for side in (far, near):
        side[pl.ds(SIDE * CY, SLOT_ROWS), :] = turned.astype(F32)
        for c in range(3):
            side[pl.ds(SIDE * CY + (1 + c) * SLOT_ROWS, SLOT_ROWS), :] = mult[c]


def pack_pair(own, near, y_pair):
    up = odd("gy") == 0
    for k in range(HALO):
        first = own[pl.ds(k, OWN, stride=CY), :]
        last = own[pl.ds(CY - HALO + k, OWN, stride=CY), :]
        y_pair[k] = jnp.where(up, last, first)


def reach():
    here = lax.axis_index("gy")
    return (
        jnp.where(here > 0, 1.0, 0.0).astype(F32),
        jnp.where(here < N_GY - 1, 1.0, 0.0).astype(F32),
    )


def pack_wide(own, wide):
    for j in range(OWN):
        wide[pl.ds(j * ROWS, CY), :] = own[rows_of(j, CY), :]
        wide[pl.ds(j * ROWS + CY, ROWS - CY), :] = jnp.zeros((ROWS - CY, NZ), F32)


def pack_second(y_other, y_pair, count, inner, corner_far, corner_near, wide, limit):
    low, high = reach()
    up = odd("gy") == 0
    wide[...] = inner[...]
    for k in range(HALO):
        wide[pl.ds(CY + k, OWN, stride=ROWS), :] = high * jnp.where(up, y_pair[k], y_other[k])
        wide[pl.ds(ROWS - HALO + k, OWN, stride=ROWS), :] = low * jnp.where(up, y_other[k], y_pair[k])
    live = jnp.full((SLOT_ROWS, 128), count[0, 0].astype(F32), F32)
    limit[...] = live
    planes = list(sent_planes())
    for corner, turn in ((corner_far, False), (corner_near, True)):
        for place, at, depth in corner_rows():
            first, k = planes[place][1:]
            base = (first + (CX - 1 - k if turn else k)) * ROWS
            corner[pl.ds(at, depth), :] = wide[pl.ds(base + CY, depth), :]
            corner[pl.ds(at + depth, depth), :] = wide[pl.ds(base + ROWS - depth, depth), :]
        corner[pl.ds(CORNER, SLOT_ROWS), :] = live


def paired(array, j):
    return jnp.concatenate([array[2 * j : 2 * j + 1], array[2 * j + 1 : 2 * j + 2]], axis=1)


def spread(cells, mult, first, columns):
    column = cells // NZ - first
    depth = cells % NZ
    total = jnp.zeros((11 * columns, NZ), F32)
    parts = [piece for c in range(3) for piece in pieces_of(mult[c])]
    parts += pieces_of((slot_number() + 1).astype(F32))[:2]
    for j in range(SLOT_ROWS // 2):
        at_column = lax.broadcasted_iota(jnp.int32, (columns, 256), 0) == paired(column, j)
        at_depth = lax.broadcasted_iota(jnp.int32, (NZ, 256), 0) == paired(depth, j)
        left = [jnp.where(at_column, paired(piece.astype(F32), j), 0.0).astype(BF16) for piece in parts]
        total = total + lax.dot_general(
            jnp.concatenate(left, axis=0),
            jnp.where(at_depth, 1.0, 0.0).astype(BF16),
            (((1,), (1,)), ((), ())),
            preferred_element_type=F32,
        )
    part = [total[i * columns : (i + 1) * columns] for i in range(11)]
    return [part[3 * c] + part[3 * c + 1] + part[3 * c + 2] for c in range(3)] + [part[9] + part[10]]


def spread_own(cells, mult, dense, at_depth):
    depth = cells[...] % NZ
    for j in range(SLOT_ROWS // 2):
        hit = lax.broadcasted_iota(jnp.int32, (NZ, 256), 0) == paired(depth, j)
        at_depth[:, pl.ds(256 * j, 256)] = jnp.where(hit, 1.0, 0.0).astype(BF16)
    values = spread(cells[...], [mult[c] for c in range(3)], 0, CX * CY)
    for i in range(4):
        dense[i] = values[i]


def is_inside():
    here = lax.axis_index("gx")
    return jnp.where((here > 0) & (here < N_GX - 1), 1.0, 0.0).astype(F32)


def spread_before(far, near, dense, last, ribbon):
    flip = odd("gx")

    def at(i):
        a = far[pl.ds(SIDE * CY + i * SLOT_ROWS, SLOT_ROWS), :]
        b = near[pl.ds(SIDE * CY + i * SLOT_ROWS, SLOT_ROWS), :]
        return jnp.where(flip == 1, b, a)

    values = spread(at(0).astype(jnp.int32), [at(1 + c) for c in range(3)], flip * (CX - 1) * CY, CY)
    values[3] = values[3] * jnp.where(flip == 1, 1.0, is_inside())
    for i in range(4):
        ribbon[i, pl.ds(0, CY), :] = values[i]
        ribbon[i, pl.ds(CY, CX * CY), :] = dense[i]
        ribbon[i, pl.ds((CX + 1) * CY, CY), :] = values[i]


def times(k, v):
    return [
        k[SYMMETRIC_INDEX[c][0]] * v[0] + k[SYMMETRIC_INDEX[c][1]] * v[1] + k[SYMMETRIC_INDEX[c][2]] * v[2]
        for c in range(3)
    ]


class Split:
    def __init__(self, at, low, high):
        self.at, self.low, self.high = at, low, high

    def of(self, c, p, count=PX, base=0):
        ref = self.low if p < self.at else self.high
        return ref, rows_of(base + c * count + p, ROWS)


class Stencil:
    def __init__(self, entry, fields, coeff, total, scale, flux):
        self.entry, self.fields, self.coeff, self.total, self.scale, self.flux = (
            entry, fields, coeff, total, scale, flux
        )
        lane = lax.broadcasted_iota(jnp.int32, (1, NZ), 1)
        self.not_first = jnp.where(lane == 0, 0.0, 0.5)
        self.not_last = jnp.where(lane == NZ - 1, 0.0, 0.5)
        self.ends = jnp.where((lane == 0) | (lane == NZ - 1), 16.0, 0.0)
        row = lax.broadcasted_iota(jnp.int32, (ROWS, NZ), 0)
        y = lax.axis_index("gy") * CY + jnp.where(row < CY + HALO, row, row - ROWS)
        self.row_inside = (y >= 0) & (y < NY) & ((row < CY + HALO) | (row >= ROWS - HALO))

    def get(self, split, c, p):
        ref, at = split.of(c, p)
        return ref[at, :]

    def put(self, split, c, p, value):
        ref, at = split.of(c, p)
        ref[at, :] = value

    def label(self, p):
        ref, at = self.fields.of(0, p, base=LAB0)
        return ref[at, :]

    def right_side(self, c, p):
        ref, at = self.fields.of(c, p, count=PR, base=RHS0 - 1)
        return ref[at, :]

    def summed(self, split, c, p, edge=None):
        f = self.get(split, c, p)
        f = (f + f) + (self.get(split, c, p - 1) + self.get(split, c, p + 1))
        f = (f + f) + (pltpu.roll(f, 1, 0) + pltpu.roll(f, ROWS - 1, 0))
        f = f + (pltpu.roll(f, 1, 1) * self.not_first + pltpu.roll(f, NZ - 1, 1) * self.not_last)
        if edge is not None:
            f = f + self.ends * (0.5 * edge)
        return f

    def coefficients(self, planes):
        for p in planes:
            label = self.label(p)
            k = [jnp.broadcast_to(self.entry(0, e), label.shape) for e in range(6)]
            for m in range(1, LABELS):
                at = label == float(m)
                k = [jnp.where(at, self.entry(m, e), k[e]) for e in range(6)]
            for e in range(6):
                self.put(self.coeff, e, p, k[e])
            self.push(self.flux, p, [self.get(self.fields, c, p) for c in range(3)])

    def weights(self, planes):
        for p in planes:
            for e in range(6):
                k = self.get(self.coeff, e, p)
                around = self.summed(self.coeff, e, p, self.entry(0, e))
                self.put(self.total, e, p, 32.0 * k + around)
                if e < 3:
                    self.put(self.scale, e, p, DAMPING / (MASS_SHIFT + 6.0 * k + 0.25 * around))

    def push(self, flux, p, v):
        pushed = times([self.get(self.coeff, e, p) for e in range(6)], v)
        for c in range(3):
            self.put(flux, c, p, pushed[c])

    def image(self, p, v_split, flux):
        v = [self.get(v_split, c, p) for c in range(3)]
        k = [self.get(self.coeff, e, p) for e in range(6)]
        m = [self.get(self.total, e, p) for e in range(6)]
        around = [self.summed(v_split, c, p) for c in range(3)]
        pushed = [self.summed(flux, c, p) for c in range(3)]
        mine, theirs = times(m, v), times(k, around)
        return v, [MASS_SHIFT * v[c] + 0.25 * (mine[c] - theirs[c] - pushed[c]) for c in range(3)]

    def sweep(self, planes, v_split, flux, to, to_flux, inside=None):
        for p in planes:
            keep = self.row_inside if p >= HALO else self.row_inside & (inside > 0.5)
            v, a = self.image(p, v_split, flux)
            new = []
            for c in range(3):
                value = v[c] + (self.right_side(c, p) - a[c]) * self.get(self.scale, c, p)
                value = jnp.where(keep, value, 0.0)
                self.put(to, c, p, value)
                new.append(value)
            self.push(to_flux, p, new)

    def remainder(self, p, v_split, flux):
        a = self.image(p, v_split, flux)[1]
        return [(self.right_side(c, p) - a[c])[:CY] for c in range(3)]


def fill_halo(fields, side, corner, plane_of, inside):
    tiles = {place: (at, depth) for place, at, depth in corner_rows()}
    for place, base, k in halo_planes():
        plane = (base + plane_of(k)) * ROWS
        at, depth = tiles[place]
        fields[pl.ds(plane, CY), :] = inside * side[rows_of(place, CY), :]
        fields[pl.ds(plane + CY, ROWS - CY), :] = jnp.zeros((ROWS - CY, NZ), F32)
        fields[pl.ds(plane + CY, depth), :] = inside * corner[pl.ds(at, depth), :]
        fields[pl.ds(plane + ROWS - depth, depth), :] = inside * corner[pl.ds(at + depth, depth), :]


def near_part(
    stiffness, own, near, corner_near,
    fields, coeff, total, scale, flux, first, flux_first, second, flux_second, table, last,
):
    for c in range(3):
        for g in range(CX):
            fields[rows_of(c * PX + HALO + g, ROWS), :] = own[rows_of(c * CX + g, ROWS), :]
            fields[rows_of(RHS0 - 1 + c * PR + HALO + g, ROWS), :] = own[rows_of(OWN_RHS0 + c * CX + g, ROWS), :]
    for g in range(CX):
        fields[rows_of(LAB0 + HALO + g, ROWS), :] = own[rows_of(OWN_LAB0 + g, ROWS), :]
    fill_halo(fields, near, corner_near, lambda k: HALO + CX + k, 1.0)
    for m in range(LABELS):
        for e in range(6):
            table[pl.ds(m * 6 + e, 1), :] = jnp.full((1, NZ), stiffness[m, e], F32)

    def whole(ref):
        return Split(0, None, ref)

    grid = Stencil(
        lambda m, e: stiffness[m, e], whole(fields), whole(coeff), whole(total), whole(scale), whole(flux)
    )
    grid.coefficients(range(HALO, PX))
    grid.weights(range(HALO + 1, PX - 1))
    grid.sweep(range(HALO + 1, PX - 1), whole(fields), whole(flux), whole(first), whole(flux_first))
    grid.sweep(range(HALO + 2, PX - 2), whole(first), whole(flux_first), whole(second), whole(flux_second))
    remainder = grid.remainder(HALO + 3, whole(second), whole(flux_second))
    for c in range(3):
        last[rows_of(c, CY), :] = remainder[c]


def far_part(
    far, corner, corner_near, limit, ribbon, cells, mult, at_depth,
    near_fields, near_coeff, near_total, near_scale, near_flux,
    near_first, near_flux_first, near_second, near_flux_second, table, last,
    message, second, updated,
    fields, coeff, total, scale, flux, first, flux_first, flux_second, coarse,
):
    inside = is_inside()
    flip = odd("gx")
    sign = jnp.where(flip == 1, -1.0, 1.0).astype(F32)
    fill_halo(fields, far, corner, lambda k: HALO - 1 - k, inside)
    v0, flux0 = Split(HALO, fields, near_fields), Split(HALO, flux, near_flux)
    v1, flux1 = Split(HALO + 1, first, near_first), Split(HALO + 1, flux_first, near_flux_first)
    v2, flux2 = Split(HALO + 2, second, near_second), Split(HALO + 2, flux_second, near_flux_second)
    grid = Stencil(
        lambda m, e: table[pl.ds(m * 6 + e, 1), :],
        v0,
        Split(HALO, coeff, near_coeff),
        Split(HALO + 1, total, near_total),
        Split(HALO + 1, scale, near_scale),
        flux0,
    )
    grid.coefficients(range(HALO))
    grid.weights(range(1, HALO + 1))
    grid.sweep(range(1, HALO + 1), v0, flux0, v1, flux1, inside)
    grid.sweep(range(2, HALO + 2), v1, flux1, v2, flux2, inside)
    used = slot_number().astype(F32) < limit[...] - 0.5
    column = cells[...] // NZ
    block = CX * CY
    left = []
    for c in range(3):
        v = [grid.get(v2, c, HALO - 1 + i)[:CY] for i in range(CX + 2)]
        jumps = [v[1 + g] - jnp.where(flip == 1, v[g], v[2 + g]) for g in range(CX)]
        left.append(jnp.concatenate(pieces_of(jnp.concatenate(jumps, axis=0)), axis=1))
    left = jnp.concatenate(left, axis=0)
    for j in range(SLOT_ROWS // 2):
        right = at_depth[:, pl.ds(256 * j, 256)]
        picked = jnp.dot(left, jnp.concatenate([right] * 3, axis=0), preferred_element_type=F32)
        at_column = lax.broadcasted_iota(jnp.int32, (block, 256), 0) == paired(column, j)
        for c in range(3):
            jump = jnp.sum(
                jnp.where(at_column, picked[c * block : (c + 1) * block], 0.0), axis=0, keepdims=True
            )
            for i in range(2):
                at = 2 * j + i
                old = mult[c, at : at + 1, :]
                new = old + PENALTY * jump[:, i * 128 : (i + 1) * 128]
                updated[c, at : at + 1, :] = jnp.where(used[at : at + 1], new, old)
    remainders = [grid.remainder(HALO + g, v2, flux2) for g in range(CX - 1)]
    remainders.append([last[rows_of(c, CY), :] for c in range(3)])

    mine = limit[:1]
    theirs = jnp.where(flip == 1, corner_near[pl.ds(CORNER, 1), :], corner[pl.ds(CORNER, 1), :])
    live = []
    for i in range(CX + 1):
        if i == 0:
            top = jnp.where(flip == 1, mine, theirs)
        elif i == CX:
            top = jnp.where(flip == 1, theirs, mine)
        else:
            top = mine
        number = ribbon[3, rows_of(i + flip, CY), :]
        live.append((number > 0.5) & (number < top + 0.5))
    for c in range(3):
        planes = [grid.get(v2, c, HALO - 1 + i)[:CY] for i in range(CX + 2)]
        pushed = []
        for i in range(CX + 1):
            jump = sign * (planes[i] - planes[i + 1])
            at = rows_of(i + flip, CY)
            pushed.append(jnp.where(live[i], ribbon[c, at, :] + PENALTY * jump, 0.0))
        parts = [remainders[g][c] - sign * (pushed[g + 1] - pushed[g]) for g in range(CX)]
        for half in range(2):
            coarse[rows_of(half * 3 + c, CY), :] = parts[2 * half] + parts[2 * half + 1]

    pairs = []
    for half in range(2):
        at = 3 * half * CY
        rows = coarse[pl.ds(at, 3 * CY // 2, stride=2), :] + coarse[pl.ds(at + 1, 3 * CY // 2, stride=2), :]
        pairs.append(rows)
    low_x = jnp.where(flip == 1, pairs[1], pairs[0])
    high_x = jnp.where(flip == 1, pairs[0], pairs[1])
    even_lane = lax.rem(lax.broadcasted_iota(jnp.int32, (1, NZ), 1), 2) == 0
    out = jnp.where(even_lane, low_x + pltpu.roll(low_x, NZ - 1, 1), high_x + pltpu.roll(high_x, 1, 1))
    for s in range(N_GY):
        message[s] = out


def finish(
    updated, low, high, gathered,
    smoothed_out, updated_out, coarse_out,
    coarse, turned, done,
):
    flip = odd("gx")
    split = Split(HALO + 2, low, high)
    copies = [pltpu.make_async_copy(updated, updated_out, done.at[0])]
    for c in range(3):
        for g in range(CX):
            x = g + flip * (CX - 1 - 2 * g)
            ref, at = split.of(c, HALO + g)
            copies.append(
                pltpu.make_async_copy(
                    ref.at[pl.ds(at.start, CY), :], smoothed_out.at[rows_of(c * CX + x, CY), :],
                    done.at[1 + c * CX + g],
                )
            )
    for copy in copies:
        copy.start()
    for c in range(3):
        parts = [gathered[s, pl.ds(c * CY // 2, CY // 2), :] for s in range(N_GY)]
        turned[c] = jnp.transpose(jnp.concatenate(parts, axis=0))
        for x in range(CX // 2):
            coarse[c, pl.ds(x * NZ // 2, NZ // 2), :] = turned[c, pl.ds(x, NZ // 2, stride=2), :]
        copies.append(pltpu.make_async_copy(coarse.at[c], coarse_out.at[c], done.at[1 + 3 * CX + c]))
        copies[-1].start()
    for copy in copies:
        copy.wait()


def in_hbm(array):
    return pltpu.with_memory_space_constraint(array, pltpu.HBM)


def call(kernel, outs, ins, out_specs=None, scratch=(), flops=1000):
    return pl.pallas_call(
        kernel,
        out_shape=outs,
        in_specs=ins,
        out_specs=out_specs or [VMEM] * len(outs),
        scratch_shapes=list(scratch),
        compiler_params=PARAMS,
        cost_estimate=pl.CostEstimate(flops=flops, bytes_accessed=1000, transcendentals=0),
    )


def pair(n):
    return [(i, i ^ 1) for i in range(n)]


def other_x():
    out = []
    for i in range(N_GX):
        for j in range(N_GY):
            partner = (i, j ^ 1) if i in (0, N_GX - 1) else (((i + 1) ^ 1) - 1, j)
            out.append((i * N_GY + j, partner[0] * N_GY + partner[1]))
    return out


def other_y():
    out = []
    for i in range(N_GX):
        for j in range(N_GY):
            partner = (i ^ 1, j) if j in (0, N_GY - 1) else (i, ((j + 1) ^ 1) - 1)
            out.append((i * N_GY + j, partner[0] * N_GY + partner[1]))
    return out


def body(displacement, rhs, labels, stiffness, rows, counts, multipliers):
    block = CX * CY
    copies = 2 + 7 * CX
    slots = jax.ShapeDtypeStruct((SLOT_ROWS, 128), jnp.int32)
    y_other, own, raw_cells, mult = call(
        pack_first,
        [f32(HALO, OWN, NZ), f32(OWN * CY, NZ), slots, f32(3, SLOT_ROWS, 128)],
        [HBM] * 5,
        scratch=[pltpu.VMEM((block, NZ), jnp.int32), pltpu.SemaphoreType.DMA((copies,))],
    )(
        in_hbm(displacement.reshape(3 * block, NZ)),
        in_hbm(rhs.reshape(3 * block, NZ)),
        in_hbm(labels.reshape(block, NZ)),
        in_hbm(rows.reshape(SLOT_ROWS, 128)),
        in_hbm(multipliers.reshape(3, SLOT_ROWS, 128)),
    )
    y_other = lax.ppermute(y_other, ("gx", "gy"), other_y())
    side = f32(SIDE * CY + IFACE, NZ)
    far, near, cells = call(pack_sides, [side, side, slots], [VMEM] * 3)(own, raw_cells, mult)
    near = lax.ppermute(near, "gx", pair(N_GX))
    far = lax.ppermute(far, ("gx", "gy"), other_x())
    (y_pair,) = call(pack_pair, [f32(HALO, OWN, NZ)], [VMEM] * 2)(own, near)
    y_pair = lax.ppermute(y_pair, "gy", pair(N_GY))
    dense, at_depth = call(
        spread_own, [f32(4, block, NZ), jax.ShapeDtypeStruct((NZ, 8 * 128), BF16)], [VMEM] * 2, flops=5 * 10**9
    )(cells, mult)
    (inner,) = call(pack_wide, [f32(OWN * ROWS, NZ)], [VMEM], flops=5 * 10**9)(own)
    tile = f32(CORNER + SLOT_ROWS, NZ)
    corner, corner_near, own, limit = call(
        pack_second, [tile, tile, f32(OWN * ROWS, NZ), f32(SLOT_ROWS, NZ)], [VMEM, VMEM, SMEM, VMEM]
    )(y_other, y_pair, counts, inner)
    corner = lax.ppermute(corner, ("gx", "gy"), other_x())
    corner_near = lax.ppermute(corner_near, "gx", pair(N_GX))
    three, six = f32(3 * PX * ROWS, NZ), f32(6 * PX * ROWS, NZ)
    arrays = [f32(FIELDS * ROWS, NZ), six, six] + [three] * 6
    half = call(
        near_part, arrays + [f32(LABELS * 6, NZ), f32(3 * CY, NZ)], [SMEM, VMEM, VMEM, VMEM]
    )(stiffness, own, near, corner_near)
    (ribbon,) = call(spread_before, [f32(4, (CX + 2) * CY, NZ)], [VMEM] * 4)(far, near, dense, half[-1])
    message, low, updated = call(
        far_part,
        [f32(N_GY, 3 * CY // 2, NZ), three, f32(3, SLOT_ROWS, 128)],
        [VMEM] * (8 + len(half)),
        scratch=[pltpu.VMEM(a.shape, F32) for a in arrays[:-1]] + [pltpu.VMEM((6 * CY, NZ), F32)],
    )(far, corner, corner_near, limit, ribbon, cells, mult, at_depth, *half)
    gathered = lax.all_to_all(message, "gy", 0, 0)
    smoothed, updated, coarse = call(
        finish,
        [pltpu.HBM(s, F32) for s in ((3 * block, NZ), (3, SLOT_ROWS, 128), (3, CX // 2 * NZ // 2, NY // 2))],
        [VMEM] * 4,
        out_specs=[HBM] * 3,
        scratch=[
            pltpu.VMEM((3, CX // 2 * NZ // 2, NY // 2), F32),
            pltpu.VMEM((3, NZ, NY // 2), F32),
            pltpu.SemaphoreType.DMA((4 + 3 * CX,)),
        ],
    )(updated, low, half[7], gathered)
    coarse = jnp.swapaxes(coarse.reshape(3, CX // 2, NZ // 2, NY // 2), 2, 3)
    return (smoothed.reshape(3, CX, CY, NZ), coarse, updated.reshape(3, 1, 1, SLOTS))


def solution(mesh):
    return jax.shard_map(
        body,
        mesh=mesh,
        in_specs=(
            P(None, "gx", "gy", None),
            P(None, "gx", "gy", None),
            P("gx", "gy", None),
            P(),
            P("gx", "gy", None),
            P("gx", "gy"),
            P(None, "gx", "gy", None),
        ),
        out_specs=(P(None, "gx", "gy", None), P(None, "gx", None, None), P(None, "gx", "gy", None)),
        check_vma=False,
    )
```

```python
import jax
import jax.numpy as jnp
from jax import lax
from jax.experimental import pallas as pl
from jax.experimental.pallas import tpu as pltpu
from jax.sharding import PartitionSpec as P

SYMMETRIC_INDEX = ((0, 3, 4), (3, 1, 5), (4, 5, 2))
DAMPING = 0.6
MASS_SHIFT = 1.0
PENALTY = 1.0

CX, CY, NZ, SLOTS = 4, 32, 128, 1024
N_GX, N_GY = 32, 8
NX, NY = CX * N_GX, CY * N_GY
LABELS = 8
HALO = 3
PX = CX + 2 * HALO
PR = PX - 2
ROWS = 40
LAB0 = 3 * PX
RHS0 = LAB0 + PX
FIELDS = RHS0 + 3 * PR
OWN_LAB0 = 3 * CX
OWN_RHS0 = OWN_LAB0 + CX
OWN = OWN_RHS0 + 3 * CX
SIDE = 3 * HALO + HALO + 3 * (HALO - 1)
SLOT_ROWS = SLOTS // 128
IFACE = 4 * SLOT_ROWS
CORNER = 2 * (4 * HALO * HALO + 3 * (HALO - 1) ** 2)
VMEM = pl.BlockSpec(memory_space=pltpu.VMEM)
SMEM = pl.BlockSpec(memory_space=pltpu.SMEM)
HBM = pl.BlockSpec(memory_space=pltpu.HBM)
F32 = jnp.float32
BF16 = jnp.bfloat16
PARAMS = pltpu.CompilerParams(vmem_limit_bytes=32 * 1024 * 1024)


def f32(*shape):
    return jax.ShapeDtypeStruct(shape, F32)


def pieces_of(value):
    high = value.astype(BF16)
    rest = value - high.astype(F32)
    middle = rest.astype(BF16)
    low = (rest - middle.astype(F32)).astype(BF16)
    return (high, middle, low)


def odd(axis):
    return lax.rem(lax.axis_index(axis), 2)


def rows_of(j, height):
    return pl.ds(j * height if isinstance(j, int) else pl.multiple_of(j * height, height), height)


def corner_rows():
    at = 0
    for place in range(SIDE):
        depth = HALO if place < 4 * HALO else HALO - 1
        yield place, at, depth
        at += 2 * depth


def sent_planes():
    place = 0
    for first, depth in [(c * CX, HALO) for c in range(3)] + [(OWN_LAB0, HALO)] + [
        (OWN_RHS0 + c * CX, HALO - 1) for c in range(3)
    ]:
        for k in range(depth):
            yield place, first, k
            place += 1


def halo_planes():
    place = 0
    for first, depth in [(c * PX, HALO) for c in range(3)] + [(LAB0, HALO)] + [
        (RHS0 + c * PR - 1, HALO - 1) for c in range(3)
    ]:
        for k in range(depth):
            yield place, first, k
            place += 1


def slot_number():
    return lax.broadcasted_iota(jnp.int32, (SLOT_ROWS, 128), 0) * 128 + lax.broadcasted_iota(
        jnp.int32, (SLOT_ROWS, 128), 1
    )


def pack_first(
    disp, rhs, labels, cells_in, mult_in,
    far, near, own, cells, mult,
    raw_labels, raw_cells, arrived,
):
    flip = odd("gx")
    pairs = []
    for g in range(CX):
        x = g + flip * (CX - 1 - 2 * g)
        pairs.append((labels.at[rows_of(x, CY)], raw_labels.at[rows_of(g, CY)]))
        for c in range(3):
            pairs.append((disp.at[rows_of(c * CX + x, CY)], own.at[rows_of(c * CX + g, CY)]))
            pairs.append((rhs.at[rows_of(c * CX + x, CY)], own.at[rows_of(OWN_RHS0 + c * CX + g, CY)]))
    pairs += [(cells_in, raw_cells), (mult_in, mult)]
    copies = [pltpu.make_async_copy(a, b, arrived.at[i]) for i, (a, b) in enumerate(pairs)]
    for copy in copies:
        copy.start()
    for copy in copies:
        copy.wait()
    own[pl.ds(OWN_LAB0 * CY, CX * CY), :] = raw_labels[...].astype(F32)
    block_plane = raw_cells[...] // (CY * NZ)
    turned = raw_cells[...] + flip * (CX - 1 - 2 * block_plane) * (CY * NZ)
    cells[...] = turned
    for place, first, k in sent_planes():
        far[rows_of(place, CY), :] = own[rows_of(first + k, CY), :]
        near[rows_of(place, CY), :] = own[rows_of(first + CX - 1 - k, CY), :]
    for side in (far, near):
        side[pl.ds(SIDE * CY, SLOT_ROWS), :] = turned.astype(F32)
        for c in range(3):
            side[pl.ds(SIDE * CY + (1 + c) * SLOT_ROWS, SLOT_ROWS), :] = mult[c]


def pack_y(own, near, y_other, y_pair):
    up = odd("gy") == 0
    for k in range(HALO):
        first = own[pl.ds(k, OWN, stride=CY), :]
        last = own[pl.ds(CY - HALO + k, OWN, stride=CY), :]
        y_pair[k] = jnp.where(up, last, first)
        y_other[k] = jnp.where(up, first, last)


def reach():
    here = lax.axis_index("gy")
    return (
        jnp.where(here > 0, 1.0, 0.0).astype(F32),
        jnp.where(here < N_GY - 1, 1.0, 0.0).astype(F32),
    )


def pack_wide(own, wide):
    for j in range(OWN):
        wide[pl.ds(j * ROWS, CY), :] = own[rows_of(j, CY), :]
        wide[pl.ds(j * ROWS + CY, ROWS - CY), :] = jnp.zeros((ROWS - CY, NZ), F32)


def pack_second(y_other, y_pair, count, inner, corner_far, corner_near, wide, limit):
    low, high = reach()
    up = odd("gy") == 0
    wide[...] = inner[...]
    for k in range(HALO):
        wide[pl.ds(CY + k, OWN, stride=ROWS), :] = high * jnp.where(up, y_pair[k], y_other[k])
        wide[pl.ds(ROWS - HALO + k, OWN, stride=ROWS), :] = low * jnp.where(up, y_other[k], y_pair[k])
    live = jnp.full((SLOT_ROWS, 128), count[0, 0].astype(F32), F32)
    limit[...] = live
    planes = list(sent_planes())
    for corner, turn in ((corner_far, False), (corner_near, True)):
        for place, at, depth in corner_rows():
            first, k = planes[place][1:]
            base = (first + (CX - 1 - k if turn else k)) * ROWS
            corner[pl.ds(at, depth), :] = wide[pl.ds(base + CY, depth), :]
            corner[pl.ds(at + depth, depth), :] = wide[pl.ds(base + ROWS - depth, depth), :]
        corner[pl.ds(CORNER, SLOT_ROWS), :] = live


def paired(array, j):
    return jnp.concatenate([array[2 * j : 2 * j + 1], array[2 * j + 1 : 2 * j + 2]], axis=1)


def spread(cells, mult, first, columns):
    column = cells // NZ - first
    depth = cells % NZ
    total = jnp.zeros((11 * columns, NZ), F32)
    parts = [piece for c in range(3) for piece in pieces_of(mult[c])]
    parts += pieces_of((slot_number() + 1).astype(F32))[:2]
    for j in range(SLOT_ROWS // 2):
        at_column = lax.broadcasted_iota(jnp.int32, (columns, 256), 0) == paired(column, j)
        at_depth = lax.broadcasted_iota(jnp.int32, (NZ, 256), 0) == paired(depth, j)
        left = [jnp.where(at_column, paired(piece.astype(F32), j), 0.0).astype(BF16) for piece in parts]
        total = total + lax.dot_general(
            jnp.concatenate(left, axis=0),
            jnp.where(at_depth, 1.0, 0.0).astype(BF16),
            (((1,), (1,)), ((), ())),
            preferred_element_type=F32,
        )
    part = [total[i * columns : (i + 1) * columns] for i in range(11)]
    return [part[3 * c] + part[3 * c + 1] + part[3 * c + 2] for c in range(3)] + [part[9] + part[10]]


def spread_own(cells, mult, dense, at_depth):
    depth = cells[...] % NZ
    for j in range(SLOT_ROWS // 2):
        hit = lax.broadcasted_iota(jnp.int32, (NZ, 256), 0) == paired(depth, j)
        at_depth[:, pl.ds(256 * j, 256)] = jnp.where(hit, 1.0, 0.0).astype(BF16)
    values = spread(cells[...], [mult[c] for c in range(3)], 0, CX * CY)
    for i in range(4):
        dense[i] = values[i]


def is_inside():
    here = lax.axis_index("gx")
    return jnp.where((here > 0) & (here < N_GX - 1), 1.0, 0.0).astype(F32)


def spread_before(far, near, dense, last, ribbon):
    flip = odd("gx")

    def at(i):
        a = far[pl.ds(SIDE * CY + i * SLOT_ROWS, SLOT_ROWS), :]
        b = near[pl.ds(SIDE * CY + i * SLOT_ROWS, SLOT_ROWS), :]
        return jnp.where(flip == 1, b, a)

    values = spread(at(0).astype(jnp.int32), [at(1 + c) for c in range(3)], flip * (CX - 1) * CY, CY)
    values[3] = values[3] * jnp.where(flip == 1, 1.0, is_inside())
    for i in range(4):
        ribbon[i, pl.ds(0, CY), :] = values[i]
        ribbon[i, pl.ds(CY, CX * CY), :] = dense[i]
        ribbon[i, pl.ds((CX + 1) * CY, CY), :] = values[i]


def times(k, v):
    return [
        k[SYMMETRIC_INDEX[c][0]] * v[0] + k[SYMMETRIC_INDEX[c][1]] * v[1] + k[SYMMETRIC_INDEX[c][2]] * v[2]
        for c in range(3)
    ]


class Split:
    def __init__(self, at, low, high):
        self.at, self.low, self.high = at, low, high

    def of(self, c, p, count=PX, base=0):
        ref = self.low if p < self.at else self.high
        return ref, rows_of(base + c * count + p, ROWS)


class Stencil:
    def __init__(self, entry, fields, coeff, total, scale, flux):
        self.entry, self.fields, self.coeff, self.total, self.scale, self.flux = (
            entry, fields, coeff, total, scale, flux
        )
        lane = lax.broadcasted_iota(jnp.int32, (1, NZ), 1)
        self.not_first = jnp.where(lane == 0, 0.0, 0.5)
        self.not_last = jnp.where(lane == NZ - 1, 0.0, 0.5)
        self.ends = jnp.where((lane == 0) | (lane == NZ - 1), 16.0, 0.0)
        row = lax.broadcasted_iota(jnp.int32, (ROWS, NZ), 0)
        y = lax.axis_index("gy") * CY + jnp.where(row < CY + HALO, row, row - ROWS)
        self.row_inside = (y >= 0) & (y < NY) & ((row < CY + HALO) | (row >= ROWS - HALO))

    def get(self, split, c, p):
        ref, at = split.of(c, p)
        return ref[at, :]

    def put(self, split, c, p, value):
        ref, at = split.of(c, p)
        ref[at, :] = value

    def label(self, p):
        ref, at = self.fields.of(0, p, base=LAB0)
        return ref[at, :]

    def right_side(self, c, p):
        ref, at = self.fields.of(c, p, count=PR, base=RHS0 - 1)
        return ref[at, :]

    def summed(self, split, c, p, edge=None):
        f = self.get(split, c, p)
        f = (f + f) + (self.get(split, c, p - 1) + self.get(split, c, p + 1))
        f = (f + f) + (pltpu.roll(f, 1, 0) + pltpu.roll(f, ROWS - 1, 0))
        f = f + (pltpu.roll(f, 1, 1) * self.not_first + pltpu.roll(f, NZ - 1, 1) * self.not_last)
        if edge is not None:
            f = f + self.ends * (0.5 * edge)
        return f

    def coefficients(self, planes):
        for p in planes:
            label = self.label(p)
            k = [jnp.broadcast_to(self.entry(0, e), label.shape) for e in range(6)]
            for m in range(1, LABELS):
                at = label == float(m)
                k = [jnp.where(at, self.entry(m, e), k[e]) for e in range(6)]
            for e in range(6):
                self.put(self.coeff, e, p, k[e])
            self.push(self.flux, p, [self.get(self.fields, c, p) for c in range(3)])

    def weights(self, planes):
        for p in planes:
            for e in range(6):
                k = self.get(self.coeff, e, p)
                around = self.summed(self.coeff, e, p, self.entry(0, e))
                self.put(self.total, e, p, 32.0 * k + around)
                if e < 3:
                    self.put(self.scale, e, p, DAMPING / (MASS_SHIFT + 6.0 * k + 0.25 * around))

    def push(self, flux, p, v):
        pushed = times([self.get(self.coeff, e, p) for e in range(6)], v)
        for c in range(3):
            self.put(flux, c, p, pushed[c])

    def image(self, p, v_split, flux):
        v = [self.get(v_split, c, p) for c in range(3)]
        k = [self.get(self.coeff, e, p) for e in range(6)]
        m = [self.get(self.total, e, p) for e in range(6)]
        around = [self.summed(v_split, c, p) for c in range(3)]
        pushed = [self.summed(flux, c, p) for c in range(3)]
        mine, theirs = times(m, v), times(k, around)
        return v, [MASS_SHIFT * v[c] + 0.25 * (mine[c] - theirs[c] - pushed[c]) for c in range(3)]

    def sweep(self, planes, v_split, flux, to, to_flux, inside=None):
        for p in planes:
            keep = self.row_inside if p >= HALO else self.row_inside & (inside > 0.5)
            v, a = self.image(p, v_split, flux)
            new = []
            for c in range(3):
                value = v[c] + (self.right_side(c, p) - a[c]) * self.get(self.scale, c, p)
                value = jnp.where(keep, value, 0.0)
                self.put(to, c, p, value)
                new.append(value)
            self.push(to_flux, p, new)

    def remainder(self, p, v_split, flux):
        a = self.image(p, v_split, flux)[1]
        return [(self.right_side(c, p) - a[c])[:CY] for c in range(3)]


def fill_halo(fields, side, corner, plane_of, inside):
    tiles = {place: (at, depth) for place, at, depth in corner_rows()}
    for place, base, k in halo_planes():
        plane = (base + plane_of(k)) * ROWS
        at, depth = tiles[place]
        fields[pl.ds(plane, CY), :] = inside * side[rows_of(place, CY), :]
        fields[pl.ds(plane + CY, ROWS - CY), :] = jnp.zeros((ROWS - CY, NZ), F32)
        fields[pl.ds(plane + CY, depth), :] = inside * corner[pl.ds(at, depth), :]
        fields[pl.ds(plane + ROWS - depth, depth), :] = inside * corner[pl.ds(at + depth, depth), :]


def near_part(
    stiffness, own, near, corner_near,
    fields, coeff, total, scale, flux, first, flux_first, second, flux_second, table, last,
):
    for c in range(3):
        for g in range(CX):
            fields[rows_of(c * PX + HALO + g, ROWS), :] = own[rows_of(c * CX + g, ROWS), :]
            fields[rows_of(RHS0 - 1 + c * PR + HALO + g, ROWS), :] = own[rows_of(OWN_RHS0 + c * CX + g, ROWS), :]
    for g in range(CX):
        fields[rows_of(LAB0 + HALO + g, ROWS), :] = own[rows_of(OWN_LAB0 + g, ROWS), :]
    fill_halo(fields, near, corner_near, lambda k: HALO + CX + k, 1.0)
    for m in range(LABELS):
        for e in range(6):
            table[pl.ds(m * 6 + e, 1), :] = jnp.full((1, NZ), stiffness[m, e], F32)

    def whole(ref):
        return Split(0, None, ref)

    grid = Stencil(
        lambda m, e: stiffness[m, e], whole(fields), whole(coeff), whole(total), whole(scale), whole(flux)
    )
    grid.coefficients(range(HALO, PX))
    grid.weights(range(HALO + 1, PX - 1))
    grid.sweep(range(HALO + 1, PX - 1), whole(fields), whole(flux), whole(first), whole(flux_first))
    grid.sweep(range(HALO + 2, PX - 2), whole(first), whole(flux_first), whole(second), whole(flux_second))
    remainder = grid.remainder(HALO + 3, whole(second), whole(flux_second))
    for c in range(3):
        last[rows_of(c, CY), :] = remainder[c]


def far_part(
    far, corner, corner_near, limit, ribbon, cells, mult, at_depth,
    near_fields, near_coeff, near_total, near_scale, near_flux,
    near_first, near_flux_first, near_second, near_flux_second, table, last,
    message, second, updated,
    fields, coeff, total, scale, flux, first, flux_first, flux_second, coarse,
):
    inside = is_inside()
    flip = odd("gx")
    sign = jnp.where(flip == 1, -1.0, 1.0).astype(F32)
    fill_halo(fields, far, corner, lambda k: HALO - 1 - k, inside)
    v0, flux0 = Split(HALO, fields, near_fields), Split(HALO, flux, near_flux)
    v1, flux1 = Split(HALO + 1, first, near_first), Split(HALO + 1, flux_first, near_flux_first)
    v2, flux2 = Split(HALO + 2, second, near_second), Split(HALO + 2, flux_second, near_flux_second)
    grid = Stencil(
        lambda m, e: table[pl.ds(m * 6 + e, 1), :],
        v0,
        Split(HALO, coeff, near_coeff),
        Split(HALO + 1, total, near_total),
        Split(HALO + 1, scale, near_scale),
        flux0,
    )
    grid.coefficients(range(HALO))
    grid.weights(range(1, HALO + 1))
    grid.sweep(range(1, HALO + 1), v0, flux0, v1, flux1, inside)
    grid.sweep(range(2, HALO + 2), v1, flux1, v2, flux2, inside)
    used = slot_number().astype(F32) < limit[...] - 0.5
    column = cells[...] // NZ
    block = CX * CY
    left = []
    for c in range(3):
        v = [grid.get(v2, c, HALO - 1 + i)[:CY] for i in range(CX + 2)]
        jumps = [v[1 + g] - jnp.where(flip == 1, v[g], v[2 + g]) for g in range(CX)]
        left.append(jnp.concatenate(pieces_of(jnp.concatenate(jumps, axis=0)), axis=1))
    left = jnp.concatenate(left, axis=0)
    for j in range(SLOT_ROWS // 2):
        right = at_depth[:, pl.ds(256 * j, 256)]
        picked = jnp.dot(left, jnp.concatenate([right] * 3, axis=0), preferred_element_type=F32)
        at_column = lax.broadcasted_iota(jnp.int32, (block, 256), 0) == paired(column, j)
        for c in range(3):
            jump = jnp.sum(
                jnp.where(at_column, picked[c * block : (c + 1) * block], 0.0), axis=0, keepdims=True
            )
            for i in range(2):
                at = 2 * j + i
                old = mult[c, at : at + 1, :]
                new = old + PENALTY * jump[:, i * 128 : (i + 1) * 128]
                updated[c, at : at + 1, :] = jnp.where(used[at : at + 1], new, old)
    remainders = [grid.remainder(HALO + g, v2, flux2) for g in range(CX - 1)]
    remainders.append([last[rows_of(c, CY), :] for c in range(3)])

    mine = limit[:1]
    theirs = jnp.where(flip == 1, corner_near[pl.ds(CORNER, 1), :], corner[pl.ds(CORNER, 1), :])
    live = []
    for i in range(CX + 1):
        if i == 0:
            top = jnp.where(flip == 1, mine, theirs)
        elif i == CX:
            top = jnp.where(flip == 1, theirs, mine)
        else:
            top = mine
        number = ribbon[3, rows_of(i + flip, CY), :]
        live.append((number > 0.5) & (number < top + 0.5))
    for c in range(3):
        planes = [grid.get(v2, c, HALO - 1 + i)[:CY] for i in range(CX + 2)]
        pushed = []
        for i in range(CX + 1):
            jump = sign * (planes[i] - planes[i + 1])
            at = rows_of(i + flip, CY)
            pushed.append(jnp.where(live[i], ribbon[c, at, :] + PENALTY * jump, 0.0))
        parts = [remainders[g][c] - sign * (pushed[g + 1] - pushed[g]) for g in range(CX)]
        for half in range(2):
            coarse[rows_of(half * 3 + c, CY), :] = parts[2 * half] + parts[2 * half + 1]

    pairs = []
    for half in range(2):
        at = 3 * half * CY
        rows = coarse[pl.ds(at, 3 * CY // 2, stride=2), :] + coarse[pl.ds(at + 1, 3 * CY // 2, stride=2), :]
        pairs.append(rows)
    low_x = jnp.where(flip == 1, pairs[1], pairs[0])
    high_x = jnp.where(flip == 1, pairs[0], pairs[1])
    even_lane = lax.rem(lax.broadcasted_iota(jnp.int32, (1, NZ), 1), 2) == 0
    out = jnp.where(even_lane, low_x + pltpu.roll(low_x, NZ - 1, 1), high_x + pltpu.roll(high_x, 1, 1))
    for s in range(N_GY):
        message[s] = out


def finish(
    updated, low, high, gathered,
    smoothed_out, updated_out, coarse_out,
    coarse, turned, done,
):
    flip = odd("gx")
    split = Split(HALO + 2, low, high)
    copies = [pltpu.make_async_copy(updated, updated_out, done.at[0])]
    for c in range(3):
        for g in range(CX):
            x = g + flip * (CX - 1 - 2 * g)
            ref, at = split.of(c, HALO + g)
            copies.append(
                pltpu.make_async_copy(
                    ref.at[pl.ds(at.start, CY), :], smoothed_out.at[rows_of(c * CX + x, CY), :],
                    done.at[1 + c * CX + g],
                )
            )
    for copy in copies:
        copy.start()
    for c in range(3):
        parts = [gathered[s, pl.ds(c * CY // 2, CY // 2), :] for s in range(N_GY)]
        turned[c] = jnp.transpose(jnp.concatenate(parts, axis=0))
        for x in range(CX // 2):
            coarse[c, pl.ds(x * NZ // 2, NZ // 2), :] = turned[c, pl.ds(x, NZ // 2, stride=2), :]
        copies.append(pltpu.make_async_copy(coarse.at[c], coarse_out.at[c], done.at[1 + 3 * CX + c]))
        copies[-1].start()
    for copy in copies:
        copy.wait()


def in_hbm(array):
    return pltpu.with_memory_space_constraint(array, pltpu.HBM)


def call(kernel, outs, ins, out_specs=None, scratch=(), flops=1000):
    return pl.pallas_call(
        kernel,
        out_shape=outs,
        in_specs=ins,
        out_specs=out_specs or [VMEM] * len(outs),
        scratch_shapes=list(scratch),
        compiler_params=PARAMS,
        cost_estimate=pl.CostEstimate(flops=flops, bytes_accessed=1000, transcendentals=0),
    )


def pair(n):
    return [(i, i ^ 1) for i in range(n)]


def other_x():
    out = []
    for i in range(N_GX):
        for j in range(N_GY):
            partner = (i, j ^ 1) if i in (0, N_GX - 1) else (((i + 1) ^ 1) - 1, j)
            out.append((i * N_GY + j, partner[0] * N_GY + partner[1]))
    return out


def other_y():
    out = []
    for i in range(N_GX):
        for j in range(N_GY):
            partner = (i ^ 1, j) if j in (0, N_GY - 1) else (i, ((j + 1) ^ 1) - 1)
            out.append((i * N_GY + j, partner[0] * N_GY + partner[1]))
    return out


def body(displacement, rhs, labels, stiffness, rows, counts, multipliers):
    block = CX * CY
    copies = 2 + 7 * CX
    slots = jax.ShapeDtypeStruct((SLOT_ROWS, 128), jnp.int32)
    side = f32(SIDE * CY + IFACE, NZ)
    far, near, own, cells, mult = call(
        pack_first,
        [side, side, f32(OWN * CY, NZ), slots, f32(3, SLOT_ROWS, 128)],
        [HBM] * 5,
        scratch=[
            pltpu.VMEM((block, NZ), jnp.int32),
            pltpu.VMEM((SLOT_ROWS, 128), jnp.int32),
            pltpu.SemaphoreType.DMA((copies,)),
        ],
    )(
        in_hbm(displacement.reshape(3 * block, NZ)),
        in_hbm(rhs.reshape(3 * block, NZ)),
        in_hbm(labels.reshape(block, NZ)),
        in_hbm(rows.reshape(SLOT_ROWS, 128)),
        in_hbm(multipliers.reshape(3, SLOT_ROWS, 128)),
    )
    near = lax.ppermute(near, "gx", pair(N_GX))
    far = lax.ppermute(far, ("gx", "gy"), other_x())
    y_other, y_pair = call(pack_y, [f32(HALO, OWN, NZ)] * 2, [VMEM] * 2)(own, near)
    y_other = lax.ppermute(y_other, ("gx", "gy"), other_y())
    y_pair = lax.ppermute(y_pair, "gy", pair(N_GY))
    dense, at_depth = call(
        spread_own, [f32(4, block, NZ), jax.ShapeDtypeStruct((NZ, 8 * 128), BF16)], [VMEM] * 2, flops=5 * 10**9
    )(cells, mult)
    (inner,) = call(pack_wide, [f32(OWN * ROWS, NZ)], [VMEM], flops=5 * 10**9)(own)
    tile = f32(CORNER + SLOT_ROWS, NZ)
    corner, corner_near, own, limit = call(
        pack_second, [tile, tile, f32(OWN * ROWS, NZ), f32(SLOT_ROWS, NZ)], [VMEM, VMEM, SMEM, VMEM]
    )(y_other, y_pair, counts, inner)
    corner = lax.ppermute(corner, ("gx", "gy"), other_x())
    corner_near = lax.ppermute(corner_near, "gx", pair(N_GX))
    three, six = f32(3 * PX * ROWS, NZ), f32(6 * PX * ROWS, NZ)
    arrays = [f32(FIELDS * ROWS, NZ), six, six] + [three] * 6
    half = call(
        near_part, arrays + [f32(LABELS * 6, NZ), f32(3 * CY, NZ)], [SMEM, VMEM, VMEM, VMEM]
    )(stiffness, own, near, corner_near)
    (ribbon,) = call(spread_before, [f32(4, (CX + 2) * CY, NZ)], [VMEM] * 4)(far, near, dense, half[-1])
    message, low, updated = call(
        far_part,
        [f32(N_GY, 3 * CY // 2, NZ), three, f32(3, SLOT_ROWS, 128)],
        [VMEM] * (8 + len(half)),
        scratch=[pltpu.VMEM(a.shape, F32) for a in arrays[:-1]] + [pltpu.VMEM((6 * CY, NZ), F32)],
    )(far, corner, corner_near, limit, ribbon, cells, mult, at_depth, *half)
    gathered = lax.all_to_all(message, "gy", 0, 0)
    smoothed, updated, coarse = call(
        finish,
        [pltpu.HBM(s, F32) for s in ((3 * block, NZ), (3, SLOT_ROWS, 128), (3, CX // 2 * NZ // 2, NY // 2))],
        [VMEM] * 4,
        out_specs=[HBM] * 3,
        scratch=[
            pltpu.VMEM((3, CX // 2 * NZ // 2, NY // 2), F32),
            pltpu.VMEM((3, NZ, NY // 2), F32),
            pltpu.SemaphoreType.DMA((4 + 3 * CX,)),
        ],
    )(updated, low, half[7], gathered)
    coarse = jnp.swapaxes(coarse.reshape(3, CX // 2, NZ // 2, NY // 2), 2, 3)
    return (smoothed.reshape(3, CX, CY, NZ), coarse, updated.reshape(3, 1, 1, SLOTS))


def solution(mesh):
    return jax.shard_map(
        body,
        mesh=mesh,
        in_specs=(
            P(None, "gx", "gy", None),
            P(None, "gx", "gy", None),
            P("gx", "gy", None),
            P(),
            P("gx", "gy", None),
            P("gx", "gy"),
            P(None, "gx", "gy", None),
        ),
        out_specs=(P(None, "gx", "gy", None), P(None, "gx", None, None), P(None, "gx", "gy", None)),
        check_vma=False,
    )
```

```python
import jax
import jax.numpy as jnp
from jax import lax
from jax.experimental import pallas as pl
from jax.experimental.pallas import tpu as pltpu
from jax.sharding import PartitionSpec as P

SYMMETRIC_INDEX = ((0, 3, 4), (3, 1, 5), (4, 5, 2))
DAMPING = 0.6
MASS_SHIFT = 1.0
PENALTY = 1.0

CX, CY, NZ, SLOTS = 4, 32, 128, 1024
N_GX, N_GY = 32, 8
NX, NY = CX * N_GX, CY * N_GY
LABELS = 8
HALO = 3
PX = CX + 2 * HALO
PR = PX - 2
ROWS = 40
LAB0 = 3 * PX
RHS0 = LAB0 + PX
FIELDS = RHS0 + 3 * PR
OWN_LAB0 = 3 * CX
OWN_RHS0 = OWN_LAB0 + CX
OWN = OWN_RHS0 + 3 * CX
ROOM = 32
SPARE = 8
SIDE = 3 * HALO + HALO + 3 * (HALO - 1)
SLOT_ROWS = SLOTS // 128
IFACE = 4 * SLOT_ROWS
CORNER = 2 * (4 * HALO * HALO + 3 * (HALO - 1) ** 2)
VMEM = pl.BlockSpec(memory_space=pltpu.VMEM)
SMEM = pl.BlockSpec(memory_space=pltpu.SMEM)
HBM = pl.BlockSpec(memory_space=pltpu.HBM)
F32 = jnp.float32
BF16 = jnp.bfloat16
PARAMS = pltpu.CompilerParams(vmem_limit_bytes=32 * 1024 * 1024)


def f32(*shape):
    return jax.ShapeDtypeStruct(shape, F32)


def pieces_of(value):
    high = value.astype(BF16)
    rest = value - high.astype(F32)
    middle = rest.astype(BF16)
    low = (rest - middle.astype(F32)).astype(BF16)
    return (high, middle, low)


def odd(axis):
    return lax.rem(lax.axis_index(axis), 2)


def rows_of(j, height):
    return pl.ds(j * height if isinstance(j, int) else pl.multiple_of(j * height, height), height)


def corner_rows():
    at = 0
    for place in range(SIDE):
        depth = HALO if place < 4 * HALO else HALO - 1
        yield place, at, depth
        at += 2 * depth


def sent_planes():
    place = 0
    for first, depth in [(c * CX, HALO) for c in range(3)] + [(OWN_LAB0, HALO)] + [
        (OWN_RHS0 + c * CX, HALO - 1) for c in range(3)
    ]:
        for k in range(depth):
            yield place, first, k
            place += 1


def halo_planes():
    place = 0
    for first, depth in [(c * PX, HALO) for c in range(3)] + [(LAB0, HALO)] + [
        (RHS0 + c * PR - 1, HALO - 1) for c in range(3)
    ]:
        for k in range(depth):
            yield place, first, k
            place += 1


def slot_number():
    return lax.broadcasted_iota(jnp.int32, (SLOT_ROWS, 128), 0) * 128 + lax.broadcasted_iota(
        jnp.int32, (SLOT_ROWS, 128), 1
    )


def pack_first(
    disp, rhs, labels, cells_in, mult_in,
    y_other, own, cells, mult,
    raw_labels, arrived,
):
    flip = odd("gx")
    pairs = []
    for g in range(CX):
        x = g + flip * (CX - 1 - 2 * g)
        pairs.append((labels.at[rows_of(x, CY)], raw_labels.at[rows_of(g, CY)]))
        for c in range(3):
            pairs.append((disp.at[rows_of(c * CX + x, CY)], own.at[rows_of(c * CX + g, CY)]))
            pairs.append((rhs.at[rows_of(c * CX + x, CY)], own.at[rows_of(OWN_RHS0 + c * CX + g, CY)]))
    pairs += [(cells_in, cells), (mult_in, mult)]
    copies = [pltpu.make_async_copy(a, b, arrived.at[i]) for i, (a, b) in enumerate(pairs)]
    for copy in copies:
        copy.start()
    for copy in copies:
        copy.wait()
    own[pl.ds(OWN_LAB0 * CY, CX * CY), :] = raw_labels[...].astype(F32)
    up = odd("gy") == 0
    for k in range(HALO):
        first = own[pl.ds(k, OWN, stride=CY), :]
        last = own[pl.ds(CY - HALO + k, OWN, stride=CY), :]
        y_other[k] = jnp.where(up, first, last)


def pack_sides(own, raw_cells, mult, far, near, cells):
    flip = odd("gx")
    block_plane = raw_cells[...] // (CY * NZ)
    turned = raw_cells[...] + flip * (CX - 1 - 2 * block_plane) * (CY * NZ)
    cells[...] = turned
    for place, first, k in sent_planes():
        far[rows_of(place, CY), :] = own[rows_of(first + k, CY), :]
        near[rows_of(place, CY), :] = own[rows_of(first + CX - 1 - k, CY), :]
    for side in (far, near):
        side[pl.ds(SIDE * CY, SLOT_ROWS), :] = turned.astype(F32)
        for c in range(3):
            side[pl.ds(SIDE * CY + (1 + c) * SLOT_ROWS, SLOT_ROWS), :] = mult[c]


def pack_pair(own, near, y_pair):
    up = odd("gy") == 0
    for k in range(HALO):
        first = own[pl.ds(k, OWN, stride=CY), :]
        last = own[pl.ds(CY - HALO + k, OWN, stride=CY), :]
        y_pair[k] = jnp.where(up, last, first)


def reach():
    here = lax.axis_index("gy")
    return (
        jnp.where(here > 0, 1.0, 0.0).astype(F32),
        jnp.where(here < N_GY - 1, 1.0, 0.0).astype(F32),
    )


def pack_wide(own, wide):
    for j in range(OWN):
        wide[pl.ds(j * ROWS, CY), :] = own[rows_of(j, CY), :]
        wide[pl.ds(j * ROWS + CY, ROWS - CY), :] = jnp.zeros((ROWS - CY, NZ), F32)


def pack_second(y_other, y_pair, count, inner, corner_far, corner_near, wide, limit):
    low, high = reach()
    up = odd("gy") == 0
    wide[pl.ds(0, OWN * ROWS), :] = inner[pl.ds(0, OWN * ROWS), :]
    for k in range(HALO):
        wide[pl.ds(CY + k, OWN, stride=ROWS), :] = high * jnp.where(up, y_pair[k], y_other[k])
        wide[pl.ds(ROWS - HALO + k, OWN, stride=ROWS), :] = low * jnp.where(up, y_other[k], y_pair[k])
    live = jnp.full((SLOT_ROWS, 128), count[0, 0].astype(F32), F32)
    limit[...] = live
    planes = list(sent_planes())
    for corner, turn in ((corner_far, False), (corner_near, True)):
        for place, at, depth in corner_rows():
            first, k = planes[place][1:]
            base = (first + (CX - 1 - k if turn else k)) * ROWS
            corner[pl.ds(at, depth), :] = wide[pl.ds(base + CY, depth), :]
            corner[pl.ds(at + depth, depth), :] = wide[pl.ds(base + ROWS - depth, depth), :]
        corner[pl.ds(CORNER, SLOT_ROWS), :] = live


def paired(array, j):
    return jnp.concatenate([array[2 * j : 2 * j + 1], array[2 * j + 1 : 2 * j + 2]], axis=1)


def spread(cells, mult, first, columns):
    column = cells // NZ - first
    depth = cells % NZ
    total = jnp.zeros((11 * columns, NZ), F32)
    parts = [piece for c in range(3) for piece in pieces_of(mult[c])]
    parts += pieces_of((slot_number() + 1).astype(F32))[:2]
    for j in range(SLOT_ROWS // 2):
        at_column = lax.broadcasted_iota(jnp.int32, (columns, 256), 0) == paired(column, j)
        at_depth = lax.broadcasted_iota(jnp.int32, (NZ, 256), 0) == paired(depth, j)
        left = [jnp.where(at_column, paired(piece.astype(F32), j), 0.0).astype(BF16) for piece in parts]
        total = total + lax.dot_general(
            jnp.concatenate(left, axis=0),
            jnp.where(at_depth, 1.0, 0.0).astype(BF16),
            (((1,), (1,)), ((), ())),
            preferred_element_type=F32,
        )
    part = [total[i * columns : (i + 1) * columns] for i in range(11)]
    return [part[3 * c] + part[3 * c + 1] + part[3 * c + 2] for c in range(3)] + [part[9] + part[10]]


def spread_own(cells, mult, dense, at_depth):
    depth = cells[...] % NZ
    for j in range(SLOT_ROWS // 2):
        hit = lax.broadcasted_iota(jnp.int32, (NZ, 256), 0) == paired(depth, j)
        at_depth[:, pl.ds(256 * j, 256)] = jnp.where(hit, 1.0, 0.0).astype(BF16)
    values = spread(cells[...], [mult[c] for c in range(3)], 0, CX * CY)
    for i in range(4):
        dense[i] = values[i]


def is_inside():
    here = lax.axis_index("gx")
    return jnp.where((here > 0) & (here < N_GX - 1), 1.0, 0.0).astype(F32)


def spread_before(far, near, dense, last, ribbon):
    flip = odd("gx")

    def at(i):
        a = far[pl.ds(SIDE * CY + i * SLOT_ROWS, SLOT_ROWS), :]
        b = near[pl.ds(SIDE * CY + i * SLOT_ROWS, SLOT_ROWS), :]
        return jnp.where(flip == 1, b, a)

    values = spread(at(0).astype(jnp.int32), [at(1 + c) for c in range(3)], flip * (CX - 1) * CY, CY)
    values[3] = values[3] * jnp.where(flip == 1, 1.0, is_inside())
    for i in range(4):
        ribbon[i, pl.ds(0, CY), :] = values[i]
        ribbon[i, pl.ds(CY, CX * CY), :] = dense[i]
        ribbon[i, pl.ds((CX + 1) * CY, CY), :] = values[i]


def times(k, v):
    return [
        k[SYMMETRIC_INDEX[c][0]] * v[0] + k[SYMMETRIC_INDEX[c][1]] * v[1] + k[SYMMETRIC_INDEX[c][2]] * v[2]
        for c in range(3)
    ]


class Split:
    def __init__(self, at, low, high):
        self.at, self.low, self.high = at, low, high

    def of(self, c, p, count=PX, base=0):
        ref = self.low if p < self.at else self.high
        return ref, rows_of(base + c * count + p, ROWS)


class Stencil:
    def __init__(self, entry, fields, coeff, total, scale, flux):
        self.entry, self.fields, self.coeff, self.total, self.scale, self.flux = (
            entry, fields, coeff, total, scale, flux
        )
        lane = lax.broadcasted_iota(jnp.int32, (1, NZ), 1)
        self.not_first = jnp.where(lane == 0, 0.0, 0.5)
        self.not_last = jnp.where(lane == NZ - 1, 0.0, 0.5)
        self.ends = jnp.where((lane == 0) | (lane == NZ - 1), 16.0, 0.0)
        row = lax.broadcasted_iota(jnp.int32, (ROWS, NZ), 0)
        y = lax.axis_index("gy") * CY + jnp.where(row < CY + HALO, row, row - ROWS)
        self.row_inside = (y >= 0) & (y < NY) & ((row < CY + HALO) | (row >= ROWS - HALO))

    def get(self, split, c, p):
        ref, at = split.of(c, p)
        return ref[at, :]

    def put(self, split, c, p, value):
        ref, at = split.of(c, p)
        ref[at, :] = value

    def label(self, p):
        ref, at = self.fields.of(0, p, base=LAB0)
        return ref[at, :]

    def right_side(self, c, p):
        ref, at = self.fields.of(c, p, count=PR, base=RHS0 - 1)
        return ref[at, :]

    def summed(self, split, c, p, edge=None):
        f = self.get(split, c, p)
        f = (f + f) + (self.get(split, c, p - 1) + self.get(split, c, p + 1))
        f = (f + f) + (pltpu.roll(f, 1, 0) + pltpu.roll(f, ROWS - 1, 0))
        f = f + (pltpu.roll(f, 1, 1) * self.not_first + pltpu.roll(f, NZ - 1, 1) * self.not_last)
        if edge is not None:
            f = f + self.ends * (0.5 * edge)
        return f

    def coefficients(self, planes):
        for p in planes:
            label = self.label(p)
            k = [jnp.broadcast_to(self.entry(0, e), label.shape) for e in range(6)]
            for m in range(1, LABELS):
                at = label == float(m)
                k = [jnp.where(at, self.entry(m, e), k[e]) for e in range(6)]
            for e in range(6):
                self.put(self.coeff, e, p, k[e])
            self.push(self.flux, p, [self.get(self.fields, c, p) for c in range(3)])

    def weights(self, planes):
        for p in planes:
            for e in range(6):
                k = self.get(self.coeff, e, p)
                around = self.summed(self.coeff, e, p, self.entry(0, e))
                self.put(self.total, e, p, 32.0 * k + around)
                if e < 3:
                    self.put(self.scale, e, p, DAMPING / (MASS_SHIFT + 6.0 * k + 0.25 * around))

    def push(self, flux, p, v):
        pushed = times([self.get(self.coeff, e, p) for e in range(6)], v)
        for c in range(3):
            self.put(flux, c, p, pushed[c])

    def image(self, p, v_split, flux):
        v = [self.get(v_split, c, p) for c in range(3)]
        k = [self.get(self.coeff, e, p) for e in range(6)]
        m = [self.get(self.total, e, p) for e in range(6)]
        around = [self.summed(v_split, c, p) for c in range(3)]
        pushed = [self.summed(flux, c, p) for c in range(3)]
        mine, theirs = times(m, v), times(k, around)
        return v, [MASS_SHIFT * v[c] + 0.25 * (mine[c] - theirs[c] - pushed[c]) for c in range(3)]

    def sweep(self, planes, v_split, flux, to, to_flux, inside=None):
        for p in planes:
            keep = self.row_inside if p >= HALO else self.row_inside & (inside > 0.5)
            v, a = self.image(p, v_split, flux)
            new = []
            for c in range(3):
                value = v[c] + (self.right_side(c, p) - a[c]) * self.get(self.scale, c, p)
                value = jnp.where(keep, value, 0.0)
                self.put(to, c, p, value)
                new.append(value)
            self.push(to_flux, p, new)

    def remainder(self, p, v_split, flux):
        a = self.image(p, v_split, flux)[1]
        return [(self.right_side(c, p) - a[c])[:CY] for c in range(3)]


def fill_halo(fields, side, corner, plane_of, inside):
    tiles = {place: (at, depth) for place, at, depth in corner_rows()}
    for place, base, k in halo_planes():
        plane = (base + plane_of(k)) * ROWS
        at, depth = tiles[place]
        fields[pl.ds(plane, CY), :] = inside * side[rows_of(place, CY), :]
        fields[pl.ds(plane + CY, ROWS - CY), :] = jnp.zeros((ROWS - CY, NZ), F32)
        fields[pl.ds(plane + CY, depth), :] = inside * corner[pl.ds(at, depth), :]
        fields[pl.ds(plane + ROWS - depth, depth), :] = inside * corner[pl.ds(at + depth, depth), :]


def near_part(
    stiffness, own, near, corner_near,
    fields, coeff, total, scale, flux, first, flux_first, second, flux_second, table, last,
):
    for c in range(3):
        for g in range(CX):
            fields[rows_of(c * PX + HALO + g, ROWS), :] = own[rows_of(c * CX + g, ROWS), :]
            fields[rows_of(RHS0 - 1 + c * PR + HALO + g, ROWS), :] = own[rows_of(OWN_RHS0 + c * CX + g, ROWS), :]
    for g in range(CX):
        fields[rows_of(LAB0 + HALO + g, ROWS), :] = own[rows_of(OWN_LAB0 + g, ROWS), :]
    fill_halo(fields, near, corner_near, lambda k: HALO + CX + k, 1.0)
    for m in range(LABELS):
        for e in range(6):
            table[pl.ds(m * 6 + e, 1), :] = jnp.full((1, NZ), stiffness[m, e], F32)

    def whole(ref):
        return Split(0, None, ref)

    grid = Stencil(
        lambda m, e: stiffness[m, e], whole(fields), whole(coeff), whole(total), whole(scale), whole(flux)
    )
    grid.coefficients(range(HALO, PX))
    grid.weights(range(HALO + 1, PX - 1))
    grid.sweep(range(HALO + 1, PX - 1), whole(fields), whole(flux), whole(first), whole(flux_first))
    grid.sweep(range(HALO + 2, PX - 2), whole(first), whole(flux_first), whole(second), whole(flux_second))
    remainder = grid.remainder(HALO + 3, whole(second), whole(flux_second))
    for c in range(3):
        last[rows_of(c, CY), :] = remainder[c]


def far_part(
    far, corner, corner_near, limit, ribbon, cells, mult, at_depth,
    near_fields, near_coeff, near_total, near_scale, near_flux,
    near_first, near_flux_first, near_second, near_flux_second, table, last,
    message, second, updated,
    fields, coeff, total, scale, flux, first, flux_first, flux_second, coarse,
):
    inside = is_inside()
    flip = odd("gx")
    sign = jnp.where(flip == 1, -1.0, 1.0).astype(F32)
    fill_halo(fields, far, corner, lambda k: HALO - 1 - k, inside)
    v0, flux0 = Split(HALO, fields, near_fields), Split(HALO, flux, near_flux)
    v1, flux1 = Split(HALO + 1, first, near_first), Split(HALO + 1, flux_first, near_flux_first)
    v2, flux2 = Split(HALO + 2, second, near_second), Split(HALO + 2, flux_second, near_flux_second)
    grid = Stencil(
        lambda m, e: table[pl.ds(m * 6 + e, 1), :],
        v0,
        Split(HALO, coeff, near_coeff),
        Split(HALO + 1, total, near_total),
        Split(HALO + 1, scale, near_scale),
        flux0,
    )
    grid.coefficients(range(HALO))
    grid.weights(range(1, HALO + 1))
    grid.sweep(range(1, HALO + 1), v0, flux0, v1, flux1, inside)
    grid.sweep(range(2, HALO + 2), v1, flux1, v2, flux2, inside)
    used = slot_number().astype(F32) < limit[...] - 0.5
    column = cells[...] // NZ
    block = CX * CY
    left = []
    for c in range(3):
        v = [grid.get(v2, c, HALO - 1 + i)[:CY] for i in range(CX + 2)]
        jumps = [v[1 + g] - jnp.where(flip == 1, v[g], v[2 + g]) for g in range(CX)]
        left.append(jnp.concatenate(pieces_of(jnp.concatenate(jumps, axis=0)), axis=1))
    left = jnp.concatenate(left, axis=0)
    for j in range(SLOT_ROWS // 2):
        right = at_depth[:, pl.ds(256 * j, 256)]
        picked = jnp.dot(left, jnp.concatenate([right] * 3, axis=0), preferred_element_type=F32)
        at_column = lax.broadcasted_iota(jnp.int32, (block, 256), 0) == paired(column, j)
        for c in range(3):
            jump = jnp.sum(
                jnp.where(at_column, picked[c * block : (c + 1) * block], 0.0), axis=0, keepdims=True
            )
            for i in range(2):
                at = 2 * j + i
                old = mult[c, at : at + 1, :]
                new = old + PENALTY * jump[:, i * 128 : (i + 1) * 128]
                updated[c, at : at + 1, :] = jnp.where(used[at : at + 1], new, old)
    remainders = [grid.remainder(HALO + g, v2, flux2) for g in range(CX - 1)]
    remainders.append([last[rows_of(c, CY), :] for c in range(3)])

    mine = limit[:1]
    theirs = jnp.where(flip == 1, corner_near[pl.ds(CORNER, 1), :], corner[pl.ds(CORNER, 1), :])
    live = []
    for i in range(CX + 1):
        if i == 0:
            top = jnp.where(flip == 1, mine, theirs)
        elif i == CX:
            top = jnp.where(flip == 1, theirs, mine)
        else:
            top = mine
        number = ribbon[3, rows_of(i + flip, CY), :]
        live.append((number > 0.5) & (number < top + 0.5))
    for c in range(3):
        planes = [grid.get(v2, c, HALO - 1 + i)[:CY] for i in range(CX + 2)]
        pushed = []
        for i in range(CX + 1):
            jump = sign * (planes[i] - planes[i + 1])
            at = rows_of(i + flip, CY)
            pushed.append(jnp.where(live[i], ribbon[c, at, :] + PENALTY * jump, 0.0))
        parts = [remainders[g][c] - sign * (pushed[g + 1] - pushed[g]) for g in range(CX)]
        for half in range(2):
            coarse[rows_of(half * 3 + c, CY), :] = parts[2 * half] + parts[2 * half + 1]

    pairs = []
    for half in range(2):
        at = 3 * half * CY
        rows = coarse[pl.ds(at, 3 * CY // 2, stride=2), :] + coarse[pl.ds(at + 1, 3 * CY // 2, stride=2), :]
        pairs.append(rows)
    low_x = jnp.where(flip == 1, pairs[1], pairs[0])
    high_x = jnp.where(flip == 1, pairs[0], pairs[1])
    even_lane = lax.rem(lax.broadcasted_iota(jnp.int32, (1, NZ), 1), 2) == 0
    out = jnp.where(even_lane, low_x + pltpu.roll(low_x, NZ - 1, 1), high_x + pltpu.roll(high_x, 1, 1))
    for s in range(N_GY):
        message[s] = out


def finish(
    updated, low, high, gathered,
    smoothed_out, updated_out, coarse_out,
    coarse, turned, done,
):
    flip = odd("gx")
    split = Split(HALO + 2, low, high)
    copies = [pltpu.make_async_copy(updated, updated_out, done.at[0])]
    for c in range(3):
        for g in range(CX):
            x = g + flip * (CX - 1 - 2 * g)
            ref, at = split.of(c, HALO + g)
            copies.append(
                pltpu.make_async_copy(
                    ref.at[pl.ds(at.start, CY), :], smoothed_out.at[rows_of(c * CX + x, CY), :],
                    done.at[1 + c * CX + g],
                )
            )
    for copy in copies:
        copy.start()
    for c in range(3):
        parts = [gathered[s, pl.ds(c * CY // 2, CY // 2), :] for s in range(N_GY)]
        turned[c] = jnp.transpose(jnp.concatenate(parts, axis=0))
        for x in range(CX // 2):
            coarse[c, pl.ds(x * NZ // 2, NZ // 2), :] = turned[c, pl.ds(x, NZ // 2, stride=2), :]
        copies.append(pltpu.make_async_copy(coarse.at[c], coarse_out.at[c], done.at[1 + 3 * CX + c]))
        copies[-1].start()
    for copy in copies:
        copy.wait()


def in_hbm(array):
    return pltpu.with_memory_space_constraint(array, pltpu.HBM)


def call(kernel, outs, ins, out_specs=None, scratch=(), flops=1000):
    return pl.pallas_call(
        kernel,
        out_shape=outs,
        in_specs=ins,
        out_specs=out_specs or [VMEM] * len(outs),
        scratch_shapes=list(scratch),
        compiler_params=PARAMS,
        cost_estimate=pl.CostEstimate(flops=flops, bytes_accessed=1000, transcendentals=0),
    )


def pair(n):
    return [(i, i ^ 1) for i in range(n)]


def other_x():
    out = []
    for i in range(N_GX):
        for j in range(N_GY):
            partner = (i, j ^ 1) if i in (0, N_GX - 1) else (((i + 1) ^ 1) - 1, j)
            out.append((i * N_GY + j, partner[0] * N_GY + partner[1]))
    return out


def other_y():
    out = []
    for i in range(N_GX):
        for j in range(N_GY):
            partner = (i ^ 1, j) if j in (0, N_GY - 1) else (i, ((j + 1) ^ 1) - 1)
            out.append((i * N_GY + j, partner[0] * N_GY + partner[1]))
    return out


def body(displacement, rhs, labels, stiffness, rows, counts, multipliers):
    block = CX * CY
    copies = 2 + 7 * CX
    slots = jax.ShapeDtypeStruct((SLOT_ROWS, 128), jnp.int32)
    y_other, own, raw_cells, mult = call(
        pack_first,
        [f32(HALO, OWN, NZ), f32(ROOM * CY, NZ), slots, f32(3, SLOT_ROWS, 128)],
        [HBM] * 5,
        scratch=[pltpu.VMEM((block, NZ), jnp.int32), pltpu.SemaphoreType.DMA((copies,))],
    )(
        in_hbm(displacement.reshape(3 * block, NZ)),
        in_hbm(rhs.reshape(3 * block, NZ)),
        in_hbm(labels.reshape(block, NZ)),
        in_hbm(rows.reshape(SLOT_ROWS, 128)),
        in_hbm(multipliers.reshape(3, SLOT_ROWS, 128)),
    )
    y_other = lax.ppermute(y_other, ("gx", "gy"), other_y())
    side = f32(SIDE * CY + IFACE, NZ)
    far, near, cells = call(pack_sides, [side, side, slots], [VMEM] * 3)(own, raw_cells, mult)
    near = lax.ppermute(near, "gx", pair(N_GX))
    far = lax.ppermute(far, ("gx", "gy"), other_x())
    (y_pair,) = call(pack_pair, [f32(HALO, OWN, NZ)], [VMEM] * 2)(own, near)
    y_pair = lax.ppermute(y_pair, "gy", pair(N_GY))
    dense, at_depth = call(
        spread_own, [f32(4, block, NZ), jax.ShapeDtypeStruct((NZ, 8 * 128), BF16)], [VMEM] * 2, flops=5 * 10**9
    )(cells, mult)
    (inner,) = call(pack_wide, [f32(ROOM * ROWS, NZ)], [VMEM], flops=5 * 10**9)(own)
    tile = f32(CORNER + SLOT_ROWS, NZ)
    corner, corner_near, own, limit = call(
        pack_second, [tile, tile, f32(ROOM * ROWS, NZ), f32(SLOT_ROWS, NZ)], [VMEM, VMEM, SMEM, VMEM]
    )(y_other, y_pair, counts, inner)
    corner = lax.ppermute(corner, ("gx", "gy"), other_x())
    corner_near = lax.ppermute(corner_near, "gx", pair(N_GX))
    three, six = f32(3 * PX * ROWS, NZ), f32(6 * PX * ROWS, NZ)
    arrays = [f32(FIELDS * ROWS + SPARE, NZ), six, six] + [three] * 6
    half = call(
        near_part, arrays + [f32(LABELS * 6, NZ), f32(3 * CY, NZ)], [SMEM, VMEM, VMEM, VMEM]
    )(stiffness, own, near, corner_near)
    (ribbon,) = call(spread_before, [f32(4, (CX + 2) * CY, NZ)], [VMEM] * 4)(far, near, dense, half[-1])
    message, low, updated = call(
        far_part,
        [f32(N_GY, 3 * CY // 2, NZ), three, f32(3, SLOT_ROWS, 128)],
        [VMEM] * (8 + len(half)),
        scratch=[pltpu.VMEM(a.shape, F32) for a in arrays[:-1]] + [pltpu.VMEM((6 * CY, NZ), F32)],
    )(far, corner, corner_near, limit, ribbon, cells, mult, at_depth, *half)
    gathered = lax.all_to_all(message, "gy", 0, 0)
    smoothed, updated, coarse = call(
        finish,
        [pltpu.HBM(s, F32) for s in ((3 * block, NZ), (3, SLOT_ROWS, 128), (3, CX // 2 * NZ // 2, NY // 2))],
        [VMEM] * 4,
        out_specs=[HBM] * 3,
        scratch=[
            pltpu.VMEM((3, CX // 2 * NZ // 2, NY // 2), F32),
            pltpu.VMEM((3, NZ, NY // 2), F32),
            pltpu.SemaphoreType.DMA((4 + 3 * CX,)),
        ],
    )(updated, low, half[7], gathered)
    coarse = jnp.swapaxes(coarse.reshape(3, CX // 2, NZ // 2, NY // 2), 2, 3)
    return (smoothed.reshape(3, CX, CY, NZ), coarse, updated.reshape(3, 1, 1, SLOTS))


def solution(mesh):
    return jax.shard_map(
        body,
        mesh=mesh,
        in_specs=(
            P(None, "gx", "gy", None),
            P(None, "gx", "gy", None),
            P("gx", "gy", None),
            P(),
            P("gx", "gy", None),
            P("gx", "gy"),
            P(None, "gx", "gy", None),
        ),
        out_specs=(P(None, "gx", "gy", None), P(None, "gx", None, None), P(None, "gx", "gy", None)),
        check_vma=False,
    )
```

```python
import jax
import jax.numpy as jnp
from jax import lax
from jax.experimental import pallas as pl
from jax.experimental.pallas import tpu as pltpu
from jax.sharding import PartitionSpec as P

SYMMETRIC_INDEX = ((0, 3, 4), (3, 1, 5), (4, 5, 2))
DAMPING = 0.6
MASS_SHIFT = 1.0
PENALTY = 1.0

CX, CY, NZ, SLOTS = 4, 32, 128, 1024
N_GX, N_GY = 32, 8
NX, NY = CX * N_GX, CY * N_GY
LABELS = 8
HALO = 3
PX = CX + 2 * HALO
PR = PX - 2
ROWS = 40
LAB0 = 3 * PX
RHS0 = LAB0 + PX
FIELDS = RHS0 + 3 * PR
OWN_LAB0 = 3 * CX
OWN_RHS0 = OWN_LAB0 + CX
OWN = OWN_RHS0 + 3 * CX
ROOM = 32
SPARE = 8
SIDE = 3 * HALO + HALO + 3 * (HALO - 1)
SLOT_ROWS = SLOTS // 128
IFACE = 4 * SLOT_ROWS
CORNER = 2 * (4 * HALO * HALO + 3 * (HALO - 1) ** 2)
VMEM = pl.BlockSpec(memory_space=pltpu.VMEM)
SMEM = pl.BlockSpec(memory_space=pltpu.SMEM)
HBM = pl.BlockSpec(memory_space=pltpu.HBM)
F32 = jnp.float32
BF16 = jnp.bfloat16
PARAMS = pltpu.CompilerParams(vmem_limit_bytes=32 * 1024 * 1024)


def f32(*shape):
    return jax.ShapeDtypeStruct(shape, F32)


def pieces_of(value):
    high = value.astype(BF16)
    rest = value - high.astype(F32)
    middle = rest.astype(BF16)
    low = (rest - middle.astype(F32)).astype(BF16)
    return (high, middle, low)


def odd(axis):
    return lax.rem(lax.axis_index(axis), 2)


def rows_of(j, height):
    return pl.ds(j * height if isinstance(j, int) else pl.multiple_of(j * height, height), height)


def corner_rows():
    at = 0
    for place in range(SIDE):
        depth = HALO if place < 4 * HALO else HALO - 1
        yield place, at, depth
        at += 2 * depth


def sent_planes():
    place = 0
    for first, depth in [(c * CX, HALO) for c in range(3)] + [(OWN_LAB0, HALO)] + [
        (OWN_RHS0 + c * CX, HALO - 1) for c in range(3)
    ]:
        for k in range(depth):
            yield place, first, k
            place += 1


def halo_planes():
    place = 0
    for first, depth in [(c * PX, HALO) for c in range(3)] + [(LAB0, HALO)] + [
        (RHS0 + c * PR - 1, HALO - 1) for c in range(3)
    ]:
        for k in range(depth):
            yield place, first, k
            place += 1


def slot_number():
    return lax.broadcasted_iota(jnp.int32, (SLOT_ROWS, 128), 0) * 128 + lax.broadcasted_iota(
        jnp.int32, (SLOT_ROWS, 128), 1
    )


def pack_first(
    disp, rhs, labels, cells_in, mult_in,
    y_other, own, cells, mult,
    raw_labels, arrived,
):
    flip = odd("gx")
    pairs = []
    for g in range(CX):
        x = g + flip * (CX - 1 - 2 * g)
        pairs.append((labels.at[rows_of(x, CY)], raw_labels.at[rows_of(g, CY)]))
        for c in range(3):
            pairs.append((disp.at[rows_of(c * CX + x, CY)], own.at[rows_of(c * CX + g, CY)]))
            pairs.append((rhs.at[rows_of(c * CX + x, CY)], own.at[rows_of(OWN_RHS0 + c * CX + g, CY)]))
    pairs += [(cells_in, cells), (mult_in, mult)]
    copies = [pltpu.make_async_copy(a, b, arrived.at[i]) for i, (a, b) in enumerate(pairs)]
    for copy in copies:
        copy.start()
    for copy in copies:
        copy.wait()
    own[pl.ds(OWN_LAB0 * CY, CX * CY), :] = raw_labels[...].astype(F32)
    up = odd("gy") == 0
    for k in range(HALO):
        first = own[pl.ds(k, OWN, stride=CY), :]
        last = own[pl.ds(CY - HALO + k, OWN, stride=CY), :]
        y_other[k] = jnp.where(up, first, last)


def pack_sides(own, raw_cells, mult, far, near, cells):
    flip = odd("gx")
    block_plane = raw_cells[...] // (CY * NZ)
    turned = raw_cells[...] + flip * (CX - 1 - 2 * block_plane) * (CY * NZ)
    cells[...] = turned
    for place, first, k in sent_planes():
        far[rows_of(place, CY), :] = own[rows_of(first + k, CY), :]
        near[rows_of(place, CY), :] = own[rows_of(first + CX - 1 - k, CY), :]
    for side in (far, near):
        side[pl.ds(SIDE * CY, SLOT_ROWS), :] = turned.astype(F32)
        for c in range(3):
            side[pl.ds(SIDE * CY + (1 + c) * SLOT_ROWS, SLOT_ROWS), :] = mult[c]


def pack_pair(own, near, y_pair):
    up = odd("gy") == 0
    for k in range(HALO):
        first = own[pl.ds(k, OWN, stride=CY), :]
        last = own[pl.ds(CY - HALO + k, OWN, stride=CY), :]
        y_pair[k] = jnp.where(up, last, first)


def reach():
    here = lax.axis_index("gy")
    return (
        jnp.where(here > 0, 1.0, 0.0).astype(F32),
        jnp.where(here < N_GY - 1, 1.0, 0.0).astype(F32),
    )


def pack_wide(own, wide):
    for j in range(OWN):
        wide[pl.ds(j * ROWS, CY), :] = own[rows_of(j, CY), :]
        wide[pl.ds(j * ROWS + CY, ROWS - CY), :] = jnp.zeros((ROWS - CY, NZ), F32)


def pack_second(y_other, y_pair, count, inner, dense, corner_far, corner_near, wide, limit):
    low, high = reach()
    up = odd("gy") == 0
    wide[pl.ds(0, OWN * ROWS), :] = inner[pl.ds(0, OWN * ROWS), :]
    for k in range(HALO):
        wide[pl.ds(CY + k, OWN, stride=ROWS), :] = high * jnp.where(up, y_pair[k], y_other[k])
        wide[pl.ds(ROWS - HALO + k, OWN, stride=ROWS), :] = low * jnp.where(up, y_other[k], y_pair[k])
    live = jnp.full((SLOT_ROWS, 128), count[0, 0].astype(F32), F32)
    limit[...] = live
    planes = list(sent_planes())
    for corner, turn in ((corner_far, False), (corner_near, True)):
        for place, at, depth in corner_rows():
            first, k = planes[place][1:]
            base = (first + (CX - 1 - k if turn else k)) * ROWS
            corner[pl.ds(at, depth), :] = wide[pl.ds(base + CY, depth), :]
            corner[pl.ds(at + depth, depth), :] = wide[pl.ds(base + ROWS - depth, depth), :]
        corner[pl.ds(CORNER, SLOT_ROWS), :] = live


def paired(array, j):
    return jnp.concatenate([array[2 * j : 2 * j + 1], array[2 * j + 1 : 2 * j + 2]], axis=1)


def spread(cells, mult, first, columns):
    column = cells // NZ - first
    depth = cells % NZ
    total = jnp.zeros((11 * columns, NZ), F32)
    parts = [piece for c in range(3) for piece in pieces_of(mult[c])]
    parts += pieces_of((slot_number() + 1).astype(F32))[:2]
    for j in range(SLOT_ROWS // 2):
        at_column = lax.broadcasted_iota(jnp.int32, (columns, 256), 0) == paired(column, j)
        at_depth = lax.broadcasted_iota(jnp.int32, (NZ, 256), 0) == paired(depth, j)
        left = [jnp.where(at_column, paired(piece.astype(F32), j), 0.0).astype(BF16) for piece in parts]
        total = total + lax.dot_general(
            jnp.concatenate(left, axis=0),
            jnp.where(at_depth, 1.0, 0.0).astype(BF16),
            (((1,), (1,)), ((), ())),
            preferred_element_type=F32,
        )
    part = [total[i * columns : (i + 1) * columns] for i in range(11)]
    return [part[3 * c] + part[3 * c + 1] + part[3 * c + 2] for c in range(3)] + [part[9] + part[10]]


def spread_own(cells, mult, dense, at_depth):
    depth = cells[...] % NZ
    for j in range(SLOT_ROWS // 2):
        hit = lax.broadcasted_iota(jnp.int32, (NZ, 256), 0) == paired(depth, j)
        at_depth[:, pl.ds(256 * j, 256)] = jnp.where(hit, 1.0, 0.0).astype(BF16)
    values = spread(cells[...], [mult[c] for c in range(3)], 0, CX * CY)
    for i in range(4):
        dense[i] = values[i]


def is_inside():
    here = lax.axis_index("gx")
    return jnp.where((here > 0) & (here < N_GX - 1), 1.0, 0.0).astype(F32)


def spread_before(far, near, dense, last, ribbon):
    flip = odd("gx")

    def at(i):
        a = far[pl.ds(SIDE * CY + i * SLOT_ROWS, SLOT_ROWS), :]
        b = near[pl.ds(SIDE * CY + i * SLOT_ROWS, SLOT_ROWS), :]
        return jnp.where(flip == 1, b, a)

    values = spread(at(0).astype(jnp.int32), [at(1 + c) for c in range(3)], flip * (CX - 1) * CY, CY)
    values[3] = values[3] * jnp.where(flip == 1, 1.0, is_inside())
    for i in range(4):
        ribbon[i, pl.ds(0, CY), :] = values[i]
        ribbon[i, pl.ds(CY, CX * CY), :] = dense[i]
        ribbon[i, pl.ds((CX + 1) * CY, CY), :] = values[i]


def times(k, v):
    return [
        k[SYMMETRIC_INDEX[c][0]] * v[0] + k[SYMMETRIC_INDEX[c][1]] * v[1] + k[SYMMETRIC_INDEX[c][2]] * v[2]
        for c in range(3)
    ]


class Split:
    def __init__(self, at, low, high):
        self.at, self.low, self.high = at, low, high

    def of(self, c, p, count=PX, base=0):
        ref = self.low if p < self.at else self.high
        return ref, rows_of(base + c * count + p, ROWS)


class Stencil:
    def __init__(self, entry, fields, coeff, total, scale, flux):
        self.entry, self.fields, self.coeff, self.total, self.scale, self.flux = (
            entry, fields, coeff, total, scale, flux
        )
        lane = lax.broadcasted_iota(jnp.int32, (1, NZ), 1)
        self.not_first = jnp.where(lane == 0, 0.0, 0.5)
        self.not_last = jnp.where(lane == NZ - 1, 0.0, 0.5)
        self.ends = jnp.where((lane == 0) | (lane == NZ - 1), 16.0, 0.0)
        row = lax.broadcasted_iota(jnp.int32, (ROWS, NZ), 0)
        y = lax.axis_index("gy") * CY + jnp.where(row < CY + HALO, row, row - ROWS)
        self.row_inside = (y >= 0) & (y < NY) & ((row < CY + HALO) | (row >= ROWS - HALO))

    def get(self, split, c, p):
        ref, at = split.of(c, p)
        return ref[at, :]

    def put(self, split, c, p, value):
        ref, at = split.of(c, p)
        ref[at, :] = value

    def label(self, p):
        ref, at = self.fields.of(0, p, base=LAB0)
        return ref[at, :]

    def right_side(self, c, p):
        ref, at = self.fields.of(c, p, count=PR, base=RHS0 - 1)
        return ref[at, :]

    def summed(self, split, c, p, edge=None):
        f = self.get(split, c, p)
        f = (f + f) + (self.get(split, c, p - 1) + self.get(split, c, p + 1))
        f = (f + f) + (pltpu.roll(f, 1, 0) + pltpu.roll(f, ROWS - 1, 0))
        f = f + (pltpu.roll(f, 1, 1) * self.not_first + pltpu.roll(f, NZ - 1, 1) * self.not_last)
        if edge is not None:
            f = f + self.ends * (0.5 * edge)
        return f

    def coefficients(self, planes):
        for p in planes:
            label = self.label(p)
            k = [jnp.broadcast_to(self.entry(0, e), label.shape) for e in range(6)]
            for m in range(1, LABELS):
                at = label == float(m)
                k = [jnp.where(at, self.entry(m, e), k[e]) for e in range(6)]
            for e in range(6):
                self.put(self.coeff, e, p, k[e])
            self.push(self.flux, p, [self.get(self.fields, c, p) for c in range(3)])

    def weights(self, planes):
        for p in planes:
            for e in range(6):
                k = self.get(self.coeff, e, p)
                around = self.summed(self.coeff, e, p, self.entry(0, e))
                self.put(self.total, e, p, 32.0 * k + around)
                if e < 3:
                    self.put(self.scale, e, p, DAMPING / (MASS_SHIFT + 6.0 * k + 0.25 * around))

    def push(self, flux, p, v):
        pushed = times([self.get(self.coeff, e, p) for e in range(6)], v)
        for c in range(3):
            self.put(flux, c, p, pushed[c])

    def image(self, p, v_split, flux):
        v = [self.get(v_split, c, p) for c in range(3)]
        k = [self.get(self.coeff, e, p) for e in range(6)]
        m = [self.get(self.total, e, p) for e in range(6)]
        around = [self.summed(v_split, c, p) for c in range(3)]
        pushed = [self.summed(flux, c, p) for c in range(3)]
        mine, theirs = times(m, v), times(k, around)
        return v, [MASS_SHIFT * v[c] + 0.25 * (mine[c] - theirs[c] - pushed[c]) for c in range(3)]

    def sweep(self, planes, v_split, flux, to, to_flux, inside=None):
        for p in planes:
            keep = self.row_inside if p >= HALO else self.row_inside & (inside > 0.5)
            v, a = self.image(p, v_split, flux)
            new = []
            for c in range(3):
                value = v[c] + (self.right_side(c, p) - a[c]) * self.get(self.scale, c, p)
                value = jnp.where(keep, value, 0.0)
                self.put(to, c, p, value)
                new.append(value)
            self.push(to_flux, p, new)

    def remainder(self, p, v_split, flux):
        a = self.image(p, v_split, flux)[1]
        return [(self.right_side(c, p) - a[c])[:CY] for c in range(3)]


def fill_halo(fields, side, corner, plane_of, inside):
    tiles = {place: (at, depth) for place, at, depth in corner_rows()}
    for place, base, k in halo_planes():
        plane = (base + plane_of(k)) * ROWS
        at, depth = tiles[place]
        fields[pl.ds(plane, CY), :] = inside * side[rows_of(place, CY), :]
        fields[pl.ds(plane + CY, ROWS - CY), :] = jnp.zeros((ROWS - CY, NZ), F32)
        fields[pl.ds(plane + CY, depth), :] = inside * corner[pl.ds(at, depth), :]
        fields[pl.ds(plane + ROWS - depth, depth), :] = inside * corner[pl.ds(at + depth, depth), :]


def near_part(
    stiffness, own, near, corner_near,
    fields, coeff, total, scale, flux, first, flux_first, second, flux_second, table, last,
):
    for c in range(3):
        for g in range(CX):
            fields[rows_of(c * PX + HALO + g, ROWS), :] = own[rows_of(c * CX + g, ROWS), :]
            fields[rows_of(RHS0 - 1 + c * PR + HALO + g, ROWS), :] = own[rows_of(OWN_RHS0 + c * CX + g, ROWS), :]
    for g in range(CX):
        fields[rows_of(LAB0 + HALO + g, ROWS), :] = own[rows_of(OWN_LAB0 + g, ROWS), :]
    fill_halo(fields, near, corner_near, lambda k: HALO + CX + k, 1.0)
    for m in range(LABELS):
        for e in range(6):
            table[pl.ds(m * 6 + e, 1), :] = jnp.full((1, NZ), stiffness[m, e], F32)

    def whole(ref):
        return Split(0, None, ref)

    grid = Stencil(
        lambda m, e: stiffness[m, e], whole(fields), whole(coeff), whole(total), whole(scale), whole(flux)
    )
    grid.coefficients(range(HALO, PX))
    grid.weights(range(HALO + 1, PX - 1))
    grid.sweep(range(HALO + 1, PX - 1), whole(fields), whole(flux), whole(first), whole(flux_first))
    grid.sweep(range(HALO + 2, PX - 2), whole(first), whole(flux_first), whole(second), whole(flux_second))
    remainder = grid.remainder(HALO + 3, whole(second), whole(flux_second))
    for c in range(3):
        last[rows_of(c, CY), :] = remainder[c]


def far_part(
    far, corner, corner_near, limit, ribbon, cells, mult, at_depth,
    near_fields, near_coeff, near_total, near_scale, near_flux,
    near_first, near_flux_first, near_second, near_flux_second, table, last,
    message, second, updated,
    fields, coeff, total, scale, flux, first, flux_first, flux_second, coarse,
):
    inside = is_inside()
    flip = odd("gx")
    sign = jnp.where(flip == 1, -1.0, 1.0).astype(F32)
    fill_halo(fields, far, corner, lambda k: HALO - 1 - k, inside)
    v0, flux0 = Split(HALO, fields, near_fields), Split(HALO, flux, near_flux)
    v1, flux1 = Split(HALO + 1, first, near_first), Split(HALO + 1, flux_first, near_flux_first)
    v2, flux2 = Split(HALO + 2, second, near_second), Split(HALO + 2, flux_second, near_flux_second)
    grid = Stencil(
        lambda m, e: table[pl.ds(m * 6 + e, 1), :],
        v0,
        Split(HALO, coeff, near_coeff),
        Split(HALO + 1, total, near_total),
        Split(HALO + 1, scale, near_scale),
        flux0,
    )
    grid.coefficients(range(HALO))
    grid.weights(range(1, HALO + 1))
    grid.sweep(range(1, HALO + 1), v0, flux0, v1, flux1, inside)
    grid.sweep(range(2, HALO + 2), v1, flux1, v2, flux2, inside)
    used = slot_number().astype(F32) < limit[...] - 0.5
    column = cells[...] // NZ
    block = CX * CY
    left = []
    for c in range(3):
        v = [grid.get(v2, c, HALO - 1 + i)[:CY] for i in range(CX + 2)]
        jumps = [v[1 + g] - jnp.where(flip == 1, v[g], v[2 + g]) for g in range(CX)]
        left.append(jnp.concatenate(pieces_of(jnp.concatenate(jumps, axis=0)), axis=1))
    left = jnp.concatenate(left, axis=0)
    for j in range(SLOT_ROWS // 2):
        right = at_depth[:, pl.ds(256 * j, 256)]
        picked = jnp.dot(left, jnp.concatenate([right] * 3, axis=0), preferred_element_type=F32)
        at_column = lax.broadcasted_iota(jnp.int32, (block, 256), 0) == paired(column, j)
        for c in range(3):
            jump = jnp.sum(
                jnp.where(at_column, picked[c * block : (c + 1) * block], 0.0), axis=0, keepdims=True
            )
            for i in range(2):
                at = 2 * j + i
                old = mult[c, at : at + 1, :]
                new = old + PENALTY * jump[:, i * 128 : (i + 1) * 128]
                updated[c, at : at + 1, :] = jnp.where(used[at : at + 1], new, old)
    remainders = [grid.remainder(HALO + g, v2, flux2) for g in range(CX - 1)]
    remainders.append([last[rows_of(c, CY), :] for c in range(3)])

    mine = limit[:1]
    theirs = jnp.where(flip == 1, corner_near[pl.ds(CORNER, 1), :], corner[pl.ds(CORNER, 1), :])
    live = []
    for i in range(CX + 1):
        if i == 0:
            top = jnp.where(flip == 1, mine, theirs)
        elif i == CX:
            top = jnp.where(flip == 1, theirs, mine)
        else:
            top = mine
        number = ribbon[3, rows_of(i + flip, CY), :]
        live.append((number > 0.5) & (number < top + 0.5))
    for c in range(3):
        planes = [grid.get(v2, c, HALO - 1 + i)[:CY] for i in range(CX + 2)]
        pushed = []
        for i in range(CX + 1):
            jump = sign * (planes[i] - planes[i + 1])
            at = rows_of(i + flip, CY)
            pushed.append(jnp.where(live[i], ribbon[c, at, :] + PENALTY * jump, 0.0))
        parts = [remainders[g][c] - sign * (pushed[g + 1] - pushed[g]) for g in range(CX)]
        for half in range(2):
            coarse[rows_of(half * 3 + c, CY), :] = parts[2 * half] + parts[2 * half + 1]

    pairs = []
    for half in range(2):
        at = 3 * half * CY
        rows = coarse[pl.ds(at, 3 * CY // 2, stride=2), :] + coarse[pl.ds(at + 1, 3 * CY // 2, stride=2), :]
        pairs.append(rows)
    low_x = jnp.where(flip == 1, pairs[1], pairs[0])
    high_x = jnp.where(flip == 1, pairs[0], pairs[1])
    even_lane = lax.rem(lax.broadcasted_iota(jnp.int32, (1, NZ), 1), 2) == 0
    out = jnp.where(even_lane, low_x + pltpu.roll(low_x, NZ - 1, 1), high_x + pltpu.roll(high_x, 1, 1))
    for s in range(N_GY):
        message[s] = out


def finish(
    updated, low, high, gathered,
    smoothed_out, updated_out, coarse_out,
    coarse, turned, done,
):
    flip = odd("gx")
    split = Split(HALO + 2, low, high)
    copies = [pltpu.make_async_copy(updated, updated_out, done.at[0])]
    for c in range(3):
        for g in range(CX):
            x = g + flip * (CX - 1 - 2 * g)
            ref, at = split.of(c, HALO + g)
            copies.append(
                pltpu.make_async_copy(
                    ref.at[pl.ds(at.start, CY), :], smoothed_out.at[rows_of(c * CX + x, CY), :],
                    done.at[1 + c * CX + g],
                )
            )
    for copy in copies:
        copy.start()
    for c in range(3):
        parts = [gathered[s, pl.ds(c * CY // 2, CY // 2), :] for s in range(N_GY)]
        turned[c] = jnp.transpose(jnp.concatenate(parts, axis=0))
        for x in range(CX // 2):
            coarse[c, pl.ds(x * NZ // 2, NZ // 2), :] = turned[c, pl.ds(x, NZ // 2, stride=2), :]
        copies.append(pltpu.make_async_copy(coarse.at[c], coarse_out.at[c], done.at[1 + 3 * CX + c]))
        copies[-1].start()
    for copy in copies:
        copy.wait()


def in_hbm(array):
    return pltpu.with_memory_space_constraint(array, pltpu.HBM)


def call(kernel, outs, ins, out_specs=None, scratch=(), flops=1000):
    return pl.pallas_call(
        kernel,
        out_shape=outs,
        in_specs=ins,
        out_specs=out_specs or [VMEM] * len(outs),
        scratch_shapes=list(scratch),
        compiler_params=PARAMS,
        cost_estimate=pl.CostEstimate(flops=flops, bytes_accessed=1000, transcendentals=0),
    )


def pair(n):
    return [(i, i ^ 1) for i in range(n)]


def other_x():
    out = []
    for i in range(N_GX):
        for j in range(N_GY):
            partner = (i, j ^ 1) if i in (0, N_GX - 1) else (((i + 1) ^ 1) - 1, j)
            out.append((i * N_GY + j, partner[0] * N_GY + partner[1]))
    return out


def other_y():
    out = []
    for i in range(N_GX):
        for j in range(N_GY):
            partner = (i ^ 1, j) if j in (0, N_GY - 1) else (i, ((j + 1) ^ 1) - 1)
            out.append((i * N_GY + j, partner[0] * N_GY + partner[1]))
    return out


def body(displacement, rhs, labels, stiffness, rows, counts, multipliers):
    block = CX * CY
    copies = 2 + 7 * CX
    slots = jax.ShapeDtypeStruct((SLOT_ROWS, 128), jnp.int32)
    y_other, own, raw_cells, mult = call(
        pack_first,
        [f32(HALO, OWN, NZ), f32(ROOM * CY, NZ), slots, f32(3, SLOT_ROWS, 128)],
        [HBM] * 5,
        scratch=[pltpu.VMEM((block, NZ), jnp.int32), pltpu.SemaphoreType.DMA((copies,))],
    )(
        in_hbm(displacement.reshape(3 * block, NZ)),
        in_hbm(rhs.reshape(3 * block, NZ)),
        in_hbm(labels.reshape(block, NZ)),
        in_hbm(rows.reshape(SLOT_ROWS, 128)),
        in_hbm(multipliers.reshape(3, SLOT_ROWS, 128)),
    )
    y_other = lax.ppermute(y_other, ("gx", "gy"), other_y())
    side = f32(SIDE * CY + IFACE, NZ)
    far, near, cells = call(pack_sides, [side, side, slots], [VMEM] * 3)(own, raw_cells, mult)
    near = lax.ppermute(near, "gx", pair(N_GX))
    far = lax.ppermute(far, ("gx", "gy"), other_x())
    (y_pair,) = call(pack_pair, [f32(HALO, OWN, NZ)], [VMEM] * 2)(own, near)
    y_pair = lax.ppermute(y_pair, "gy", pair(N_GY))
    dense, at_depth = call(
        spread_own, [f32(4, block, NZ), jax.ShapeDtypeStruct((NZ, 8 * 128), BF16)], [VMEM] * 2, flops=5 * 10**9
    )(cells, mult)
    (inner,) = call(pack_wide, [f32(ROOM * ROWS, NZ)], [VMEM], flops=5 * 10**9)(own)
    tile = f32(CORNER + SLOT_ROWS, NZ)
    corner, corner_near, own, limit = call(
        pack_second, [tile, tile, f32(ROOM * ROWS, NZ), f32(SLOT_ROWS, NZ)], [VMEM, VMEM, SMEM, VMEM, VMEM]
    )(y_other, y_pair, counts, inner, dense)
    corner = lax.ppermute(corner, ("gx", "gy"), other_x())
    corner_near = lax.ppermute(corner_near, "gx", pair(N_GX))
    three, six = f32(3 * PX * ROWS, NZ), f32(6 * PX * ROWS, NZ)
    arrays = [f32(FIELDS * ROWS + SPARE, NZ), six, six] + [three] * 6
    half = call(
        near_part, arrays + [f32(LABELS * 6, NZ), f32(3 * CY, NZ)], [SMEM, VMEM, VMEM, VMEM]
    )(stiffness, own, near, corner_near)
    (ribbon,) = call(spread_before, [f32(4, (CX + 2) * CY, NZ)], [VMEM] * 4)(far, near, dense, half[-1])
    message, low, updated = call(
        far_part,
        [f32(N_GY, 3 * CY // 2, NZ), three, f32(3, SLOT_ROWS, 128)],
        [VMEM] * (8 + len(half)),
        scratch=[pltpu.VMEM(a.shape, F32) for a in arrays[:-1]] + [pltpu.VMEM((6 * CY, NZ), F32)],
    )(far, corner, corner_near, limit, ribbon, cells, mult, at_depth, *half)
    gathered = lax.all_to_all(message, "gy", 0, 0)
    smoothed, updated, coarse = call(
        finish,
        [pltpu.HBM(s, F32) for s in ((3 * block, NZ), (3, SLOT_ROWS, 128), (3, CX // 2 * NZ // 2, NY // 2))],
        [VMEM] * 4,
        out_specs=[HBM] * 3,
        scratch=[
            pltpu.VMEM((3, CX // 2 * NZ // 2, NY // 2), F32),
            pltpu.VMEM((3, NZ, NY // 2), F32),
            pltpu.SemaphoreType.DMA((4 + 3 * CX,)),
        ],
    )(updated, low, half[7], gathered)
    coarse = jnp.swapaxes(coarse.reshape(3, CX // 2, NZ // 2, NY // 2), 2, 3)
    return (smoothed.reshape(3, CX, CY, NZ), coarse, updated.reshape(3, 1, 1, SLOTS))


def solution(mesh):
    return jax.shard_map(
        body,
        mesh=mesh,
        in_specs=(
            P(None, "gx", "gy", None),
            P(None, "gx", "gy", None),
            P("gx", "gy", None),
            P(),
            P("gx", "gy", None),
            P("gx", "gy"),
            P(None, "gx", "gy", None),
        ),
        out_specs=(P(None, "gx", "gy", None), P(None, "gx", None, None), P(None, "gx", "gy", None)),
        check_vma=False,
    )
```

```python
import jax
import jax.numpy as jnp
from jax import lax
from jax.experimental import pallas as pl
from jax.experimental.pallas import tpu as pltpu
from jax.sharding import PartitionSpec as P

SYMMETRIC_INDEX = ((0, 3, 4), (3, 1, 5), (4, 5, 2))
DAMPING = 0.6
MASS_SHIFT = 1.0
PENALTY = 1.0

CX, CY, NZ, SLOTS = 4, 32, 128, 1024
N_GX, N_GY = 32, 8
NX, NY = CX * N_GX, CY * N_GY
LABELS = 8
HALO = 3
PX = CX + 2 * HALO
PR = PX - 2
ROWS = 40
LAB0 = 3 * PX
RHS0 = LAB0 + PX
FIELDS = RHS0 + 3 * PR
OWN_LAB0 = 3 * CX
OWN_RHS0 = OWN_LAB0 + CX
OWN = OWN_RHS0 + 3 * CX
ROOM = 32
SPARE = 8
SIDE = 3 * HALO + HALO + 3 * (HALO - 1)
SLOT_ROWS = SLOTS // 128
IFACE = 4 * SLOT_ROWS
CORNER = 2 * (4 * HALO * HALO + 3 * (HALO - 1) ** 2)
VMEM = pl.BlockSpec(memory_space=pltpu.VMEM)
SMEM = pl.BlockSpec(memory_space=pltpu.SMEM)
HBM = pl.BlockSpec(memory_space=pltpu.HBM)
F32 = jnp.float32
BF16 = jnp.bfloat16
PARAMS = pltpu.CompilerParams(vmem_limit_bytes=32 * 1024 * 1024)


def f32(*shape):
    return jax.ShapeDtypeStruct(shape, F32)


def pieces_of(value):
    high = value.astype(BF16)
    rest = value - high.astype(F32)
    middle = rest.astype(BF16)
    low = (rest - middle.astype(F32)).astype(BF16)
    return (high, middle, low)


def odd(axis):
    return lax.rem(lax.axis_index(axis), 2)


def rows_of(j, height):
    return pl.ds(j * height if isinstance(j, int) else pl.multiple_of(j * height, height), height)


def corner_rows():
    at = 0
    for place in range(SIDE):
        depth = HALO if place < 4 * HALO else HALO - 1
        yield place, at, depth
        at += 2 * depth


def sent_planes():
    place = 0
    for first, depth in [(c * CX, HALO) for c in range(3)] + [(OWN_LAB0, HALO)] + [
        (OWN_RHS0 + c * CX, HALO - 1) for c in range(3)
    ]:
        for k in range(depth):
            yield place, first, k
            place += 1


def halo_planes():
    place = 0
    for first, depth in [(c * PX, HALO) for c in range(3)] + [(LAB0, HALO)] + [
        (RHS0 + c * PR - 1, HALO - 1) for c in range(3)
    ]:
        for k in range(depth):
            yield place, first, k
            place += 1


def slot_number():
    return lax.broadcasted_iota(jnp.int32, (SLOT_ROWS, 128), 0) * 128 + lax.broadcasted_iota(
        jnp.int32, (SLOT_ROWS, 128), 1
    )


def pack_first(
    disp, rhs, labels, cells_in, mult_in,
    y_other, own, cells, mult,
    raw_labels, arrived,
):
    flip = odd("gx")
    pairs = []
    for g in range(CX):
        x = g + flip * (CX - 1 - 2 * g)
        pairs.append((labels.at[rows_of(x, CY)], raw_labels.at[rows_of(g, CY)]))
        for c in range(3):
            pairs.append((disp.at[rows_of(c * CX + x, CY)], own.at[rows_of(c * CX + g, CY)]))
            pairs.append((rhs.at[rows_of(c * CX + x, CY)], own.at[rows_of(OWN_RHS0 + c * CX + g, CY)]))
    pairs += [(cells_in, cells), (mult_in, mult)]
    copies = [pltpu.make_async_copy(a, b, arrived.at[i]) for i, (a, b) in enumerate(pairs)]
    for copy in copies:
        copy.start()
    for copy in copies:
        copy.wait()
    own[pl.ds(OWN_LAB0 * CY, CX * CY), :] = raw_labels[...].astype(F32)
    up = odd("gy") == 0
    for k in range(HALO):
        first = own[pl.ds(k, OWN, stride=CY), :]
        last = own[pl.ds(CY - HALO + k, OWN, stride=CY), :]
        y_other[k] = jnp.where(up, first, last)


def pack_sides(own, raw_cells, mult, far, near, cells):
    flip = odd("gx")
    block_plane = raw_cells[...] // (CY * NZ)
    turned = raw_cells[...] + flip * (CX - 1 - 2 * block_plane) * (CY * NZ)
    cells[...] = turned
    for place, first, k in sent_planes():
        far[rows_of(place, CY), :] = own[rows_of(first + k, CY), :]
        near[rows_of(place, CY), :] = own[rows_of(first + CX - 1 - k, CY), :]
    for side in (far, near):
        side[pl.ds(SIDE * CY, SLOT_ROWS), :] = turned.astype(F32)
        for c in range(3):
            side[pl.ds(SIDE * CY + (1 + c) * SLOT_ROWS, SLOT_ROWS), :] = mult[c]


def pack_pair(own, near, y_pair):
    up = odd("gy") == 0
    for k in range(HALO):
        first = own[pl.ds(k, OWN, stride=CY), :]
        last = own[pl.ds(CY - HALO + k, OWN, stride=CY), :]
        y_pair[k] = jnp.where(up, last, first)


def reach():
    here = lax.axis_index("gy")
    return (
        jnp.where(here > 0, 1.0, 0.0).astype(F32),
        jnp.where(here < N_GY - 1, 1.0, 0.0).astype(F32),
    )


def pack_wide(own, wide):
    for j in range(OWN):
        wide[pl.ds(j * ROWS, CY), :] = own[rows_of(j, CY), :]
        wide[pl.ds(j * ROWS + CY, ROWS - CY), :] = jnp.zeros((ROWS - CY, NZ), F32)


def pack_second(y_other, y_pair, count, inner, dense, corner_far, corner_near, wide, limit):
    low, high = reach()
    up = odd("gy") == 0
    wide[pl.ds(0, OWN * ROWS), :] = inner[pl.ds(0, OWN * ROWS), :]
    for k in range(HALO):
        wide[pl.ds(CY + k, OWN, stride=ROWS), :] = high * jnp.where(up, y_pair[k], y_other[k])
        wide[pl.ds(ROWS - HALO + k, OWN, stride=ROWS), :] = low * jnp.where(up, y_other[k], y_pair[k])
    live = jnp.full((SLOT_ROWS, 128), count[0, 0].astype(F32), F32)
    limit[...] = live
    planes = list(sent_planes())
    for corner, turn in ((corner_far, False), (corner_near, True)):
        for place, at, depth in corner_rows():
            first, k = planes[place][1:]
            base = (first + (CX - 1 - k if turn else k)) * ROWS
            corner[pl.ds(at, depth), :] = wide[pl.ds(base + CY, depth), :]
            corner[pl.ds(at + depth, depth), :] = wide[pl.ds(base + ROWS - depth, depth), :]
        corner[pl.ds(CORNER, SLOT_ROWS), :] = live


def paired(array, j):
    return jnp.concatenate([array[2 * j : 2 * j + 1], array[2 * j + 1 : 2 * j + 2]], axis=1)


def spread(cells, mult, first, columns):
    column = cells // NZ - first
    depth = cells % NZ
    total = jnp.zeros((11 * columns, NZ), F32)
    parts = [piece for c in range(3) for piece in pieces_of(mult[c])]
    parts += pieces_of((slot_number() + 1).astype(F32))[:2]
    for j in range(SLOT_ROWS // 2):
        at_column = lax.broadcasted_iota(jnp.int32, (columns, 256), 0) == paired(column, j)
        at_depth = lax.broadcasted_iota(jnp.int32, (NZ, 256), 0) == paired(depth, j)
        left = [jnp.where(at_column, paired(piece.astype(F32), j), 0.0).astype(BF16) for piece in parts]
        total = total + lax.dot_general(
            jnp.concatenate(left, axis=0),
            jnp.where(at_depth, 1.0, 0.0).astype(BF16),
            (((1,), (1,)), ((), ())),
            preferred_element_type=F32,
        )
    part = [total[i * columns : (i + 1) * columns] for i in range(11)]
    return [part[3 * c] + part[3 * c + 1] + part[3 * c + 2] for c in range(3)] + [part[9] + part[10]]


def depth_table(cells, at_depth):
    depth = cells[...] % NZ
    for j in range(SLOT_ROWS // 2):
        hit = lax.broadcasted_iota(jnp.int32, (NZ, 256), 0) == paired(depth, j)
        at_depth[:, pl.ds(256 * j, 256)] = jnp.where(hit, 1.0, 0.0).astype(BF16)


def spread_own(cells, mult, dense):
    values = spread(cells[...], [mult[c] for c in range(3)], 0, CX * CY)
    for i in range(4):
        dense[i] = values[i]


def is_inside():
    here = lax.axis_index("gx")
    return jnp.where((here > 0) & (here < N_GX - 1), 1.0, 0.0).astype(F32)


def spread_before(far, near, dense, last, ribbon):
    flip = odd("gx")

    def at(i):
        a = far[pl.ds(SIDE * CY + i * SLOT_ROWS, SLOT_ROWS), :]
        b = near[pl.ds(SIDE * CY + i * SLOT_ROWS, SLOT_ROWS), :]
        return jnp.where(flip == 1, b, a)

    values = spread(at(0).astype(jnp.int32), [at(1 + c) for c in range(3)], flip * (CX - 1) * CY, CY)
    values[3] = values[3] * jnp.where(flip == 1, 1.0, is_inside())
    for i in range(4):
        ribbon[i, pl.ds(0, CY), :] = values[i]
        ribbon[i, pl.ds(CY, CX * CY), :] = dense[i]
        ribbon[i, pl.ds((CX + 1) * CY, CY), :] = values[i]


def times(k, v):
    return [
        k[SYMMETRIC_INDEX[c][0]] * v[0] + k[SYMMETRIC_INDEX[c][1]] * v[1] + k[SYMMETRIC_INDEX[c][2]] * v[2]
        for c in range(3)
    ]


class Split:
    def __init__(self, at, low, high):
        self.at, self.low, self.high = at, low, high

    def of(self, c, p, count=PX, base=0):
        ref = self.low if p < self.at else self.high
        return ref, rows_of(base + c * count + p, ROWS)


class Stencil:
    def __init__(self, entry, fields, coeff, total, scale, flux):
        self.entry, self.fields, self.coeff, self.total, self.scale, self.flux = (
            entry, fields, coeff, total, scale, flux
        )
        lane = lax.broadcasted_iota(jnp.int32, (1, NZ), 1)
        self.not_first = jnp.where(lane == 0, 0.0, 0.5)
        self.not_last = jnp.where(lane == NZ - 1, 0.0, 0.5)
        self.ends = jnp.where((lane == 0) | (lane == NZ - 1), 16.0, 0.0)
        row = lax.broadcasted_iota(jnp.int32, (ROWS, NZ), 0)
        y = lax.axis_index("gy") * CY + jnp.where(row < CY + HALO, row, row - ROWS)
        self.row_inside = (y >= 0) & (y < NY) & ((row < CY + HALO) | (row >= ROWS - HALO))

    def get(self, split, c, p):
        ref, at = split.of(c, p)
        return ref[at, :]

    def put(self, split, c, p, value):
        ref, at = split.of(c, p)
        ref[at, :] = value

    def label(self, p):
        ref, at = self.fields.of(0, p, base=LAB0)
        return ref[at, :]

    def right_side(self, c, p):
        ref, at = self.fields.of(c, p, count=PR, base=RHS0 - 1)
        return ref[at, :]

    def summed(self, split, c, p, edge=None):
        f = self.get(split, c, p)
        f = (f + f) + (self.get(split, c, p - 1) + self.get(split, c, p + 1))
        f = (f + f) + (pltpu.roll(f, 1, 0) + pltpu.roll(f, ROWS - 1, 0))
        f = f + (pltpu.roll(f, 1, 1) * self.not_first + pltpu.roll(f, NZ - 1, 1) * self.not_last)
        if edge is not None:
            f = f + self.ends * (0.5 * edge)
        return f

    def coefficients(self, planes):
        for p in planes:
            label = self.label(p)
            k = [jnp.broadcast_to(self.entry(0, e), label.shape) for e in range(6)]
            for m in range(1, LABELS):
                at = label == float(m)
                k = [jnp.where(at, self.entry(m, e), k[e]) for e in range(6)]
            for e in range(6):
                self.put(self.coeff, e, p, k[e])
            self.push(self.flux, p, [self.get(self.fields, c, p) for c in range(3)])

    def weights(self, planes):
        for p in planes:
            for e in range(6):
                k = self.get(self.coeff, e, p)
                around = self.summed(self.coeff, e, p, self.entry(0, e))
                self.put(self.total, e, p, 32.0 * k + around)
                if e < 3:
                    self.put(self.scale, e, p, DAMPING / (MASS_SHIFT + 6.0 * k + 0.25 * around))

    def push(self, flux, p, v):
        pushed = times([self.get(self.coeff, e, p) for e in range(6)], v)
        for c in range(3):
            self.put(flux, c, p, pushed[c])

    def image(self, p, v_split, flux):
        v = [self.get(v_split, c, p) for c in range(3)]
        k = [self.get(self.coeff, e, p) for e in range(6)]
        m = [self.get(self.total, e, p) for e in range(6)]
        around = [self.summed(v_split, c, p) for c in range(3)]
        pushed = [self.summed(flux, c, p) for c in range(3)]
        mine, theirs = times(m, v), times(k, around)
        return v, [MASS_SHIFT * v[c] + 0.25 * (mine[c] - theirs[c] - pushed[c]) for c in range(3)]

    def sweep(self, planes, v_split, flux, to, to_flux, inside=None):
        for p in planes:
            keep = self.row_inside if p >= HALO else self.row_inside & (inside > 0.5)
            v, a = self.image(p, v_split, flux)
            new = []
            for c in range(3):
                value = v[c] + (self.right_side(c, p) - a[c]) * self.get(self.scale, c, p)
                value = jnp.where(keep, value, 0.0)
                self.put(to, c, p, value)
                new.append(value)
            self.push(to_flux, p, new)

    def remainder(self, p, v_split, flux):
        a = self.image(p, v_split, flux)[1]
        return [(self.right_side(c, p) - a[c])[:CY] for c in range(3)]


def fill_halo(fields, side, corner, plane_of, inside):
    tiles = {place: (at, depth) for place, at, depth in corner_rows()}
    for place, base, k in halo_planes():
        plane = (base + plane_of(k)) * ROWS
        at, depth = tiles[place]
        fields[pl.ds(plane, CY), :] = inside * side[rows_of(place, CY), :]
        fields[pl.ds(plane + CY, ROWS - CY), :] = jnp.zeros((ROWS - CY, NZ), F32)
        fields[pl.ds(plane + CY, depth), :] = inside * corner[pl.ds(at, depth), :]
        fields[pl.ds(plane + ROWS - depth, depth), :] = inside * corner[pl.ds(at + depth, depth), :]


def near_part(
    stiffness, own, near, corner_near,
    fields, coeff, total, scale, flux, first, flux_first, second, flux_second, table, last,
):
    for c in range(3):
        for g in range(CX):
            fields[rows_of(c * PX + HALO + g, ROWS), :] = own[rows_of(c * CX + g, ROWS), :]
            fields[rows_of(RHS0 - 1 + c * PR + HALO + g, ROWS), :] = own[rows_of(OWN_RHS0 + c * CX + g, ROWS), :]
    for g in range(CX):
        fields[rows_of(LAB0 + HALO + g, ROWS), :] = own[rows_of(OWN_LAB0 + g, ROWS), :]
    fill_halo(fields, near, corner_near, lambda k: HALO + CX + k, 1.0)
    for m in range(LABELS):
        for e in range(6):
            table[pl.ds(m * 6 + e, 1), :] = jnp.full((1, NZ), stiffness[m, e], F32)

    def whole(ref):
        return Split(0, None, ref)

    grid = Stencil(
        lambda m, e: stiffness[m, e], whole(fields), whole(coeff), whole(total), whole(scale), whole(flux)
    )
    grid.coefficients(range(HALO, PX))
    grid.weights(range(HALO + 1, PX - 1))
    grid.sweep(range(HALO + 1, PX - 1), whole(fields), whole(flux), whole(first), whole(flux_first))
    grid.sweep(range(HALO + 2, PX - 2), whole(first), whole(flux_first), whole(second), whole(flux_second))
    remainder = grid.remainder(HALO + 3, whole(second), whole(flux_second))
    for c in range(3):
        last[rows_of(c, CY), :] = remainder[c]


def far_part(
    far, corner, corner_near, limit, ribbon, cells, mult, at_depth,
    near_fields, near_coeff, near_total, near_scale, near_flux,
    near_first, near_flux_first, near_second, near_flux_second, table, last,
    message, second, updated,
    fields, coeff, total, scale, flux, first, flux_first, flux_second, coarse,
):
    inside = is_inside()
    flip = odd("gx")
    sign = jnp.where(flip == 1, -1.0, 1.0).astype(F32)
    fill_halo(fields, far, corner, lambda k: HALO - 1 - k, inside)
    v0, flux0 = Split(HALO, fields, near_fields), Split(HALO, flux, near_flux)
    v1, flux1 = Split(HALO + 1, first, near_first), Split(HALO + 1, flux_first, near_flux_first)
    v2, flux2 = Split(HALO + 2, second, near_second), Split(HALO + 2, flux_second, near_flux_second)
    grid = Stencil(
        lambda m, e: table[pl.ds(m * 6 + e, 1), :],
        v0,
        Split(HALO, coeff, near_coeff),
        Split(HALO + 1, total, near_total),
        Split(HALO + 1, scale, near_scale),
        flux0,
    )
    grid.coefficients(range(HALO))
    grid.weights(range(1, HALO + 1))
    grid.sweep(range(1, HALO + 1), v0, flux0, v1, flux1, inside)
    grid.sweep(range(2, HALO + 2), v1, flux1, v2, flux2, inside)
    used = slot_number().astype(F32) < limit[...] - 0.5
    column = cells[...] // NZ
    block = CX * CY
    left = []
    for c in range(3):
        v = [grid.get(v2, c, HALO - 1 + i)[:CY] for i in range(CX + 2)]
        jumps = [v[1 + g] - jnp.where(flip == 1, v[g], v[2 + g]) for g in range(CX)]
        left.append(jnp.concatenate(pieces_of(jnp.concatenate(jumps, axis=0)), axis=1))
    left = jnp.concatenate(left, axis=0)
    for j in range(SLOT_ROWS // 2):
        right = at_depth[:, pl.ds(256 * j, 256)]
        picked = jnp.dot(left, jnp.concatenate([right] * 3, axis=0), preferred_element_type=F32)
        at_column = lax.broadcasted_iota(jnp.int32, (block, 256), 0) == paired(column, j)
        for c in range(3):
            jump = jnp.sum(
                jnp.where(at_column, picked[c * block : (c + 1) * block], 0.0), axis=0, keepdims=True
            )
            for i in range(2):
                at = 2 * j + i
                old = mult[c, at : at + 1, :]
                new = old + PENALTY * jump[:, i * 128 : (i + 1) * 128]
                updated[c, at : at + 1, :] = jnp.where(used[at : at + 1], new, old)
    remainders = [grid.remainder(HALO + g, v2, flux2) for g in range(CX - 1)]
    remainders.append([last[rows_of(c, CY), :] for c in range(3)])

    mine = limit[:1]
    theirs = jnp.where(flip == 1, corner_near[pl.ds(CORNER, 1), :], corner[pl.ds(CORNER, 1), :])
    live = []
    for i in range(CX + 1):
        if i == 0:
            top = jnp.where(flip == 1, mine, theirs)
        elif i == CX:
            top = jnp.where(flip == 1, theirs, mine)
        else:
            top = mine
        number = ribbon[3, rows_of(i + flip, CY), :]
        live.append((number > 0.5) & (number < top + 0.5))
    for c in range(3):
        planes = [grid.get(v2, c, HALO - 1 + i)[:CY] for i in range(CX + 2)]
        pushed = []
        for i in range(CX + 1):
            jump = sign * (planes[i] - planes[i + 1])
            at = rows_of(i + flip, CY)
            pushed.append(jnp.where(live[i], ribbon[c, at, :] + PENALTY * jump, 0.0))
        parts = [remainders[g][c] - sign * (pushed[g + 1] - pushed[g]) for g in range(CX)]
        for half in range(2):
            coarse[rows_of(half * 3 + c, CY), :] = parts[2 * half] + parts[2 * half + 1]

    pairs = []
    for half in range(2):
        at = 3 * half * CY
        rows = coarse[pl.ds(at, 3 * CY // 2, stride=2), :] + coarse[pl.ds(at + 1, 3 * CY // 2, stride=2), :]
        pairs.append(rows)
    low_x = jnp.where(flip == 1, pairs[1], pairs[0])
    high_x = jnp.where(flip == 1, pairs[0], pairs[1])
    even_lane = lax.rem(lax.broadcasted_iota(jnp.int32, (1, NZ), 1), 2) == 0
    out = jnp.where(even_lane, low_x + pltpu.roll(low_x, NZ - 1, 1), high_x + pltpu.roll(high_x, 1, 1))
    for s in range(N_GY):
        message[s] = out


def finish(
    updated, low, high, gathered,
    smoothed_out, updated_out, coarse_out,
    coarse, turned, done,
):
    flip = odd("gx")
    split = Split(HALO + 2, low, high)
    copies = [pltpu.make_async_copy(updated, updated_out, done.at[0])]
    for c in range(3):
        for g in range(CX):
            x = g + flip * (CX - 1 - 2 * g)
            ref, at = split.of(c, HALO + g)
            copies.append(
                pltpu.make_async_copy(
                    ref.at[pl.ds(at.start, CY), :], smoothed_out.at[rows_of(c * CX + x, CY), :],
                    done.at[1 + c * CX + g],
                )
            )
    for copy in copies:
        copy.start()
    for c in range(3):
        parts = [gathered[s, pl.ds(c * CY // 2, CY // 2), :] for s in range(N_GY)]
        turned[c] = jnp.transpose(jnp.concatenate(parts, axis=0))
        for x in range(CX // 2):
            coarse[c, pl.ds(x * NZ // 2, NZ // 2), :] = turned[c, pl.ds(x, NZ // 2, stride=2), :]
        copies.append(pltpu.make_async_copy(coarse.at[c], coarse_out.at[c], done.at[1 + 3 * CX + c]))
        copies[-1].start()
    for copy in copies:
        copy.wait()


def in_hbm(array):
    return pltpu.with_memory_space_constraint(array, pltpu.HBM)


def call(kernel, outs, ins, out_specs=None, scratch=(), flops=1000):
    return pl.pallas_call(
        kernel,
        out_shape=outs,
        in_specs=ins,
        out_specs=out_specs or [VMEM] * len(outs),
        scratch_shapes=list(scratch),
        compiler_params=PARAMS,
        cost_estimate=pl.CostEstimate(flops=flops, bytes_accessed=1000, transcendentals=0),
    )


def pair(n):
    return [(i, i ^ 1) for i in range(n)]


def other_x():
    out = []
    for i in range(N_GX):
        for j in range(N_GY):
            partner = (i, j ^ 1) if i in (0, N_GX - 1) else (((i + 1) ^ 1) - 1, j)
            out.append((i * N_GY + j, partner[0] * N_GY + partner[1]))
    return out


def other_y():
    out = []
    for i in range(N_GX):
        for j in range(N_GY):
            partner = (i ^ 1, j) if j in (0, N_GY - 1) else (i, ((j + 1) ^ 1) - 1)
            out.append((i * N_GY + j, partner[0] * N_GY + partner[1]))
    return out


def body(displacement, rhs, labels, stiffness, rows, counts, multipliers):
    block = CX * CY
    copies = 2 + 7 * CX
    slots = jax.ShapeDtypeStruct((SLOT_ROWS, 128), jnp.int32)
    y_other, own, raw_cells, mult = call(
        pack_first,
        [f32(HALO, OWN, NZ), f32(ROOM * CY, NZ), slots, f32(3, SLOT_ROWS, 128)],
        [HBM] * 5,
        scratch=[pltpu.VMEM((block, NZ), jnp.int32), pltpu.SemaphoreType.DMA((copies,))],
    )(
        in_hbm(displacement.reshape(3 * block, NZ)),
        in_hbm(rhs.reshape(3 * block, NZ)),
        in_hbm(labels.reshape(block, NZ)),
        in_hbm(rows.reshape(SLOT_ROWS, 128)),
        in_hbm(multipliers.reshape(3, SLOT_ROWS, 128)),
    )
    y_other = lax.ppermute(y_other, ("gx", "gy"), other_y())
    side = f32(SIDE * CY + IFACE, NZ)
    far, near, cells = call(pack_sides, [side, side, slots], [VMEM] * 3)(own, raw_cells, mult)
    near = lax.ppermute(near, "gx", pair(N_GX))
    far = lax.ppermute(far, ("gx", "gy"), other_x())
    (y_pair,) = call(pack_pair, [f32(HALO, OWN, NZ)], [VMEM] * 2)(own, near)
    y_pair = lax.ppermute(y_pair, "gy", pair(N_GY))
    (dense,) = call(spread_own, [f32(4, block, NZ)], [VMEM] * 2)(cells, mult)
    (at_depth,) = call(depth_table, [jax.ShapeDtypeStruct((NZ, 8 * 128), BF16)], [VMEM], flops=5 * 10**9)(cells)
    (inner,) = call(pack_wide, [f32(ROOM * ROWS, NZ)], [VMEM], flops=5 * 10**9)(own)
    tile = f32(CORNER + SLOT_ROWS, NZ)
    corner, corner_near, own, limit = call(
        pack_second, [tile, tile, f32(ROOM * ROWS, NZ), f32(SLOT_ROWS, NZ)], [VMEM, VMEM, SMEM, VMEM, VMEM]
    )(y_other, y_pair, counts, inner, dense)
    corner = lax.ppermute(corner, ("gx", "gy"), other_x())
    corner_near = lax.ppermute(corner_near, "gx", pair(N_GX))
    three, six = f32(3 * PX * ROWS, NZ), f32(6 * PX * ROWS, NZ)
    arrays = [f32(FIELDS * ROWS + SPARE, NZ), six, six] + [three] * 6
    half = call(
        near_part, arrays + [f32(LABELS * 6, NZ), f32(3 * CY, NZ)], [SMEM, VMEM, VMEM, VMEM]
    )(stiffness, own, near, corner_near)
    (ribbon,) = call(spread_before, [f32(4, (CX + 2) * CY, NZ)], [VMEM] * 4)(far, near, dense, half[-1])
    message, low, updated = call(
        far_part,
        [f32(N_GY, 3 * CY // 2, NZ), three, f32(3, SLOT_ROWS, 128)],
        [VMEM] * (8 + len(half)),
        scratch=[pltpu.VMEM(a.shape, F32) for a in arrays[:-1]] + [pltpu.VMEM((6 * CY, NZ), F32)],
    )(far, corner, corner_near, limit, ribbon, cells, mult, at_depth, *half)
    gathered = lax.all_to_all(message, "gy", 0, 0)
    smoothed, updated, coarse = call(
        finish,
        [pltpu.HBM(s, F32) for s in ((3 * block, NZ), (3, SLOT_ROWS, 128), (3, CX // 2 * NZ // 2, NY // 2))],
        [VMEM] * 4,
        out_specs=[HBM] * 3,
        scratch=[
            pltpu.VMEM((3, CX // 2 * NZ // 2, NY // 2), F32),
            pltpu.VMEM((3, NZ, NY // 2), F32),
            pltpu.SemaphoreType.DMA((4 + 3 * CX,)),
        ],
    )(updated, low, half[7], gathered)
    coarse = jnp.swapaxes(coarse.reshape(3, CX // 2, NZ // 2, NY // 2), 2, 3)
    return (smoothed.reshape(3, CX, CY, NZ), coarse, updated.reshape(3, 1, 1, SLOTS))


def solution(mesh):
    return jax.shard_map(
        body,
        mesh=mesh,
        in_specs=(
            P(None, "gx", "gy", None),
            P(None, "gx", "gy", None),
            P("gx", "gy", None),
            P(),
            P("gx", "gy", None),
            P("gx", "gy"),
            P(None, "gx", "gy", None),
        ),
        out_specs=(P(None, "gx", "gy", None), P(None, "gx", None, None), P(None, "gx", "gy", None)),
        check_vma=False,
    )
```

```python
import jax
import jax.numpy as jnp
from jax import lax
from jax.experimental import pallas as pl
from jax.experimental.pallas import tpu as pltpu
from jax.sharding import PartitionSpec as P

SYMMETRIC_INDEX = ((0, 3, 4), (3, 1, 5), (4, 5, 2))
DAMPING = 0.6
MASS_SHIFT = 1.0
PENALTY = 1.0

CX, CY, NZ, SLOTS = 4, 32, 128, 1024
N_GX, N_GY = 32, 8
NX, NY = CX * N_GX, CY * N_GY
LABELS = 8
HALO = 3
PX = CX + 2 * HALO
PR = PX - 2
ROWS = 40
LAB0 = 3 * PX
RHS0 = LAB0 + PX
FIELDS = RHS0 + 3 * PR
OWN_LAB0 = 3 * CX
OWN_RHS0 = OWN_LAB0 + CX
OWN = OWN_RHS0 + 3 * CX
ROOM = 32
SPARE = 8
Y_ROWS = HALO * OWN_RHS0 + (HALO - 1) * OWN_RHS0
SIDE = 3 * HALO + HALO + 3 * (HALO - 1)
SLOT_ROWS = SLOTS // 128
IFACE = 4 * SLOT_ROWS
CORNER = 2 * (4 * HALO * HALO + 3 * (HALO - 1) ** 2)
VMEM = pl.BlockSpec(memory_space=pltpu.VMEM)
SMEM = pl.BlockSpec(memory_space=pltpu.SMEM)
HBM = pl.BlockSpec(memory_space=pltpu.HBM)
F32 = jnp.float32
BF16 = jnp.bfloat16
PARAMS = pltpu.CompilerParams(vmem_limit_bytes=32 * 1024 * 1024)


def f32(*shape):
    return jax.ShapeDtypeStruct(shape, F32)


def pieces_of(value):
    high = value.astype(BF16)
    rest = value - high.astype(F32)
    middle = rest.astype(BF16)
    low = (rest - middle.astype(F32)).astype(BF16)
    return (high, middle, low)


def odd(axis):
    return lax.rem(lax.axis_index(axis), 2)


def rows_of(j, height):
    return pl.ds(j * height if isinstance(j, int) else pl.multiple_of(j * height, height), height)


def corner_rows():
    at = 0
    for place in range(SIDE):
        depth = HALO if place < 4 * HALO else HALO - 1
        yield place, at, depth
        at += 2 * depth


def sent_planes():
    place = 0
    for first, depth in [(c * CX, HALO) for c in range(3)] + [(OWN_LAB0, HALO)] + [
        (OWN_RHS0 + c * CX, HALO - 1) for c in range(3)
    ]:
        for k in range(depth):
            yield place, first, k
            place += 1


def halo_planes():
    place = 0
    for first, depth in [(c * PX, HALO) for c in range(3)] + [(LAB0, HALO)] + [
        (RHS0 + c * PR - 1, HALO - 1) for c in range(3)
    ]:
        for k in range(depth):
            yield place, first, k
            place += 1


def slot_number():
    return lax.broadcasted_iota(jnp.int32, (SLOT_ROWS, 128), 0) * 128 + lax.broadcasted_iota(
        jnp.int32, (SLOT_ROWS, 128), 1
    )


def y_planes():
    for k in range(HALO):
        yield k * OWN_RHS0, 0, OWN_RHS0, k
    for k in range(HALO - 1):
        yield (HALO + k) * OWN_RHS0, OWN_RHS0, OWN - OWN_RHS0, k


def pack_y(own, out, low_face):
    for at, plane, n, k in y_planes():
        depth = HALO if plane == 0 else HALO - 1
        first = own[pl.ds(plane * CY + k, n, stride=CY), :]
        last = own[pl.ds(plane * CY + CY - depth + k, n, stride=CY), :]
        out[pl.ds(at, n), :] = jnp.where(low_face, first, last)


def pack_first(
    disp, rhs, labels, cells_in, mult_in,
    y_other, own, cells, mult,
    raw_labels, arrived,
):
    flip = odd("gx")
    pairs = []
    for g in range(CX):
        x = g + flip * (CX - 1 - 2 * g)
        pairs.append((labels.at[rows_of(x, CY)], raw_labels.at[rows_of(g, CY)]))
        for c in range(3):
            pairs.append((disp.at[rows_of(c * CX + x, CY)], own.at[rows_of(c * CX + g, CY)]))
            pairs.append((rhs.at[rows_of(c * CX + x, CY)], own.at[rows_of(OWN_RHS0 + c * CX + g, CY)]))
    pairs += [(cells_in, cells), (mult_in, mult)]
    copies = [pltpu.make_async_copy(a, b, arrived.at[i]) for i, (a, b) in enumerate(pairs)]
    for copy in copies:
        copy.start()
    for copy in copies:
        copy.wait()
    own[pl.ds(OWN_LAB0 * CY, CX * CY), :] = raw_labels[...].astype(F32)
    up = odd("gy") == 0
    pack_y(own, y_other, up)


def pack_sides(own, raw_cells, mult, far, near, cells):
    flip = odd("gx")
    block_plane = raw_cells[...] // (CY * NZ)
    turned = raw_cells[...] + flip * (CX - 1 - 2 * block_plane) * (CY * NZ)
    cells[...] = turned
    for place, first, k in sent_planes():
        far[rows_of(place, CY), :] = own[rows_of(first + k, CY), :]
        near[rows_of(place, CY), :] = own[rows_of(first + CX - 1 - k, CY), :]
    for side in (far, near):
        side[pl.ds(SIDE * CY, SLOT_ROWS), :] = turned.astype(F32)
        for c in range(3):
            side[pl.ds(SIDE * CY + (1 + c) * SLOT_ROWS, SLOT_ROWS), :] = mult[c]


def pack_pair(own, near, y_pair):
    up = odd("gy") == 0
    pack_y(own, y_pair, jnp.logical_not(up))


def reach():
    here = lax.axis_index("gy")
    return (
        jnp.where(here > 0, 1.0, 0.0).astype(F32),
        jnp.where(here < N_GY - 1, 1.0, 0.0).astype(F32),
    )


def pack_wide(own, wide):
    for j in range(OWN):
        wide[pl.ds(j * ROWS, CY), :] = own[rows_of(j, CY), :]
        wide[pl.ds(j * ROWS + CY, ROWS - CY), :] = jnp.zeros((ROWS - CY, NZ), F32)


def pack_second(y_other, y_pair, count, inner, dense, corner_far, corner_near, wide, limit):
    low, high = reach()
    up = odd("gy") == 0
    wide[pl.ds(0, OWN * ROWS), :] = inner[pl.ds(0, OWN * ROWS), :]
    for at, plane, n, k in y_planes():
        depth = HALO if plane == 0 else HALO - 1
        one, two = y_pair[pl.ds(at, n), :], y_other[pl.ds(at, n), :]
        wide[pl.ds(plane * ROWS + CY + k, n, stride=ROWS), :] = high * jnp.where(up, one, two)
        wide[pl.ds(plane * ROWS + ROWS - depth + k, n, stride=ROWS), :] = low * jnp.where(up, two, one)
    live = jnp.full((SLOT_ROWS, 128), count[0, 0].astype(F32), F32)
    limit[...] = live
    planes = list(sent_planes())
    for corner, turn in ((corner_far, False), (corner_near, True)):
        for place, at, depth in corner_rows():
            first, k = planes[place][1:]
            base = (first + (CX - 1 - k if turn else k)) * ROWS
            corner[pl.ds(at, depth), :] = wide[pl.ds(base + CY, depth), :]
            corner[pl.ds(at + depth, depth), :] = wide[pl.ds(base + ROWS - depth, depth), :]
        corner[pl.ds(CORNER, SLOT_ROWS), :] = live


def paired(array, j):
    return jnp.concatenate([array[2 * j : 2 * j + 1], array[2 * j + 1 : 2 * j + 2]], axis=1)


def spread(cells, mult, first, columns):
    column = cells // NZ - first
    depth = cells % NZ
    total = jnp.zeros((11 * columns, NZ), F32)
    parts = [piece for c in range(3) for piece in pieces_of(mult[c])]
    parts += pieces_of((slot_number() + 1).astype(F32))[:2]
    for j in range(SLOT_ROWS // 2):
        at_column = lax.broadcasted_iota(jnp.int32, (columns, 256), 0) == paired(column, j)
        at_depth = lax.broadcasted_iota(jnp.int32, (NZ, 256), 0) == paired(depth, j)
        left = [jnp.where(at_column, paired(piece.astype(F32), j), 0.0).astype(BF16) for piece in parts]
        total = total + lax.dot_general(
            jnp.concatenate(left, axis=0),
            jnp.where(at_depth, 1.0, 0.0).astype(BF16),
            (((1,), (1,)), ((), ())),
            preferred_element_type=F32,
        )
    part = [total[i * columns : (i + 1) * columns] for i in range(11)]
    return [part[3 * c] + part[3 * c + 1] + part[3 * c + 2] for c in range(3)] + [part[9] + part[10]]


def depth_table(cells, at_depth):
    depth = cells[...] % NZ
    for j in range(SLOT_ROWS // 2):
        hit = lax.broadcasted_iota(jnp.int32, (NZ, 256), 0) == paired(depth, j)
        at_depth[:, pl.ds(256 * j, 256)] = jnp.where(hit, 1.0, 0.0).astype(BF16)


def spread_own(cells, mult, dense):
    values = spread(cells[...], [mult[c] for c in range(3)], 0, CX * CY)
    for i in range(4):
        dense[i] = values[i]


def is_inside():
    here = lax.axis_index("gx")
    return jnp.where((here > 0) & (here < N_GX - 1), 1.0, 0.0).astype(F32)


def spread_before(far, near, dense, last, ribbon):
    flip = odd("gx")

    def at(i):
        a = far[pl.ds(SIDE * CY + i * SLOT_ROWS, SLOT_ROWS), :]
        b = near[pl.ds(SIDE * CY + i * SLOT_ROWS, SLOT_ROWS), :]
        return jnp.where(flip == 1, b, a)

    values = spread(at(0).astype(jnp.int32), [at(1 + c) for c in range(3)], flip * (CX - 1) * CY, CY)
    values[3] = values[3] * jnp.where(flip == 1, 1.0, is_inside())
    for i in range(4):
        ribbon[i, pl.ds(0, CY), :] = values[i]
        ribbon[i, pl.ds(CY, CX * CY), :] = dense[i]
        ribbon[i, pl.ds((CX + 1) * CY, CY), :] = values[i]


def times(k, v):
    return [
        k[SYMMETRIC_INDEX[c][0]] * v[0] + k[SYMMETRIC_INDEX[c][1]] * v[1] + k[SYMMETRIC_INDEX[c][2]] * v[2]
        for c in range(3)
    ]


class Split:
    def __init__(self, at, low, high):
        self.at, self.low, self.high = at, low, high

    def of(self, c, p, count=PX, base=0):
        ref = self.low if p < self.at else self.high
        return ref, rows_of(base + c * count + p, ROWS)


class Stencil:
    def __init__(self, entry, fields, coeff, total, scale, flux):
        self.entry, self.fields, self.coeff, self.total, self.scale, self.flux = (
            entry, fields, coeff, total, scale, flux
        )
        lane = lax.broadcasted_iota(jnp.int32, (1, NZ), 1)
        self.not_first = jnp.where(lane == 0, 0.0, 0.5)
        self.not_last = jnp.where(lane == NZ - 1, 0.0, 0.5)
        self.ends = jnp.where((lane == 0) | (lane == NZ - 1), 16.0, 0.0)
        row = lax.broadcasted_iota(jnp.int32, (ROWS, NZ), 0)
        y = lax.axis_index("gy") * CY + jnp.where(row < CY + HALO, row, row - ROWS)
        self.row_inside = (y >= 0) & (y < NY) & ((row < CY + HALO) | (row >= ROWS - HALO))

    def get(self, split, c, p):
        ref, at = split.of(c, p)
        return ref[at, :]

    def put(self, split, c, p, value):
        ref, at = split.of(c, p)
        ref[at, :] = value

    def label(self, p):
        ref, at = self.fields.of(0, p, base=LAB0)
        return ref[at, :]

    def right_side(self, c, p):
        ref, at = self.fields.of(c, p, count=PR, base=RHS0 - 1)
        return ref[at, :]

    def summed(self, split, c, p, edge=None):
        f = self.get(split, c, p)
        f = (f + f) + (self.get(split, c, p - 1) + self.get(split, c, p + 1))
        f = (f + f) + (pltpu.roll(f, 1, 0) + pltpu.roll(f, ROWS - 1, 0))
        f = f + (pltpu.roll(f, 1, 1) * self.not_first + pltpu.roll(f, NZ - 1, 1) * self.not_last)
        if edge is not None:
            f = f + self.ends * (0.5 * edge)
        return f

    def coefficients(self, planes):
        for p in planes:
            label = self.label(p)
            k = [jnp.broadcast_to(self.entry(0, e), label.shape) for e in range(6)]
            for m in range(1, LABELS):
                at = label == float(m)
                k = [jnp.where(at, self.entry(m, e), k[e]) for e in range(6)]
            for e in range(6):
                self.put(self.coeff, e, p, k[e])
            self.push(self.flux, p, [self.get(self.fields, c, p) for c in range(3)])

    def weights(self, planes):
        for p in planes:
            for e in range(6):
                k = self.get(self.coeff, e, p)
                around = self.summed(self.coeff, e, p, self.entry(0, e))
                self.put(self.total, e, p, 32.0 * k + around)
                if e < 3:
                    self.put(self.scale, e, p, DAMPING / (MASS_SHIFT + 6.0 * k + 0.25 * around))

    def push(self, flux, p, v):
        pushed = times([self.get(self.coeff, e, p) for e in range(6)], v)
        for c in range(3):
            self.put(flux, c, p, pushed[c])

    def image(self, p, v_split, flux):
        v = [self.get(v_split, c, p) for c in range(3)]
        k = [self.get(self.coeff, e, p) for e in range(6)]
        m = [self.get(self.total, e, p) for e in range(6)]
        around = [self.summed(v_split, c, p) for c in range(3)]
        pushed = [self.summed(flux, c, p) for c in range(3)]
        mine, theirs = times(m, v), times(k, around)
        return v, [MASS_SHIFT * v[c] + 0.25 * (mine[c] - theirs[c] - pushed[c]) for c in range(3)]

    def sweep(self, planes, v_split, flux, to, to_flux, inside=None):
        for p in planes:
            keep = self.row_inside if p >= HALO else self.row_inside & (inside > 0.5)
            v, a = self.image(p, v_split, flux)
            new = []
            for c in range(3):
                value = v[c] + (self.right_side(c, p) - a[c]) * self.get(self.scale, c, p)
                value = jnp.where(keep, value, 0.0)
                self.put(to, c, p, value)
                new.append(value)
            self.push(to_flux, p, new)

    def remainder(self, p, v_split, flux):
        a = self.image(p, v_split, flux)[1]
        return [(self.right_side(c, p) - a[c])[:CY] for c in range(3)]


def fill_halo(fields, side, corner, plane_of, inside):
    tiles = {place: (at, depth) for place, at, depth in corner_rows()}
    for place, base, k in halo_planes():
        plane = (base + plane_of(k)) * ROWS
        at, depth = tiles[place]
        fields[pl.ds(plane, CY), :] = inside * side[rows_of(place, CY), :]
        fields[pl.ds(plane + CY, ROWS - CY), :] = jnp.zeros((ROWS - CY, NZ), F32)
        fields[pl.ds(plane + CY, depth), :] = inside * corner[pl.ds(at, depth), :]
        fields[pl.ds(plane + ROWS - depth, depth), :] = inside * corner[pl.ds(at + depth, depth), :]


def near_part(
    stiffness, own, near, corner_near,
    fields, coeff, total, scale, flux, first, flux_first, second, flux_second, table, last,
):
    for c in range(3):
        for g in range(CX):
            fields[rows_of(c * PX + HALO + g, ROWS), :] = own[rows_of(c * CX + g, ROWS), :]
            fields[rows_of(RHS0 - 1 + c * PR + HALO + g, ROWS), :] = own[rows_of(OWN_RHS0 + c * CX + g, ROWS), :]
    for g in range(CX):
        fields[rows_of(LAB0 + HALO + g, ROWS), :] = own[rows_of(OWN_LAB0 + g, ROWS), :]
    fill_halo(fields, near, corner_near, lambda k: HALO + CX + k, 1.0)
    for m in range(LABELS):
        for e in range(6):
            table[pl.ds(m * 6 + e, 1), :] = jnp.full((1, NZ), stiffness[m, e], F32)

    def whole(ref):
        return Split(0, None, ref)

    grid = Stencil(
        lambda m, e: stiffness[m, e], whole(fields), whole(coeff), whole(total), whole(scale), whole(flux)
    )
    grid.coefficients(range(HALO, PX))
    grid.weights(range(HALO + 1, PX - 1))
    grid.sweep(range(HALO + 1, PX - 1), whole(fields), whole(flux), whole(first), whole(flux_first))
    grid.sweep(range(HALO + 2, PX - 2), whole(first), whole(flux_first), whole(second), whole(flux_second))
    remainder = grid.remainder(HALO + 3, whole(second), whole(flux_second))
    for c in range(3):
        last[rows_of(c, CY), :] = remainder[c]


def far_part(
    far, corner, corner_near, limit, ribbon, cells, mult, at_depth,
    near_fields, near_coeff, near_total, near_scale, near_flux,
    near_first, near_flux_first, near_second, near_flux_second, table, last,
    message, second, updated,
    fields, coeff, total, scale, flux, first, flux_first, flux_second, coarse,
):
    inside = is_inside()
    flip = odd("gx")
    sign = jnp.where(flip == 1, -1.0, 1.0).astype(F32)
    fill_halo(fields, far, corner, lambda k: HALO - 1 - k, inside)
    v0, flux0 = Split(HALO, fields, near_fields), Split(HALO, flux, near_flux)
    v1, flux1 = Split(HALO + 1, first, near_first), Split(HALO + 1, flux_first, near_flux_first)
    v2, flux2 = Split(HALO + 2, second, near_second), Split(HALO + 2, flux_second, near_flux_second)
    grid = Stencil(
        lambda m, e: table[pl.ds(m * 6 + e, 1), :],
        v0,
        Split(HALO, coeff, near_coeff),
        Split(HALO + 1, total, near_total),
        Split(HALO + 1, scale, near_scale),
        flux0,
    )
    grid.coefficients(range(HALO))
    grid.weights(range(1, HALO + 1))
    grid.sweep(range(1, HALO + 1), v0, flux0, v1, flux1, inside)
    grid.sweep(range(2, HALO + 2), v1, flux1, v2, flux2, inside)
    used = slot_number().astype(F32) < limit[...] - 0.5
    column = cells[...] // NZ
    block = CX * CY
    left = []
    for c in range(3):
        v = [grid.get(v2, c, HALO - 1 + i)[:CY] for i in range(CX + 2)]
        jumps = [v[1 + g] - jnp.where(flip == 1, v[g], v[2 + g]) for g in range(CX)]
        left.append(jnp.concatenate(pieces_of(jnp.concatenate(jumps, axis=0)), axis=1))
    left = jnp.concatenate(left, axis=0)
    for j in range(SLOT_ROWS // 2):
        right = at_depth[:, pl.ds(256 * j, 256)]
        picked = jnp.dot(left, jnp.concatenate([right] * 3, axis=0), preferred_element_type=F32)
        at_column = lax.broadcasted_iota(jnp.int32, (block, 256), 0) == paired(column, j)
        for c in range(3):
            jump = jnp.sum(
                jnp.where(at_column, picked[c * block : (c + 1) * block], 0.0), axis=0, keepdims=True
            )
            for i in range(2):
                at = 2 * j + i
                old = mult[c, at : at + 1, :]
                new = old + PENALTY * jump[:, i * 128 : (i + 1) * 128]
                updated[c, at : at + 1, :] = jnp.where(used[at : at + 1], new, old)
    remainders = [grid.remainder(HALO + g, v2, flux2) for g in range(CX - 1)]
    remainders.append([last[rows_of(c, CY), :] for c in range(3)])

    mine = limit[:1]
    theirs = jnp.where(flip == 1, corner_near[pl.ds(CORNER, 1), :], corner[pl.ds(CORNER, 1), :])
    live = []
    for i in range(CX + 1):
        if i == 0:
            top = jnp.where(flip == 1, mine, theirs)
        elif i == CX:
            top = jnp.where(flip == 1, theirs, mine)
        else:
            top = mine
        number = ribbon[3, rows_of(i + flip, CY), :]
        live.append((number > 0.5) & (number < top + 0.5))
    for c in range(3):
        planes = [grid.get(v2, c, HALO - 1 + i)[:CY] for i in range(CX + 2)]
        pushed = []
        for i in range(CX + 1):
            jump = sign * (planes[i] - planes[i + 1])
            at = rows_of(i + flip, CY)
            pushed.append(jnp.where(live[i], ribbon[c, at, :] + PENALTY * jump, 0.0))
        parts = [remainders[g][c] - sign * (pushed[g + 1] - pushed[g]) for g in range(CX)]
        for half in range(2):
            coarse[rows_of(half * 3 + c, CY), :] = parts[2 * half] + parts[2 * half + 1]

    pairs = []
    for half in range(2):
        at = 3 * half * CY
        rows = coarse[pl.ds(at, 3 * CY // 2, stride=2), :] + coarse[pl.ds(at + 1, 3 * CY // 2, stride=2), :]
        pairs.append(rows)
    low_x = jnp.where(flip == 1, pairs[1], pairs[0])
    high_x = jnp.where(flip == 1, pairs[0], pairs[1])
    even_lane = lax.rem(lax.broadcasted_iota(jnp.int32, (1, NZ), 1), 2) == 0
    out = jnp.where(even_lane, low_x + pltpu.roll(low_x, NZ - 1, 1), high_x + pltpu.roll(high_x, 1, 1))
    for s in range(N_GY):
        message[s] = out


def finish(
    updated, low, high, gathered,
    smoothed_out, updated_out, coarse_out,
    coarse, turned, done,
):
    flip = odd("gx")
    split = Split(HALO + 2, low, high)
    copies = [pltpu.make_async_copy(updated, updated_out, done.at[0])]
    for c in range(3):
        for g in range(CX):
            x = g + flip * (CX - 1 - 2 * g)
            ref, at = split.of(c, HALO + g)
            copies.append(
                pltpu.make_async_copy(
                    ref.at[pl.ds(at.start, CY), :], smoothed_out.at[rows_of(c * CX + x, CY), :],
                    done.at[1 + c * CX + g],
                )
            )
    for copy in copies:
        copy.start()
    for c in range(3):
        parts = [gathered[s, pl.ds(c * CY // 2, CY // 2), :] for s in range(N_GY)]
        turned[c] = jnp.transpose(jnp.concatenate(parts, axis=0))
        for x in range(CX // 2):
            coarse[c, pl.ds(x * NZ // 2, NZ // 2), :] = turned[c, pl.ds(x, NZ // 2, stride=2), :]
        copies.append(pltpu.make_async_copy(coarse.at[c], coarse_out.at[c], done.at[1 + 3 * CX + c]))
        copies[-1].start()
    for copy in copies:
        copy.wait()


def in_hbm(array):
    return pltpu.with_memory_space_constraint(array, pltpu.HBM)


def call(kernel, outs, ins, out_specs=None, scratch=(), flops=1000):
    return pl.pallas_call(
        kernel,
        out_shape=outs,
        in_specs=ins,
        out_specs=out_specs or [VMEM] * len(outs),
        scratch_shapes=list(scratch),
        compiler_params=PARAMS,
        cost_estimate=pl.CostEstimate(flops=flops, bytes_accessed=1000, transcendentals=0),
    )


def pair(n):
    return [(i, i ^ 1) for i in range(n)]


def other_x():
    out = []
    for i in range(N_GX):
        for j in range(N_GY):
            partner = (i, j ^ 1) if i in (0, N_GX - 1) else (((i + 1) ^ 1) - 1, j)
            out.append((i * N_GY + j, partner[0] * N_GY + partner[1]))
    return out


def other_y():
    out = []
    for i in range(N_GX):
        for j in range(N_GY):
            partner = (i ^ 1, j) if j in (0, N_GY - 1) else (i, ((j + 1) ^ 1) - 1)
            out.append((i * N_GY + j, partner[0] * N_GY + partner[1]))
    return out


def body(displacement, rhs, labels, stiffness, rows, counts, multipliers):
    block = CX * CY
    copies = 2 + 7 * CX
    slots = jax.ShapeDtypeStruct((SLOT_ROWS, 128), jnp.int32)
    y_other, own, raw_cells, mult = call(
        pack_first,
        [f32(Y_ROWS, NZ), f32(ROOM * CY, NZ), slots, f32(3, SLOT_ROWS, 128)],
        [HBM] * 5,
        scratch=[pltpu.VMEM((block, NZ), jnp.int32), pltpu.SemaphoreType.DMA((copies,))],
    )(
        in_hbm(displacement.reshape(3 * block, NZ)),
        in_hbm(rhs.reshape(3 * block, NZ)),
        in_hbm(labels.reshape(block, NZ)),
        in_hbm(rows.reshape(SLOT_ROWS, 128)),
        in_hbm(multipliers.reshape(3, SLOT_ROWS, 128)),
    )
    y_other = lax.ppermute(y_other, ("gx", "gy"), other_y())
    side = f32(SIDE * CY + IFACE, NZ)
    far, near, cells = call(pack_sides, [side, side, slots], [VMEM] * 3)(own, raw_cells, mult)
    near = lax.ppermute(near, "gx", pair(N_GX))
    far = lax.ppermute(far, ("gx", "gy"), other_x())
    (y_pair,) = call(pack_pair, [f32(Y_ROWS, NZ)], [VMEM] * 2)(own, near)
    y_pair = lax.ppermute(y_pair, "gy", pair(N_GY))
    (dense,) = call(spread_own, [f32(4, block, NZ)], [VMEM] * 2)(cells, mult)
    (at_depth,) = call(depth_table, [jax.ShapeDtypeStruct((NZ, 8 * 128), BF16)], [VMEM], flops=5 * 10**9)(cells)
    (inner,) = call(pack_wide, [f32(ROOM * ROWS, NZ)], [VMEM], flops=5 * 10**9)(own)
    tile = f32(CORNER + SLOT_ROWS, NZ)
    corner, corner_near, own, limit = call(
        pack_second, [tile, tile, f32(ROOM * ROWS, NZ), f32(SLOT_ROWS, NZ)], [VMEM, VMEM, SMEM, VMEM, VMEM]
    )(y_other, y_pair, counts, inner, dense)
    corner = lax.ppermute(corner, ("gx", "gy"), other_x())
    corner_near = lax.ppermute(corner_near, "gx", pair(N_GX))
    three, six = f32(3 * PX * ROWS, NZ), f32(6 * PX * ROWS, NZ)
    arrays = [f32(FIELDS * ROWS + SPARE, NZ), six, six] + [three] * 6
    half = call(
        near_part, arrays + [f32(LABELS * 6, NZ), f32(3 * CY, NZ)], [SMEM, VMEM, VMEM, VMEM]
    )(stiffness, own, near, corner_near)
    (ribbon,) = call(spread_before, [f32(4, (CX + 2) * CY, NZ)], [VMEM] * 4)(far, near, dense, half[-1])
    message, low, updated = call(
        far_part,
        [f32(N_GY, 3 * CY // 2, NZ), three, f32(3, SLOT_ROWS, 128)],
        [VMEM] * (8 + len(half)),
        scratch=[pltpu.VMEM(a.shape, F32) for a in arrays[:-1]] + [pltpu.VMEM((6 * CY, NZ), F32)],
    )(far, corner, corner_near, limit, ribbon, cells, mult, at_depth, *half)
    gathered = lax.all_to_all(message, "gy", 0, 0)
    smoothed, updated, coarse = call(
        finish,
        [pltpu.HBM(s, F32) for s in ((3 * block, NZ), (3, SLOT_ROWS, 128), (3, CX // 2 * NZ // 2, NY // 2))],
        [VMEM] * 4,
        out_specs=[HBM] * 3,
        scratch=[
            pltpu.VMEM((3, CX // 2 * NZ // 2, NY // 2), F32),
            pltpu.VMEM((3, NZ, NY // 2), F32),
            pltpu.SemaphoreType.DMA((4 + 3 * CX,)),
        ],
    )(updated, low, half[7], gathered)
    coarse = jnp.swapaxes(coarse.reshape(3, CX // 2, NZ // 2, NY // 2), 2, 3)
    return (smoothed.reshape(3, CX, CY, NZ), coarse, updated.reshape(3, 1, 1, SLOTS))


def solution(mesh):
    return jax.shard_map(
        body,
        mesh=mesh,
        in_specs=(
            P(None, "gx", "gy", None),
            P(None, "gx", "gy", None),
            P("gx", "gy", None),
            P(),
            P("gx", "gy", None),
            P("gx", "gy"),
            P(None, "gx", "gy", None),
        ),
        out_specs=(P(None, "gx", "gy", None), P(None, "gx", None, None), P(None, "gx", "gy", None)),
        check_vma=False,
    )
```
